32 devices in a mesh: win: 16 (over z, x, core), mlp: 2 (over y).
Axes of the slice: x: 2, y: 2, z: 4, core: 2. Of those that a mesh axis runs over, the one named last changes fastest.
Arguments:
- tokens: bfloat16 [32, 28, 28, 384], P(('win', 'mlp')), may hold values from -6 to 6
- crop_ids: int32 [32, 28, 28], P(('win', 'mlp')), may hold values from 0 to 3, as said below
- norm_gain: float32 [2, 2, 384], replicated, may hold values from 0.5 to 1.5
- norm_bias: float32 [2, 2, 384], replicated, may hold values from -2 to 2
- input_proj: bfloat16 [2, 384, 1152], replicated, may hold values from -0.3125 to 0.3125
- input_bias: float32 [2, 2, 384], replicated, may hold values from -3 to 3
- position_table: float32 [2, 169, 12], replicated, may hold values from -4 to 4
- output_proj: bfloat16 [2, 384, 384], replicated, may hold values from -1.25 to 1.25
- output_bias: float32 [2, 384], replicated, may hold values from -2 to 2
- expand_weight: bfloat16 [2, 384, 1536], P(None, None, 'mlp'), may hold values from -0.3125 to 0.3125
- expand_bias: bfloat16 [2, 1536], P(None, 'mlp'), may hold values from -3 to 3
- reduce_weight: bfloat16 [2, 1536, 384], P(None, 'mlp'), may hold values from -0.21875 to 0.21875
- reduce_bias: float32 [2, 384], replicated, may hold values from -2 to 2
- cotangent: bfloat16 [32, 28, 28, 384], P(('win', 'mlp')), may hold values from -6 to 6
Outputs:
- out: bfloat16 [32, 28, 28, 384], P(('win', 'mlp'))
- grad_tokens: bfloat16 [32, 28, 28, 384], P(('win', 'mlp'))
- grad_norm_gain: float32 [2, 2, 384], replicated
- grad_norm_bias: float32 [2, 2, 384], replicated
- grad_input_proj: float32 [2, 384, 1152], replicated
- grad_input_bias: float32 [2, 2, 384], replicated
- grad_position_table: float32 [2, 169, 12], replicated
- grad_output_proj: float32 [2, 384, 384], replicated
- grad_output_bias: float32 [2, 384], replicated
- grad_expand_weight: float32 [2, 384, 1536], P(None, None, 'mlp')
- grad_expand_bias: float32 [2, 1536], P(None, 'mlp')
- grad_reduce_weight: float32 [2, 1536, 384], P(None, 'mlp')
- grad_reduce_bias: float32 [2, 384], replicated
The draws below stay inside these ranges and needn't reach their ends.
Inputs may be any that keep to these rules, and one draw needn't show every extreme that they name: `crop_ids`: in each canvas one row cut and one column cut split the slots into four rectangles, each non-empty, carrying the ids 0, 1, 2, 3 in a drawn order; 0 marks empty slots.
All inputs are finite; a program needn't handle non-finite values.
Results may differ from the reference program's by a relative error of at most 0.02.
Values may be sent and summed in bfloat16 or wider, within the bound.
A program may use at most 256 MiB of HBM per device.

```python
import jax
import jax.numpy as jnp
from jax import lax

C = 384
HEADS = 12
HEAD_DIM = 32
FF = 1536
WIN = 7
SHIFT = 3
SIDE = 28
LAYERS = 2
SPAN = 169
CANVASES = 32


def draw_crop_ids(key, part):
    key = jax.random.fold_in(key, 7)
    row_key, col_key, order_key = jax.random.split(key, 3)
    row_cut = jax.random.randint(row_key, (CANVASES, 1, 1), 1, SIDE)
    col_cut = jax.random.randint(col_key, (CANVASES, 1, 1), 1, SIDE)
    places = jnp.arange(SIDE, dtype=jnp.int32)
    quarter = (places[None, :, None] >= row_cut).astype(jnp.int32) * 2 + (places[None, None, :] >= col_cut).astype(jnp.int32)
    ranking = jax.vmap(lambda sub_key: jax.random.permutation(sub_key, 4))(jax.random.split(order_key, CANVASES))
    ranking = ranking.astype(jnp.int32)
    picked = jnp.take_along_axis(ranking, quarter.reshape(CANVASES, SIDE * SIDE), axis=1)
    return picked.reshape(CANVASES, SIDE, SIDE).astype(jnp.int32)


def block_levels(stream_key, extent, shards, low, high):
    def one(dim, blocks):
        heights = jax.random.uniform(jax.random.fold_in(jax.random.fold_in(stream_key, 6), dim), (blocks,), jnp.float32, low / len(shards), high / len(shards))
        return jnp.repeat(jnp.exp(heights), extent[dim] // blocks).reshape((-1,) + (1,) * (len(extent) - dim - 1))

    level = one(*shards[0])
    for cut in shards[1:]:
        level = level * one(*cut)
    return level


def bell_draw(key, dims, scale, most, cuts=(), kind=jnp.bfloat16):
    drawn = scale * jax.random.normal(key, dims, jnp.float32)
    if cuts:
        drawn = drawn * block_levels(key, dims, cuts, -0.22, 0.18)
    return jnp.clip(drawn, -most, most).astype(kind)


def setup_inputs(seed: int = 0) -> dict:
    keys = jax.random.split(jax.random.key(seed), 15)
    tokens = bell_draw(keys[0], (CANVASES, SIDE, SIDE, C), 1.0, 6.0, ((0, 32),))
    crop_ids = draw_crop_ids(jax.random.fold_in(keys[14], 71), 0)
    norm_gain = jnp.clip(1.0 + 0.1 * jax.random.normal(keys[2], (LAYERS, 2, C), jnp.float32), 0.5, 1.5)
    norm_bias = bell_draw(keys[3], (LAYERS, 2, C), 0.3, 2.0, (), jnp.float32)
    input_proj = bell_draw(keys[4], (LAYERS, C, 3 * C), C ** -0.5, 0.3125)
    input_bias = bell_draw(keys[5], (LAYERS, 2, C), 0.5, 3.0, (), jnp.float32)
    position_table = bell_draw(keys[6], (LAYERS, SPAN, HEADS), 1.0, 4.0, (), jnp.float32)
    output_proj = bell_draw(keys[7], (LAYERS, C, C), (C // 16) ** -0.5, 1.25)
    output_bias = bell_draw(keys[8], (LAYERS, C), 0.3, 2.0, (), jnp.float32)
    expand_weight = bell_draw(keys[9], (LAYERS, C, FF), C ** -0.5, 0.3125, ((2, 2),))
    expand_bias = bell_draw(keys[10], (LAYERS, FF), 0.5, 3.0, ((1, 2),))
    reduce_weight = bell_draw(keys[11], (LAYERS, FF, C), (FF // 2) ** -0.5, 0.21875, ((1, 2),))
    reduce_bias = bell_draw(keys[12], (LAYERS, C), 0.3, 2.0, (), jnp.float32)
    cotangent = bell_draw(keys[13], (CANVASES, SIDE, SIDE, C), 1.0, 6.0, ((0, 32),))
    return dict(tokens=tokens, crop_ids=crop_ids, norm_gain=norm_gain, norm_bias=norm_bias, input_proj=input_proj, input_bias=input_bias, position_table=position_table, output_proj=output_proj, output_bias=output_bias, expand_weight=expand_weight, expand_bias=expand_bias, reduce_weight=reduce_weight, reduce_bias=reduce_bias, cotangent=cotangent)


epsilon = 1e-05
masked_score = -1e+30
top_precision = lax.Precision.HIGHEST

@jax.custom_vjp
def low(v):
    return lax.optimization_barrier(v.astype(jnp.bfloat16)).astype(jnp.float32)

@jax.custom_vjp
def low_back(v):
    return v

def low_keep(v):
    return (low(v), None)

def low_pass(kept, grad):
    return (grad,)

def back_keep(v):
    return (v, None)

def back_low(kept, grad):
    return (low(grad),)
low.defvjp(low_keep, low_pass)
low_back.defvjp(back_keep, back_low)

def layer_norm(values, gain, offset):
    centre = lax.optimization_barrier(jnp.mean(values, axis=-1, keepdims=True))
    centred = values - centre
    variance = lax.optimization_barrier(jnp.mean(centred * centred, axis=-1, keepdims=True))
    return centred * lax.rsqrt(variance + epsilon) * gain + offset

def relative_index():
    coords = jnp.arange(WIN * WIN, dtype=jnp.int32)
    row_pos = coords // WIN
    col_pos = coords % WIN
    delta_row = row_pos[:, None] - row_pos[None, :] + WIN - 1
    delta_col = col_pos[:, None] - col_pos[None, :] + WIN - 1
    return delta_row * (2 * WIN - 1) + delta_col

def to_windows(grid_vals):
    canvas_count, side_len = (grid_vals.shape[0], grid_vals.shape[1])
    per_side = side_len // WIN
    tail_shape = grid_vals.shape[3:]
    shaped = grid_vals.reshape((canvas_count, per_side, WIN, per_side, WIN) + tail_shape)
    shaped = jnp.swapaxes(shaped, 2, 3)
    return shaped.reshape((canvas_count, per_side * per_side, WIN * WIN) + tail_shape)

def from_windows(windows, side_len):
    per_side = side_len // WIN
    tail_shape = windows.shape[3:]
    shaped = windows.reshape((windows.shape[0], per_side, per_side, WIN, WIN) + tail_shape)
    shaped = jnp.swapaxes(shaped, 2, 3)
    return shaped.reshape((windows.shape[0], side_len, side_len) + tail_shape)

def window_keys(crop_ids, shifted):
    if shifted:
        side_len = crop_ids.shape[1]
        places = jnp.arange(side_len, dtype=jnp.int32)
        labels = (places >= side_len - WIN).astype(jnp.int32) + (places >= side_len - SHIFT).astype(jnp.int32)
        region = labels[:, None] * 3 + labels[None, :]
        rolled = jnp.roll(crop_ids, (-SHIFT, -SHIFT), axis=(1, 2))
        return to_windows(rolled * 9 + region[None])
    return to_windows(crop_ids * 9)

def attend_canvas(qkv_win, key_win, bias_heads):
    win_count = qkv_win.shape[0]
    heads_split = qkv_win.reshape(win_count, WIN * WIN, 3, HEADS, HEAD_DIM)
    queries = heads_split[:, :, 0]
    key_rows = heads_split[:, :, 1]
    value_rows = heads_split[:, :, 2]
    scores = jnp.einsum('wqhd,wkhd->whqk', queries, key_rows, precision=top_precision) * HEAD_DIM ** (-0.5) + bias_heads[None]
    allowed = key_win[:, None, :, None] == key_win[:, None, None, :]
    scores = low_back(jnp.where(allowed, scores, masked_score))
    attn_probs = low(jax.nn.softmax(scores, axis=-1))
    attended = jnp.einsum('whqk,wkhd->wqhd', attn_probs, value_rows, precision=top_precision)
    return attended.reshape(win_count, WIN * WIN, HEADS * HEAD_DIM)

def run_block(field_in, key_win, params, shifted):
    gain_pair, offset_pair, in_proj, in_bias, table_vals, out_proj, out_bias, expand_w, expand_b, reduce_w, reduce_b = params
    canvas_count, side_len, width = (field_in.shape[0], field_in.shape[1], field_in.shape[3])
    normed = low(layer_norm(field_in, gain_pair[0], offset_pair[0])).reshape(-1, width)
    bias_full = jnp.concatenate([in_bias[0], jnp.zeros_like(in_bias[0]), in_bias[1]])
    qkv_all = low(low_back(jnp.dot(normed, in_proj, precision=top_precision)) + bias_full)
    qkv_all = qkv_all.reshape(canvas_count, side_len, side_len, 3 * width)
    if shifted:
        qkv_all = jnp.roll(qkv_all, (-SHIFT, -SHIFT), axis=(1, 2))
    bias_heads = jnp.transpose(table_vals[relative_index()], (2, 0, 1))
    canvas_fn = jax.checkpoint(lambda bundle: attend_canvas(bundle[0], bundle[1], bias_heads))
    attended = lax.map(canvas_fn, (to_windows(qkv_all), key_win))
    attended = from_windows(attended, side_len)
    if shifted:
        attended = jnp.roll(attended, (SHIFT, SHIFT), axis=(1, 2))
    attended = low(low_back(attended.reshape(-1, width)))
    branch = low_back(jnp.dot(attended, out_proj, precision=top_precision)) + out_bias
    middle = field_in.reshape(-1, width) + branch
    second = low(layer_norm(middle, gain_pair[1], offset_pair[1]))
    before = low_back(jnp.dot(second, expand_w, precision=top_precision)) + expand_b
    hidden = low(jax.nn.gelu(before, approximate=False))
    result = middle + low_back(jnp.dot(hidden, reduce_w, precision=top_precision)) + reduce_b
    return result.reshape(field_in.shape)

def run_group(field_in, ids_group, params):
    first_params = tuple((member[0] for member in params))
    second_params = tuple((member[1] for member in params))
    first = run_block(field_in, window_keys(ids_group, False), first_params, False)
    return run_block(first, window_keys(ids_group, True), second_params, True)

def reference(tokens, crop_ids, norm_gain, norm_bias, input_proj, input_bias, position_table, output_proj, output_bias, expand_weight, expand_bias, reduce_weight, reduce_bias, cotangent):
    params = tuple((member.astype(jnp.float32) for member in (norm_gain, norm_bias, input_proj, input_bias, position_table, output_proj, output_bias, expand_weight, expand_bias, reduce_weight, reduce_bias)))
    group_size = 4
    group_count = tokens.shape[0] // group_size
    tok_groups = tokens.astype(jnp.float32).reshape((group_count, group_size) + tokens.shape[1:])
    id_groups = crop_ids.reshape((group_count, group_size) + crop_ids.shape[1:])
    cot_groups = cotangent.astype(jnp.float32).reshape((group_count, group_size) + cotangent.shape[1:])

    def one_group(totals, items):
        field_in, ids_group, cot_group = items
        result, pullback = jax.vjp(lambda field_arg, param_arg: run_group(field_arg, ids_group, param_arg), field_in, params)
        grad_field, grad_params = pullback(cot_group)
        totals = tuple((left_val + right_val for left_val, right_val in zip(totals, grad_params)))
        return (totals, (result, grad_field))
    zero_grads = tuple((jnp.zeros_like(member) for member in params))
    totals, (results, grad_fields) = lax.scan(one_group, zero_grads, (tok_groups, id_groups, cot_groups))
    out = results.reshape(tokens.shape).astype(jnp.bfloat16)
    grad_tokens = grad_fields.reshape(tokens.shape).astype(jnp.bfloat16)
    return (out, grad_tokens, totals[0], totals[1], totals[2], totals[3], totals[4], totals[5], totals[6], totals[7], totals[8], totals[9], totals[10])
```

```python
import functools

import jax
import jax.numpy as jnp
from jax import lax
from jax.experimental import pallas as pl
from jax.experimental.pallas import tpu as pltpu
from jax.sharding import PartitionSpec as P

HEADS = 12
HEAD_DIM = 32
WIN = 7
SHIFT = 3
SPAN_SIDE = 2 * WIN - 1

EPS = 1e-05
MASKED = -1e30

PITCH = 8
SLOTS = WIN * PITCH
GROUP = 4
GROUPS = HEADS // GROUP
GLANES = GROUP * HEAD_DIM
GQ = GROUP * SLOTS

F32 = jnp.float32
BF16 = jnp.bfloat16

ERF_P = 0.39
ERF_C = (
    0.22003399505358215,
    0.22002241291251284,
    0.20367769093249805,
    0.16514655576456758,
    0.15214218925854978,
    -0.024768996902218943,
    0.20836931643666226,
    -0.19248882577712367,
    0.04786540601145673,
)


def dot(a, b):
    return lax.dot_general(a, b, (((1,), (0,)), ((), ())), preferred_element_type=F32)


def dot_nt(a, b):
    return lax.dot_general(a, b, (((1,), (1,)), ((), ())), preferred_element_type=F32)


def dot_tn(a, b):
    return lax.dot_general(a, b, (((0,), (0,)), ((), ())), preferred_element_type=F32)


def gelu_pair(u):
    bell = jnp.exp(-0.5 * u * u)
    t = 1.0 / (1.0 + (ERF_P * 0.5**0.5) * jnp.abs(u))
    poly = jnp.full_like(u, ERF_C[-1])
    for coef in ERF_C[-2::-1]:
        poly = poly * t + coef
    tail = 0.5 * bell * t * poly
    phi = jnp.where(u < 0, tail, 1.0 - tail)
    return u * phi, phi + u * bell * (0.5 * 2**0.5 * 0.5641895835477563)


def norm_stats(v):
    centred = v - jnp.mean(v, axis=-1, keepdims=True)
    rstd = lax.rsqrt(jnp.mean(centred * centred, axis=-1, keepdims=True) + EPS)
    return centred * rstd, rstd


def norm_back(v, gain, upstream):
    xhat, rstd = norm_stats(v)
    scaled = upstream * gain
    inner = (
        scaled
        - jnp.mean(scaled, axis=-1, keepdims=True)
        - xhat * jnp.mean(scaled * xhat, axis=-1, keepdims=True)
    )
    return rstd * inner, jnp.sum(upstream * xhat, axis=0, keepdims=True), jnp.sum(upstream, axis=0, keepdims=True)


def iota(shape, dim):
    return lax.broadcasted_iota(jnp.int32, shape, dim)


def expand_heads(rows):
    head = iota(rows.shape, 1) // HEAD_DIM
    return jnp.concatenate([jnp.where(head == j, rows, 0.0) for j in range(GROUP)], axis=0).astype(BF16)


def fold_heads(rows):
    head = iota((SLOTS, GLANES), 1) // HEAD_DIM
    out = rows[:SLOTS]
    for j in range(1, GROUP):
        out = jnp.where(head == j, rows[j * SLOTS : (j + 1) * SLOTS], out)
    return out


def window_row(per_side, wr, wc, r):
    return pl.multiple_of((wr * per_side + wc) * SLOTS + r * PITCH, PITCH)


def grid_to_windows(src, side, shifted, emit):
    per_side = side // WIN

    def step(wr, carry):
        for r in range(WIN):
            row = lax.rem(wr * WIN + r + (SHIFT if shifted else 0), side)
            line = src[row].astype(F32)
            width = line.shape[1]
            line = jnp.concatenate([line, jnp.zeros((32 - side, width), F32)], axis=0)
            if shifted:
                i = iota(line.shape, 0)
                line = jnp.where(i < side - SHIFT, pltpu.roll(line, 32 - SHIFT, 0), pltpu.roll(line, side - SHIFT, 0))
            for wc in range(per_side):
                part = line if wc == 0 else pltpu.roll(line, 32 - WIN * wc, 0)
                part = part[:PITCH]
                part = jnp.where(iota(part.shape, 0) < WIN, part, 0.0)
                emit(wr, wc, r, part)
        return carry

    lax.fori_loop(0, per_side, step, 0)


def windows_to_grid(src, dst, side, shifted):
    per_side = side // WIN

    def step(wr, carry):
        for r in range(WIN):
            row = lax.rem(wr * WIN + r + (SHIFT if shifted else 0), side)
            width = src.shape[1]
            line = jnp.zeros((32, width), F32)
            i = iota(line.shape, 0)
            for wc in range(per_side):
                tile = src[pl.ds(window_row(per_side, wr, wc, r), PITCH), :]
                tile = jnp.concatenate([tile, jnp.zeros((32 - PITCH, width), F32)], axis=0)
                if wc:
                    tile = pltpu.roll(tile, WIN * wc, 0)
                line = jnp.where((i >= WIN * wc) & (i < WIN * (wc + 1)), tile, line)
            if shifted:
                line = jnp.where(i < SHIFT, pltpu.roll(line, 32 - side + SHIFT, 0), pltpu.roll(line, SHIFT, 0))
            dst[row] = line[:side].astype(dst.dtype)
        return carry

    lax.fori_loop(0, per_side, step, 0)


def regular_to_shifted(src, dst, side):
    per_side = side // WIN

    def step(wr, carry):
        below = lax.rem(wr + 1, per_side)
        for r in range(WIN):
            sr, srr = (wr, r + SHIFT) if r + SHIFT < WIN else (below, r + SHIFT - WIN)
            for wc in range(per_side):
                here = src[pl.ds(window_row(per_side, sr, wc, srr), PITCH), :]
                right = src[pl.ds(window_row(per_side, sr, (wc + 1) % per_side, srr), PITCH), :]
                i = iota(here.shape, 0)
                tile = jnp.where(
                    i < WIN - SHIFT,
                    pltpu.roll(here, PITCH - SHIFT, 0),
                    jnp.where(i < WIN, pltpu.roll(right, WIN - SHIFT, 0), 0.0),
                )
                dst[pl.ds(window_row(per_side, wr, wc, r), PITCH), :] = tile
        return carry

    lax.fori_loop(0, per_side, step, 0)


def shifted_to_regular(src, dst, side):
    per_side = side // WIN

    def step(wr, carry):
        above = lax.rem(wr + per_side - 1, per_side)
        for r in range(WIN):
            sr, srr = (wr, r - SHIFT) if r >= SHIFT else (above, r - SHIFT + WIN)
            for wc in range(per_side):
                here = src[pl.ds(window_row(per_side, sr, wc, srr), PITCH), :]
                left = src[pl.ds(window_row(per_side, sr, (wc + per_side - 1) % per_side, srr), PITCH), :]
                i = iota(here.shape, 0)
                tile = jnp.where(
                    i < SHIFT,
                    pltpu.roll(left, PITCH - (WIN - SHIFT), 0),
                    jnp.where(i < WIN, pltpu.roll(here, SHIFT, 0), 0.0),
                )
                dst[pl.ds(window_row(per_side, wr, wc, r), PITCH), :] = tile
        return carry

    lax.fori_loop(0, per_side, step, 0)


ROWS_BLOCK = 4 * SLOTS
SMALL = {"gain1": 0, "gain2": 1, "bias1": 2, "bias2": 3, "query": 4, "value": 5, "output": 6, "reduce": 7}
TABLE_ROW = 8


def kernel(
    side,
    tokens,
    ids,
    gain,
    offset,
    w_in,
    b_in,
    table,
    w_out,
    b_out,
    w_exp,
    b_exp,
    w_red,
    b_red,
    cot,
    out,
    grad_tokens,
    d_in,
    d_out,
    d_exp,
    d_red,
    small,
    d_table,
    d_bexp,
    x,
    normed,
    qkv,
    probs,
    mixed,
    mid,
    second,
    hidden,
    slope,
    keys,
    bias,
    bias_sum,
    g,
    gs,
    gz,
    gb_low,
    dqkv,
    go,
):
    per_side = side // WIN
    windows = per_side * per_side
    rows = windows * SLOTS
    blocks = rows // ROWS_BLOCK
    shards, _, width, ff = w_exp.shape
    chunk = 256 if ff % 256 == 0 else ff

    def over_blocks(body):
        def step(i, carry):
            body(pl.ds(pl.multiple_of(i * ROWS_BLOCK, ROWS_BLOCK), ROWS_BLOCK))
            return carry

        lax.fori_loop(0, blocks, step, 0)

    def over_shards(body):
        def step(i, carry):
            body(i)
            return carry

        lax.fori_loop(0, shards, step, 0)

    def put_tokens(wr, wc, r, tile):
        x[0, pl.ds(window_row(per_side, wr, wc, r), PITCH), :] = tile

    grid_to_windows(tokens, side, False, put_tokens)

    for l in range(2):
        shifted = l == 1

        def put_keys(wr, wc, r, tile, shifted=shifted):
            lane = iota(tile.shape, 1).astype(F32)
            slot = iota(tile.shape, 0)
            label = tile
            if shifted:
                row_at = wr * WIN + r
                row_label = jnp.where(row_at >= side - WIN, 1, 0) + jnp.where(row_at >= side - SHIFT, 1, 0)
                col_at = wc * WIN + slot
                col_label = jnp.where(col_at >= side - WIN, 1, 0) + jnp.where(col_at >= side - SHIFT, 1, 0)
                label = label + (12 * row_label + 4 * col_label).astype(F32)
            hot = jnp.where((lane == label) & (slot < WIN), 1.0, 0.0)
            keys[pl.ds(window_row(per_side, wr, wc, r), PITCH), :] = hot

        grid_to_windows(ids, side, shifted, put_keys)

        krow = iota((SLOTS, 128), 0)
        qlane = iota((SLOTS, 128), 1)
        ahead = (qlane & (PITCH - 1)) >= (krow & (PITCH - 1))
        for grp in range(GROUPS):
            low = jnp.zeros((SLOTS, 128), F32)
            high = jnp.zeros((SLOTS, 128), F32)
            for j in range(GROUP):
                h = grp * GROUP + j
                both = [
                    pltpu.roll(
                        jnp.broadcast_to(table[l, 2 * h + s : 2 * h + s + 1, :], (SLOTS, 128)),
                        0,
                        1,
                        stride=1,
                        stride_axis=0,
                    )
                    for s in range(2)
                ]
                one = jnp.where(ahead, both[0], both[1])
                at = j * SLOTS
                if at < 128:
                    moved = pltpu.roll(one, at, 1) if at else one
                    low = jnp.where((qlane >= at) & (qlane < at + SLOTS), moved, low)
                if at + SLOTS > 128:
                    moved = pltpu.roll(one, (at - 128) % 128, 1)
                    high = jnp.where((qlane >= at - 128) & (qlane < at - 128 + SLOTS), moved, high)
            bias[grp, :, :128] = low
            bias[grp, :, 128:] = high[:, : GQ - 128]

        bias_row = jnp.concatenate(
            [b_in[l, 0:1, :], jnp.zeros((1, width), F32), b_in[l, 1:2, :]], axis=1
        )

        def project(at, l=l, bias_row=bias_row):
            xhat, _ = norm_stats(x[l, at, :])
            a = (xhat * gain[l, 0:1, :] + offset[l, 0:1, :]).astype(BF16)
            normed[l, at, :] = a
            for c in range(3):
                cols = slice(c * width, (c + 1) * width)
                qkv[l, at, cols] = (dot(a, w_in[l, :, cols]) + bias_row[:, cols]).astype(BF16)

        over_blocks(project)

        def attend(i, carry, l=l):
            at = pl.ds(pl.multiple_of(i * 2 * SLOTS, 2 * SLOTS), 2 * SLOTS)
            q = qkv[l, at, :width].astype(F32)
            k = qkv[l, at, width : 2 * width].astype(F32)
            v = qkv[l, at, 2 * width :].astype(F32)
            hot = keys[at, :]
            parts = []
            for w in range(2):
                here = slice(w * SLOTS, (w + 1) * SLOTS)
                hot_w = hot[here]
                allowed = dot_nt(hot_w.astype(BF16), jnp.concatenate([hot_w] * GROUP, axis=0).astype(BF16)) > 0.5
                outs = []
                for grp in range(GROUPS):
                    lanes = slice(grp * GLANES, (grp + 1) * GLANES)
                    q_all = expand_heads(q[here, lanes])
                    s = dot_nt(k[here, lanes].astype(BF16), q_all) * HEAD_DIM**-0.5 + bias[grp]
                    s = jnp.where(allowed, s, MASKED)
                    e = jnp.exp(s - jnp.max(s, axis=0, keepdims=True))
                    p = e / jnp.sum(e, axis=0, keepdims=True)
                    probs[l, 2 * i + w, grp] = p
                    outs.append(fold_heads(dot_tn(p.astype(BF16), v[here, lanes].astype(BF16))))
                parts.append(jnp.concatenate(outs, axis=1))
            mixed[l, at, :] = jnp.concatenate(parts, axis=0).astype(BF16)
            return carry

        lax.fori_loop(0, windows // 2, attend, 0)

        def middle(at, l=l):
            m = x[l, at, :] + dot(mixed[l, at, :], w_out[l]) + b_out[l : l + 1, :]
            mid[l, at, :] = m
            xhat, _ = norm_stats(m)
            second[l, at, :] = (xhat * gain[l, 1:2, :] + offset[l, 1:2, :]).astype(BF16)
            gs[at, :] = m + b_red[l : l + 1, :]

        over_blocks(middle)

        def feed(at, l=l):
            s = second[l, at, :]

            def one(i):
                for c in range(0, ff, chunk):
                    cols = slice(c, c + chunk)
                    before = dot(s, w_exp[i, l, :, cols]) + b_exp[i, l : l + 1, cols]
                    value, slope_now = gelu_pair(before)
                    hidden[l, i, at, cols] = value.astype(BF16)
                    slope[l, i, at, cols] = slope_now.astype(BF16)
                gs[at, :] += dot(hidden[l, i, at, :], w_red[i, l])

            over_shards(one)

        over_blocks(feed)

        if l == 0:
            regular_to_shifted(gs, x.at[1], side)
        else:
            windows_to_grid(gs, out, side, True)

    def put_cot(wr, wc, r, tile):
        g[pl.ds(window_row(per_side, wr, wc, r), PITCH), :] = tile

    grid_to_windows(cot, side, True, put_cot)
    small[...] = jnp.zeros(small.shape, F32)
    d_bexp[...] = jnp.zeros(d_bexp.shape, F32)

    for l in (1, 0):

        def add_small(name, value, l=l):
            at = SMALL[name]
            small[l, at : at + 1, :] += value

        def feed_back(at, l=l):
            g_now = g[at, :]
            add_small("reduce", jnp.sum(g_now, axis=0, keepdims=True))
            g_low = g_now.astype(BF16)
            gz[at, :] = g_low
            gs[at, :] = jnp.zeros(g_now.shape, F32)

            def one(i):
                for c in range(0, ff, chunk):
                    cols = slice(c, c + chunk)
                    gh = dot_nt(g_low, w_red[i, l, cols, :])
                    gb = gh * slope[l, i, at, cols].astype(F32)
                    d_bexp[i, l : l + 1, cols] += jnp.sum(gb, axis=0, keepdims=True)
                    gb_low[i, at, cols] = gb.astype(BF16)
                gs[at, :] += dot_nt(gb_low[i, at, :], w_exp[i, l])

            over_shards(one)

        over_blocks(feed_back)

        def feed_weights(i, l=l):
            for c in range(0, ff, chunk):
                cols = slice(c, c + chunk)
                d_red[i, l, cols, :] = dot_tn(hidden[l, i, :, cols], gz[...]).astype(BF16)
                d_exp[i, l, :, cols] = dot_tn(second[l], gb_low[i, :, cols]).astype(BF16)

        over_shards(feed_weights)

        def middle_back(at, l=l):
            dmid, dgain, doffset = norm_back(mid[l, at, :], gain[l, 1:2, :], gs[at, :])
            add_small("gain2", dgain)
            add_small("bias2", doffset)
            gm = g[at, :] + dmid
            g[at, :] = gm
            add_small("output", jnp.sum(gm, axis=0, keepdims=True))
            low = gm.astype(BF16)
            gz[at, :] = low
            go[at, :] = dot_nt(low, w_out[l]).astype(BF16)

        over_blocks(middle_back)
        d_out[l] = dot_tn(mixed[l], gz[...]).astype(BF16)
        bias_sum[...] = jnp.zeros(bias_sum.shape, F32)

        def attend_back(i, carry, l=l):
            at = pl.ds(pl.multiple_of(i * 2 * SLOTS, 2 * SLOTS), 2 * SLOTS)
            q = qkv[l, at, :width].astype(F32)
            k = qkv[l, at, width : 2 * width].astype(F32)
            v = qkv[l, at, 2 * width :].astype(F32)
            go_now = go[at, :].astype(F32)
            made = ([], [], [])
            for w in range(2):
                here = slice(w * SLOTS, (w + 1) * SLOTS)
                for grp in range(GROUPS):
                    lanes = slice(grp * GLANES, (grp + 1) * GLANES)
                    q_all = expand_heads(q[here, lanes])
                    go_all = expand_heads(go_now[here, lanes])
                    k_low = k[here, lanes].astype(BF16)
                    dp = dot_nt(v[here, lanes].astype(BF16), go_all)
                    p = probs[l, 2 * i + w, grp]
                    ds = (p * (dp - jnp.sum(p * dp, axis=0, keepdims=True))).astype(BF16)
                    bias_sum[grp] += ds.astype(F32)
                    made[0].append(fold_heads(dot_tn(ds, k_low)) * HEAD_DIM**-0.5)
                    made[1].append(dot(ds, q_all) * HEAD_DIM**-0.5)
                    made[2].append(dot(p.astype(BF16), go_all))
            for part in range(3):
                whole = jnp.concatenate(
                    [
                        jnp.concatenate(made[part][w * GROUPS : (w + 1) * GROUPS], axis=1)
                        for w in range(2)
                    ],
                    axis=0,
                )
                if part == 0:
                    add_small("query", jnp.sum(whole, axis=0, keepdims=True))
                if part == 2:
                    add_small("value", jnp.sum(whole, axis=0, keepdims=True))
                dqkv[at, part * width : (part + 1) * width] = whole.astype(BF16)
            return carry

        lax.fori_loop(0, windows // 2, attend_back, 0)

        for c in range(3):
            cols = slice(c * width, (c + 1) * width)
            d_in[l, :, cols] = dot_tn(normed[l], dqkv[:, cols]).astype(BF16)

        krow = iota((SLOTS, 128), 0)
        qlane = iota((SLOTS, 128), 1)
        ahead = (qlane & (PITCH - 1)) >= (krow & (PITCH - 1))
        for grp in range(GROUPS):
            low = bias_sum[grp, :, :128]
            high = jnp.concatenate([bias_sum[grp, :, 128:], jnp.zeros((SLOTS, 256 - GQ), F32)], axis=1)
            for j in range(GROUP):
                h = grp * GROUP + j
                at = j * SLOTS
                if at + SLOTS <= 128:
                    one = pltpu.roll(low, 128 - at, 1) if at else low
                elif at < 128:
                    one = jnp.where(qlane < 128 - at, pltpu.roll(low, 128 - at, 1), pltpu.roll(high, 128 - at, 1))
                else:
                    one = pltpu.roll(high, (256 - at) % 128, 1)
                one = jnp.where(qlane < SLOTS, one, 0.0)
                for s in range(2):
                    picked = jnp.where(ahead if s == 0 else jnp.logical_not(ahead), one, 0.0)
                    tile = picked[:PITCH]
                    for r in range(1, WIN):
                        tile = tile + pltpu.roll(picked[r * PITCH : (r + 1) * PITCH], 128 - r * PITCH, 1)
                    for step in (1, 2, 4):
                        tile = jnp.where((iota(tile.shape, 0) & step) > 0, pltpu.roll(tile, 128 - step, 1), tile)
                    d_table[l, 2 * h + s : 2 * h + s + 1, :] = jnp.sum(tile, axis=0, keepdims=True)

        def input_back(at, l=l):
            ga = dot_nt(dqkv[at, :], w_in[l])
            dx, dgain, doffset = norm_back(x[l, at, :], gain[l, 0:1, :], ga)
            add_small("gain1", dgain)
            add_small("bias1", doffset)
            gs[at, :] = g[at, :] + dx

        over_blocks(input_back)
        if l == 1:
            shifted_to_regular(gs, g, side)
        else:
            windows_to_grid(gs, grad_tokens, side, False)


def table_lanes(table):
    layers, _, heads = table.shape
    square = table.reshape(layers, SPAN_SIDE, SPAN_SIDE, heads).transpose(0, 3, 1, 2)
    right = jnp.pad(square[..., WIN - 1 :], ((0, 0),) * 3 + ((0, PITCH - WIN),))
    left = jnp.pad(square[..., : WIN - 1], ((0, 0),) * 3 + ((PITCH - WIN + 1, 0),))
    span = SPAN_SIDE * PITCH

    def lanes(part, back):
        flat = jnp.pad(part.reshape(layers, heads, span), ((0, 0), (0, 0), (0, 128 - span)))
        return jnp.roll(flat, -back, axis=-1)

    both = jnp.stack([lanes(right, (WIN - 1) * PITCH), lanes(left, WIN * PITCH)], axis=2)
    return both.reshape(layers, 2 * heads, 128)


def lanes_table(lanes):
    layers, heads = lanes.shape[0], lanes.shape[1] // 2
    both = lanes.reshape(layers, heads, 2, 128)
    span = SPAN_SIDE * PITCH

    def square(part, back):
        return jnp.roll(part, back, axis=-1)[..., :span].reshape(layers, heads, SPAN_SIDE, PITCH)

    right = square(both[:, :, 0], (WIN - 1) * PITCH)[..., :WIN]
    left = square(both[:, :, 1], WIN * PITCH)[..., PITCH - WIN + 1 :]
    whole = jnp.concatenate([left, right], axis=-1)
    return whole.reshape(layers, heads, SPAN_SIDE * SPAN_SIDE).transpose(0, 2, 1)


def on_device(
    tokens,
    crop_ids,
    norm_gain,
    norm_bias,
    input_proj,
    input_bias,
    position_table,
    output_proj,
    output_bias,
    expand_weight,
    expand_bias,
    reduce_weight,
    reduce_bias,
    cotangent,
):
    _, side, _, width = tokens.shape
    layers, _, ff = expand_weight.shape
    w_exp = lax.all_gather(expand_weight, "mlp", axis=0)
    w_red = lax.all_gather(reduce_weight, "mlp", axis=0)
    b_exp = lax.all_gather(expand_bias, "mlp", axis=0).astype(F32)
    shards = w_exp.shape[0]
    ids = jnp.broadcast_to(crop_ids[0, :, :, None].astype(F32), (side, side, 128))
    windows = (side // WIN) ** 2
    rows = windows * SLOTS
    vmem = pl.BlockSpec(memory_space=pltpu.VMEM)
    outs = pl.pallas_call(
        functools.partial(kernel, side),
        out_shape=(
            jax.ShapeDtypeStruct(tokens.shape[1:], BF16),
            jax.ShapeDtypeStruct(tokens.shape[1:], BF16),
            jax.ShapeDtypeStruct(input_proj.shape, BF16),
            jax.ShapeDtypeStruct(output_proj.shape, BF16),
            jax.ShapeDtypeStruct(w_exp.shape, BF16),
            jax.ShapeDtypeStruct(w_red.shape, BF16),
            jax.ShapeDtypeStruct((layers, 8, width), F32),
            jax.ShapeDtypeStruct((layers, 2 * HEADS, 128), F32),
            jax.ShapeDtypeStruct(b_exp.shape, F32),
        ),
        in_specs=[vmem] * 14,
        out_specs=[vmem] * 9,
        scratch_shapes=[
            pltpu.VMEM((layers, rows, width), F32),
            pltpu.VMEM((layers, rows, width), BF16),
            pltpu.VMEM((layers, rows, 3 * width), BF16),
            pltpu.VMEM((layers, windows, GROUPS, SLOTS, GQ), F32),
            pltpu.VMEM((layers, rows, width), BF16),
            pltpu.VMEM((layers, rows, width), F32),
            pltpu.VMEM((layers, rows, width), BF16),
            pltpu.VMEM((layers, shards, rows, ff), BF16),
            pltpu.VMEM((layers, shards, rows, ff), BF16),
            pltpu.VMEM((rows, 128), F32),
            pltpu.VMEM((GROUPS, SLOTS, GQ), F32),
            pltpu.VMEM((GROUPS, SLOTS, GQ), F32),
            pltpu.VMEM((rows, width), F32),
            pltpu.VMEM((rows, width), F32),
            pltpu.VMEM((rows, width), BF16),
            pltpu.VMEM((shards, rows, ff), BF16),
            pltpu.VMEM((rows, 3 * width), BF16),
            pltpu.VMEM((rows, width), BF16),
        ],
        compiler_params=pltpu.CompilerParams(vmem_limit_bytes=64 * 1024 * 1024),
    )(
        tokens[0],
        ids,
        norm_gain,
        norm_bias,
        input_proj,
        input_bias,
        table_lanes(position_table),
        output_proj,
        output_bias,
        w_exp,
        b_exp,
        w_red,
        reduce_bias,
        cotangent[0],
    )
    out, grad_tokens, d_in, d_out, d_exp, d_red, small, d_table, d_bexp = outs
    d_in, d_out = lax.psum((d_in, d_out), ("win", "mlp"))
    small, d_table = lax.psum((small, d_table), ("win", "mlp"))
    d_exp = lax.psum(lax.psum_scatter(d_exp, "mlp", scatter_dimension=0, tiled=False), "win")
    d_red = lax.psum(lax.psum_scatter(d_red, "mlp", scatter_dimension=0, tiled=False), "win")
    d_bexp = lax.psum(lax.psum_scatter(d_bexp, "mlp", scatter_dimension=0, tiled=False), "win")
    return (
        out[None],
        grad_tokens[None],
        small[:, 0:2],
        small[:, 2:4],
        d_in.astype(F32),
        small[:, 4:6],
        lanes_table(d_table),
        d_out.astype(F32),
        small[:, 6],
        d_exp.astype(F32),
        d_bexp,
        d_red.astype(F32),
        small[:, 7],
    )


def solution(mesh):
    tokens = P(("win", "mlp"), None, None, None)
    placed = (
        tokens,
        P(("win", "mlp"), None, None),
        P(),
        P(),
        P(),
        P(),
        P(),
        P(),
        P(),
        P(None, None, "mlp"),
        P(None, "mlp"),
        P(None, "mlp", None),
        P(),
        tokens,
    )
    return jax.shard_map(
        on_device,
        mesh=mesh,
        in_specs=placed,
        out_specs=(
            tokens,
            tokens,
            P(),
            P(),
            P(),
            P(),
            P(),
            P(),
            P(),
            P(None, None, "mlp"),
            P(None, "mlp"),
            P(None, "mlp", None),
            P(),
        ),
        check_vma=False,
    )
```

```python
import functools

import jax
import jax.numpy as jnp
from jax import lax
from jax.experimental import pallas as pl
from jax.experimental.pallas import tpu as pltpu
from jax.sharding import PartitionSpec as P

HEADS = 12
HEAD_DIM = 32
WIN = 7
SHIFT = 3
SPAN_SIDE = 2 * WIN - 1

EPS = 1e-05
MASKED = -1e30

PITCH = 8
SLOTS = WIN * PITCH
GROUP = 4
GROUPS = HEADS // GROUP
GLANES = GROUP * HEAD_DIM
GQ = GROUP * SLOTS

F32 = jnp.float32
BF16 = jnp.bfloat16

ERF_P = 0.39
ERF_C = (
    0.22003399505358215,
    0.22002241291251284,
    0.20367769093249805,
    0.16514655576456758,
    0.15214218925854978,
    -0.024768996902218943,
    0.20836931643666226,
    -0.19248882577712367,
    0.04786540601145673,
)


def dot(a, b):
    return lax.dot_general(a, b, (((1,), (0,)), ((), ())), preferred_element_type=F32)


def dot_nt(a, b):
    return lax.dot_general(a, b, (((1,), (1,)), ((), ())), preferred_element_type=F32)


def dot_tn(a, b):
    return lax.dot_general(a, b, (((0,), (0,)), ((), ())), preferred_element_type=F32)


def gelu_pair(u):
    bell = jnp.exp(-0.5 * u * u)
    t = 1.0 / (1.0 + (ERF_P * 0.5**0.5) * jnp.abs(u))
    poly = jnp.full_like(u, ERF_C[-1])
    for coef in ERF_C[-2::-1]:
        poly = poly * t + coef
    tail = 0.5 * bell * t * poly
    phi = jnp.where(u < 0, tail, 1.0 - tail)
    return u * phi, phi + u * bell * (0.5 * 2**0.5 * 0.5641895835477563)


def norm_stats(v):
    centred = v - jnp.mean(v, axis=-1, keepdims=True)
    rstd = lax.rsqrt(jnp.mean(centred * centred, axis=-1, keepdims=True) + EPS)
    return centred * rstd, rstd


def norm_back(v, gain, upstream):
    xhat, rstd = norm_stats(v)
    scaled = upstream * gain
    inner = (
        scaled
        - jnp.mean(scaled, axis=-1, keepdims=True)
        - xhat * jnp.mean(scaled * xhat, axis=-1, keepdims=True)
    )
    return rstd * inner, jnp.sum(upstream * xhat, axis=0, keepdims=True), jnp.sum(upstream, axis=0, keepdims=True)


def iota(shape, dim):
    return lax.broadcasted_iota(jnp.int32, shape, dim)


def expand_heads(rows):
    head = iota(rows.shape, 1) // HEAD_DIM
    return jnp.concatenate([jnp.where(head == j, rows, 0.0) for j in range(GROUP)], axis=0).astype(BF16)


def fold_heads(rows):
    head = iota((SLOTS, GLANES), 1) // HEAD_DIM
    out = rows[:SLOTS]
    for j in range(1, GROUP):
        out = jnp.where(head == j, rows[j * SLOTS : (j + 1) * SLOTS], out)
    return out


def window_row(per_side, wr, wc, r):
    return pl.multiple_of((wr * per_side + wc) * SLOTS + r * PITCH, PITCH)


def grid_to_windows(src, side, shifted, emit):
    per_side = side // WIN

    def step(wr, carry):
        for r in range(WIN):
            row = lax.rem(wr * WIN + r + (SHIFT if shifted else 0), side)
            line = src[row].astype(F32)
            width = line.shape[1]
            line = jnp.concatenate([line, jnp.zeros((32 - side, width), F32)], axis=0)
            if shifted:
                i = iota(line.shape, 0)
                line = jnp.where(i < side - SHIFT, pltpu.roll(line, 32 - SHIFT, 0), pltpu.roll(line, side - SHIFT, 0))
            for wc in range(per_side):
                part = line if wc == 0 else pltpu.roll(line, 32 - WIN * wc, 0)
                part = part[:PITCH]
                part = jnp.where(iota(part.shape, 0) < WIN, part, 0.0)
                emit(wr, wc, r, part)
        return carry

    lax.fori_loop(0, per_side, step, 0)


def windows_to_grid(src, dst, side, shifted):
    per_side = side // WIN

    def step(wr, carry):
        for r in range(WIN):
            row = lax.rem(wr * WIN + r + (SHIFT if shifted else 0), side)
            width = src.shape[1]
            line = jnp.zeros((32, width), F32)
            i = iota(line.shape, 0)
            for wc in range(per_side):
                tile = src[pl.ds(window_row(per_side, wr, wc, r), PITCH), :]
                tile = jnp.concatenate([tile, jnp.zeros((32 - PITCH, width), F32)], axis=0)
                if wc:
                    tile = pltpu.roll(tile, WIN * wc, 0)
                line = jnp.where((i >= WIN * wc) & (i < WIN * (wc + 1)), tile, line)
            if shifted:
                line = jnp.where(i < SHIFT, pltpu.roll(line, 32 - side + SHIFT, 0), pltpu.roll(line, SHIFT, 0))
            dst[row] = line[:side].astype(dst.dtype)
        return carry

    lax.fori_loop(0, per_side, step, 0)


def regular_to_shifted(src, dst, side):
    per_side = side // WIN

    def step(wr, carry):
        below = lax.rem(wr + 1, per_side)
        for r in range(WIN):
            sr, srr = (wr, r + SHIFT) if r + SHIFT < WIN else (below, r + SHIFT - WIN)
            for wc in range(per_side):
                here = src[pl.ds(window_row(per_side, sr, wc, srr), PITCH), :]
                right = src[pl.ds(window_row(per_side, sr, (wc + 1) % per_side, srr), PITCH), :]
                i = iota(here.shape, 0)
                tile = jnp.where(
                    i < WIN - SHIFT,
                    pltpu.roll(here, PITCH - SHIFT, 0),
                    jnp.where(i < WIN, pltpu.roll(right, WIN - SHIFT, 0), 0.0),
                )
                dst[pl.ds(window_row(per_side, wr, wc, r), PITCH), :] = tile
        return carry

    lax.fori_loop(0, per_side, step, 0)


def shifted_to_regular(src, dst, side):
    per_side = side // WIN

    def step(wr, carry):
        above = lax.rem(wr + per_side - 1, per_side)
        for r in range(WIN):
            sr, srr = (wr, r - SHIFT) if r >= SHIFT else (above, r - SHIFT + WIN)
            for wc in range(per_side):
                here = src[pl.ds(window_row(per_side, sr, wc, srr), PITCH), :]
                left = src[pl.ds(window_row(per_side, sr, (wc + per_side - 1) % per_side, srr), PITCH), :]
                i = iota(here.shape, 0)
                tile = jnp.where(
                    i < SHIFT,
                    pltpu.roll(left, PITCH - (WIN - SHIFT), 0),
                    jnp.where(i < WIN, pltpu.roll(here, SHIFT, 0), 0.0),
                )
                dst[pl.ds(window_row(per_side, wr, wc, r), PITCH), :] = tile
        return carry

    lax.fori_loop(0, per_side, step, 0)


ROWS_BLOCK = 4 * SLOTS
SMALL = {"gain1": 0, "gain2": 1, "bias1": 2, "bias2": 3, "query": 4, "value": 5, "output": 6, "reduce": 7}
SMALL_TABLE = 8
SMALL_EXPAND = 16
SMALL_ROWS = 24
ADD_ROWS = 96


def rounded(value, step):
    return -(-value // step) * step


def feed_layout(width, ff):
    blocked = ff % width == 0
    return 2 * ff, blocked


class Links:
    def __init__(self, mesh_shape, send_sem, recv_sem):
        self.win, self.mlp = mesh_shape
        self.send_sem, self.recv_sem = send_sem, recv_sem
        self.used = 0
        w, m = lax.axis_index("win"), lax.axis_index("mlp")
        self.core, self.x, self.z, self.m = lax.rem(w, 2), lax.rem(lax.div(w, 2), 2), lax.div(w, 4), m
        self.depth = self.win // 4
        self.groups = {
            "core": (2, self.core, lambda q: self.at(core=q)),
            "x": (2, self.x, lambda q: self.at(x=q)),
            "z": (self.depth, self.z, lambda q: self.at(z=q)),
            "mlp": (self.mlp, m, lambda q: self.at(m=q)),
            "plane": (
                2 * self.mlp,
                self.x * self.mlp + m,
                lambda q: self.at(x=lax.div(q, self.mlp), m=lax.rem(q, self.mlp)),
            ),
        }

    def at(self, core=None, x=None, z=None, m=None):
        core = self.core if core is None else core
        x = self.x if x is None else x
        z = self.z if z is None else z
        m = self.m if m is None else m
        return ((z * 2 + x) * 2 + core, m)

    def peers(self, group):
        size, me, _ = self.groups[group]
        return [(d, lax.rem(me + d, size), lax.rem(me + size - d, size)) for d in range(1, size)]

    def me(self, group):
        return self.groups[group][1]

    def size(self, group):
        return self.groups[group][0]

    def barrier(self):
        sem = pltpu.get_barrier_semaphore()
        count = 0
        for group in ("core", "plane", "z"):
            for _, q, _ in self.peers(group):
                pl.semaphore_signal(
                    sem, inc=1, device_id=self.groups[group][2](q), device_id_type=pl.DeviceIdType.MESH
                )
                count += 1
        pl.semaphore_wait(sem, count)

    def copy(self, group, q, src, dst):
        n = self.used
        self.used += 1
        made = pltpu.make_async_remote_copy(
            src_ref=src,
            dst_ref=dst,
            send_sem=self.send_sem.at[n],
            recv_sem=self.recv_sem.at[n],
            device_id=self.groups[group][2](q),
            device_id_type=pl.DeviceIdType.MESH,
        )
        made.start()
        return made


def add_rows(dst, sources, start, count):
    step = next(n for n in (ADD_ROWS, 48, 32, 16) if count % n == 0)

    def one(i, carry):
        at = pl.multiple_of(start + i * step, 16)
        total = dst[pl.ds(at, step), :].astype(F32)
        for source, first in sources:
            total = total + source[pl.ds(pl.multiple_of(first + i * step, 16), step), :].astype(F32)
        dst[pl.ds(at, step), :] = total.astype(dst.dtype)
        return carry

    lax.fori_loop(0, count // step, one, 0)


class Reduction:
    def __init__(self, links, staged, out, stages, buffers, local_sem):
        self.links, self.staged, self.out = links, staged, out
        self.stages, self.buffers, self.local_sem = stages, buffers, local_sem
        self.level = 0
        self.base, self.rows = 0, staged.shape[0]
        self.waiting = None
        self.trail = []

    def send(self):
        group = self.stages[self.level]
        links, block = self.links, self.rows // self.links.size(group)
        self.waiting = [
            links.copy(
                group,
                q,
                self.staged.at[pl.ds(pl.multiple_of(self.base + q * block, 16), block)],
                self.buffers[self.level].at[d - 1],
            )
            for d, q, _ in links.peers(group)
        ]

    def take(self):
        group = self.stages[self.level]
        links, block = self.links, self.rows // self.links.size(group)
        for copy in self.waiting:
            copy.wait()
        self.trail.append((group, self.base, block))
        self.base = self.base + links.me(group) * block
        self.rows = block
        buffer = self.buffers[self.level]
        add_rows(
            self.staged,
            [(buffer.at[d - 1], 0) for d, _, _ in links.peers(group)],
            self.base,
            block,
        )
        self.level += 1

    def turn(self):
        mine = pl.ds(pl.multiple_of(self.base, 16), self.rows)
        self.local = pltpu.make_async_copy(self.staged.at[mine], self.out.at[mine], self.local_sem)
        self.local.start()
        self.spread(self.staged)

    def spread(self, source):
        group, base, block = self.trail[-1]
        links = self.links
        mine = pl.ds(pl.multiple_of(self.base, 16), self.rows)
        self.waiting = [links.copy(group, q, source.at[mine], self.out.at[mine]) for _, q, _ in links.peers(group)]

    def collect(self):
        group, base, block = self.trail.pop()
        for copy in self.waiting:
            copy.wait()
        if self.local is not None:
            self.local.wait()
            self.local = None
        self.base, self.rows = base, block * self.links.size(group)

    def widen(self):
        self.collect()
        if self.trail:
            self.spread(self.out)


class FeedReduction(Reduction):
    def __init__(self, links, staged, out, buffers, local_sem):
        shards, rows, width = staged.shape
        self.all = staged
        self.first = buffers[0]
        self.second = buffers[1]
        super().__init__(links, staged.at[links.m], out, ("core", "mlp", "x", "z"), (None, None) + tuple(buffers[2:]), local_sem)

    def send(self):
        if self.level > 1:
            return super().send()
        links = self.links
        half = self.staged.shape[0] // 2
        if self.level == 0:
            (_, q, _), = links.peers("core")
            self.waiting = [
                links.copy("core", q, self.all.at[:, pl.ds(pl.multiple_of(q * half, 16), half)], self.first)
            ]
        else:
            mine = pl.ds(pl.multiple_of(self.base, 16), half)
            self.waiting = [
                links.copy("mlp", q, self.all.at[q, mine], self.second.at[d - 1])
                for d, q, _ in links.peers("mlp")
            ]

    def take(self):
        if self.level > 1:
            return super().take()
        links = self.links
        for copy in self.waiting:
            copy.wait()
        half = self.staged.shape[0] // 2
        if self.level == 0:
            self.trail.append(("core", 0, half))
            self.base = links.core * half
            self.rows = half
            for i in range(self.all.shape[0]):
                add_rows(self.all.at[i], [(self.first.at[i], 0)], self.base, half)
        else:
            add_rows(
                self.staged,
                [(self.second.at[d - 1], 0) for d, _, _ in links.peers("mlp")],
                self.base,
                half,
            )
        self.level += 1


class SmallSum:
    def __init__(self, links, value, buffers, out):
        self.links, self.value, self.buffers, self.out = links, value, buffers, out
        self.level = 0
        self.stages = ("core", "plane", "z")

    def send(self):
        group = self.stages[self.level]
        links, buffer = self.links, self.buffers[self.level]
        me = links.me(group)
        buffer[me] = self.value[...]
        self.waiting = [links.copy(group, q, buffer.at[me], buffer.at[me]) for _, q, _ in links.peers(group)]

    def take(self):
        for copy in self.waiting:
            copy.wait()
        buffer = self.buffers[self.level]
        total = buffer[0]
        for j in range(1, buffer.shape[0]):
            total = total + buffer[j]
        self.level += 1
        if self.level == len(self.stages):
            self.out[...] = total
        else:
            self.value[...] = total

    def step(self):
        self.take()
        if self.level < len(self.stages):
            self.send()


class Idle:
    def skip(self):
        pass

    send = take = turn = widen = step = skip


def kernel(side, mesh_shape, *refs):
    refs = list(refs)

    def take(n):
        got = refs[:n]
        del refs[:n]
        return got

    tokens, ids, gain, offset, w_in, b_in, table, w_out, b_out, w_exp, b_exp, w_red, b_red, cot = take(14)
    fused = mesh_shape is not None
    out, grad_tokens, d_attn, d_feed, small = take(5)
    (x, normed, qkv, probs, mixed, mid, second, hidden, slope) = take(9)
    (keys, bias, bias_sum, g, gs, gz, gb_low, dqkv, go, d_bexp) = take(10)
    if fused:
        out_attn, out_feed, out_small = d_attn, d_feed, small
        d_attn, d_feed, small = take(3)
        local_exp, local_bexp, local_red = w_exp, b_exp, w_red
        w_exp, b_exp, w_red = take(3)
        feed_buffers, attn_buffers, small_buffers = take(4), take(3), take(3)
        local_sems, send_sem, recv_sem = take(3)
        links = Links(mesh_shape, send_sem, recv_sem)
        feeds = [
            FeedReduction(links, d_feed.at[l], out_feed.at[l], [b.at[l] for b in feed_buffers], local_sems.at[2 * l])
            for l in range(2)
        ]
        attns = [
            Reduction(
                links, d_attn.at[l], out_attn.at[l], ("core", "plane", "z"), [b.at[l] for b in attn_buffers], local_sems.at[2 * l + 1]
            )
            for l in range(2)
        ]
        smalls = [SmallSum(links, small.at[l], [b.at[l] for b in small_buffers], out_small.at[l]) for l in range(2)]

    def hook(*actions):
        for action in actions:
            action()

    if not fused:
        idle = Idle()
        feeds = attns = smalls = (idle, idle)

    per_side = side // WIN
    windows = per_side * per_side
    rows = windows * SLOTS
    blocks = rows // ROWS_BLOCK
    shards, _, width, ff = w_exp.shape
    chunk = 256 if ff % 256 == 0 else ff
    _, blocked = feed_layout(width, ff)

    if fused:
        locals_ = [
            pltpu.make_async_copy(local_exp, w_exp.at[links.m], local_sems.at[4]),
            pltpu.make_async_copy(local_red, w_red.at[links.m], local_sems.at[5]),
            pltpu.make_async_copy(local_bexp, b_exp.at[links.m], local_sems.at[6]),
        ]
        for copy in locals_:
            copy.start()
        links.barrier()
        halves = (
            pl.ds(pl.multiple_of(links.core * (width // 2), 16), width // 2),
            pl.ds(pl.multiple_of(links.core * (ff // 2), 16), ff // 2),
        )
        fetched = [
            [
                copy
                for _, q, _ in links.peers("mlp")
                for copy in (
                    links.copy("mlp", q, local_exp.at[l, halves[0]], w_exp.at[links.m, l, halves[0]]),
                    links.copy("mlp", q, local_red.at[l, halves[1]], w_red.at[links.m, l, halves[1]]),
                )
            ]
            for l in range(2)
        ]
        fetched_bias = [links.copy("mlp", q, local_bexp, b_exp.at[links.m]) for _, q, _ in links.peers("mlp")]
        passed = [None, None]

        def pass_weights(l):
            for copy in fetched[l]:
                copy.wait()
            (_, sibling, _), = links.peers("core")
            passed[l] = [
                copy
                for _, _, q in links.peers("mlp")
                for copy in (
                    links.copy("core", sibling, w_exp.at[q, l, halves[0]], w_exp.at[q, l, halves[0]]),
                    links.copy("core", sibling, w_red.at[q, l, halves[1]], w_red.at[q, l, halves[1]]),
                )
            ]

        def have_weights(l):
            for copy in passed[l]:
                copy.wait()
            if l == 0:
                for copy in locals_ + fetched_bias:
                    copy.wait()

    def over_blocks(body):
        def step(i, carry):
            body(pl.ds(pl.multiple_of(i * ROWS_BLOCK, ROWS_BLOCK), ROWS_BLOCK))
            return carry

        lax.fori_loop(0, blocks, step, 0)

    def over_shards(body):
        def step(i, carry):
            body(i)
            return carry

        lax.fori_loop(0, shards, step, 0)

    def put_tokens(wr, wc, r, tile):
        x[0, pl.ds(window_row(per_side, wr, wc, r), PITCH), :] = tile

    grid_to_windows(tokens, side, False, put_tokens)

    for l in range(2):
        shifted = l == 1

        def put_keys(wr, wc, r, tile, shifted=shifted):
            lane = iota(tile.shape, 1).astype(F32)
            slot = iota(tile.shape, 0)
            label = tile
            if shifted:
                row_at = wr * WIN + r
                row_label = jnp.where(row_at >= side - WIN, 1, 0) + jnp.where(row_at >= side - SHIFT, 1, 0)
                col_at = wc * WIN + slot
                col_label = jnp.where(col_at >= side - WIN, 1, 0) + jnp.where(col_at >= side - SHIFT, 1, 0)
                label = label + (12 * row_label + 4 * col_label).astype(F32)
            hot = jnp.where((lane == label) & (slot < WIN), 1.0, 0.0)
            keys[pl.ds(window_row(per_side, wr, wc, r), PITCH), :] = hot

        grid_to_windows(ids, side, shifted, put_keys)

        krow = iota((SLOTS, 128), 0)
        qlane = iota((SLOTS, 128), 1)
        ahead = (qlane & (PITCH - 1)) >= (krow & (PITCH - 1))
        for grp in range(GROUPS):
            low = jnp.zeros((SLOTS, 128), F32)
            high = jnp.zeros((SLOTS, 128), F32)
            for j in range(GROUP):
                h = grp * GROUP + j
                both = [
                    pltpu.roll(
                        jnp.broadcast_to(table[l, 2 * h + s : 2 * h + s + 1, :], (SLOTS, 128)),
                        0,
                        1,
                        stride=1,
                        stride_axis=0,
                    )
                    for s in range(2)
                ]
                one = jnp.where(ahead, both[0], both[1])
                at = j * SLOTS
                if at < 128:
                    moved = pltpu.roll(one, at, 1) if at else one
                    low = jnp.where((qlane >= at) & (qlane < at + SLOTS), moved, low)
                if at + SLOTS > 128:
                    moved = pltpu.roll(one, (at - 128) % 128, 1)
                    high = jnp.where((qlane >= at - 128) & (qlane < at - 128 + SLOTS), moved, high)
            bias[grp, :, :128] = low
            bias[grp, :, 128:] = high[:, : GQ - 128]

        bias_row = jnp.concatenate(
            [b_in[l, 0:1, :], jnp.zeros((1, width), F32), b_in[l, 1:2, :]], axis=1
        )

        def project(at, l=l, bias_row=bias_row):
            xhat, _ = norm_stats(x[l, at, :])
            a = (xhat * gain[l, 0:1, :] + offset[l, 0:1, :]).astype(BF16)
            normed[l, at, :] = a
            for c in range(3):
                cols = slice(c * width, (c + 1) * width)
                qkv[l, at, cols] = (dot(a, w_in[l, :, cols]) + bias_row[:, cols]).astype(BF16)

        over_blocks(project)

        def attend(i, carry, l=l):
            at = pl.ds(pl.multiple_of(i * 2 * SLOTS, 2 * SLOTS), 2 * SLOTS)
            q = qkv[l, at, :width].astype(F32)
            k = qkv[l, at, width : 2 * width].astype(F32)
            v = qkv[l, at, 2 * width :].astype(F32)
            hot = keys[at, :]
            parts = []
            for w in range(2):
                here = slice(w * SLOTS, (w + 1) * SLOTS)
                hot_w = hot[here]
                allowed = dot_nt(hot_w.astype(BF16), jnp.concatenate([hot_w] * GROUP, axis=0).astype(BF16)) > 0.5
                outs = []
                for grp in range(GROUPS):
                    lanes = slice(grp * GLANES, (grp + 1) * GLANES)
                    q_all = expand_heads(q[here, lanes])
                    s = dot_nt(k[here, lanes].astype(BF16), q_all) * HEAD_DIM**-0.5 + bias[grp]
                    s = jnp.where(allowed, s, MASKED)
                    e = jnp.exp(s - jnp.max(s, axis=0, keepdims=True))
                    p = e / jnp.sum(e, axis=0, keepdims=True)
                    probs[l, 2 * i + w, grp] = p
                    outs.append(fold_heads(dot_tn(p.astype(BF16), v[here, lanes].astype(BF16))))
                parts.append(jnp.concatenate(outs, axis=1))
            mixed[l, at, :] = jnp.concatenate(parts, axis=0).astype(BF16)
            return carry

        lax.fori_loop(0, windows // 2, attend, 0)
        if fused:
            pass_weights(l)

        def middle(at, l=l):
            m = x[l, at, :] + dot(mixed[l, at, :], w_out[l]) + b_out[l : l + 1, :]
            mid[l, at, :] = m
            xhat, _ = norm_stats(m)
            second[l, at, :] = (xhat * gain[l, 1:2, :] + offset[l, 1:2, :]).astype(BF16)
            gs[at, :] = m + b_red[l : l + 1, :]

        over_blocks(middle)
        if fused:
            have_weights(l)

        def feed(at, l=l):
            s = second[l, at, :]

            def one(i):
                for c in range(0, ff, chunk):
                    cols = slice(c, c + chunk)
                    before = dot(s, w_exp[i, l, :, cols]) + b_exp[i, l : l + 1, cols]
                    value, slope_now = gelu_pair(before)
                    hidden[l, i, at, cols] = value.astype(BF16)
                    slope[l, i, at, cols] = slope_now.astype(BF16)
                gs[at, :] += dot(hidden[l, i, at, :], w_red[i, l])

            over_shards(one)

        over_blocks(feed)

        if l == 0:
            regular_to_shifted(gs, x.at[1], side)
        else:
            windows_to_grid(gs, out, side, True)

    def put_cot(wr, wc, r, tile):
        g[pl.ds(window_row(per_side, wr, wc, r), PITCH), :] = tile

    grid_to_windows(cot, side, True, put_cot)
    small[...] = jnp.zeros(small.shape, F32)

    for l in (1, 0):

        def add_small(name, value, l=l):
            at = SMALL[name]
            small[l, at : at + 1, :] += value

        def feed_back(at, l=l):
            g_now = g[at, :]
            add_small("reduce", jnp.sum(g_now, axis=0, keepdims=True))
            g_low = g_now.astype(BF16)
            gz[at, :] = g_low
            gs[at, :] = jnp.zeros(g_now.shape, F32)

            def one(i):
                for c in range(0, ff, chunk):
                    cols = slice(c, c + chunk)
                    gh = dot_nt(g_low, w_red[i, l, cols, :])
                    gb = gh * slope[l, i, at, cols].astype(F32)
                    summed = jnp.sum(gb, axis=0, keepdims=True)
                    d_bexp[i, 0:1, cols] += summed
                    gb_low[i, at, cols] = gb.astype(BF16)
                gs[at, :] += dot_nt(gb_low[i, at, :], w_exp[i, l])

            over_shards(one)

        d_bexp[...] = jnp.zeros(d_bexp.shape, F32)
        over_blocks(feed_back)
        span = min(width, ff)
        for n in range(shards * (ff // span)):
            i, c = n // (ff // span), n % (ff // span) * span
            small[l, SMALL_EXPAND + n : SMALL_EXPAND + n + 1, :span] = d_bexp[i, 0:1, c : c + span]
        if l == 0:
            hook(smalls[1].step, feeds[1].take, feeds[1].turn)

        def feed_weights(i, l=l):
            for c in range(0, ff, chunk):
                cols = slice(c, c + chunk)
                d_feed[l, i, ff + c : ff + c + chunk, :] = dot_tn(hidden[l, i, :, cols], gz[...]).astype(BF16)
            if blocked:
                for c in range(0, ff, width):
                    d_feed[l, i, c : c + width, :] = dot_tn(second[l], gb_low[i, :, c : c + width]).astype(BF16)
            else:
                d_feed[l, i, :ff, :] = dot_tn(gb_low[i], second[l]).astype(BF16)

        over_shards(feed_weights)
        hook(feeds[l].send)
        if l == 0:
            hook(attns[1].take, attns[1].send, smalls[1].step)

        def middle_back(at, l=l):
            dmid, dgain, doffset = norm_back(mid[l, at, :], gain[l, 1:2, :], gs[at, :])
            add_small("gain2", dgain)
            add_small("bias2", doffset)
            gm = g[at, :] + dmid
            g[at, :] = gm
            add_small("output", jnp.sum(gm, axis=0, keepdims=True))
            low = gm.astype(BF16)
            gz[at, :] = low
            go[at, :] = dot_nt(low, w_out[l]).astype(BF16)

        over_blocks(middle_back)
        hook(feeds[l].take, feeds[l].send)
        if l == 0:
            hook(feeds[1].widen, attns[1].take, attns[1].turn, smalls[1].step)
        d_attn[l, 3 * width :, :] = dot_tn(mixed[l], gz[...]).astype(BF16)
        bias_sum[...] = jnp.zeros(bias_sum.shape, F32)

        def attend_back(i, carry, l=l):
            at = pl.ds(pl.multiple_of(i * 2 * SLOTS, 2 * SLOTS), 2 * SLOTS)
            q = qkv[l, at, :width].astype(F32)
            k = qkv[l, at, width : 2 * width].astype(F32)
            v = qkv[l, at, 2 * width :].astype(F32)
            go_now = go[at, :].astype(F32)
            made = ([], [], [])
            for w in range(2):
                here = slice(w * SLOTS, (w + 1) * SLOTS)
                for grp in range(GROUPS):
                    lanes = slice(grp * GLANES, (grp + 1) * GLANES)
                    q_all = expand_heads(q[here, lanes])
                    go_all = expand_heads(go_now[here, lanes])
                    k_low = k[here, lanes].astype(BF16)
                    dp = dot_nt(v[here, lanes].astype(BF16), go_all)
                    p = probs[l, 2 * i + w, grp]
                    ds = (p * (dp - jnp.sum(p * dp, axis=0, keepdims=True))).astype(BF16)
                    bias_sum[grp] += ds.astype(F32)
                    made[0].append(fold_heads(dot_tn(ds, k_low)) * HEAD_DIM**-0.5)
                    made[1].append(dot(ds, q_all) * HEAD_DIM**-0.5)
                    made[2].append(dot(p.astype(BF16), go_all))
            for part in range(3):
                whole = jnp.concatenate(
                    [
                        jnp.concatenate(made[part][w * GROUPS : (w + 1) * GROUPS], axis=1)
                        for w in range(2)
                    ],
                    axis=0,
                )
                if part == 0:
                    add_small("query", jnp.sum(whole, axis=0, keepdims=True))
                if part == 2:
                    add_small("value", jnp.sum(whole, axis=0, keepdims=True))
                dqkv[at, part * width : (part + 1) * width] = whole.astype(BF16)
            return carry

        lax.fori_loop(0, windows // 4, attend_back, 0)
        hook(feeds[l].take, feeds[l].send)
        if l == 0:
            hook(feeds[1].widen, attns[1].widen)
        lax.fori_loop(windows // 4, windows // 2, attend_back, 0)
        if l == 0:
            hook(feeds[0].take, feeds[0].send)

        for c in range(3):
            cols = slice(c * width, (c + 1) * width)
            d_attn[l, cols, :] = dot_tn(normed[l], dqkv[:, cols]).astype(BF16)
        hook(attns[l].send)
        if l == 0:
            hook(feeds[1].widen, attns[1].widen)

        krow = iota((SLOTS, 128), 0)
        qlane = iota((SLOTS, 128), 1)
        ahead = (qlane & (PITCH - 1)) >= (krow & (PITCH - 1))
        for grp in range(GROUPS):
            low = bias_sum[grp, :, :128]
            high = jnp.concatenate([bias_sum[grp, :, 128:], jnp.zeros((SLOTS, 256 - GQ), F32)], axis=1)
            for j in range(GROUP):
                h = grp * GROUP + j
                at = j * SLOTS
                if at + SLOTS <= 128:
                    one = pltpu.roll(low, 128 - at, 1) if at else low
                elif at < 128:
                    one = jnp.where(qlane < 128 - at, pltpu.roll(low, 128 - at, 1), pltpu.roll(high, 128 - at, 1))
                else:
                    one = pltpu.roll(high, (256 - at) % 128, 1)
                one = jnp.where(qlane < SLOTS, one, 0.0)
                for s in range(2):
                    picked = jnp.where(ahead if s == 0 else jnp.logical_not(ahead), one, 0.0)
                    tile = picked[:PITCH]
                    for r in range(1, WIN):
                        tile = tile + pltpu.roll(picked[r * PITCH : (r + 1) * PITCH], 128 - r * PITCH, 1)
                    for step in (1, 2, 4):
                        tile = jnp.where((iota(tile.shape, 0) & step) > 0, pltpu.roll(tile, 128 - step, 1), tile)
                    n = 2 * h + s
                    small[l, SMALL_TABLE + n // 3 : SMALL_TABLE + n // 3 + 1, n % 3 * 128 : (n % 3 + 1) * 128] = jnp.sum(
                        tile, axis=0, keepdims=True
                    )

        if l == 0:
            hook(attns[0].take, attns[0].send, feeds[0].take, feeds[0].turn)

        def input_back(at, l=l):
            ga = dot_nt(dqkv[at, :], w_in[l])
            dx, dgain, doffset = norm_back(x[l, at, :], gain[l, 0:1, :], ga)
            add_small("gain1", dgain)
            add_small("bias1", doffset)
            gs[at, :] = g[at, :] + dx

        over_blocks(input_back)
        hook(smalls[l].send)
        if l == 1:
            hook(feeds[1].take, feeds[1].send, attns[1].take, attns[1].send)
            shifted_to_regular(gs, g, side)
        else:
            hook(attns[0].take, attns[0].send, feeds[0].widen)
            windows_to_grid(gs, grad_tokens, side, False)
            hook(smalls[0].step, attns[0].take, attns[0].turn, feeds[0].widen)
            hook(smalls[0].step, attns[0].widen, smalls[0].step, feeds[0].widen, attns[1].widen)
            hook(attns[0].widen, attns[0].widen)


def table_lanes(table):
    layers, _, heads = table.shape
    square = table.reshape(layers, SPAN_SIDE, SPAN_SIDE, heads).transpose(0, 3, 1, 2)
    right = jnp.pad(square[..., WIN - 1 :], ((0, 0),) * 3 + ((0, PITCH - WIN),))
    left = jnp.pad(square[..., : WIN - 1], ((0, 0),) * 3 + ((PITCH - WIN + 1, 0),))
    span = SPAN_SIDE * PITCH

    def lanes(part, back):
        flat = jnp.pad(part.reshape(layers, heads, span), ((0, 0), (0, 0), (0, 128 - span)))
        return jnp.roll(flat, -back, axis=-1)

    both = jnp.stack([lanes(right, (WIN - 1) * PITCH), lanes(left, WIN * PITCH)], axis=2)
    return both.reshape(layers, 2 * heads, 128)


def lanes_table(lanes):
    layers, heads = lanes.shape[0], lanes.shape[1] // 2
    both = lanes.reshape(layers, heads, 2, 128)
    span = SPAN_SIDE * PITCH

    def square(part, back):
        return jnp.roll(part, back, axis=-1)[..., :span].reshape(layers, heads, SPAN_SIDE, PITCH)

    right = square(both[:, :, 0], (WIN - 1) * PITCH)[..., :WIN]
    left = square(both[:, :, 1], WIN * PITCH)[..., PITCH - WIN + 1 :]
    whole = jnp.concatenate([left, right], axis=-1)
    return whole.reshape(layers, heads, SPAN_SIDE * SPAN_SIDE).transpose(0, 2, 1)


def on_device(
    mesh_shape,
    tokens,
    crop_ids,
    norm_gain,
    norm_bias,
    input_proj,
    input_bias,
    position_table,
    output_proj,
    output_bias,
    expand_weight,
    expand_bias,
    reduce_weight,
    reduce_bias,
    cotangent,
):
    _, side, _, width = tokens.shape
    layers, _, ff = expand_weight.shape
    win, shards = mesh_shape
    ids = jnp.broadcast_to(crop_ids[0, :, :, None].astype(F32), (side, side, 128))
    windows = (side // WIN) ** 2
    rows = windows * SLOTS
    attn_rows, feed_rows = 4 * width, 2 * ff
    fused = win % 4 == 0 and attn_rows % (16 * win * shards) == 0 and feed_rows % (16 * win) == 0
    vmem = pl.BlockSpec(memory_space=pltpu.VMEM)
    hbm = pl.BlockSpec(memory_space=pl.ANY)
    if fused:
        w_exp, w_red = expand_weight, reduce_weight
        b_exp = jnp.pad(expand_bias.astype(F32), ((0, 8 - layers), (0, 0)))
    else:
        w_exp = lax.all_gather(expand_weight, "mlp", axis=0)
        w_red = lax.all_gather(reduce_weight, "mlp", axis=0)
        b_exp = lax.all_gather(expand_bias, "mlp", axis=0).astype(F32)
    scratch = [
        pltpu.VMEM((layers, rows, width), F32),
        pltpu.VMEM((layers, rows, width), BF16),
        pltpu.VMEM((layers, rows, 3 * width), BF16),
        pltpu.VMEM((layers, windows, GROUPS, SLOTS, GQ), F32),
        pltpu.VMEM((layers, rows, width), BF16),
        pltpu.VMEM((layers, rows, width), F32),
        pltpu.VMEM((layers, rows, width), BF16),
        pltpu.VMEM((layers, shards, rows, ff), BF16),
        pltpu.VMEM((layers, shards, rows, ff), BF16),
        pltpu.VMEM((rows, 128), F32),
        pltpu.VMEM((GROUPS, SLOTS, GQ), F32),
        pltpu.VMEM((GROUPS, SLOTS, GQ), F32),
        pltpu.VMEM((rows, width), F32),
        pltpu.VMEM((rows, width), F32),
        pltpu.VMEM((rows, width), BF16),
        pltpu.VMEM((shards, rows, ff), BF16),
        pltpu.VMEM((rows, 3 * width), BF16),
        pltpu.VMEM((rows, width), BF16),
        pltpu.VMEM((shards, 8, ff), F32),
    ]
    small_shape = (layers, SMALL_ROWS, width)
    if fused:
        plane, depth = 2 * shards, win // 4
        half = feed_rows // 2
        scratch += [
            pltpu.VMEM((layers, attn_rows, width), BF16),
            pltpu.VMEM((layers, shards, feed_rows, width), BF16),
            pltpu.VMEM(small_shape, F32),
            pltpu.VMEM((shards, layers, width, ff), BF16),
            pltpu.VMEM((shards, 8, ff), F32),
            pltpu.VMEM((shards, layers, ff, width), BF16),
            pltpu.VMEM((layers, shards, half, width), BF16),
            pltpu.VMEM((layers, shards - 1, half, width), BF16),
            pltpu.VMEM((layers, 1, half // 2, width), BF16),
            pltpu.VMEM((layers, depth - 1, half // 2 // depth, width), BF16),
            pltpu.VMEM((layers, 1, attn_rows // 2, width), BF16),
            pltpu.VMEM((layers, plane - 1, attn_rows // 2 // plane, width), BF16),
            pltpu.VMEM((layers, depth - 1, attn_rows // 2 // plane // depth, width), BF16),
            pltpu.VMEM((layers, 2) + small_shape[1:], F32),
            pltpu.VMEM((layers, plane) + small_shape[1:], F32),
            pltpu.VMEM((layers, depth) + small_shape[1:], F32),
            pltpu.SemaphoreType.DMA((7,)),
            pltpu.SemaphoreType.DMA((96,)),
            pltpu.SemaphoreType.DMA((96,)),
        ]
    outs = pl.pallas_call(
        functools.partial(kernel, side, mesh_shape if fused else None),
        out_shape=(
            jax.ShapeDtypeStruct(tokens.shape[1:], BF16),
            jax.ShapeDtypeStruct(tokens.shape[1:], BF16),
            jax.ShapeDtypeStruct((layers, attn_rows, width), BF16),
            jax.ShapeDtypeStruct((layers, feed_rows, width) if fused else (layers, shards, feed_rows, width), BF16),
            jax.ShapeDtypeStruct(small_shape, F32),
        ),
        in_specs=[vmem] * 9 + ([hbm, vmem, hbm] if fused else [vmem] * 3) + [vmem] * 2,
        out_specs=[vmem] * 2 + ([hbm] * 2 if fused else [vmem] * 2) + [vmem],
        scratch_shapes=scratch,
        compiler_params=pltpu.CompilerParams(
            vmem_limit_bytes=64 * 1024 * 1024,
            **(dict(collective_id=0, has_side_effects=True) if fused else {}),
        ),
    )(
        tokens[0],
        ids,
        norm_gain,
        norm_bias,
        input_proj,
        input_bias,
        table_lanes(position_table),
        output_proj,
        output_bias,
        w_exp,
        b_exp,
        w_red,
        reduce_bias,
        cotangent[0],
    )
    out, grad_tokens, d_attn, d_feed, small = outs
    if not fused:
        d_attn, small = lax.psum((d_attn, small), ("win", "mlp"))
        d_feed = lax.psum(lax.psum_scatter(d_feed, "mlp", scatter_dimension=1, tiled=False), "win")
    d_in = jnp.concatenate([d_attn[:, c * width : (c + 1) * width] for c in range(3)], axis=2)
    if ff % width == 0:
        d_exp = jnp.concatenate([d_feed[:, c : c + width] for c in range(0, ff, width)], axis=2)
    else:
        d_exp = d_feed[:, :ff].swapaxes(1, 2)
    span = min(width, ff)
    d_bexp = small[:, SMALL_EXPAND : SMALL_EXPAND + shards * (ff // span), :span].reshape(layers, shards, ff)
    d_bexp = lax.dynamic_index_in_dim(d_bexp, lax.axis_index("mlp"), 1, keepdims=False)
    d_table = small[:, SMALL_TABLE : SMALL_TABLE + 8].reshape(layers, 2 * HEADS, 128)
    return (
        out[None],
        grad_tokens[None],
        small[:, 0:2],
        small[:, 2:4],
        d_in.astype(F32),
        small[:, 4:6],
        lanes_table(d_table),
        d_attn[:, 3 * width :].astype(F32),
        small[:, 6],
        d_exp.astype(F32),
        d_bexp,
        d_feed[:, ff:].astype(F32),
        small[:, 7],
    )


def solution(mesh):
    tokens = P(("win", "mlp"), None, None, None)
    placed = (
        tokens,
        P(("win", "mlp"), None, None),
        P(),
        P(),
        P(),
        P(),
        P(),
        P(),
        P(),
        P(None, None, "mlp"),
        P(None, "mlp"),
        P(None, "mlp", None),
        P(),
        tokens,
    )
    return jax.shard_map(
        functools.partial(on_device, (mesh.shape["win"], mesh.shape["mlp"])),
        mesh=mesh,
        in_specs=placed,
        out_specs=(
            tokens,
            tokens,
            P(),
            P(),
            P(),
            P(),
            P(),
            P(),
            P(),
            P(None, None, "mlp"),
            P(None, "mlp"),
            P(None, "mlp", None),
            P(),
        ),
        check_vma=False,
    )
```

```python
import functools

import jax
import jax.numpy as jnp
from jax import lax
from jax.experimental import pallas as pl
from jax.experimental.pallas import tpu as pltpu
from jax.sharding import PartitionSpec as P

HEADS = 12
HEAD_DIM = 32
WIN = 7
SHIFT = 3
SPAN_SIDE = 2 * WIN - 1

EPS = 1e-05
MASKED = -1e30

PITCH = 8
SLOTS = WIN * PITCH
GROUP = 4
GROUPS = HEADS // GROUP
GLANES = GROUP * HEAD_DIM
GQ = GROUP * SLOTS

F32 = jnp.float32
BF16 = jnp.bfloat16

ERF_P = 0.39
ERF_C = (
    0.22003399505358215,
    0.22002241291251284,
    0.20367769093249805,
    0.16514655576456758,
    0.15214218925854978,
    -0.024768996902218943,
    0.20836931643666226,
    -0.19248882577712367,
    0.04786540601145673,
)


LOG2E = 1.4426950408889634
BELL = 0.3989422804014327


def dot(a, b):
    return lax.dot_general(a, b, (((1,), (0,)), ((), ())), preferred_element_type=F32)


def dot_nt(a, b):
    return lax.dot_general(a, b, (((1,), (1,)), ((), ())), preferred_element_type=F32)


def dot_tn(a, b):
    return lax.dot_general(a, b, (((0,), (0,)), ((), ())), preferred_element_type=F32)


def gelu_pair(u):
    bell = jnp.exp2(u * u * (-0.5 * LOG2E))
    size = jnp.abs(u)
    t = 1.0 / (1.0 + (ERF_P * 0.5**0.5) * size)
    poly = 0.5 * ERF_C[-1] * t + 0.5 * ERF_C[-2]
    for coef in ERF_C[-3::-1]:
        poly = poly * t + 0.5 * coef
    tail = bell * (t * poly)
    phi = jnp.where(u < 0, tail, 1.0 - tail)
    return jnp.maximum(u, 0.0) - size * tail, phi + u * (bell * BELL)


def norm_stats(v):
    centred = v - jnp.mean(v, axis=-1, keepdims=True)
    rstd = lax.rsqrt(jnp.mean(centred * centred, axis=-1, keepdims=True) + EPS)
    return centred * rstd, rstd


def norm_back(v, gain, upstream):
    xhat, rstd = norm_stats(v)
    scaled = upstream * gain
    inner = (
        scaled
        - jnp.mean(scaled, axis=-1, keepdims=True)
        - xhat * jnp.mean(scaled * xhat, axis=-1, keepdims=True)
    )
    return rstd * inner, jnp.sum(upstream * xhat, axis=0, keepdims=True), jnp.sum(upstream, axis=0, keepdims=True)


def iota(shape, dim):
    return lax.broadcasted_iota(jnp.int32, shape, dim)


def expand_heads(rows):
    head = iota(rows.shape, 1) // HEAD_DIM
    return jnp.concatenate([jnp.where(head == j, rows, 0.0) for j in range(GROUP)], axis=0).astype(BF16)


def fold_heads(rows):
    head = iota((SLOTS, GLANES), 1) // HEAD_DIM
    out = rows[:SLOTS]
    for j in range(1, GROUP):
        out = jnp.where(head == j, rows[j * SLOTS : (j + 1) * SLOTS], out)
    return out


def by_window(parts):
    return jnp.concatenate(
        [jnp.concatenate(parts[w * GROUPS : (w + 1) * GROUPS], axis=1) for w in range(BLOCK_WINDOWS)], axis=0
    )


def window_row(per_side, wr, wc, r):
    return pl.multiple_of((wr * per_side + wc) * SLOTS + r * PITCH, PITCH)


def grid_to_windows(src, side, shifted, emit):
    per_side = side // WIN

    def step(wr, carry):
        for r in range(WIN):
            row = lax.rem(wr * WIN + r + (SHIFT if shifted else 0), side)
            line = src[row].astype(F32)
            width = line.shape[1]
            line = jnp.concatenate([line, jnp.zeros((32 - side, width), F32)], axis=0)
            if shifted:
                i = iota(line.shape, 0)
                line = jnp.where(i < side - SHIFT, pltpu.roll(line, 32 - SHIFT, 0), pltpu.roll(line, side - SHIFT, 0))
            for wc in range(per_side):
                part = line if wc == 0 else pltpu.roll(line, 32 - WIN * wc, 0)
                part = part[:PITCH]
                part = jnp.where(iota(part.shape, 0) < WIN, part, 0.0)
                emit(wr, wc, r, part)
        return carry

    lax.fori_loop(0, per_side, step, 0)


def windows_to_grid(src, dst, side, shifted):
    per_side = side // WIN

    def step(wr, carry):
        for r in range(WIN):
            row = lax.rem(wr * WIN + r + (SHIFT if shifted else 0), side)
            width = src.shape[1]
            line = jnp.zeros((32, width), F32)
            i = iota(line.shape, 0)
            for wc in range(per_side):
                tile = src[pl.ds(window_row(per_side, wr, wc, r), PITCH), :]
                tile = jnp.concatenate([tile, jnp.zeros((32 - PITCH, width), F32)], axis=0)
                if wc:
                    tile = pltpu.roll(tile, WIN * wc, 0)
                line = jnp.where((i >= WIN * wc) & (i < WIN * (wc + 1)), tile, line)
            if shifted:
                line = jnp.where(i < SHIFT, pltpu.roll(line, 32 - side + SHIFT, 0), pltpu.roll(line, SHIFT, 0))
            dst[row] = line[:side].astype(dst.dtype)
        return carry

    lax.fori_loop(0, per_side, step, 0)


def regular_to_shifted(src, dst, side):
    per_side = side // WIN

    def step(wr, carry):
        below = lax.rem(wr + 1, per_side)
        for r in range(WIN):
            sr, srr = (wr, r + SHIFT) if r + SHIFT < WIN else (below, r + SHIFT - WIN)
            for wc in range(per_side):
                here = src[pl.ds(window_row(per_side, sr, wc, srr), PITCH), :]
                right = src[pl.ds(window_row(per_side, sr, (wc + 1) % per_side, srr), PITCH), :]
                i = iota(here.shape, 0)
                tile = jnp.where(
                    i < WIN - SHIFT,
                    pltpu.roll(here, PITCH - SHIFT, 0),
                    jnp.where(i < WIN, pltpu.roll(right, WIN - SHIFT, 0), 0.0),
                )
                dst[pl.ds(window_row(per_side, wr, wc, r), PITCH), :] = tile
        return carry

    lax.fori_loop(0, per_side, step, 0)


def shifted_to_regular(src, dst, side):
    per_side = side // WIN

    def step(wr, carry):
        above = lax.rem(wr + per_side - 1, per_side)
        for r in range(WIN):
            sr, srr = (wr, r - SHIFT) if r >= SHIFT else (above, r - SHIFT + WIN)
            for wc in range(per_side):
                here = src[pl.ds(window_row(per_side, sr, wc, srr), PITCH), :]
                left = src[pl.ds(window_row(per_side, sr, (wc + per_side - 1) % per_side, srr), PITCH), :]
                i = iota(here.shape, 0)
                tile = jnp.where(
                    i < SHIFT,
                    pltpu.roll(left, PITCH - (WIN - SHIFT), 0),
                    jnp.where(i < WIN, pltpu.roll(here, SHIFT, 0), 0.0),
                )
                dst[pl.ds(window_row(per_side, wr, wc, r), PITCH), :] = tile
        return carry

    lax.fori_loop(0, per_side, step, 0)


BLOCK_WINDOWS = 4
ROWS_BLOCK = BLOCK_WINDOWS * SLOTS
JOBS = [
    (w, grp, slice(w * SLOTS, (w + 1) * SLOTS), slice(grp * GLANES, (grp + 1) * GLANES))
    for w in range(BLOCK_WINDOWS)
    for grp in range(GROUPS)
]
SMALL = {"gain1": 0, "gain2": 1, "bias1": 2, "bias2": 3, "query": 4, "value": 5, "output": 6, "reduce": 7}
SMALL_TABLE = 8
SMALL_EXPAND = 16
SMALL_ROWS = 24
ADD_ROWS = 96
PART = 3
ATTN_PARTS = (((0, 2), (2, 1)), ((0, 3),))


def table_spans():
    spans = []
    for dr in range(SPAN_SIDE):
        at = PITCH * (dr - WIN + 1)
        spans.append((at % 128, dr * SPAN_SIDE + WIN - 1, WIN, 0))
        spans.append(((at - PITCH) % 128 + PITCH - WIN + 1, dr * SPAN_SIDE, WIN - 1, 1))
    return spans


class Links:
    def __init__(self, mesh_shape, send_sem, recv_sem):
        self.win, self.mlp = mesh_shape
        self.send_sem, self.recv_sem = send_sem, recv_sem
        w, m = lax.axis_index("win"), lax.axis_index("mlp")
        self.core, self.x, self.z, self.m = lax.rem(w, 2), lax.rem(lax.div(w, 2), 2), lax.div(w, 4), m
        self.depth = self.win // 4
        self.groups = {
            "core": (2, self.core, lambda q: self.at(core=q)),
            "x": (2, self.x, lambda q: self.at(x=q)),
            "z": (self.depth, self.z, lambda q: self.at(z=q)),
            "mlp": (self.mlp, m, lambda q: self.at(m=q)),
            "plane": (
                2 * self.mlp,
                self.x * self.mlp + m,
                lambda q: self.at(x=lax.div(q, self.mlp), m=lax.rem(q, self.mlp)),
            ),
        }
        self.used = 0

    def at(self, core=None, x=None, z=None, m=None):
        core = self.core if core is None else core
        x = self.x if x is None else x
        z = self.z if z is None else z
        m = self.m if m is None else m
        return ((z * 2 + x) * 2 + core, m)

    def peers(self, group):
        size, me, _ = self.groups[group]
        return [(d, lax.rem(me + d, size)) for d in range(1, size)]

    def me(self, group):
        return self.groups[group][1]

    def size(self, group):
        return self.groups[group][0]

    def greet(self):
        sem = pltpu.get_barrier_semaphore()
        for group in ("core", "plane", "z"):
            for _, q in self.peers(group):
                pl.semaphore_signal(
                    sem, inc=1, device_id=self.groups[group][2](q), device_id_type=pl.DeviceIdType.MESH
                )

    def meet(self):
        pl.semaphore_wait(pltpu.get_barrier_semaphore(), sum(self.size(g) - 1 for g in ("core", "plane", "z")))

    def reserve(self, count):
        first = self.used
        self.used += count
        return first

    def copy(self, group, q, src, dst, n):
        return pltpu.make_async_remote_copy(
            src_ref=src,
            dst_ref=dst,
            send_sem=self.send_sem.at[n],
            recv_sem=self.recv_sem.at[n],
            device_id=self.groups[group][2](q),
            device_id_type=pl.DeviceIdType.MESH,
        )


def add_rows(dst, sources, start, count):
    step = next(n for n in (ADD_ROWS, 64, 48, 32, 16) if count % n == 0)

    def one(i, carry):
        at = pl.multiple_of(start + i * step, 16)
        total = dst[pl.ds(at, step), :].astype(F32)
        for source in sources:
            total = total + source[pl.ds(pl.multiple_of(i * step, 16), step), :].astype(F32)
        dst[pl.ds(at, step), :] = total.astype(dst.dtype)
        return carry

    lax.fori_loop(0, count // step, one, 0)


def flow_table(mesh_shape, width, ff):
    part = 4 * width // PART
    flows = {}
    for l in (1, 0):
        flows[f"R{l}"] = (l, ff, ff, ("core", "mlp", "x", "z"))
        flows[f"E{l}"] = (l, 0, ff, ("core", "mlp", "x", "z"))
        for first, count in ATTN_PARTS[l]:
            flows[f"A{first + count - 1}{l}"] = (l, first * part, count * part, ("core", "plane", "z"))
    win, mlp = mesh_shape
    sizes = {"core": 2, "x": 2, "z": win // 4, "mlp": mlp, "plane": 2 * mlp}
    shapes = {}
    for name, (_, _, rows, stages) in flows.items():
        slots = mlp if "mlp" in stages else 1
        shapes[name] = []
        for stage in stages:
            if stage == "mlp":
                slots = 1
            else:
                rows //= sizes[stage]
            shapes[name].append((sizes[stage] - 1, slots, rows, width))
    return flows, shapes


class Flow:
    def __init__(self, links, staged, out, first, rows, stages, buffers, local_sem):
        self.links, self.staged, self.out, self.local_sem = links, staged, out, local_sem
        self.stages, self.buffers = stages, buffers
        self.spans = [(first, rows)]
        for stage in stages:
            first, rows = self.spans[-1]
            if stage != "mlp":
                rows = rows // links.size(stage)
                first = first + links.me(stage) * rows
            self.spans.append((first, rows))
        self.down = [n for n in reversed(range(len(stages))) if stages[n] != "mlp"]
        self.steps = len(stages) + len(self.down)
        self.sems = [
            links.reserve(links.size(stages[n]) - 1) for n in list(range(len(stages))) + self.down
        ]
        self.at = 0
        self.done = False

    def slots(self, n):
        return self.staged.shape[0] if "mlp" in self.stages[n:] else 1

    def copies(self, k):
        links = self.links
        made = []
        if k < len(self.stages):
            stage = self.stages[k]
            for d, q in links.peers(stage):
                first, rows = self.spans[k]
                if stage == "mlp":
                    src = self.staged.at[pl.ds(d, 1), pl.ds(pl.multiple_of(first, 16), rows)]
                else:
                    rows = self.spans[k + 1][1]
                    src = self.staged.at[pl.ds(0, self.slots(k)), pl.ds(pl.multiple_of(first + q * rows, 16), rows)]
                made.append(links.copy(stage, q, src, self.buffers[k].at[d - 1], self.sems[k] + d - 1))
            return made
        n = self.down[k - len(self.stages)]
        first, rows = self.spans[n + 1]
        mine = pl.ds(pl.multiple_of(first, 16), rows)
        src = self.staged.at[0, mine] if k == len(self.stages) else self.out.at[mine]
        for d, q in links.peers(self.stages[n]):
            made.append(links.copy(self.stages[n], q, src, self.out.at[mine], self.sems[k] + d - 1))
        return made

    def local(self):
        first, rows = self.spans[-1]
        mine = pl.ds(pl.multiple_of(first, 16), rows)
        return pltpu.make_async_copy(self.staged.at[0, mine], self.out.at[mine], self.local_sem)

    def advance(self):
        k = self.at
        if k:
            for copy in self.copies(k - 1):
                copy.wait()
            if k - 1 < len(self.stages):
                first, rows = self.spans[k]
                for slot in range(self.slots(k)):
                    add_rows(
                        self.staged.at[slot],
                        [self.buffers[k - 1].at[d - 1, slot] for d, _ in self.links.peers(self.stages[k - 1])],
                        first,
                        rows,
                    )
            elif k - 1 == len(self.stages):
                self.local().wait()
        if k < self.steps:
            if k == len(self.stages):
                self.local().start()
            for copy in self.copies(k):
                copy.start()
        else:
            self.done = True
        self.at += 1


class SmallFlow:
    def __init__(self, links, value, buffers, out):
        self.links, self.value, self.buffers, self.out = links, value, buffers, out
        self.stages = ("core", "plane", "z")
        self.sems = [links.reserve(links.size(stage) - 1) for stage in self.stages]
        self.at = 0
        self.done = False

    def copies(self, k):
        stage, buffer = self.stages[k], self.buffers[k]
        me = self.links.me(stage)
        return [
            self.links.copy(stage, q, buffer.at[me], buffer.at[me], self.sems[k] + d - 1)
            for d, q in self.links.peers(stage)
        ]

    def advance(self):
        k = self.at
        total = self.value[...] if k == 0 else None
        if k:
            for copy in self.copies(k - 1):
                copy.wait()
            buffer = self.buffers[k - 1]
            total = buffer[0]
            for j in range(1, buffer.shape[0]):
                total = total + buffer[j]
        if k < len(self.stages):
            self.buffers[k][self.links.me(self.stages[k])] = total
            for copy in self.copies(k):
                copy.start()
        else:
            self.out[...] = total
            self.done = True
        self.at += 1


PLAN = {
    (1, "feed_back"): {1: ("R1",)},
    (1, "middle_back"): {3: ("E1",)},
    (1, "attend_back0"): {0: ("R1",)},
    (1, "attend_back2"): {1: ("R1", "E1")},
    (1, "input_back"): {2: ("A21",)},
    (1, "placed"): {None: ("E1", "R1", "S1")},
    (0, "feed_back"): {2: ("R0", "E1", "A21"), 3: ("S1", "R1")},
    (0, "middle_back"): {3: ("E0", "E1", "R1", "R0")},
    (0, "attend_back0"): {0: ("A21", "R1")},
    (0, "group0"): {None: ("S1",)},
    (0, "attend_back1"): {1: ("E1",)},
    (0, "attend_back2"): {1: ("E0", "R0", "E1", "A10", "A21")},
    (0, "input_back"): {0: ("A20",), 3: ("E0",)},
    (0, "placed"): {None: ("R0",)},
}
LAST = ("S0", "A10", "E0", "A21", "R0", "A20", "A21", "A10", "S0", "E0", "R0", "A20", "R0", "A10", "E0", "S0", "A20", "E0", "A10", "A20", "A10", "A20")


def kernel(side, mesh_shape, *refs):
    refs = list(refs)

    def take(n):
        got = refs[:n]
        del refs[:n]
        return got

    tokens, ids, gain, offset, w_in, b_in, table, w_out, b_out, w_exp, b_exp, w_red, b_red, cot = take(14)
    fused = mesh_shape is not None
    out, grad_tokens, d_attn, d_feed, small = take(5)
    (x, normed, qkv, probs, mixed, mid, second, hidden, slope) = take(9)
    (keys, bias, bias_sum, g, gs, gz, gb_low, dqkv, go, d_bexp, turn, spread) = take(12)
    flows = {}
    if fused:
        out_attn, out_feed, out_small = d_attn, d_feed, small
        d_attn, d_feed, small = take(3)
        local_exp, local_bexp, local_red = w_exp, b_exp, w_red
        w_exp, b_exp, w_red = take(3)
        small_buffers = take(3)
        flow_rows, shapes = flow_table(mesh_shape, x.shape[2], local_exp.shape[2])
        landing = {name: take(len(shapes[name])) for name in flow_rows}
        local_sems, send_sem, recv_sem = take(3)
        links = Links(mesh_shape, send_sem, recv_sem)
        for n, (name, (l, first, count, stages)) in enumerate(flow_rows.items()):
            feed_flow = "mlp" in stages
            flows[name] = Flow(
                links,
                d_feed.at[l] if feed_flow else d_attn.at[pl.ds(l, 1)],
                out_feed.at[l] if feed_flow else out_attn.at[l],
                first,
                count,
                stages,
                landing[name],
                local_sems.at[3 + n],
            )
        for l in (1, 0):
            flows[f"S{l}"] = SmallFlow(links, small.at[l], [b.at[l] for b in small_buffers], out_small.at[l])

    def advance(*names):
        if fused:
            for name in names:
                flows[name].advance()

    def ticks(l, phase, i=None):
        for iteration, names in PLAN.get((l, phase), {}).items():
            if i is None:
                advance(*names)
            elif fused:
                pl.when(i == iteration)(functools.partial(advance, *names))

    per_side = side // WIN
    windows = per_side * per_side
    rows = windows * SLOTS
    blocks = rows // ROWS_BLOCK
    shards, _, width, ff = w_exp.shape
    chunk = 256 if ff % 256 == 0 else ff
    blocked = ff % width == 0
    part_rows = 4 * width // PART

    if fused:
        links.greet()
        own = [
            pltpu.make_async_copy(local_exp, w_exp.at[0], local_sems.at[0]),
            pltpu.make_async_copy(local_red, w_red.at[0], local_sems.at[1]),
        ]
        for copy in own:
            copy.start()
        b_exp[0, 0:2, :] = local_bexp[...].astype(F32)
        halves = (
            pl.ds(pl.multiple_of(links.core * (width // 2), 16), width // 2),
            pl.ds(pl.multiple_of(links.core * (ff // 2), 16), ff // 2),
        )
        weights = ((local_exp, w_exp, halves[0]), (local_red, w_red, halves[1]))
        fetch_sems = links.reserve(4 * (shards - 1))
        pass_sems = links.reserve(4 * (shards - 1))
        bias_sems = links.reserve(shards - 1)

        def fetches(l, n):
            source, dest, half = weights[n]
            return [
                links.copy("mlp", q, source.at[l, half], dest.at[shards - d, l, half], fetch_sems + (2 * l + n) * (shards - 1) + d - 1)
                for d, q in links.peers("mlp")
            ]

        def passes(l, n):
            _, dest, half = weights[n]
            ((_, sibling),) = links.peers("core")
            return [
                links.copy("core", sibling, dest.at[d, l, half], dest.at[d, l, half], pass_sems + (2 * l + n) * (shards - 1) + d - 1)
                for d, _ in links.peers("mlp")
            ]

        def bias_fetches():
            return [links.copy("mlp", q, b_exp.at[0], b_exp.at[shards - d], bias_sems + d - 1) for d, q in links.peers("mlp")]

        def fetch_all():
            for copy in bias_fetches():
                copy.start()
            for l in range(2):
                for n in range(2):
                    for copy in fetches(l, n):
                        copy.start()

        def pass_on(l, n):
            for copy in fetches(l, n):
                copy.wait()
            for copy in passes(l, n):
                copy.start()

        def passed(l, n):
            for copy in passes(l, n):
                copy.wait()

    def over_blocks(body, tick=None):
        def step(i, carry):
            body(pl.ds(pl.multiple_of(i * ROWS_BLOCK, ROWS_BLOCK), ROWS_BLOCK))
            if tick:
                ticks(*tick, i)
            return carry

        lax.fori_loop(0, blocks, step, 0)

    def put_tokens(wr, wc, r, tile):
        x[0, pl.ds(window_row(per_side, wr, wc, r), PITCH), :] = tile

    grid_to_windows(tokens, side, False, put_tokens)
    if fused:
        links.meet()
        fetch_all()

    for l in range(2):
        shifted = l == 1

        def put_keys(wr, wc, r, tile, shifted=shifted):
            lane = iota(tile.shape, 1).astype(F32)
            slot = iota(tile.shape, 0)
            label = tile
            if shifted:
                row_at = wr * WIN + r
                row_label = jnp.where(row_at >= side - WIN, 1, 0) + jnp.where(row_at >= side - SHIFT, 1, 0)
                col_at = wc * WIN + slot
                col_label = jnp.where(col_at >= side - WIN, 1, 0) + jnp.where(col_at >= side - SHIFT, 1, 0)
                label = label + (12 * row_label + 4 * col_label).astype(F32)
            hot = jnp.where((lane == label) & (slot < WIN), 1.0, 0.0)
            keys[pl.ds(window_row(per_side, wr, wc, r), PITCH), :] = hot

        grid_to_windows(ids, side, shifted, put_keys)

        krow = iota((SLOTS, 128), 0)
        qlane = iota((SLOTS, 128), 1)
        ahead = (qlane & (PITCH - 1)) >= (krow & (PITCH - 1))
        turn[...] = jnp.zeros(turn.shape, F32)
        for lane, entry, count, s in table_spans():
            turn[s, lane : lane + count, :HEADS] = table[l, entry : entry + count, :]
        for s in range(2):
            spread[s] = turn[s].T[: spread.shape[1]]
        for grp in range(GROUPS):
            low = jnp.zeros((SLOTS, 128), F32)
            high = jnp.zeros((SLOTS, 128), F32)
            for j in range(GROUP):
                h = grp * GROUP + j
                both = [
                    pltpu.roll(
                        jnp.broadcast_to(spread[s, h : h + 1, :], (SLOTS, 128)),
                        0,
                        1,
                        stride=1,
                        stride_axis=0,
                    )
                    for s in range(2)
                ]
                one = jnp.where(ahead, both[0], both[1])
                at = j * SLOTS
                if at < 128:
                    moved = pltpu.roll(one, at, 1) if at else one
                    low = jnp.where((qlane >= at) & (qlane < at + SLOTS), moved, low)
                if at + SLOTS > 128:
                    moved = pltpu.roll(one, (at - 128) % 128, 1)
                    high = jnp.where((qlane >= at - 128) & (qlane < at - 128 + SLOTS), moved, high)
            bias[grp, :, :128] = low
            bias[grp, :, 128:] = high[:, : GQ - 128]

        bias_row = jnp.concatenate(
            [b_in[l, 0:1, :], jnp.zeros((1, width), F32), b_in[l, 1:2, :]], axis=1
        )

        def project(at, l=l, bias_row=bias_row):
            xhat, _ = norm_stats(x[l, at, :])
            a = (xhat * gain[l, 0:1, :] + offset[l, 0:1, :]).astype(BF16)
            normed[l, at, :] = a
            for c in range(3):
                cols = slice(c * width, (c + 1) * width)
                qkv[l, at, cols] = (dot(a, w_in[l, :, cols]) + bias_row[:, cols]).astype(BF16)

        over_blocks(project)
        if fused and l == 1:
            pass_on(1, 0)
            pass_on(1, 1)

        def attend(i, carry, l=l):
            at = pl.ds(pl.multiple_of(i * ROWS_BLOCK, ROWS_BLOCK), ROWS_BLOCK)
            q = qkv[l, at, :width].astype(F32)
            k = qkv[l, at, width : 2 * width].astype(F32)
            v = qkv[l, at, 2 * width :].astype(F32)
            hot = keys[at, :]
            allowed = []
            for w in range(BLOCK_WINDOWS):
                hot_w = hot[w * SLOTS : (w + 1) * SLOTS]
                same = dot_nt(hot_w.astype(BF16), jnp.concatenate([hot_w] * GROUP, axis=0).astype(BF16))
                allowed.append(same > 0.5)
            scores = [
                dot_nt(k[here, lanes].astype(BF16), expand_heads(q[here, lanes])) for _, _, here, lanes in JOBS
            ]
            scores = [
                jnp.where(allowed[w], s * HEAD_DIM**-0.5 + bias[grp], MASKED)
                for s, (w, grp, _, _) in zip(scores, JOBS)
            ]
            tops = [jnp.max(s, axis=0, keepdims=True) for s in scores]
            raised = [jnp.exp(s - top) for s, top in zip(scores, tops)]
            shares = [1.0 / jnp.sum(e, axis=0, keepdims=True) for e in raised]
            ps = [(e * share).astype(BF16) for e, share in zip(raised, shares)]
            for p, (w, grp, _, _) in zip(ps, JOBS):
                probs[l, BLOCK_WINDOWS * i + w, grp] = p
            outs = [
                fold_heads(dot_tn(p, v[here, lanes].astype(BF16)))
                for p, (_, _, here, lanes) in zip(ps, JOBS)
            ]
            mixed[l, at, :] = by_window(outs).astype(BF16)
            return carry

        lax.fori_loop(0, blocks, attend, 0)

        def middle(at, l=l):
            m = x[l, at, :] + dot(mixed[l, at, :], w_out[l]) + b_out[l : l + 1, :]
            mid[l, at, :] = m
            xhat, _ = norm_stats(m)
            second[l, at, :] = (xhat * gain[l, 1:2, :] + offset[l, 1:2, :]).astype(BF16)
            gs[at, :] = m + b_red[l : l + 1, :]

        over_blocks(middle)
        if fused and l == 0:
            pass_on(0, 0)
            for copy in own:
                copy.wait()

        def feed(at, i, l=l):
            s = second[l, at, :]
            total = gs[at, :]
            jobs = [slice(c, c + chunk) for c in range(0, ff, chunk)]
            before = dot(s, w_exp[i, l, :, jobs[0]])
            held = None
            for n, cols in enumerate(jobs):
                after = dot(s, w_exp[i, l, :, jobs[n + 1]]) if n + 1 < len(jobs) else None
                if held is not None:
                    total = total + dot(*held)
                value, slope_now = gelu_pair(before + b_exp[i, l : l + 1, cols])
                value = value.astype(BF16)
                hidden[l, i, at, cols] = value
                slope[l, i, at, cols] = slope_now.astype(BF16)
                held = (value, w_red[i, l, cols, :])
                before = after
            gs[at, :] = total + dot(*held)

        over_blocks(functools.partial(feed, i=0))
        if fused:
            if l == 0:
                pass_on(0, 1)
                for copy in bias_fetches():
                    copy.wait()
            passed(l, 0)
            passed(l, 1)

        def feed_rest(i, carry, feed=feed):
            over_blocks(functools.partial(feed, i=i))
            return carry

        lax.fori_loop(1, shards, feed_rest, 0)

        if l == 0:
            regular_to_shifted(gs, x.at[1], side)

    def put_cot(wr, wc, r, tile):
        g[pl.ds(window_row(per_side, wr, wc, r), PITCH), :] = tile

    grid_to_windows(cot, side, True, put_cot)
    small[...] = jnp.zeros(small.shape, F32)

    for l in (1, 0):

        def add_small(name, value, l=l):
            at = SMALL[name]
            small[l, at : at + 1, :] += value

        def lower(at, l=l):
            g_now = g[at, :]
            add_small("reduce", jnp.sum(g_now, axis=0, keepdims=True))
            gz[at, :] = g_now.astype(BF16)

        over_blocks(lower)

        def reduce_weights(i, carry, l=l):
            for c in range(0, ff, chunk):
                d_feed[l, i, ff + c : ff + c + chunk, :] = dot_tn(hidden[l, i, :, c : c + chunk], gz[...]).astype(BF16)
            return carry

        lax.fori_loop(0, shards, reduce_weights, 0)
        advance(f"R{l}")
        ticks(l, "reduce_weights")
        if l == 1:
            windows_to_grid(gs, out, side, True)
        d_bexp[...] = jnp.zeros(d_bexp.shape, F32)

        def feed_back(at, l=l):
            g_low = gz[at, :]

            def one(i, total):
                jobs = [slice(c, c + chunk) for c in range(0, ff, chunk)]
                ahead_of = dot_nt(g_low, w_red[i, l, jobs[0], :])
                held = None
                for n, cols in enumerate(jobs):
                    after = dot_nt(g_low, w_red[i, l, jobs[n + 1], :]) if n + 1 < len(jobs) else None
                    if held is not None:
                        total = total + dot_nt(*held)
                    gb = ahead_of * slope[l, i, at, cols].astype(F32)
                    d_bexp[i, 0:1, cols] += jnp.sum(gb, axis=0, keepdims=True)
                    low = gb.astype(BF16)
                    gb_low[i, at, cols] = low
                    held = (low, w_exp[i, l, :, cols])
                    ahead_of = after
                return total + dot_nt(*held)

            gs[at, :] = lax.fori_loop(0, shards, one, jnp.zeros((ROWS_BLOCK, width), F32))

        over_blocks(feed_back, (l, "feed_back"))
        span = min(width, ff)
        for n in range(shards * (ff // span)):
            i, c = n // (ff // span), n % (ff // span) * span
            row = n
            if fused:
                row = lax.rem(links.m + i, shards) * (ff // span) + n % (ff // span)
            small[l, pl.ds(SMALL_EXPAND + row, 1), :span] = d_bexp[i, 0:1, c : c + span]

        def expand_weights(i, carry, l=l):
            if blocked:
                for c in range(0, ff, width):
                    d_feed[l, i, c : c + width, :] = dot_tn(second[l], gb_low[i, :, c : c + width]).astype(BF16)
            else:
                d_feed[l, i, :ff, :] = dot_tn(gb_low[i], second[l]).astype(BF16)
            return carry

        lax.fori_loop(0, shards, expand_weights, 0)
        advance(f"E{l}")
        ticks(l, "expand_weights")

        def middle_back(at, l=l):
            dmid, dgain, doffset = norm_back(mid[l, at, :], gain[l, 1:2, :], gs[at, :])
            add_small("gain2", dgain)
            add_small("bias2", doffset)
            gm = g[at, :] + dmid
            g[at, :] = gm
            add_small("output", jnp.sum(gm, axis=0, keepdims=True))
            low = gm.astype(BF16)
            gz[at, :] = low
            go[at, :] = dot_nt(low, w_out[l]).astype(BF16)

        over_blocks(middle_back, (l, "middle_back"))
        d_mixed = dot_tn(mixed[l], gz[...]).astype(BF16)
        for part in range(PART):
            at = part * part_rows + width
            d_attn[l, at : at + width // PART, :] = d_mixed[part * (width // PART) : (part + 1) * (width // PART)]
        bias_sum[...] = jnp.zeros(bias_sum.shape, F32)

        def attend_back(i, carry, l=l, grp=0):
            count = windows // 2
            at = pl.ds(pl.multiple_of(i * count * SLOTS, count * SLOTS), count * SLOTS)
            parts = [slice(p * width + grp * GLANES, p * width + (grp + 1) * GLANES) for p in range(3)]
            heres = [slice(w * SLOTS, (w + 1) * SLOTS) for w in range(count)]
            q, k, v = (qkv[l, at, part].astype(F32) for part in parts)
            go_now = go[at, parts[0]].astype(F32)
            go_all = [expand_heads(go_now[here]) for here in heres]
            dps = [dot_nt(v[here].astype(BF16), one) for one, here in zip(go_all, heres)]
            lows = [probs[l, count * i + w, grp] for w in range(count)]
            dvs = [dot(p, one) for p, one in zip(lows, go_all)]
            ps = [p.astype(F32) for p in lows]
            pds = [p * dp for p, dp in zip(ps, dps)]
            totals = [jnp.sum(pd, axis=0, keepdims=True) for pd in pds]
            dss = [(pd - p * total).astype(BF16) for pd, p, total in zip(pds, ps, totals)]
            dqs = [
                fold_heads(dot_tn(ds, k[here].astype(BF16))) * HEAD_DIM**-0.5 for ds, here in zip(dss, heres)
            ]
            dks = [dot(ds, expand_heads(q[here])) * HEAD_DIM**-0.5 for ds, here in zip(dss, heres)]
            total = bias_sum[grp]
            for ds in dss:
                total = total + ds.astype(F32)
            bias_sum[grp] = total
            for name, part, made in zip(("query", None, "value"), parts, (dqs, dks, dvs)):
                whole = jnp.concatenate(made, axis=0)
                if name:
                    row = SMALL[name]
                    small[l, row : row + 1, parts[0]] += jnp.sum(whole, axis=0, keepdims=True)
                dqkv[at, part] = whole.astype(BF16)
            ticks(l, f"attend_back{grp}", i)
            return carry

        for grp in range(GROUPS):
            lax.fori_loop(0, 2, functools.partial(attend_back, grp=grp), 0)
            for p in range(3):
                lanes = slice(p * width + grp * GLANES, p * width + (grp + 1) * GLANES)
                d_attn[l, grp * part_rows : grp * part_rows + width, p * GLANES : (p + 1) * GLANES] = dot_tn(
                    normed[l], dqkv[:, lanes]
                ).astype(BF16)
            if f"A{grp}{l}" in flows:
                advance(f"A{grp}{l}")
            ticks(l, f"group{grp}")

        krow = iota((SLOTS, 128), 0)
        qlane = iota((SLOTS, 128), 1)
        ahead = (qlane & (PITCH - 1)) >= (krow & (PITCH - 1))
        for grp in range(GROUPS):
            low = bias_sum[grp, :, :128]
            high = jnp.concatenate([bias_sum[grp, :, 128:], jnp.zeros((SLOTS, 256 - GQ), F32)], axis=1)
            for j in range(GROUP):
                h = grp * GROUP + j
                at = j * SLOTS
                if at + SLOTS <= 128:
                    one = pltpu.roll(low, 128 - at, 1) if at else low
                elif at < 128:
                    one = jnp.where(qlane < 128 - at, pltpu.roll(low, 128 - at, 1), pltpu.roll(high, 128 - at, 1))
                else:
                    one = pltpu.roll(high, (256 - at) % 128, 1)
                one = jnp.where(qlane < SLOTS, one, 0.0)
                for s in range(2):
                    picked = jnp.where(ahead if s == 0 else jnp.logical_not(ahead), one, 0.0)
                    tile = picked[:PITCH]
                    for r in range(1, WIN):
                        tile = tile + pltpu.roll(picked[r * PITCH : (r + 1) * PITCH], 128 - r * PITCH, 1)
                    for step in (1, 2, 4):
                        tile = jnp.where((iota(tile.shape, 0) & step) > 0, pltpu.roll(tile, 128 - step, 1), tile)
                    n = s * HEADS + h
                    small[l, SMALL_TABLE + n // 3 : SMALL_TABLE + n // 3 + 1, n % 3 * 128 : (n % 3 + 1) * 128] = jnp.sum(
                        tile, axis=0, keepdims=True
                    )

        def input_back(at, l=l):
            ga = dot_nt(dqkv[at, :], w_in[l])
            dx, dgain, doffset = norm_back(x[l, at, :], gain[l, 0:1, :], ga)
            add_small("gain1", dgain)
            add_small("bias1", doffset)
            gs[at, :] = g[at, :] + dx

        over_blocks(input_back, (l, "input_back"))
        advance(f"S{l}")
        ticks(l, "input_done")
        if l == 1:
            shifted_to_regular(gs, g, side)
        else:
            windows_to_grid(gs, grad_tokens, side, False)
        ticks(l, "placed")

    advance(*LAST)
    while not all(flow.done for flow in flows.values()):
        advance(*(name for name, flow in flows.items() if not flow.done))


def lanes_table(lanes):
    layers, heads = lanes.shape[0], lanes.shape[1] // 2
    both = lanes.reshape(layers, 2, heads, 128)
    span = SPAN_SIDE * PITCH

    def square(part, back):
        return jnp.roll(part, back, axis=-1)[..., :span].reshape(layers, heads, SPAN_SIDE, PITCH)

    right = square(both[:, 0], (WIN - 1) * PITCH)[..., :WIN]
    left = square(both[:, 1], WIN * PITCH)[..., PITCH - WIN + 1 :]
    whole = jnp.concatenate([left, right], axis=-1)
    return whole.reshape(layers, heads, SPAN_SIDE * SPAN_SIDE).transpose(0, 2, 1)


def on_device(
    mesh_shape,
    tokens,
    crop_ids,
    norm_gain,
    norm_bias,
    input_proj,
    input_bias,
    position_table,
    output_proj,
    output_bias,
    expand_weight,
    expand_bias,
    reduce_weight,
    reduce_bias,
    cotangent,
):
    _, side, _, width = tokens.shape
    layers, _, ff = expand_weight.shape
    win, shards = mesh_shape
    ids = jnp.broadcast_to(crop_ids[0, :, :, None], (side, side, 128))
    windows = (side // WIN) ** 2
    rows = windows * SLOTS
    attn_rows, feed_rows = 4 * width, 2 * ff
    fused = win % 4 == 0 and attn_rows % (16 * PART * win * shards) == 0 and ff % (16 * win) == 0
    vmem = pl.BlockSpec(memory_space=pltpu.VMEM)
    hbm = pl.BlockSpec(memory_space=pl.ANY)
    if fused:
        w_exp, w_red = expand_weight, reduce_weight
        b_exp = expand_bias
    else:
        w_exp = lax.all_gather(expand_weight, "mlp", axis=0)
        w_red = lax.all_gather(reduce_weight, "mlp", axis=0)
        b_exp = lax.all_gather(expand_bias, "mlp", axis=0).astype(F32)
    scratch = [
        pltpu.VMEM((layers, rows, width), F32),
        pltpu.VMEM((layers, rows, width), BF16),
        pltpu.VMEM((layers, rows, 3 * width), BF16),
        pltpu.VMEM((layers, windows, GROUPS, SLOTS, GQ), BF16),
        pltpu.VMEM((layers, rows, width), BF16),
        pltpu.VMEM((layers, rows, width), F32),
        pltpu.VMEM((layers, rows, width), BF16),
        pltpu.VMEM((layers, shards, rows, ff), BF16),
        pltpu.VMEM((layers, shards, rows, ff), BF16),
        pltpu.VMEM((rows, 128), F32),
        pltpu.VMEM((GROUPS, SLOTS, GQ), F32),
        pltpu.VMEM((GROUPS, SLOTS, GQ), F32),
        pltpu.VMEM((rows, width), F32),
        pltpu.VMEM((rows, width), F32),
        pltpu.VMEM((rows, width), BF16),
        pltpu.VMEM((shards, rows, ff), BF16),
        pltpu.VMEM((rows, 3 * width), BF16),
        pltpu.VMEM((rows, width), BF16),
        pltpu.VMEM((shards, 8, ff), F32),
    ]
    small_shape = (layers, SMALL_ROWS, width)
    scratch += [pltpu.VMEM((2, 128, 128), F32), pltpu.VMEM((2, 16, 128), F32)]
    if fused:
        plane, depth = 2 * shards, win // 4
        _, shapes = flow_table(mesh_shape, width, ff)
        scratch += [
            pltpu.VMEM((layers, attn_rows, width), BF16),
            pltpu.VMEM((layers, shards, feed_rows, width), BF16),
            pltpu.VMEM(small_shape, F32),
            pltpu.VMEM((shards, layers, width, ff), BF16),
            pltpu.VMEM((shards, 8, ff), F32),
            pltpu.VMEM((shards, layers, ff, width), BF16),
            pltpu.VMEM((layers, 2) + small_shape[1:], F32),
            pltpu.VMEM((layers, plane) + small_shape[1:], F32),
            pltpu.VMEM((layers, depth) + small_shape[1:], F32),
        ]
        scratch += [pltpu.VMEM(shape, BF16) for group in shapes.values() for shape in group]
        scratch += [
            pltpu.SemaphoreType.DMA((3 + len(shapes),)),
            pltpu.SemaphoreType.DMA((160,)),
            pltpu.SemaphoreType.DMA((160,)),
        ]
    outs = pl.pallas_call(
        functools.partial(kernel, side, mesh_shape if fused else None),
        out_shape=(
            jax.ShapeDtypeStruct(tokens.shape[1:], BF16),
            jax.ShapeDtypeStruct(tokens.shape[1:], BF16),
            jax.ShapeDtypeStruct((layers, attn_rows, width), BF16),
            jax.ShapeDtypeStruct((layers, feed_rows, width) if fused else (layers, shards, feed_rows, width), BF16),
            jax.ShapeDtypeStruct(small_shape, F32),
        ),
        in_specs=[vmem] * 9 + ([hbm, vmem, hbm] if fused else [vmem] * 3) + [vmem] * 2,
        out_specs=[vmem] * 2 + ([hbm] * 2 if fused else [vmem] * 2) + [vmem],
        scratch_shapes=scratch,
        compiler_params=pltpu.CompilerParams(
            vmem_limit_bytes=64 * 1024 * 1024,
            **(dict(collective_id=0, has_side_effects=True) if fused else {}),
        ),
    )(
        tokens[0],
        ids,
        norm_gain,
        norm_bias,
        input_proj,
        input_bias,
        position_table,
        output_proj,
        output_bias,
        w_exp,
        b_exp,
        w_red,
        reduce_bias,
        cotangent[0],
    )
    out, grad_tokens, d_attn, d_feed, small = outs
    if not fused:
        d_attn, small = lax.psum((d_attn, small), ("win", "mlp"))
        d_feed = lax.psum(lax.psum_scatter(d_feed, "mlp", scatter_dimension=1, tiled=False), "win")
    parts = d_attn.reshape(layers, PART, attn_rows // PART, width)
    d_in = jnp.concatenate(
        [parts[:, grp, :width, p * GLANES : (p + 1) * GLANES] for p in range(3) for grp in range(GROUPS)], axis=2
    )
    d_out = parts[:, :, width:].reshape(layers, width, width)
    if ff % width == 0:
        d_exp = jnp.concatenate([d_feed[:, c : c + width] for c in range(0, ff, width)], axis=2)
    else:
        d_exp = d_feed[:, :ff].swapaxes(1, 2)
    span = min(width, ff)
    d_bexp = small[:, SMALL_EXPAND : SMALL_EXPAND + shards * (ff // span), :span].reshape(layers, shards, ff)
    d_bexp = lax.dynamic_index_in_dim(d_bexp, lax.axis_index("mlp"), 1, keepdims=False)
    d_table = small[:, SMALL_TABLE : SMALL_TABLE + 8].reshape(layers, 2 * HEADS, 128)
    return (
        out[None],
        grad_tokens[None],
        small[:, 0:2],
        small[:, 2:4],
        d_in.astype(F32),
        small[:, 4:6],
        lanes_table(d_table),
        d_out.astype(F32),
        small[:, 6],
        d_exp.astype(F32),
        d_bexp,
        d_feed[:, ff:].astype(F32),
        small[:, 7],
    )


def solution(mesh):
    tokens = P(("win", "mlp"), None, None, None)
    placed = (
        tokens,
        P(("win", "mlp"), None, None),
        P(),
        P(),
        P(),
        P(),
        P(),
        P(),
        P(),
        P(None, None, "mlp"),
        P(None, "mlp"),
        P(None, "mlp", None),
        P(),
        tokens,
    )
    return jax.shard_map(
        functools.partial(on_device, (mesh.shape["win"], mesh.shape["mlp"])),
        mesh=mesh,
        in_specs=placed,
        out_specs=(
            tokens,
            tokens,
            P(),
            P(),
            P(),
            P(),
            P(),
            P(),
            P(),
            P(None, None, "mlp"),
            P(None, "mlp"),
            P(None, "mlp", None),
            P(),
        ),
        check_vma=False,
    )
```

```python
import functools

import jax
import jax.numpy as jnp
from jax import lax
from jax.experimental import pallas as pl
from jax.experimental.pallas import tpu as pltpu
from jax.sharding import PartitionSpec as P

HEADS = 12
HEAD_DIM = 32
WIN = 7
SHIFT = 3
SPAN_SIDE = 2 * WIN - 1

EPS = 1e-05
MASKED = -1e30

PITCH = 8
SLOTS = WIN * PITCH
GROUP = 4
GROUPS = HEADS // GROUP
GLANES = GROUP * HEAD_DIM
GQ = GROUP * SLOTS

F32 = jnp.float32
BF16 = jnp.bfloat16

ERF_P = 0.4
ERF_C = (
    0.22567691835428957,
    0.22565742813591003,
    0.2069437219941218,
    0.18213740047970625,
    0.06806251607656177,
    0.1868261013466735,
    -0.09530889147438172,
)


LOG2E = 1.4426950408889634
BELL = 0.3989422804014327


def dot(a, b):
    return lax.dot_general(a, b, (((1,), (0,)), ((), ())), preferred_element_type=F32)


def dot_nt(a, b):
    return lax.dot_general(a, b, (((1,), (1,)), ((), ())), preferred_element_type=F32)


def dot_tn(a, b):
    return lax.dot_general(a, b, (((0,), (0,)), ((), ())), preferred_element_type=F32)


def gelu_pair(u):
    bell = jnp.exp2(u * u * (-0.5 * LOG2E))
    size = jnp.abs(u)
    t = 1.0 / (1.0 + (ERF_P * 0.5**0.5) * size)
    poly = 0.5 * ERF_C[-1] * t + 0.5 * ERF_C[-2]
    for coef in ERF_C[-3::-1]:
        poly = poly * t + 0.5 * coef
    tail = bell * (t * poly)
    phi = jnp.where(u < 0, tail, 1.0 - tail)
    return jnp.maximum(u, 0.0) - size * tail, phi + u * (bell * BELL)


def norm_stats(v):
    centred = v - jnp.mean(v, axis=-1, keepdims=True)
    rstd = lax.rsqrt(jnp.mean(centred * centred, axis=-1, keepdims=True) + EPS)
    return centred * rstd, rstd


def norm_back(v, gain, upstream):
    xhat, rstd = norm_stats(v)
    scaled = upstream * gain
    inner = (
        scaled
        - jnp.mean(scaled, axis=-1, keepdims=True)
        - xhat * jnp.mean(scaled * xhat, axis=-1, keepdims=True)
    )
    return rstd * inner, jnp.sum(upstream * xhat, axis=0, keepdims=True), jnp.sum(upstream, axis=0, keepdims=True)


def iota(shape, dim):
    return lax.broadcasted_iota(jnp.int32, shape, dim)


def expand_heads(rows):
    head = iota(rows.shape, 1) // HEAD_DIM
    return jnp.concatenate([jnp.where(head == j, rows, 0.0) for j in range(GROUP)], axis=0).astype(BF16)


def fold_heads(rows):
    head = iota((SLOTS, GLANES), 1) // HEAD_DIM
    out = rows[:SLOTS]
    for j in range(1, GROUP):
        out = jnp.where(head == j, rows[j * SLOTS : (j + 1) * SLOTS], out)
    return out


def by_window(parts):
    return jnp.concatenate(
        [jnp.concatenate(parts[w * GROUPS : (w + 1) * GROUPS], axis=1) for w in range(BLOCK_WINDOWS)], axis=0
    )


def window_row(per_side, wr, wc, r):
    return pl.multiple_of((wr * per_side + wc) * SLOTS + r * PITCH, PITCH)


def grid_to_windows(src, side, shifted, emit):
    per_side = side // WIN

    def step(wr, carry):
        for r in range(WIN):
            row = lax.rem(wr * WIN + r + (SHIFT if shifted else 0), side)
            line = src[row].astype(F32)
            width = line.shape[1]
            if line.shape[0] < 32:
                line = jnp.concatenate([line, jnp.zeros((32 - line.shape[0], width), F32)], axis=0)
            if shifted:
                i = iota(line.shape, 0)
                line = jnp.where(i < side - SHIFT, pltpu.roll(line, 32 - SHIFT, 0), pltpu.roll(line, side - SHIFT, 0))
            for wc in range(per_side):
                part = line if wc == 0 else pltpu.roll(line, 32 - WIN * wc, 0)
                part = part[:PITCH]
                part = jnp.where(iota(part.shape, 0) < WIN, part, 0.0)
                emit(wr, wc, r, part)
        return carry

    lax.fori_loop(0, per_side, step, 0)


def windows_to_grid(src, dst, side, shifted):
    per_side = side // WIN

    def step(wr, carry):
        for r in range(WIN):
            row = lax.rem(wr * WIN + r + (SHIFT if shifted else 0), side)
            width = src.shape[1]
            line = jnp.zeros((32, width), F32)
            i = iota(line.shape, 0)
            for wc in range(per_side):
                tile = src[pl.ds(window_row(per_side, wr, wc, r), PITCH), :]
                tile = jnp.concatenate([tile, jnp.zeros((32 - PITCH, width), F32)], axis=0)
                if wc:
                    tile = pltpu.roll(tile, WIN * wc, 0)
                line = jnp.where((i >= WIN * wc) & (i < WIN * (wc + 1)), tile, line)
            if shifted:
                line = jnp.where(i < SHIFT, pltpu.roll(line, 32 - side + SHIFT, 0), pltpu.roll(line, SHIFT, 0))
            dst[row] = line[:side].astype(dst.dtype)
        return carry

    lax.fori_loop(0, per_side, step, 0)


def regular_to_shifted(src, dst, side):
    per_side = side // WIN

    def step(wr, carry):
        below = lax.rem(wr + 1, per_side)
        for r in range(WIN):
            sr, srr = (wr, r + SHIFT) if r + SHIFT < WIN else (below, r + SHIFT - WIN)
            for wc in range(per_side):
                here = src[pl.ds(window_row(per_side, sr, wc, srr), PITCH), :]
                right = src[pl.ds(window_row(per_side, sr, (wc + 1) % per_side, srr), PITCH), :]
                i = iota(here.shape, 0)
                tile = jnp.where(
                    i < WIN - SHIFT,
                    pltpu.roll(here, PITCH - SHIFT, 0),
                    jnp.where(i < WIN, pltpu.roll(right, WIN - SHIFT, 0), 0.0),
                )
                dst[pl.ds(window_row(per_side, wr, wc, r), PITCH), :] = tile
        return carry

    lax.fori_loop(0, per_side, step, 0)


def shifted_to_regular(src, dst, side):
    per_side = side // WIN

    def step(wr, carry):
        above = lax.rem(wr + per_side - 1, per_side)
        for r in range(WIN):
            sr, srr = (wr, r - SHIFT) if r >= SHIFT else (above, r - SHIFT + WIN)
            for wc in range(per_side):
                here = src[pl.ds(window_row(per_side, sr, wc, srr), PITCH), :]
                left = src[pl.ds(window_row(per_side, sr, (wc + per_side - 1) % per_side, srr), PITCH), :]
                i = iota(here.shape, 0)
                tile = jnp.where(
                    i < SHIFT,
                    pltpu.roll(left, PITCH - (WIN - SHIFT), 0),
                    jnp.where(i < WIN, pltpu.roll(here, SHIFT, 0), 0.0),
                )
                dst[pl.ds(window_row(per_side, wr, wc, r), PITCH), :] = tile
        return carry

    lax.fori_loop(0, per_side, step, 0)


BLOCK_WINDOWS = 4
ROWS_BLOCK = BLOCK_WINDOWS * SLOTS
JOBS = [
    (w, grp, slice(w * SLOTS, (w + 1) * SLOTS)) for w in range(BLOCK_WINDOWS) for grp in range(GROUPS)
]
SMALL = {"gain1": 0, "gain2": 1, "bias1": 2, "bias2": 3, "query": 4, "value": 5, "output": 6, "reduce": 7}
SMALL_EXPAND = 8
SMALL_EARLY = 16
SMALL_TABLE = {0: 16, 1: 24}
SMALL_ROWS = 32
ADD_ROWS = 96
PART = 3


def table_spans():
    spans = []
    for dr in range(SPAN_SIDE):
        at = PITCH * (dr - WIN + 1)
        spans.append((at % 128, dr * SPAN_SIDE + WIN - 1, WIN, 0))
        spans.append(((at - PITCH) % 128 + PITCH - WIN + 1, dr * SPAN_SIDE, WIN - 1, 1))
    return spans


class Links:
    def __init__(self, mesh_shape, send_sem, recv_sem):
        self.win, self.mlp = mesh_shape
        self.send_sem, self.recv_sem = send_sem, recv_sem
        w, m = lax.axis_index("win"), lax.axis_index("mlp")
        self.core, self.x, self.z, self.m = lax.rem(w, 2), lax.rem(lax.div(w, 2), 2), lax.div(w, 4), m
        self.depth = self.win // 4
        self.groups = {
            "core": (2, self.core, lambda q: self.at(core=q)),
            "x": (2, self.x, lambda q: self.at(x=q)),
            "z": (self.depth, self.z, lambda q: self.at(z=q)),
            "mlp": (self.mlp, m, lambda q: self.at(m=q)),
            "y": (self.mlp, m, lambda q: self.at(m=q)),
            "plane": (
                2 * self.mlp,
                self.x * self.mlp + m,
                lambda q: self.at(x=lax.div(q, self.mlp), m=lax.rem(q, self.mlp)),
            ),
        }
        self.used = 0

    def at(self, core=None, x=None, z=None, m=None):
        core = self.core if core is None else core
        x = self.x if x is None else x
        z = self.z if z is None else z
        m = self.m if m is None else m
        return ((z * 2 + x) * 2 + core, m)

    def peers(self, group):
        size, me, _ = self.groups[group]
        return [(d, lax.rem(me + d, size)) for d in range(1, size)]

    def me(self, group):
        return self.groups[group][1]

    def size(self, group):
        return self.groups[group][0]

    def greet(self):
        sem = pltpu.get_barrier_semaphore()
        for group in ("core", "plane", "z"):
            for _, q in self.peers(group):
                pl.semaphore_signal(
                    sem, inc=1, device_id=self.groups[group][2](q), device_id_type=pl.DeviceIdType.MESH
                )

    def meet(self):
        pl.semaphore_wait(pltpu.get_barrier_semaphore(), sum(self.size(g) - 1 for g in ("core", "plane", "z")))

    def reserve(self, count):
        first = self.used
        self.used += count
        return first

    def copy(self, group, q, src, dst, n):
        return pltpu.make_async_remote_copy(
            src_ref=src,
            dst_ref=dst,
            send_sem=self.send_sem.at[n],
            recv_sem=self.recv_sem.at[n],
            device_id=self.groups[group][2](q),
            device_id_type=pl.DeviceIdType.MESH,
        )


def add_rows(dst, sources, count):
    step = next(n for n in (ADD_ROWS, 64, 48, 32, 16) if count % n == 0)

    def one(i, carry):
        at = pl.ds(pl.multiple_of(i * step, 16), step)
        total = dst[at, :].astype(F32)
        for source in sources:
            total = total + source[at, :].astype(F32)
        dst[at, :] = total.astype(dst.dtype)
        return carry

    lax.fori_loop(0, count // step, one, 0)


FLOWS = {
    "R1": ("R1", 1, 0, ("core", "plane", "z")),
    "E1": ("E1", 1, 0, ("core", "plane", "z")),
    "A01": ("A011", 1, 0, ("core", "y", "x", "z")),
    "A21": ("A121", 1, 0, ("core", "y", "x", "z")),
    "R0a": ("R0", 3, 0, ("core", "mlp", "x", "z")),
    "R0b": ("R0", 3, 1, ("core", "mlp", "x", "z")),
    "R0c": ("R0", 3, 2, ("core", "mlp", "x", "z")),
    "E0a": ("E0", 3, 0, ("core", "mlp", "x", "z")),
    "E0b": ("E0", 3, 1, ("core", "mlp", "x", "z")),
    "E0c": ("E0", 3, 2, ("core", "mlp", "x", "z")),
    "A00": ("A010", 1, 0, ("core", "plane", "z")),
    "A20a": ("A120", 3, 0, ("core", "plane", "z")),
    "A20b": ("A120", 3, 1, ("core", "plane", "z")),
    "A20c": ("A120", 3, 2, ("core", "plane", "z")),
}


def flow_table(mesh_shape, width, ff):
    part = 4 * width // PART
    win, mlp = mesh_shape
    sizes = {"core": 2, "x": 2, "z": win // 4, "mlp": mlp, "y": mlp, "plane": 2 * mlp}
    flows, shapes = {}, {}
    for name, (what, splits, split, stages) in FLOWS.items():
        kind, l = what[0], int(what[-1])
        if kind == "A":
            first, rows = int(what[1]) * part, int(what[2]) * part
        else:
            first, rows = (ff if kind == "R" else 0), ff
        lanes = (split * (width // splits), width // splits)
        slots = mlp if kind in "RE" else 1
        flows[name] = (l, kind in "RE", (first, rows), lanes, stages)
        shapes[name] = []
        for stage in stages:
            if stage == "mlp":
                slots = 1
            elif stage == "plane" and slots > 1:
                slots, rows = 1, rows // 2
            else:
                rows //= sizes[stage]
            shapes[name].append((sizes[stage] - 1, slots, rows, lanes[1]))
    return flows, shapes


def flow_after(what):
    return what if what[0] in "RE" else f"A{int(what[1]) + int(what[2]) - 1}{what[-1]}"


class Flow:
    def __init__(self, links, staged, out, slots, span, lanes, stages, buffers, local_sem):
        self.links, self.staged, self.out, self.local_sem = links, staged, out, local_sem
        self.stages, self.buffers, self.lanes = stages, buffers, pl.ds(*lanes)
        self.spans, self.slots, self.down = [span], [slots], []
        for n, stage in enumerate(stages):
            first, rows = self.spans[-1]
            if stage == "mlp":
                slots = 1
            elif stage == "plane" and slots > 1:
                slots, rows = 1, rows // 2
                first = first + links.x * rows
                self.down.insert(0, (n, "x"))
            else:
                rows = rows // links.size(stage)
                first = first + links.me(stage) * rows
                self.down.insert(0, (n, stage))
            self.spans.append((first, rows))
            self.slots.append(slots)
        self.steps = len(stages) + len(self.down)
        self.sems = [links.reserve(links.size(group) - 1) for group in stages + tuple(group for _, group in self.down)]
        self.at = 0
        self.done = False

    def copies(self, k):
        links = self.links
        made = []
        if k < len(self.stages):
            stage, slots = self.stages[k], self.slots[k]
            (first, _), (_, rows) = self.spans[k], self.spans[k + 1]
            for d, q in links.peers(stage):
                if stage == "mlp":
                    slot, at = pl.ds(d, 1), first
                elif stage == "plane" and slots > 1:
                    slot, at = pl.ds(d % links.mlp, 1), first + lax.div(q, links.mlp) * rows
                else:
                    slot, at = pl.ds(0, slots), first + q * rows
                src = self.staged.at[slot, pl.ds(pl.multiple_of(at, 16), rows), self.lanes]
                made.append(links.copy(stage, q, src, self.buffers[k].at[d - 1], self.sems[k] + d - 1))
            return made
        n, group = self.down[k - len(self.stages)]
        src = self.mine(n + 1, self.staged.at[0] if k == len(self.stages) else self.out)
        for d, q in links.peers(group):
            made.append(links.copy(group, q, src, self.mine(n + 1, self.out), self.sems[k] + d - 1))
        return made

    def mine(self, n, ref):
        first, rows = self.spans[n]
        return ref.at[pl.ds(pl.multiple_of(first, 16), rows), self.lanes]

    def local(self):
        return pltpu.make_async_copy(
            self.mine(len(self.stages), self.staged.at[0]), self.mine(len(self.stages), self.out), self.local_sem
        )

    def advance(self):
        k = self.at
        if k:
            for copy in self.copies(k - 1):
                copy.wait()
            if k - 1 < len(self.stages):
                for slot in range(self.slots[k]):
                    add_rows(
                        self.mine(k, self.staged.at[slot]),
                        [self.buffers[k - 1].at[d - 1, slot] for d, _ in self.links.peers(self.stages[k - 1])],
                        self.spans[k][1],
                    )
            elif k - 1 == len(self.stages):
                self.local().wait()
        if k < self.steps:
            if k == len(self.stages):
                self.local().start()
            for copy in self.copies(k):
                copy.start()
        else:
            self.done = True
        self.at += 1


class SmallFlow:
    def __init__(self, links, value, buffers, out):
        self.links, self.value, self.buffers, self.out = links, value, buffers, out
        self.stages = ("core", "plane", "z")
        self.sems = [links.reserve(links.size(stage) - 1) for stage in self.stages]
        self.at = 0
        self.done = False

    def copies(self, k):
        stage, buffer = self.stages[k], self.buffers[k]
        me = self.links.me(stage)
        return [
            self.links.copy(stage, q, buffer.at[me], buffer.at[me], self.sems[k] + d - 1)
            for d, q in self.links.peers(stage)
        ]

    def advance(self):
        k = self.at
        total = self.value[...] if k == 0 else None
        if k:
            for copy in self.copies(k - 1):
                copy.wait()
            buffer = self.buffers[k - 1]
            total = buffer[0]
            for j in range(1, buffer.shape[0]):
                total = total + buffer[j]
        if k < len(self.stages):
            self.buffers[k][self.links.me(self.stages[k])] = total
            for copy in self.copies(k):
                copy.start()
        else:
            self.out[...] = total
            self.done = True
        self.at += 1


PLAN = {
    (1, "feed_back"): {1: ("R1",)},
    (1, "attend_back0"): {0: ("E1",)},
    (1, "attend_back1"): {0: ("R1",), 1: ("A01",)},
    (1, "input_done"): {None: ("A21",)},
    (1, "placed"): {None: ("E1", "S1", "R1")},
    (0, "reduce_weights"): {None: ("A01",)},
    (0, "feed_back"): {1: ("R0b", "R0c", "R0a"), 2: ("A21", "A01"), 3: ("E1", "S1")},
    (0, "expand_weights"): {None: ("R0b", "R1")},
    (0, "middle_back"): {2: ("E0a", "A21", "R0c", "A01", "E0b", "E0c")},
    (0, "attend_back0"): {0: ("R0b", "R0a", "E1")},
    (0, "group0"): {None: ("E0a",)},
    (0, "attend_back1"): {0: ("S1", "R1", "A00", "R0c"), 1: ("R0a", "A21", "E0b", "R1")},
    (0, "group1"): {None: ("A01",)},
    (0, "attend_back2"): {0: ("R0b", "E0c"), 1: ("E1",)},
    (0, "group2"): {None: ("E0a", "R0c")},
    (0, "input_back"): {1: ("R0a", "E1", "A20a"), 2: ("A20b", "A20c", "A00"), 3: ("E0b", "A21")},
    (0, "table1"): {None: ("R0b", "A01")},
    (0, "placed"): {None: ("E0a", "E0c")},
}
LAST = ("R0c", "S0", "A20a", "R0a", "A20b", "A00", "A20c", "E0a", "A01", "E0b", "A21", "R0b", "A01", "A20a", "A20b", "R0c", "R0b", "A00", "R0c", "A20c", "E0c", "S0", "R0a", "E0b", "E0a", "A20a", "A20b", "R0a", "E0a", "A21", "A20c", "A00", "A21", "E0b", "E0c", "A20a", "A00", "E0b", "A20b", "A20a", "A20c", "A20b", "S0", "E0c", "A20c", "E0c")


def kernel(side, mesh_shape, *refs):
    refs = list(refs)

    def take(n):
        got = refs[:n]
        del refs[:n]
        return got

    tokens, ids, gain, offset, global_in, b_in, table, w_out, b_out, w_exp, b_exp, w_red, b_red, cot = take(14)
    fused = mesh_shape is not None
    out, grad_tokens, d_attn, d_feed, small = take(5)
    (x, normed, qkv, probs, mixed, mid, second, hidden, slope) = take(9)
    (keys, bias, bias_sum, g, gs, gz, gb_low, dqkv, go, d_bexp, turn, spread, w_in, turned, wide, tall, hot_grid, in_sems) = take(18)
    flows = {}
    if fused:
        out_attn, out_feed, out_small = d_attn, d_feed, small
        d_attn, d_feed, small = take(3)
        local_exp, local_bexp, local_red = w_exp, b_exp, w_red
        w_exp, b_exp, w_red = take(3)
        small_buffers = [take(3) for _ in range(2)]
        flow_rows, shapes = flow_table(mesh_shape, x.shape[2], local_exp.shape[2])
        landing = {name: take(len(shapes[name])) for name in flow_rows}
        local_sems, send_sem, recv_sem = take(3)
        links = Links(mesh_shape, send_sem, recv_sem)
        for n, (name, (l, feed_flow, span, lanes, stages)) in enumerate(flow_rows.items()):
            flows[name] = Flow(
                links,
                d_feed.at[l] if feed_flow else d_attn.at[pl.ds(l, 1)],
                out_feed.at[l] if feed_flow else out_attn.at[l],
                mesh_shape[1] if feed_flow else 1,
                span,
                lanes,
                stages,
                landing[name],
                local_sems.at[3 + n],
            )
        for l in (1, 0):
            part = pl.ds(0, SMALL_EARLY if l else SMALL_ROWS)
            flows[f"S{l}"] = SmallFlow(links, small.at[l, part], small_buffers[l], out_small.at[l, part])

    def advance(*names):
        if fused:
            for name in names:
                flows[name].advance()

    def begin(point):
        advance(*(name for name in flows if name in FLOWS and flow_after(FLOWS[name][0]) == point))

    def ticks(l, phase, i=None):
        for iteration, names in PLAN.get((l, phase), {}).items():
            if i is None:
                advance(*names)
            elif fused:
                pl.when(i == iteration)(functools.partial(advance, *names))

    per_side = side // WIN
    windows = per_side * per_side
    rows = windows * SLOTS
    blocks = rows // ROWS_BLOCK
    shards, _, width, ff = w_exp.shape
    chunk = 256 if ff % 256 == 0 else ff
    blocked = ff % width == 0
    part_rows = 4 * width // PART

    gathers = [
        pltpu.make_async_copy(
            global_in.at[l, :, pl.ds(p * width + grp * GLANES, GLANES)],
            w_in.at[l, :, pl.ds(grp * width + p * GLANES, GLANES)],
            in_sems.at[(l * GROUPS + grp) * 3 + p],
        )
        for l in range(2)
        for grp in range(GROUPS)
        for p in range(3)
    ]
    for copy in gathers:
        copy.start()
    if fused:
        links.greet()
        own = [
            pltpu.make_async_copy(local_exp, w_exp.at[0], local_sems.at[0]),
            pltpu.make_async_copy(local_red, w_red.at[0], local_sems.at[1]),
        ]
        for copy in own:
            copy.start()
        b_exp[0, 0:2, :] = local_bexp[...].astype(F32)
        halves = (
            pl.ds(pl.multiple_of(links.core * (width // 2), 16), width // 2),
            pl.ds(pl.multiple_of(links.core * (ff // 2), 16), ff // 2),
        )
        weights = ((local_exp, w_exp, halves[0]), (local_red, w_red, halves[1]))
        fetch_sems = links.reserve(4 * (shards - 1))
        pass_sems = links.reserve(4 * (shards - 1))
        bias_sems = links.reserve(shards - 1)

        def fetches(l, n):
            source, dest, half = weights[n]
            return [
                links.copy("mlp", q, source.at[l, half], dest.at[shards - d, l, half], fetch_sems + (2 * l + n) * (shards - 1) + d - 1)
                for d, q in links.peers("mlp")
            ]

        def passes(l, n):
            _, dest, half = weights[n]
            ((_, sibling),) = links.peers("core")
            return [
                links.copy("core", sibling, dest.at[d, l, half], dest.at[d, l, half], pass_sems + (2 * l + n) * (shards - 1) + d - 1)
                for d, _ in links.peers("mlp")
            ]

        def bias_fetches():
            return [links.copy("mlp", q, b_exp.at[0], b_exp.at[shards - d], bias_sems + d - 1) for d, q in links.peers("mlp")]

        def fetch_all():
            for copy in bias_fetches():
                copy.start()
            for l in range(2):
                for n in range(2):
                    for copy in fetches(l, n):
                        copy.start()

        def pass_on(l, n):
            for copy in fetches(l, n):
                copy.wait()
            for copy in passes(l, n):
                copy.start()

        def passed(l, n):
            for copy in passes(l, n):
                copy.wait()

    def over_blocks(body, tick=None, after=None):
        def step(i, carry):
            body(pl.ds(pl.multiple_of(i * ROWS_BLOCK, ROWS_BLOCK), ROWS_BLOCK))
            if tick:
                ticks(*tick, i)
            if after:
                after(i)
            return carry

        lax.fori_loop(0, blocks, step, 0)

    wide[...] = jnp.zeros(wide.shape, F32)
    for row in range(side):
        wide[row : row + 1, :side] = ids[row].astype(F32)
    by_column = wide[:, :128].T[:32]
    for row in range(side):
        hot_grid[row] = jnp.broadcast_to(by_column[:, row : row + 1], (32, 128))
    wide[...] = jnp.zeros(wide.shape, F32)

    def put_tokens(wr, wc, r, tile):
        x[0, pl.ds(window_row(per_side, wr, wc, r), PITCH), :] = tile

    grid_to_windows(tokens, side, False, put_tokens)
    if fused:
        links.meet()
        fetch_all()

    for l in range(2):
        shifted = l == 1

        def put_keys(wr, wc, r, tile, shifted=shifted):
            lane = iota(tile.shape, 1).astype(F32)
            slot = iota(tile.shape, 0)
            label = tile
            if shifted:
                row_at = wr * WIN + r
                row_label = jnp.where(row_at >= side - WIN, 1, 0) + jnp.where(row_at >= side - SHIFT, 1, 0)
                col_at = wc * WIN + slot
                col_label = jnp.where(col_at >= side - WIN, 1, 0) + jnp.where(col_at >= side - SHIFT, 1, 0)
                label = label + (12 * row_label + 4 * col_label).astype(F32)
            hot = jnp.where((lane == label) & (slot < WIN), 1.0, 0.0)
            keys[pl.ds(window_row(per_side, wr, wc, r), PITCH), :] = hot

        grid_to_windows(hot_grid, side, shifted, put_keys)

        krow = iota((SLOTS, 128), 0)
        qlane = iota((SLOTS, 128), 1)
        ahead = (qlane & (PITCH - 1)) >= (krow & (PITCH - 1))
        turn[...] = jnp.zeros(turn.shape, F32)
        for h in range(HEADS):
            wide[h : h + 1, : table.shape[2]] = table[h, l : l + 1, :]
        tall[...] = wide[...].T
        for lane, entry, count, s in table_spans():
            turn[s, lane : lane + count, :] = tall[entry : entry + count, :]
        for s in range(2):
            spread[s] = turn[s].T[: spread.shape[1]]
        for grp in range(GROUPS):
            low = jnp.zeros((SLOTS, 128), F32)
            high = jnp.zeros((SLOTS, 128), F32)
            for j in range(GROUP):
                h = grp * GROUP + j
                both = [
                    pltpu.roll(
                        jnp.broadcast_to(spread[s, h : h + 1, :], (SLOTS, 128)),
                        0,
                        1,
                        stride=1,
                        stride_axis=0,
                    )
                    for s in range(2)
                ]
                one = jnp.where(ahead, both[0], both[1])
                at = j * SLOTS
                if at < 128:
                    moved = pltpu.roll(one, at, 1) if at else one
                    low = jnp.where((qlane >= at) & (qlane < at + SLOTS), moved, low)
                if at + SLOTS > 128:
                    moved = pltpu.roll(one, (at - 128) % 128, 1)
                    high = jnp.where((qlane >= at - 128) & (qlane < at - 128 + SLOTS), moved, high)
            bias[grp, :, :128] = low
            bias[grp, :, 128:] = high[:, : GQ - 128]

        bias_row = jnp.concatenate(
            [
                one[:, grp * GLANES : (grp + 1) * GLANES]
                for grp in range(GROUPS)
                for one in (b_in[l, 0:1, :], jnp.zeros((1, width), F32), b_in[l, 1:2, :])
            ],
            axis=1,
        )
        if l == 0:
            for copy in gathers:
                copy.wait()

        def project(at, l=l, bias_row=bias_row):
            xhat, _ = norm_stats(x[l, at, :])
            a = (xhat * gain[l, 0:1, :] + offset[l, 0:1, :]).astype(BF16)
            normed[l, at, :] = a
            for c in range(3):
                cols = slice(c * width, (c + 1) * width)
                qkv[l, at, cols] = (dot(a, w_in[l, :, cols]) + bias_row[:, cols]).astype(BF16)

        over_blocks(project)
        if fused and l == 1:
            pass_on(1, 0)
            pass_on(1, 1)

        def attend(i, carry, l=l):
            at = pl.ds(pl.multiple_of(i * ROWS_BLOCK, ROWS_BLOCK), ROWS_BLOCK)
            q, k, v = (
                [
                    qkv[l, at, grp * width + p * GLANES : grp * width + (p + 1) * GLANES].astype(F32)
                    for grp in range(GROUPS)
                ]
                for p in range(3)
            )
            hot = keys[at, :]
            allowed = []
            for w in range(BLOCK_WINDOWS):
                hot_w = hot[w * SLOTS : (w + 1) * SLOTS]
                same = dot_nt(hot_w.astype(BF16), jnp.concatenate([hot_w] * GROUP, axis=0).astype(BF16))
                allowed.append(same > 0.5)
            scores = [
                dot_nt(k[grp][here].astype(BF16), expand_heads(q[grp][here])) for _, grp, here in JOBS
            ]
            scores = [
                jnp.where(allowed[w], s * HEAD_DIM**-0.5 + bias[grp], MASKED)
                for s, (w, grp, _) in zip(scores, JOBS)
            ]
            tops = [jnp.max(s, axis=0, keepdims=True) for s in scores]
            raised = [jnp.exp(s - top) for s, top in zip(scores, tops)]
            shares = [1.0 / jnp.sum(e, axis=0, keepdims=True) for e in raised]
            ps = [(e * share).astype(BF16) for e, share in zip(raised, shares)]
            for p, (w, grp, _) in zip(ps, JOBS):
                probs[l, BLOCK_WINDOWS * i + w, grp] = p
            outs = [
                fold_heads(dot_tn(p, v[grp][here].astype(BF16))) for p, (_, grp, here) in zip(ps, JOBS)
            ]
            mixed[l, at, :] = by_window(outs).astype(BF16)
            return carry

        lax.fori_loop(0, blocks, attend, 0)

        def middle(at, l=l):
            m = x[l, at, :] + dot(mixed[l, at, :], w_out[l]) + b_out[l : l + 1, :]
            mid[l, at, :] = m
            xhat, _ = norm_stats(m)
            second[l, at, :] = (xhat * gain[l, 1:2, :] + offset[l, 1:2, :]).astype(BF16)
            gs[at, :] = m + b_red[l : l + 1, :]

        over_blocks(middle)
        if fused and l == 0:
            pass_on(0, 0)
            for copy in own:
                copy.wait()

        def feed(at, i, l=l):
            s = second[l, at, :]
            total = gs[at, :]
            jobs = [slice(c, c + chunk) for c in range(0, ff, chunk)]
            before = dot(s, w_exp[i, l, :, jobs[0]])
            held = None
            for n, cols in enumerate(jobs):
                after = dot(s, w_exp[i, l, :, jobs[n + 1]]) if n + 1 < len(jobs) else None
                if held is not None:
                    total = total + dot(*held)
                value, slope_now = gelu_pair(before + b_exp[i, l : l + 1, cols])
                value = value.astype(BF16)
                hidden[l, i, at, cols] = value
                slope[l, i, at, cols] = slope_now.astype(BF16)
                held = (value, w_red[i, l, cols, :])
                before = after
            gs[at, :] = total + dot(*held)

        over_blocks(functools.partial(feed, i=0))
        if fused:
            if l == 0:
                for copy in bias_fetches():
                    copy.wait()
            passed(l, 0)

        def feed_up(at, i, l=l):
            s = second[l, at, :]
            jobs = [slice(c, c + chunk) for c in range(0, ff, chunk)]
            befores = [dot(s, w_exp[i, l, :, cols]) for cols in jobs]
            for before, cols in zip(befores, jobs):
                value, slope_now = gelu_pair(before + b_exp[i, l : l + 1, cols])
                hidden[l, i, at, cols] = value.astype(BF16)
                slope[l, i, at, cols] = slope_now.astype(BF16)

        def feed_down(at, i, l=l):
            gs[at, :] += dot(hidden[l, i, at, :], w_red[i, l])

        def second_fetch(block, shard, l=l):
            if fused and l == 0:
                pl.when((block == blocks // 2) & (shard == 1))(functools.partial(pass_on, 0, 1))

        def up(i, carry, feed_up=feed_up):
            over_blocks(functools.partial(feed_up, i=i), after=functools.partial(second_fetch, shard=i))
            return carry

        def down(i, carry, feed_down=feed_down):
            over_blocks(functools.partial(feed_down, i=i))
            return carry

        lax.fori_loop(1, shards, up, 0)
        if fused:
            passed(l, 1)
        lax.fori_loop(1, shards, down, 0)

        if l == 0:
            regular_to_shifted(gs, x.at[1], side)

    def put_cot(wr, wc, r, tile):
        g[pl.ds(window_row(per_side, wr, wc, r), PITCH), :] = tile

    grid_to_windows(cot, side, True, put_cot)
    small[...] = jnp.zeros(small.shape, F32)

    def table_back(l):
        krow = iota((SLOTS, 128), 0)
        qlane = iota((SLOTS, 128), 1)
        ahead = (qlane & (PITCH - 1)) >= (krow & (PITCH - 1))
        kept = (ahead & (qlane < SLOTS), jnp.logical_not(ahead) & (qlane < SLOTS))
        lined = []
        for grp in range(GROUPS):
            low = bias_sum[l, grp, :, :128]
            high = jnp.concatenate([bias_sum[l, grp, :, 128:], jnp.zeros((SLOTS, 256 - GQ), F32)], axis=1)
            for j in range(GROUP):
                at = j * SLOTS
                if at + SLOTS <= 128:
                    one = pltpu.roll(low, 128 - at, 1) if at else low
                elif at < 128:
                    one = jnp.where(qlane < 128 - at, pltpu.roll(low, 128 - at, 1), pltpu.roll(high, 128 - at, 1))
                else:
                    one = pltpu.roll(high, (256 - at) % 128, 1)
                lined.append(one)
        picked = [jnp.where(keep, one, 0.0) for keep in kept for one in lined]
        tiles = [one[:PITCH] for one in picked]
        for r in range(1, WIN):
            turned_rows = [pltpu.roll(one[r * PITCH : (r + 1) * PITCH], 128 - r * PITCH, 1) for one in picked]
            tiles = [tile + one for tile, one in zip(tiles, turned_rows)]
        odd = iota((PITCH, 128), 0)
        for step in (1, 2, 4):
            tiles = [jnp.where((odd & step) > 0, pltpu.roll(tile, 128 - step, 1), tile) for tile in tiles]
        for n, tile in enumerate(tiles):
            row = SMALL_TABLE[l] + n // 3
            small[0, row : row + 1, n % 3 * 128 : (n % 3 + 1) * 128] = jnp.sum(tile, axis=0, keepdims=True)


    for l in (1, 0):

        def add_small(name, value, l=l):
            at = SMALL[name]
            small[l, at : at + 1, :] += value

        def lower(at, l=l):
            g_now = g[at, :]
            add_small("reduce", jnp.sum(g_now, axis=0, keepdims=True))
            gz[at, :] = g_now.astype(BF16)

        over_blocks(lower)

        if blocked:
            turned[...] = gz[...].T

        def reduce_weights(i, carry, l=l):
            if blocked:
                for c in range(0, ff, width):
                    d_feed[l, i, ff + c : ff + c + width, :] = dot(turned[...], hidden[l, i, :, c : c + width]).astype(BF16)
            else:
                d_feed[l, i, ff:, :] = dot_tn(hidden[l, i], gz[...]).astype(BF16)
            return carry

        lax.fori_loop(0, shards, reduce_weights, 0)
        begin(f"R{l}")
        ticks(l, "reduce_weights")
        if l == 1:
            windows_to_grid(gs, out, side, True)
        d_bexp[...] = jnp.zeros(d_bexp.shape, F32)

        def feed_back(at, l=l):
            g_low = gz[at, :]

            def one(i, first):
                jobs = [slice(c, c + chunk) for c in range(0, ff, chunk)]
                ghs = [dot_nt(g_low, w_red[i, l, cols, :]) for cols in jobs]
                for gh, cols in zip(ghs, jobs):
                    gb = gh * slope[l, i, at, cols].astype(F32)
                    d_bexp[i, 0:1, cols] += jnp.sum(gb, axis=0, keepdims=True)
                    gb_low[i, at, cols] = gb.astype(BF16)
                part = dot_nt(gb_low[i, at, :], w_exp[i, l])
                if first:
                    gs[at, :] = part
                else:
                    gs[at, :] += part

            one(0, True)

            def rest(i, carry):
                one(i, False)
                return carry

            lax.fori_loop(1, shards, rest, 0)

        over_blocks(feed_back, (l, "feed_back"))
        span = min(width, ff)
        for n in range(shards * (ff // span)):
            i, c = n // (ff // span), n % (ff // span) * span
            row = n
            if fused:
                row = lax.rem(links.m + i, shards) * (ff // span) + n % (ff // span)
            small[l, pl.ds(SMALL_EXPAND + row, 1), :span] = d_bexp[i, 0:1, c : c + span]

        if blocked:
            turned[...] = second[l].T

        def expand_weights(i, carry, l=l):
            if blocked:
                for c in range(0, ff, width):
                    d_feed[l, i, c : c + width, :] = dot(turned[...], gb_low[i, :, c : c + width]).astype(BF16)
            else:
                d_feed[l, i, :ff, :] = dot_tn(gb_low[i], second[l]).astype(BF16)
            return carry

        lax.fori_loop(0, shards, expand_weights, 0)
        begin(f"E{l}")
        ticks(l, "expand_weights")

        def middle_back(at, l=l):
            dmid, dgain, doffset = norm_back(mid[l, at, :], gain[l, 1:2, :], gs[at, :])
            add_small("gain2", dgain)
            add_small("bias2", doffset)
            gm = g[at, :] + dmid
            g[at, :] = gm
            add_small("output", jnp.sum(gm, axis=0, keepdims=True))
            low = gm.astype(BF16)
            gz[at, :] = low
            go[at, :] = dot_nt(low, w_out[l]).astype(BF16)

        over_blocks(middle_back, (l, "middle_back"))
        d_mixed = dot_tn(mixed[l], gz[...]).astype(BF16)
        for part in range(PART):
            at = part * part_rows + width
            d_attn[l, at : at + width // PART, :] = d_mixed[part * (width // PART) : (part + 1) * (width // PART)]
        bias_sum[l] = jnp.zeros(bias_sum.shape[1:], F32)
        turned[...] = normed[l].T

        def attend_back(i, carry, l=l, grp=0):
            count = windows // 2
            at = pl.ds(pl.multiple_of(i * count * SLOTS, count * SLOTS), count * SLOTS)
            parts = [slice(grp * width + p * GLANES, grp * width + (p + 1) * GLANES) for p in range(3)]
            lanes = slice(grp * GLANES, (grp + 1) * GLANES)
            heres = [slice(w * SLOTS, (w + 1) * SLOTS) for w in range(count)]
            q, k, v = (qkv[l, at, part].astype(F32) for part in parts)
            go_now = go[at, lanes].astype(F32)
            go_all = [expand_heads(go_now[here]) for here in heres]
            dps = [dot_nt(v[here].astype(BF16), one) for one, here in zip(go_all, heres)]
            lows = [probs[l, count * i + w, grp] for w in range(count)]
            dvs = [dot(p, one) for p, one in zip(lows, go_all)]
            ps = [p.astype(F32) for p in lows]
            pds = [p * dp for p, dp in zip(ps, dps)]
            totals = [jnp.sum(pd, axis=0, keepdims=True) for pd in pds]
            dss = [(pd - p * total).astype(BF16) for pd, p, total in zip(pds, ps, totals)]
            dqs = [
                fold_heads(dot_tn(ds, k[here].astype(BF16))) * HEAD_DIM**-0.5 for ds, here in zip(dss, heres)
            ]
            dks = [dot(ds, expand_heads(q[here])) * HEAD_DIM**-0.5 for ds, here in zip(dss, heres)]
            total = bias_sum[l, grp]
            for ds in dss:
                total = total + ds.astype(F32)
            bias_sum[l, grp] = total
            for name, part, made in zip(("query", None, "value"), parts, (dqs, dks, dvs)):
                whole = jnp.concatenate(made, axis=0)
                if name:
                    row = SMALL[name]
                    small[l, row : row + 1, lanes] += jnp.sum(whole, axis=0, keepdims=True)
                dqkv[at, part] = whole.astype(BF16)
            ticks(l, f"attend_back{grp}", i)
            return carry

        for grp in range(GROUPS):
            lax.fori_loop(0, 2, functools.partial(attend_back, grp=grp), 0)
            at = grp * part_rows
            cols = slice(grp * width, (grp + 1) * width)
            d_attn[l, at : at + width, :] = dot(turned[...], dqkv[:, cols]).astype(BF16)
            begin(f"A{grp}{l}")
            ticks(l, f"group{grp}")

        def input_back(at, l=l):
            ga = dot_nt(dqkv[at, :], w_in[l])
            dx, dgain, doffset = norm_back(x[l, at, :], gain[l, 0:1, :], ga)
            add_small("gain1", dgain)
            add_small("bias1", doffset)
            gs[at, :] = g[at, :] + dx

        over_blocks(input_back, (l, "input_back"))
        if l == 1:
            advance("S1")
            ticks(l, "input_done")
            shifted_to_regular(gs, g, side)
            ticks(l, "placed")
        else:
            ticks(l, "input_done")
            for one in range(2):
                table_back(one)
                ticks(l, f"table{one}")
            advance("S0")
            windows_to_grid(gs, grad_tokens, side, False)
            ticks(l, "placed")

    advance(*LAST)
    while not all(flow.done for flow in flows.values()):
        advance(*(name for name, flow in flows.items() if not flow.done))


def lanes_table(lanes):
    layers, heads = lanes.shape[0], lanes.shape[1] // 2
    both = lanes.reshape(layers, 2, heads, 128)
    span = SPAN_SIDE * PITCH

    def square(part, back):
        return jnp.roll(part, back, axis=-1)[..., :span].reshape(layers, heads, SPAN_SIDE, PITCH)

    right = square(both[:, 0], (WIN - 1) * PITCH)[..., :WIN]
    left = square(both[:, 1], WIN * PITCH)[..., PITCH - WIN + 1 :]
    whole = jnp.concatenate([left, right], axis=-1)
    return whole.reshape(layers, heads, SPAN_SIDE * SPAN_SIDE).transpose(0, 2, 1)


def on_device(
    mesh_shape,
    tokens,
    crop_ids,
    norm_gain,
    norm_bias,
    input_proj,
    input_bias,
    position_table,
    output_proj,
    output_bias,
    expand_weight,
    expand_bias,
    reduce_weight,
    reduce_bias,
    cotangent,
):
    _, side, _, width = tokens.shape
    layers, _, ff = expand_weight.shape
    win, shards = mesh_shape
    ids = crop_ids.transpose(1, 0, 2)
    windows = (side // WIN) ** 2
    rows = windows * SLOTS
    attn_rows, feed_rows = 4 * width, 2 * ff
    fused = win % 4 == 0 and attn_rows % (16 * PART * win * shards) == 0 and ff % (16 * win) == 0
    vmem = pl.BlockSpec(memory_space=pltpu.VMEM)
    hbm = pl.BlockSpec(memory_space=pl.ANY)
    if fused:
        w_exp, w_red = expand_weight, reduce_weight
        b_exp = expand_bias
    else:
        w_exp = lax.all_gather(expand_weight, "mlp", axis=0)
        w_red = lax.all_gather(reduce_weight, "mlp", axis=0)
        b_exp = lax.all_gather(expand_bias, "mlp", axis=0).astype(F32)
    scratch = [
        pltpu.VMEM((layers, rows, width), F32),
        pltpu.VMEM((layers, rows, width), BF16),
        pltpu.VMEM((layers, rows, 3 * width), BF16),
        pltpu.VMEM((layers, windows, GROUPS, SLOTS, GQ), BF16),
        pltpu.VMEM((layers, rows, width), BF16),
        pltpu.VMEM((layers, rows, width), F32),
        pltpu.VMEM((layers, rows, width), BF16),
        pltpu.VMEM((layers, shards, rows, ff), BF16),
        pltpu.VMEM((layers, shards, rows, ff), BF16),
        pltpu.VMEM((rows, 128), F32),
        pltpu.VMEM((GROUPS, SLOTS, GQ), F32),
        pltpu.VMEM((layers, GROUPS, SLOTS, GQ), F32),
        pltpu.VMEM((rows, width), F32),
        pltpu.VMEM((rows, width), F32),
        pltpu.VMEM((rows, width), BF16),
        pltpu.VMEM((shards, rows, ff), BF16),
        pltpu.VMEM((rows, 3 * width), BF16),
        pltpu.VMEM((rows, width), BF16),
        pltpu.VMEM((shards, 8, ff), F32),
    ]
    small_shape = (layers, SMALL_ROWS, width)
    scratch += [
        pltpu.VMEM((2, 128, 128), F32),
        pltpu.VMEM((2, 16, 128), F32),
        pltpu.VMEM(input_proj.shape, BF16),
        pltpu.VMEM((width, rows), BF16),
        pltpu.VMEM((128, 256), F32),
        pltpu.VMEM((256, 128), F32),
        pltpu.VMEM((side, 32, 128), F32),
        pltpu.SemaphoreType.DMA((layers * GROUPS * 3,)),
    ]
    if fused:
        plane, depth = 2 * shards, win // 4
        _, shapes = flow_table(mesh_shape, width, ff)
        scratch += [
            pltpu.VMEM((layers, attn_rows, width), BF16),
            pltpu.VMEM((layers, shards, feed_rows, width), BF16),
            pltpu.VMEM(small_shape, F32),
            pltpu.VMEM((shards, layers, width, ff), BF16),
            pltpu.VMEM((shards, 8, ff), F32),
            pltpu.VMEM((shards, layers, ff, width), BF16),
        ]
        scratch += [
            pltpu.VMEM((members, count, width), F32)
            for count in (SMALL_ROWS, SMALL_EARLY)
            for members in (2, plane, depth)
        ]
        scratch += [pltpu.VMEM(shape, BF16) for group in shapes.values() for shape in group]
        scratch += [
            pltpu.SemaphoreType.DMA((3 + len(shapes),)),
            pltpu.SemaphoreType.DMA((256,)),
            pltpu.SemaphoreType.DMA((256,)),
        ]
    outs = pl.pallas_call(
        functools.partial(kernel, side, mesh_shape if fused else None),
        out_shape=(
            jax.ShapeDtypeStruct(tokens.shape[1:], BF16),
            jax.ShapeDtypeStruct(tokens.shape[1:], BF16),
            jax.ShapeDtypeStruct((layers, attn_rows, width), BF16),
            jax.ShapeDtypeStruct((layers, feed_rows, width) if fused else (layers, shards, feed_rows, width), BF16),
            jax.ShapeDtypeStruct(small_shape, F32),
        ),
        in_specs=[vmem] * 4 + [hbm] + [vmem] * 4 + ([hbm, vmem, hbm] if fused else [vmem] * 3) + [vmem] * 2,
        out_specs=[vmem] * 2 + ([hbm] * 2 if fused else [vmem] * 2) + [vmem],
        scratch_shapes=scratch,
        compiler_params=pltpu.CompilerParams(
            vmem_limit_bytes=64 * 1024 * 1024,
            **(dict(collective_id=0, has_side_effects=True) if fused else {}),
        ),
    )(
        tokens[0],
        ids,
        norm_gain,
        norm_bias,
        input_proj,
        input_bias,
        position_table.transpose(2, 0, 1),
        output_proj,
        output_bias,
        w_exp,
        b_exp,
        w_red,
        reduce_bias,
        cotangent[0],
    )
    out, grad_tokens, d_attn, d_feed, small = outs
    if not fused:
        d_attn, small = lax.psum((d_attn, small), ("win", "mlp"))
        d_feed = lax.psum(lax.psum_scatter(d_feed, "mlp", scatter_dimension=1, tiled=False), "win")
    if fused and ff % width == 0 and width % 128 == 0 and side % 2 == 0:
        return finish(out, grad_tokens, d_attn, d_feed, small, side, ff)
    parts = d_attn.reshape(layers, PART, attn_rows // PART, width)
    d_in = jnp.concatenate(
        [parts[:, grp, :width, p * GLANES : (p + 1) * GLANES] for p in range(3) for grp in range(GROUPS)], axis=2
    )
    d_out = parts[:, :, width:].reshape(layers, width, width)
    if ff % width == 0:
        d_exp, d_red = (
            jnp.concatenate([d_feed[:, c : c + width] for c in range(first, first + ff, width)], axis=2)
            for first in (0, ff)
        )
        d_red = d_red.swapaxes(1, 2)
    else:
        d_exp, d_red = d_feed[:, :ff].swapaxes(1, 2), d_feed[:, ff:]
    span = min(width, ff)
    d_bexp = small[:, SMALL_EXPAND : SMALL_EXPAND + shards * (ff // span), :span].reshape(layers, shards, ff)
    d_bexp = lax.dynamic_index_in_dim(d_bexp, lax.axis_index("mlp"), 1, keepdims=False)
    d_table = jnp.stack([small[0, SMALL_TABLE[l] : SMALL_TABLE[l] + 8] for l in range(layers)])
    return (
        out[None],
        grad_tokens[None],
        small[:, 0:2],
        small[:, 2:4],
        d_in.astype(F32),
        small[:, 4:6],
        lanes_table(d_table.reshape(layers, 2 * HEADS, 128)),
        d_out.astype(F32),
        small[:, 6],
        d_exp.astype(F32),
        d_bexp,
        d_red.astype(F32),
        small[:, 7],
    )


def finish_kernel(blocks, *refs):
    (a_in, a_out, f_exp, f_red, small, out, grad_tokens) = refs[:7]
    (out_to, grad_to, gain, offset, d_in, b_in, table, d_out, b_out, d_exp, b_exp, d_red, b_red, tall) = refs[7:]
    width = a_in.shape[3]
    out_to[0] = out[...]
    grad_to[0] = grad_tokens[...]
    for grp in range(GROUPS):
        for p in range(3):
            at = p * width + grp * GLANES
            d_in[0, :, at : at + GLANES] = a_in[0, grp, :, p * GLANES : (p + 1) * GLANES].astype(F32)
    d_out[0] = a_out[0, 0].astype(F32)
    for b in range(blocks):
        cols = slice(b * width, (b + 1) * width)
        d_exp[0, :, cols] = f_exp[0, b].astype(F32)
        d_red[0, cols, :] = f_red[0, b].astype(F32).T

    @pl.when((pl.program_id(0) == 0) & (pl.program_id(1) == 0))
    def _():
        for l in range(2):
            gain[l] = small[l, 0:2, :]
            offset[l] = small[l, 2:4, :]
            b_in[l] = small[l, 4:6, :]
            b_out[l : l + 1, :] = small[l, 6:7, :]
            b_red[l : l + 1, :] = small[l, 7:8, :]
            for b in range(blocks):
                row = SMALL_EXPAND + lax.axis_index("mlp") * blocks + b
                b_exp[l : l + 1, b * width : (b + 1) * width] = small[l, pl.ds(row, 1), :]
            turned = []
            for s in range(2):
                heads = []
                for h in range(HEADS):
                    n = s * HEADS + h
                    row = SMALL_TABLE[l] + n // 3
                    heads.append(small[0, row : row + 1, n % 3 * 128 : (n % 3 + 1) * 128])
                heads.append(jnp.zeros((128 - HEADS, 128), F32))
                turned.append(jnp.concatenate(heads, axis=0).T)
            tall[...] = jnp.zeros(tall.shape, F32)
            for lane, entry, count, s in table_spans():
                tall[entry : entry + count, :] = turned[s][lane : lane + count]
            wide = tall[...].T
            for h in range(HEADS):
                table[h, l : l + 1, :] = wide[h : h + 1, : table.shape[2]]


def finish(out, grad_tokens, d_attn, d_feed, small, side, ff):
    layers, attn_rows, width = d_attn.shape
    blocks, steps, half = ff // width, width // 128, side // 2
    part = attn_rows // PART
    attn = d_attn.reshape(layers, PART, part, width)
    feed = d_feed.reshape(layers, 2 * blocks, width, width)
    fixed = lambda *shape: pl.BlockSpec(shape, lambda l, i: (0,) * len(shape))
    grid_in = pl.BlockSpec((half, side, width), lambda l, i: (l, 0, 0))
    grid_out = pl.BlockSpec((1, half, side, width), lambda l, i: (0, l, 0, 0))
    pair, row = fixed(layers, 2, width), fixed(layers, width)
    span = SPAN_SIDE * SPAN_SIDE
    shape = lambda *dims: jax.ShapeDtypeStruct(dims, F32)
    grid_shape = jax.ShapeDtypeStruct((1, side, side, width), BF16)
    made = pl.pallas_call(
        functools.partial(finish_kernel, blocks),
        grid=(layers, steps),
        in_specs=[
            pl.BlockSpec((1, PART, 128, width), lambda l, i: (l, 0, i, 0)),
            pl.BlockSpec((1, 1, 128, width), lambda l, i: (l, i, steps, 0)),
            pl.BlockSpec((1, blocks, 128, width), lambda l, i: (l, 0, i, 0)),
            pl.BlockSpec((1, blocks, 128, width), lambda l, i: (l, 1, i, 0)),
            fixed(*small.shape),
            grid_in,
            grid_in,
        ],
        out_specs=[
            grid_out,
            grid_out,
            pair,
            pair,
            pl.BlockSpec((1, 128, 3 * width), lambda l, i: (l, i, 0)),
            pair,
            fixed(HEADS, layers, span),
            pl.BlockSpec((1, 128, width), lambda l, i: (l, i, 0)),
            row,
            pl.BlockSpec((1, 128, ff), lambda l, i: (l, i, 0)),
            fixed(layers, ff),
            pl.BlockSpec((1, ff, 128), lambda l, i: (l, 0, i)),
            row,
        ],
        out_shape=[
            grid_shape,
            grid_shape,
            shape(layers, 2, width),
            shape(layers, 2, width),
            shape(layers, width, 3 * width),
            shape(layers, 2, width),
            shape(HEADS, layers, span),
            shape(layers, width, width),
            shape(layers, width),
            shape(layers, width, ff),
            shape(layers, ff),
            shape(layers, ff, width),
            shape(layers, width),
        ],
        scratch_shapes=[pltpu.VMEM((256, 128), F32)],
        compiler_params=pltpu.CompilerParams(vmem_limit_bytes=64 * 1024 * 1024),
    )(attn, attn, feed, feed, small, out, grad_tokens)
    return (*made[:6], made[6].transpose(1, 2, 0), *made[7:])


def solution(mesh):
    tokens = P(("win", "mlp"), None, None, None)
    placed = (
        tokens,
        P(("win", "mlp"), None, None),
        P(),
        P(),
        P(),
        P(),
        P(),
        P(),
        P(),
        P(None, None, "mlp"),
        P(None, "mlp"),
        P(None, "mlp", None),
        P(),
        tokens,
    )
    return jax.shard_map(
        functools.partial(on_device, (mesh.shape["win"], mesh.shape["mlp"])),
        mesh=mesh,
        in_specs=placed,
        out_specs=(
            tokens,
            tokens,
            P(),
            P(),
            P(),
            P(),
            P(),
            P(),
            P(),
            P(None, None, "mlp"),
            P(None, "mlp"),
            P(None, "mlp", None),
            P(),
        ),
        check_vma=False,
    )
```

```python
import functools

import jax
import jax.numpy as jnp
from jax import lax
from jax.experimental import pallas as pl
from jax.experimental.pallas import tpu as pltpu
from jax.sharding import PartitionSpec as P

HEADS = 12
HEAD_DIM = 32
WIN = 7
SHIFT = 3
SPAN_SIDE = 2 * WIN - 1

EPS = 1e-05
MASKED = -1e30

PITCH = 8
SLOTS = WIN * PITCH
GROUP = 4
GROUPS = HEADS // GROUP
GLANES = GROUP * HEAD_DIM
GQ = GROUP * SLOTS

F32 = jnp.float32
BF16 = jnp.bfloat16

ERF_P = 0.4
ERF_C = (
    0.22567691835428957,
    0.22565742813591003,
    0.2069437219941218,
    0.18213740047970625,
    0.06806251607656177,
    0.1868261013466735,
    -0.09530889147438172,
)


LOG2E = 1.4426950408889634
BELL = 0.3989422804014327


def dot(a, b):
    return lax.dot_general(a, b, (((1,), (0,)), ((), ())), preferred_element_type=F32)


def dot_nt(a, b):
    return lax.dot_general(a, b, (((1,), (1,)), ((), ())), preferred_element_type=F32)


def dot_tn(a, b):
    return lax.dot_general(a, b, (((0,), (0,)), ((), ())), preferred_element_type=F32)


def gelu_pair(u):
    bell = jnp.exp2(u * u * (-0.5 * LOG2E))
    size = jnp.abs(u)
    t = 1.0 / (1.0 + (ERF_P * 0.5**0.5) * size)
    poly = 0.5 * ERF_C[-1] * t + 0.5 * ERF_C[-2]
    for coef in ERF_C[-3::-1]:
        poly = poly * t + 0.5 * coef
    tail = bell * (t * poly)
    phi = jnp.where(u < 0, tail, 1.0 - tail)
    return jnp.maximum(u, 0.0) - size * tail, phi + u * (bell * BELL)


def norm_stats(v):
    centred = v - jnp.mean(v, axis=-1, keepdims=True)
    rstd = lax.rsqrt(jnp.mean(centred * centred, axis=-1, keepdims=True) + EPS)
    return centred * rstd, rstd


def norm_back(v, gain, upstream):
    xhat, rstd = norm_stats(v)
    scaled = upstream * gain
    inner = (
        scaled
        - jnp.mean(scaled, axis=-1, keepdims=True)
        - xhat * jnp.mean(scaled * xhat, axis=-1, keepdims=True)
    )
    return rstd * inner, jnp.sum(upstream * xhat, axis=0, keepdims=True), jnp.sum(upstream, axis=0, keepdims=True)


def iota(shape, dim):
    return lax.broadcasted_iota(jnp.int32, shape, dim)


def expand_heads(rows):
    head = iota(rows.shape, 1) // HEAD_DIM
    return jnp.concatenate([jnp.where(head == j, rows, 0.0) for j in range(GROUP)], axis=0).astype(BF16)


def fold_heads(rows):
    head = iota((SLOTS, GLANES), 1) // HEAD_DIM
    out = rows[:SLOTS]
    for j in range(1, GROUP):
        out = jnp.where(head == j, rows[j * SLOTS : (j + 1) * SLOTS], out)
    return out


def by_window(parts):
    return jnp.concatenate(
        [jnp.concatenate(parts[w * GROUPS : (w + 1) * GROUPS], axis=1) for w in range(BLOCK_WINDOWS)], axis=0
    )


def window_row(per_side, wr, wc, r):
    return pl.multiple_of((wr * per_side + wc) * SLOTS + r * PITCH, PITCH)


def grid_to_windows(src, side, shifted, emit):
    per_side = side // WIN

    def step(wr, carry):
        for r in range(WIN):
            row = lax.rem(wr * WIN + r + (SHIFT if shifted else 0), side)
            line = src[row].astype(F32)
            width = line.shape[1]
            if line.shape[0] < 32:
                line = jnp.concatenate([line, jnp.zeros((32 - line.shape[0], width), F32)], axis=0)
            if shifted:
                i = iota(line.shape, 0)
                line = jnp.where(i < side - SHIFT, pltpu.roll(line, 32 - SHIFT, 0), pltpu.roll(line, side - SHIFT, 0))
            for wc in range(per_side):
                part = line if wc == 0 else pltpu.roll(line, 32 - WIN * wc, 0)
                part = part[:PITCH]
                part = jnp.where(iota(part.shape, 0) < WIN, part, 0.0)
                emit(wr, wc, r, part)
        return carry

    lax.fori_loop(0, per_side, step, 0)


def windows_to_grid(src, dst, side, shifted):
    per_side = side // WIN

    def step(wr, carry):
        for r in range(WIN):
            row = lax.rem(wr * WIN + r + (SHIFT if shifted else 0), side)
            width = src.shape[1]
            line = jnp.zeros((32, width), F32)
            i = iota(line.shape, 0)
            for wc in range(per_side):
                tile = src[pl.ds(window_row(per_side, wr, wc, r), PITCH), :]
                tile = jnp.concatenate([tile, jnp.zeros((32 - PITCH, width), F32)], axis=0)
                if wc:
                    tile = pltpu.roll(tile, WIN * wc, 0)
                line = jnp.where((i >= WIN * wc) & (i < WIN * (wc + 1)), tile, line)
            if shifted:
                line = jnp.where(i < SHIFT, pltpu.roll(line, 32 - side + SHIFT, 0), pltpu.roll(line, SHIFT, 0))
            dst[row] = line[:side].astype(dst.dtype)
        return carry

    lax.fori_loop(0, per_side, step, 0)


def regular_to_shifted(src, dst, side):
    per_side = side // WIN

    def step(wr, carry):
        below = lax.rem(wr + 1, per_side)
        for r in range(WIN):
            sr, srr = (wr, r + SHIFT) if r + SHIFT < WIN else (below, r + SHIFT - WIN)
            for wc in range(per_side):
                here = src[pl.ds(window_row(per_side, sr, wc, srr), PITCH), :]
                right = src[pl.ds(window_row(per_side, sr, (wc + 1) % per_side, srr), PITCH), :]
                i = iota(here.shape, 0)
                tile = jnp.where(
                    i < WIN - SHIFT,
                    pltpu.roll(here, PITCH - SHIFT, 0),
                    jnp.where(i < WIN, pltpu.roll(right, WIN - SHIFT, 0), 0.0),
                )
                dst[pl.ds(window_row(per_side, wr, wc, r), PITCH), :] = tile
        return carry

    lax.fori_loop(0, per_side, step, 0)


def shifted_to_regular(src, dst, side):
    per_side = side // WIN

    def step(wr, carry):
        above = lax.rem(wr + per_side - 1, per_side)
        for r in range(WIN):
            sr, srr = (wr, r - SHIFT) if r >= SHIFT else (above, r - SHIFT + WIN)
            for wc in range(per_side):
                here = src[pl.ds(window_row(per_side, sr, wc, srr), PITCH), :]
                left = src[pl.ds(window_row(per_side, sr, (wc + per_side - 1) % per_side, srr), PITCH), :]
                i = iota(here.shape, 0)
                tile = jnp.where(
                    i < SHIFT,
                    pltpu.roll(left, PITCH - (WIN - SHIFT), 0),
                    jnp.where(i < WIN, pltpu.roll(here, SHIFT, 0), 0.0),
                )
                dst[pl.ds(window_row(per_side, wr, wc, r), PITCH), :] = tile
        return carry

    lax.fori_loop(0, per_side, step, 0)


BLOCK_WINDOWS = 4
ROWS_BLOCK = BLOCK_WINDOWS * SLOTS
JOBS = [
    (w, grp, slice(w * SLOTS, (w + 1) * SLOTS)) for w in range(BLOCK_WINDOWS) for grp in range(GROUPS)
]
GAIN_1, GAIN_2, OFFSET_1, OFFSET_2, BIAS_Q, BIAS_V, BIAS_OUT, BIAS_REDUCE = range(8)
SMALL_EXPAND = 8
SMALL_EARLY = 16
SMALL_TABLE = {0: 16, 1: 24}
SMALL_ROWS = 32
ADD_ROWS = 96
PART = 3


def table_spans():
    spans = []
    for dr in range(SPAN_SIDE):
        at = PITCH * (dr - WIN + 1)
        spans.append((at % 128, dr * SPAN_SIDE + WIN - 1, WIN, 0))
        spans.append(((at - PITCH) % 128 + PITCH - WIN + 1, dr * SPAN_SIDE, WIN - 1, 1))
    return spans


CORE, X, Y, Z, MLP, PLANE = range(6)


class Links:
    def __init__(self, mesh_shape, send_sem, recv_sem):
        self.win, self.mlp = mesh_shape
        self.send_sem, self.recv_sem = send_sem, recv_sem
        w, m = lax.axis_index("win"), lax.axis_index("mlp")
        self.core, self.x, self.z, self.m = lax.rem(w, 2), lax.rem(lax.div(w, 2), 2), lax.div(w, 4), m
        self.depth = self.win // 4
        self.groups = {
            CORE: (2, self.core, lambda q: self.at(core=q)),
            X: (2, self.x, lambda q: self.at(x=q)),
            Z: (self.depth, self.z, lambda q: self.at(z=q)),
            MLP: (self.mlp, m, lambda q: self.at(m=q)),
            Y: (self.mlp, m, lambda q: self.at(m=q)),
            PLANE: (
                2 * self.mlp,
                self.x * self.mlp + m,
                lambda q: self.at(x=lax.div(q, self.mlp), m=lax.rem(q, self.mlp)),
            ),
        }
        self.used = 0

    def at(self, core=None, x=None, z=None, m=None):
        core = self.core if core is None else core
        x = self.x if x is None else x
        z = self.z if z is None else z
        m = self.m if m is None else m
        return ((z * 2 + x) * 2 + core, m)

    def peers(self, group):
        size, me, _ = self.groups[group]
        return [(d, lax.rem(me + d, size)) for d in range(1, size)]

    def me(self, group):
        return self.groups[group][1]

    def size(self, group):
        return self.groups[group][0]

    def greet(self):
        sem = pltpu.get_barrier_semaphore()
        for group in (CORE, PLANE, Z):
            for _, q in self.peers(group):
                pl.semaphore_signal(
                    sem, inc=1, device_id=self.groups[group][2](q), device_id_type=pl.DeviceIdType.MESH
                )

    def meet(self):
        pl.semaphore_wait(pltpu.get_barrier_semaphore(), sum(self.size(g) - 1 for g in (CORE, PLANE, Z)))

    def reserve(self, count):
        first = self.used
        self.used += count
        return first

    def copy(self, group, q, src, dst, n):
        return pltpu.make_async_remote_copy(
            src_ref=src,
            dst_ref=dst,
            send_sem=self.send_sem.at[n],
            recv_sem=self.recv_sem.at[n],
            device_id=self.groups[group][2](q),
            device_id_type=pl.DeviceIdType.MESH,
        )


def add_rows(dst, sources, count):
    step = next(n for n in (ADD_ROWS, 64, 48, 32, 16) if count % n == 0)

    def one(i, carry):
        at = pl.ds(pl.multiple_of(i * step, 16), step)
        total = dst[at, :].astype(F32)
        for source in sources:
            total = total + source[at, :].astype(F32)
        dst[at, :] = total.astype(dst.dtype)
        return carry

    lax.fori_loop(0, count // step, one, 0)


REDUCE, EXPAND, ATTEND = range(3)
FLOWS = (
    (REDUCE, 1, 0, 0, 3, 0, (CORE, PLANE, Z)),
    (REDUCE, 1, 0, 0, 3, 1, (CORE, PLANE, Z)),
    (REDUCE, 1, 0, 0, 3, 2, (CORE, PLANE, Z)),
    (EXPAND, 1, 0, 0, 3, 0, (CORE, PLANE, Z)),
    (EXPAND, 1, 0, 0, 3, 1, (CORE, PLANE, Z)),
    (EXPAND, 1, 0, 0, 3, 2, (CORE, PLANE, Z)),
    (ATTEND, 1, 0, 1, 1, 0, (CORE, X, Y, Z)),
    (ATTEND, 1, 1, 1, 1, 0, (CORE, Y, X, Z)),
    (ATTEND, 1, 2, 1, 1, 0, (CORE, Y, Z, X)),
    (REDUCE, 0, 0, 0, 3, 0, (CORE, PLANE, Z)),
    (REDUCE, 0, 0, 0, 3, 1, (CORE, PLANE, Z)),
    (REDUCE, 0, 0, 0, 3, 2, (CORE, PLANE, Z)),
    (EXPAND, 0, 0, 0, 3, 0, (CORE, MLP, X, Z)),
    (EXPAND, 0, 0, 0, 3, 1, (CORE, MLP, X, Z)),
    (EXPAND, 0, 0, 0, 3, 2, (CORE, MLP, X, Z)),
    (ATTEND, 0, 0, 1, 1, 0, (CORE, PLANE, Z)),
    (ATTEND, 0, 1, 1, 1, 0, (CORE, PLANE, Z)),
    (ATTEND, 0, 2, 1, 1, 0, (CORE, PLANE, Z)),
)


def flow_table(mesh_shape, width, ff):
    part = 4 * width // PART
    win, mlp = mesh_shape
    sizes = {CORE: 2, X: 2, Y: mlp, Z: win // 4, MLP: mlp, PLANE: 2 * mlp}
    flows, shapes = [], []
    for kind, l, first, count, splits, split, stages in FLOWS:
        if kind == ATTEND:
            first, rows = first * part, count * part
        else:
            first, rows = (ff if kind == REDUCE else 0), ff
        lanes = (split * (width // splits), width // splits)
        slots = 1 if kind == ATTEND else mlp
        flows.append((l, kind != ATTEND, (first, rows), lanes, stages))
        landing = []
        for stage in stages:
            if stage == MLP:
                slots = 1
            elif stage == PLANE and slots > 1:
                slots, rows = 1, rows // 2
            else:
                rows //= sizes[stage]
            landing.append((sizes[stage] - 1, slots, rows, lanes[1]))
        shapes.append(landing)
    return flows, shapes


def small_flow(l):
    return len(FLOWS) + 1 - l


class Flow:
    def __init__(self, links, staged, out, slots, span, lanes, stages, buffers, local_sem):
        self.links, self.staged, self.out, self.local_sem = links, staged, out, local_sem
        self.stages, self.buffers, self.lanes = stages, buffers, pl.ds(*lanes)
        self.spans, self.slots, self.down = [span], [slots], []
        for n, stage in enumerate(stages):
            first, rows = self.spans[-1]
            if stage == MLP:
                slots = 1
            elif stage == PLANE and slots > 1:
                slots, rows = 1, rows // 2
                first = first + links.x * rows
                self.down.insert(0, (n, X))
            else:
                rows = rows // links.size(stage)
                first = first + links.me(stage) * rows
                self.down.insert(0, (n, stage))
            self.spans.append((first, rows))
            self.slots.append(slots)
        self.steps = len(stages) + len(self.down)
        self.sems = [links.reserve(links.size(group) - 1) for group in stages + tuple(group for _, group in self.down)]
        self.at = 0
        self.done = False

    def copies(self, k):
        links = self.links
        made = []
        if k < len(self.stages):
            stage, slots = self.stages[k], self.slots[k]
            (first, _), (_, rows) = self.spans[k], self.spans[k + 1]
            for d, q in links.peers(stage):
                if stage == MLP:
                    slot, at = pl.ds(d, 1), first
                elif stage == PLANE and slots > 1:
                    slot, at = pl.ds(d % links.mlp, 1), first + lax.div(q, links.mlp) * rows
                else:
                    slot, at = pl.ds(0, slots), first + q * rows
                src = self.staged.at[slot, pl.ds(pl.multiple_of(at, 16), rows), self.lanes]
                made.append(links.copy(stage, q, src, self.buffers[k].at[d - 1], self.sems[k] + d - 1))
            return made
        n, group = self.down[k - len(self.stages)]
        src = self.mine(n + 1, self.staged.at[0] if k == len(self.stages) else self.out)
        for d, q in links.peers(group):
            made.append(links.copy(group, q, src, self.mine(n + 1, self.out), self.sems[k] + d - 1))
        return made

    def mine(self, n, ref):
        first, rows = self.spans[n]
        return ref.at[pl.ds(pl.multiple_of(first, 16), rows), self.lanes]

    def local(self):
        return pltpu.make_async_copy(
            self.mine(len(self.stages), self.staged.at[0]), self.mine(len(self.stages), self.out), self.local_sem
        )

    def advance(self):
        k = self.at
        if k:
            for copy in self.copies(k - 1):
                copy.wait()
            if k - 1 < len(self.stages):
                for slot in range(self.slots[k]):
                    add_rows(
                        self.mine(k, self.staged.at[slot]),
                        [self.buffers[k - 1].at[d - 1, slot] for d, _ in self.links.peers(self.stages[k - 1])],
                        self.spans[k][1],
                    )
            elif k - 1 == len(self.stages):
                self.local().wait()
        if k < self.steps:
            if k == len(self.stages):
                self.local().start()
            for copy in self.copies(k):
                copy.start()
        else:
            self.done = True
        self.at += 1


class SmallFlow:
    def __init__(self, links, value, buffers, out):
        self.links, self.value, self.buffers, self.out = links, value, buffers, out
        self.stages = (CORE, PLANE, Z)
        self.sems = [links.reserve(links.size(stage) - 1) for stage in self.stages]
        self.at = 0
        self.done = False

    def copies(self, k):
        stage, buffer = self.stages[k], self.buffers[k]
        me = self.links.me(stage)
        return [
            self.links.copy(stage, q, buffer.at[me], buffer.at[me], self.sems[k] + d - 1)
            for d, q in self.links.peers(stage)
        ]

    def advance(self):
        k = self.at
        total = self.value[...] if k == 0 else None
        if k:
            for copy in self.copies(k - 1):
                copy.wait()
            buffer = self.buffers[k - 1]
            total = buffer[0]
            for j in range(1, buffer.shape[0]):
                total = total + buffer[j]
        if k < len(self.stages):
            self.buffers[k][self.links.me(self.stages[k])] = total
            for copy in self.copies(k):
                copy.start()
        else:
            self.out[...] = total
            self.done = True
        self.at += 1


(AT_REDUCE, AT_FEED, AT_EXPAND, AT_MIDDLE, AT_ATTEND, AT_GROUP, AT_INPUT, AT_SUMS, AT_TABLE, AT_PLACED, AT_OUT) = range(11)
PLAN = {
    (1, AT_MIDDLE, 0): (0, 1),
    (1, AT_MIDDLE, 1): (2,),
    (1, AT_MIDDLE, 2): (3, 4),
    (1, AT_MIDDLE, 3): (5,),
    (1, AT_ATTEND, 2): (0,),
    (1, AT_ATTEND, 3): (6, 1),
    (1, AT_ATTEND, 5): (2, 7),
    (1, AT_INPUT, 0): (0, 3),
    (1, AT_INPUT, 2): (8, 1),
    (1, AT_PLACED, 0): (4,),
    (0, AT_REDUCE, 0): (18, 2, 0, 5),
    (0, AT_FEED, 0): (9, 6, 10, 7, 11, 1, 3),
    (0, AT_FEED, 1): (8, 4),
    (0, AT_FEED, 3): (18, 2, 0),
    (0, AT_EXPAND, 0): (0, 5, 6, 9, 3),
    (0, AT_MIDDLE, 1): (12,),
    (0, AT_MIDDLE, 2): (13, 14, 8),
    (0, AT_MIDDLE, 3): (10, 7),
    (0, AT_ATTEND, 0): (4,),
    (0, AT_ATTEND, 1): (18, 11, 1),
    (0, AT_ATTEND, 2): (2, 15, 6, 8, 9, 13, 1, 3),
    (0, AT_ATTEND, 3): (2, 10, 4, 3),
    (0, AT_ATTEND, 4): (16, 11, 4, 5),
    (0, AT_ATTEND, 5): (6,),
    (0, AT_GROUP, 0): (12, 5),
    (0, AT_GROUP, 1): (14, 12, 7),
    (0, AT_GROUP, 2): (15, 9, 8, 5),
    (0, AT_INPUT, 0): (13,),
    (0, AT_INPUT, 1): (17, 10, 14),
    (0, AT_INPUT, 2): (12,),
    (0, AT_TABLE, 0): (7,),
    (0, AT_TABLE, 1): (6, 11, 16),
    (0, AT_PLACED, 0): (15, 9),
    (0, AT_OUT, 0): (17, 9, 19, 10, 13, 8),
}
LAST = (7, 14, 10, 12, 6, 16, 11, 15, 6, 11, 17, 13, 19, 8, 12, 14, 16, 8, 12, 7, 13, 17, 7, 14, 13, 15, 14, 15, 16, 19, 16, 17, 17)


def kernel(side, mesh_shape, *refs):
    refs = list(refs)

    def take(n):
        got = refs[:n]
        del refs[:n]
        return got

    tokens, ids, gain, offset, global_in, b_in, table, w_out, b_out, w_exp, b_exp, w_red, b_red, cot = take(14)
    fused = mesh_shape is not None
    out, grad_tokens, d_attn, d_feed, small = take(5)
    (x, normed, qkv, probs, mixed, mid, second, hidden, slope) = take(9)
    (keys, bias, bias_sum, g, gs, gz, gb_low, dqkv, go, d_bexp, turn, spread, w_in, turned, gz_turned, wide, tall, hot_grid, in_sems) = take(19)
    flows = []
    if fused:
        out_attn, out_feed, out_small = d_attn, d_feed, small
        d_attn, d_feed, small = take(3)
        local_exp, local_bexp, local_red = w_exp, b_exp, w_red
        w_exp, b_exp, w_red = take(3)
        small_buffers = [take(3) for _ in range(2)]
        flow_rows, shapes = flow_table(mesh_shape, x.shape[2], local_exp.shape[2])
        landing = [take(len(shape)) for shape in shapes]
        local_sems, send_sem, recv_sem = take(3)
        links = Links(mesh_shape, send_sem, recv_sem)
        for n, (l, feed_flow, span, lanes, stages) in enumerate(flow_rows):
            flows.append(
                Flow(
                    links,
                    d_feed.at[l] if feed_flow else d_attn.at[pl.ds(l, 1)],
                    out_feed.at[l] if feed_flow else out_attn.at[l],
                    mesh_shape[1] if feed_flow else 1,
                    span,
                    lanes,
                    stages,
                    landing[n],
                    local_sems.at[3 + n],
                )
            )
        for l in (1, 0):
            part = pl.ds(0, SMALL_EARLY if l else SMALL_ROWS)
            flows.append(SmallFlow(links, small.at[l, part], small_buffers[l], out_small.at[l, part]))

    def advance(*names):
        if fused:
            for name in names:
                flows[name].advance()

    def begin(kind, l, part=0):
        advance(
            *(n for n, flow in enumerate(FLOWS) if flow[:2] == (kind, l) and (kind != ATTEND or flow[2] + flow[3] - 1 == part))
        )

    def ticks(l, point, i=0):
        advance(*PLAN.get((l, point, i), ()))

    def ticks_in_loop(l, point, i, first, count):
        for n in range(count):
            if fused and (l, point, first + n) in PLAN:
                pl.when(i == n)(functools.partial(advance, *PLAN[l, point, first + n]))

    per_side = side // WIN
    windows = per_side * per_side
    rows = windows * SLOTS
    blocks = rows // ROWS_BLOCK
    shards, _, width, ff = w_exp.shape
    chunk = 256 if ff % 256 == 0 else ff
    blocked = ff % width == 0
    part_rows = 4 * width // PART

    gathers = [
        pltpu.make_async_copy(
            global_in.at[l, :, pl.ds(p * width + grp * GLANES, GLANES)],
            w_in.at[l, :, pl.ds(grp * width + p * GLANES, GLANES)],
            in_sems.at[(l * GROUPS + grp) * 3 + p],
        )
        for l in range(2)
        for grp in range(GROUPS)
        for p in range(3)
    ]
    for copy in gathers:
        copy.start()
    if fused:
        links.greet()
        own = [
            pltpu.make_async_copy(local_exp, w_exp.at[0], local_sems.at[0]),
            pltpu.make_async_copy(local_red, w_red.at[0], local_sems.at[1]),
        ]
        for copy in own:
            copy.start()
        b_exp[0, 0:2, :] = local_bexp[...].astype(F32)
        halves = (
            pl.ds(pl.multiple_of(links.core * (width // 2), 16), width // 2),
            pl.ds(pl.multiple_of(links.core * (ff // 2), 16), ff // 2),
        )
        weights = ((local_exp, w_exp, halves[0], width // 4), (local_red, w_red, halves[1], ff // 4))
        fetch_sems = links.reserve(4 * (shards - 1))
        relay_sems = links.reserve(2 * (shards - 1))
        pass_sems = links.reserve(4 * (shards - 1))
        bias_sems = links.reserve(shards - 1)

        def quarter(n):
            rows = weights[n][3]
            return pl.ds(pl.multiple_of((links.core * 2 + links.x) * rows, 16), rows)

        def fetches(l, n):
            source, dest, half, _ = weights[n]
            part = quarter(n) if l else half
            return [
                links.copy(MLP, q, source.at[l, part], dest.at[shards - d, l, part], fetch_sems + (2 * l + n) * (shards - 1) + d - 1)
                for d, q in links.peers(MLP)
            ]

        def relays(n):
            dest, part = weights[n][1], quarter(n)
            ((_, beside),) = links.peers(X)
            return [
                links.copy(X, beside, dest.at[d, 1, part], dest.at[d, 1, part], relay_sems + n * (shards - 1) + d - 1)
                for d, _ in links.peers(MLP)
            ]

        def passes(l, n):
            _, dest, half, _ = weights[n]
            ((_, sibling),) = links.peers(CORE)
            return [
                links.copy(CORE, sibling, dest.at[d, l, half], dest.at[d, l, half], pass_sems + (2 * l + n) * (shards - 1) + d - 1)
                for d, _ in links.peers(MLP)
            ]

        def bias_fetches():
            return [links.copy(MLP, q, b_exp.at[0], b_exp.at[shards - d], bias_sems + d - 1) for d, q in links.peers(MLP)]

        def fetch_all():
            for copy in bias_fetches():
                copy.start()
            for l in range(2):
                for n in range(2):
                    for copy in fetches(l, n):
                        copy.start()

        def relay(n):
            for copy in fetches(1, n):
                copy.wait()
            for copy in relays(n):
                copy.start()

        def pass_on(l, n):
            for copy in relays(n) if l else fetches(l, n):
                copy.wait()
            for copy in passes(l, n):
                copy.start()

        def passed(l, n):
            for copy in passes(l, n):
                copy.wait()

    def over_blocks(body, tick=None, after=None):
        for i in range(blocks):
            body(pl.ds(i * ROWS_BLOCK, ROWS_BLOCK))
            if tick:
                ticks(*tick, i)
            if after:
                after(i)

    wide[...] = jnp.zeros(wide.shape, F32)
    for row in range(side):
        wide[row : row + 1, :side] = ids[row].astype(F32)
    by_column = wide[:, :128].T[:32]
    for row in range(side):
        hot_grid[row] = jnp.broadcast_to(by_column[:, row : row + 1], (32, 128))
    wide[...] = jnp.zeros(wide.shape, F32)

    def put_tokens(wr, wc, r, tile):
        x[0, pl.ds(window_row(per_side, wr, wc, r), PITCH), :] = tile

    grid_to_windows(tokens, side, False, put_tokens)
    if fused:
        links.meet()
        fetch_all()

    def prepare(l):
        shifted = l == 1

        def put_keys(wr, wc, r, tile, shifted=shifted):
            lane = iota(tile.shape, 1).astype(F32)
            slot = iota(tile.shape, 0)
            label = tile
            if shifted:
                row_at = wr * WIN + r
                row_label = jnp.where(row_at >= side - WIN, 1, 0) + jnp.where(row_at >= side - SHIFT, 1, 0)
                col_at = wc * WIN + slot
                col_label = jnp.where(col_at >= side - WIN, 1, 0) + jnp.where(col_at >= side - SHIFT, 1, 0)
                label = label + (12 * row_label + 4 * col_label).astype(F32)
            hot = jnp.where((lane == label) & (slot < WIN), 1.0, 0.0)
            keys[l, pl.ds(window_row(per_side, wr, wc, r), PITCH), :] = hot

        grid_to_windows(hot_grid, side, shifted, put_keys)

        krow = iota((SLOTS, 128), 0)
        qlane = iota((SLOTS, 128), 1)
        ahead = (qlane & (PITCH - 1)) >= (krow & (PITCH - 1))
        turn[...] = jnp.zeros(turn.shape, F32)
        for h in range(HEADS):
            wide[h : h + 1, : table.shape[2]] = table[h, l : l + 1, :]
        tall[...] = wide[...].T
        for lane, entry, count, s in table_spans():
            turn[s, lane : lane + count, :] = tall[entry : entry + count, :]
        for s in range(2):
            spread[s] = turn[s].T[: spread.shape[1]]
        for grp in range(GROUPS):
            low = jnp.zeros((SLOTS, 128), F32)
            high = jnp.zeros((SLOTS, 128), F32)
            for j in range(GROUP):
                h = grp * GROUP + j
                both = [
                    pltpu.roll(
                        jnp.broadcast_to(spread[s, h : h + 1, :], (SLOTS, 128)),
                        0,
                        1,
                        stride=1,
                        stride_axis=0,
                    )
                    for s in range(2)
                ]
                one = jnp.where(ahead, both[0], both[1])
                at = j * SLOTS
                if at < 128:
                    moved = pltpu.roll(one, at, 1) if at else one
                    low = jnp.where((qlane >= at) & (qlane < at + SLOTS), moved, low)
                if at + SLOTS > 128:
                    moved = pltpu.roll(one, (at - 128) % 128, 1)
                    high = jnp.where((qlane >= at - 128) & (qlane < at - 128 + SLOTS), moved, high)
            bias[l, grp, :, :128] = low
            bias[l, grp, :, 128:] = high[:, : GQ - 128]

    def put_cot(wr, wc, r, tile):
        g[pl.ds(window_row(per_side, wr, wc, r), PITCH), :] = tile

    def add_small(l, at, value):
        small[l, at : at + 1, :] += value

    def lower(at, l):
        g_now = g[at, :]
        add_small(l, BIAS_REDUCE, jnp.sum(g_now, axis=0, keepdims=True))
        gz[at, :] = g_now.astype(BF16)

    def feed_up(at, i, l):
        s = second[l, at, :]
        jobs = [slice(c, c + chunk) for c in range(0, ff, chunk)]
        befores = [dot(s, w_exp[i, l, :, cols]) for cols in jobs]
        for before, cols in zip(befores, jobs):
            value, slope_now = gelu_pair(before + b_exp[i, l : l + 1, cols])
            hidden[l, i, at, cols] = value.astype(BF16)
            slope[l, i, at, cols] = slope_now.astype(BF16)

    def feed_down(at, i, l):
        gs[at, :] += dot(hidden[l, i, at, :], w_red[i, l])

    def feed_back(at, i, l, first):
        g_low = gz[at, :]
        jobs = [slice(c, c + chunk) for c in range(0, ff, chunk)]
        ghs = [dot_nt(g_low, w_red[i, l, cols, :]) for cols in jobs]
        for gh, cols in zip(ghs, jobs):
            gb = gh * slope[l, i, at, cols].astype(F32)
            d_bexp[i, 0:1, cols] += jnp.sum(gb, axis=0, keepdims=True)
            gb_low[i, at, cols] = gb.astype(BF16)
        part = dot_nt(gb_low[i, at, :], w_exp[i, l])
        if first:
            gs[at, :] = part
        else:
            gs[at, :] += part

    def reduce_weights(i, l):
        if blocked:
            for c in range(0, ff, width):
                d_feed[l, i, ff + c : ff + c + width, :] = dot(gz_turned[...], hidden[l, i, :, c : c + width]).astype(BF16)
        else:
            d_feed[l, i, ff:, :] = dot_tn(hidden[l, i], gz[...]).astype(BF16)

    def expand_weights(i, l):
        if blocked:
            for c in range(0, ff, width):
                d_feed[l, i, c : c + width, :] = dot(turned[...], gb_low[i, :, c : c + width]).astype(BF16)
        else:
            d_feed[l, i, :ff, :] = dot_tn(gb_low[i], second[l]).astype(BF16)

    def over_shards(first, body):
        def step(i, carry):
            body(i)
            return carry

        lax.fori_loop(first, shards, step, 0)

    small[...] = jnp.zeros(small.shape, F32)
    prepare(0)

    for l in range(2):
        bias_row = jnp.concatenate(
            [
                one[:, grp * GLANES : (grp + 1) * GLANES]
                for grp in range(GROUPS)
                for one in (b_in[l, 0:1, :], jnp.zeros((1, width), F32), b_in[l, 1:2, :])
            ],
            axis=1,
        )
        if l == 0:
            for copy in gathers:
                copy.wait()

        def project(at, l=l, bias_row=bias_row):
            xhat, _ = norm_stats(x[l, at, :])
            a = (xhat * gain[l, 0:1, :] + offset[l, 0:1, :]).astype(BF16)
            normed[l, at, :] = a
            for c in range(3):
                cols = slice(c * width, (c + 1) * width)
                qkv[l, at, cols] = (dot(a, w_in[l, :, cols]) + bias_row[:, cols]).astype(BF16)

        over_blocks(project)

        def attend(i, l=l):
            at = pl.ds(i * ROWS_BLOCK, ROWS_BLOCK)
            q, k, v = (
                [
                    qkv[l, at, grp * width + p * GLANES : grp * width + (p + 1) * GLANES].astype(F32)
                    for grp in range(GROUPS)
                ]
                for p in range(3)
            )
            hot = keys[l, at, :]
            allowed = []
            for w in range(BLOCK_WINDOWS):
                hot_w = hot[w * SLOTS : (w + 1) * SLOTS]
                same = dot_nt(hot_w.astype(BF16), jnp.concatenate([hot_w] * GROUP, axis=0).astype(BF16))
                allowed.append(same > 0.5)
            scores = [
                dot_nt(k[grp][here].astype(BF16), expand_heads(q[grp][here])) for _, grp, here in JOBS
            ]
            scores = [
                jnp.where(allowed[w], s * HEAD_DIM**-0.5 + bias[l, grp], MASKED)
                for s, (w, grp, _) in zip(scores, JOBS)
            ]
            tops = [jnp.max(s, axis=0, keepdims=True) for s in scores]
            raised = [jnp.exp(s - top) for s, top in zip(scores, tops)]
            shares = [1.0 / jnp.sum(e, axis=0, keepdims=True) for e in raised]
            ps = [(e * share).astype(BF16) for e, share in zip(raised, shares)]
            for p, (w, grp, _) in zip(ps, JOBS):
                probs[l, BLOCK_WINDOWS * i + w, grp] = p
            outs = [
                fold_heads(dot_tn(p, v[grp][here].astype(BF16))) for p, (_, grp, here) in zip(ps, JOBS)
            ]
            mixed[l, at, :] = by_window(outs).astype(BF16)

        for i in range(blocks):
            attend(i)

        def middle(at, l=l):
            m = x[l, at, :] + dot(mixed[l, at, :], w_out[l]) + b_out[l : l + 1, :]
            mid[l, at, :] = m
            xhat, _ = norm_stats(m)
            second[l, at, :] = (xhat * gain[l, 1:2, :] + offset[l, 1:2, :]).astype(BF16)
            if l == 0:
                gs[at, :] = m + b_red[l : l + 1, :]

        if fused and l == 1:
            relay(0)
        over_blocks(middle)
        if l == 1:
            break
        if fused:
            pass_on(0, 0)
            for copy in own:
                copy.wait()

        def feed(at, i, l=l):
            s = second[l, at, :]
            total = gs[at, :]
            jobs = [slice(c, c + chunk) for c in range(0, ff, chunk)]
            before = dot(s, w_exp[i, l, :, jobs[0]])
            held = None
            for n, cols in enumerate(jobs):
                after = dot(s, w_exp[i, l, :, jobs[n + 1]]) if n + 1 < len(jobs) else None
                if held is not None:
                    total = total + dot(*held)
                value, slope_now = gelu_pair(before + b_exp[i, l : l + 1, cols])
                value = value.astype(BF16)
                hidden[l, i, at, cols] = value
                slope[l, i, at, cols] = slope_now.astype(BF16)
                held = (value, w_red[i, l, cols, :])
                before = after
            gs[at, :] = total + dot(*held)

        over_blocks(functools.partial(feed, i=0))
        if fused:
            for copy in bias_fetches():
                copy.wait()
            passed(0, 0)

        def second_fetch(block, shard):
            if fused and block == blocks // 2:
                pl.when(shard == 1)(functools.partial(pass_on, 0, 1))

        over_shards(
            1,
            lambda i: over_blocks(functools.partial(feed_up, i=i, l=0), after=functools.partial(second_fetch, shard=i)),
        )
        prepare(1)
        grid_to_windows(cot, side, True, put_cot)
        over_blocks(functools.partial(lower, l=1))
        if blocked:
            gz_turned[...] = gz[...].T
        if fused:
            passed(0, 1)
        over_shards(1, lambda i: over_blocks(functools.partial(feed_down, i=i, l=0)))
        regular_to_shifted(gs, x.at[1], side)

    d_bexp[...] = jnp.zeros(d_bexp.shape, F32)
    if blocked:
        turned[...] = second[1].T
    if fused:
        relay(1)
    over_blocks(functools.partial(feed_up, i=0, l=1))
    if fused:
        pass_on(1, 0)
    over_blocks(functools.partial(feed_back, i=0, l=1, first=True))
    if fused:
        pass_on(1, 1)
    reduce_weights(0, 1)
    expand_weights(0, 1)
    if fused:
        passed(1, 0)
        passed(1, 1)

    def rest(i):
        over_blocks(functools.partial(feed_up, i=i, l=1))
        over_blocks(functools.partial(feed_back, i=i, l=1, first=False))
        reduce_weights(i, 1)

    over_shards(1, rest)

    def table_back(l):
        krow = iota((SLOTS, 128), 0)
        qlane = iota((SLOTS, 128), 1)
        ahead = (qlane & (PITCH - 1)) >= (krow & (PITCH - 1))
        kept = (ahead & (qlane < SLOTS), jnp.logical_not(ahead) & (qlane < SLOTS))
        lined = []
        for grp in range(GROUPS):
            low = bias_sum[l, grp, :, :128]
            high = jnp.concatenate([bias_sum[l, grp, :, 128:], jnp.zeros((SLOTS, 256 - GQ), F32)], axis=1)
            for j in range(GROUP):
                at = j * SLOTS
                if at + SLOTS <= 128:
                    one = pltpu.roll(low, 128 - at, 1) if at else low
                elif at < 128:
                    one = jnp.where(qlane < 128 - at, pltpu.roll(low, 128 - at, 1), pltpu.roll(high, 128 - at, 1))
                else:
                    one = pltpu.roll(high, (256 - at) % 128, 1)
                lined.append(one)
        picked = [jnp.where(keep, one, 0.0) for keep in kept for one in lined]
        tiles = [one[:PITCH] for one in picked]
        for r in range(1, WIN):
            turned_rows = [pltpu.roll(one[r * PITCH : (r + 1) * PITCH], 128 - r * PITCH, 1) for one in picked]
            tiles = [tile + one for tile, one in zip(tiles, turned_rows)]
        odd = iota((PITCH, 128), 0)
        for step in (1, 2, 4):
            tiles = [jnp.where((odd & step) > 0, pltpu.roll(tile, 128 - step, 1), tile) for tile in tiles]
        for n, tile in enumerate(tiles):
            row = SMALL_TABLE[l] + n // 3
            small[0, row : row + 1, n % 3 * 128 : (n % 3 + 1) * 128] = jnp.sum(tile, axis=0, keepdims=True)


    for l in (1, 0):

        if l == 0:
            over_blocks(functools.partial(lower, l=0))
            if blocked:
                gz_turned[...] = gz[...].T
            over_shards(0, functools.partial(reduce_weights, l=0))
        begin(REDUCE, l)
        ticks(l, AT_REDUCE)
        if l == 0:
            d_bexp[...] = jnp.zeros(d_bexp.shape, F32)

            def both(at):
                feed_back(at, 0, 0, True)
                over_shards(1, lambda i: feed_back(at, i, 0, False))

            over_blocks(both, (l, AT_FEED))
        span = min(width, ff)
        for n in range(shards * (ff // span)):
            i, c = n // (ff // span), n % (ff // span) * span
            row = n
            if fused:
                row = lax.rem(links.m + i, shards) * (ff // span) + n % (ff // span)
            small[l, pl.ds(SMALL_EXPAND + row, 1), :span] = d_bexp[i, 0:1, c : c + span]

        if l == 0:
            if blocked:
                turned[...] = second[0].T
            over_shards(0, functools.partial(expand_weights, l=0))
        else:
            over_shards(1, functools.partial(expand_weights, l=1))
        begin(EXPAND, l)
        ticks(l, AT_EXPAND)

        def middle_back(at, l=l):
            dmid, dgain, doffset = norm_back(mid[l, at, :], gain[l, 1:2, :], gs[at, :])
            add_small(l, GAIN_2, dgain)
            add_small(l, OFFSET_2, doffset)
            gm = g[at, :] + dmid
            g[at, :] = gm
            add_small(l, BIAS_OUT, jnp.sum(gm, axis=0, keepdims=True))
            low = gm.astype(BF16)
            gz[at, :] = low
            go[at, :] = dot_nt(low, w_out[l]).astype(BF16)

        over_blocks(middle_back, (l, AT_MIDDLE))
        d_mixed = dot_tn(mixed[l], gz[...]).astype(BF16)
        for part in range(PART):
            at = part * part_rows + width
            d_attn[l, at : at + width // PART, :] = d_mixed[part * (width // PART) : (part + 1) * (width // PART)]
        bias_sum[l] = jnp.zeros(bias_sum.shape[1:], F32)
        turned[...] = normed[l].T

        def attend_back(i, carry, l=l, grp=0):
            count = windows // 2
            at = pl.ds(pl.multiple_of(i * count * SLOTS, count * SLOTS), count * SLOTS)
            parts = [slice(grp * width + p * GLANES, grp * width + (p + 1) * GLANES) for p in range(3)]
            lanes = slice(grp * GLANES, (grp + 1) * GLANES)
            heres = [slice(w * SLOTS, (w + 1) * SLOTS) for w in range(count)]
            q, k, v = (qkv[l, at, part].astype(F32) for part in parts)
            go_now = go[at, lanes].astype(F32)
            go_all = [expand_heads(go_now[here]) for here in heres]
            dps = [dot_nt(v[here].astype(BF16), one) for one, here in zip(go_all, heres)]
            lows = [probs[l, count * i + w, grp] for w in range(count)]
            dvs = [dot(p, one) for p, one in zip(lows, go_all)]
            ps = [p.astype(F32) for p in lows]
            pds = [p * dp for p, dp in zip(ps, dps)]
            totals = [jnp.sum(pd, axis=0, keepdims=True) for pd in pds]
            dss = [(pd - p * total).astype(BF16) for pd, p, total in zip(pds, ps, totals)]
            dqs = [
                fold_heads(dot_tn(ds, k[here].astype(BF16))) * HEAD_DIM**-0.5 for ds, here in zip(dss, heres)
            ]
            dks = [dot(ds, expand_heads(q[here])) * HEAD_DIM**-0.5 for ds, here in zip(dss, heres)]
            total = bias_sum[l, grp]
            for ds in dss:
                total = total + ds.astype(F32)
            bias_sum[l, grp] = total
            for row, part, made in zip((BIAS_Q, None, BIAS_V), parts, (dqs, dks, dvs)):
                whole = jnp.concatenate(made, axis=0)
                if row is not None:
                    small[l, row : row + 1, lanes] += jnp.sum(whole, axis=0, keepdims=True)
                dqkv[at, part] = whole.astype(BF16)
            ticks_in_loop(l, AT_ATTEND, i, 2 * grp, 2)
            return carry

        for grp in range(GROUPS):
            lax.fori_loop(0, 2, functools.partial(attend_back, grp=grp), 0)
            at = grp * part_rows
            cols = slice(grp * width, (grp + 1) * width)
            d_attn[l, at : at + width, :] = dot(turned[...], dqkv[:, cols]).astype(BF16)
            begin(ATTEND, l, grp)
            ticks(l, AT_GROUP, grp)

        def input_back(at, l=l):
            ga = dot_nt(dqkv[at, :], w_in[l])
            dx, dgain, doffset = norm_back(x[l, at, :], gain[l, 0:1, :], ga)
            add_small(l, GAIN_1, dgain)
            add_small(l, OFFSET_1, doffset)
            gs[at, :] = g[at, :] + dx

        over_blocks(input_back, (l, AT_INPUT))
        if l == 1:
            advance(small_flow(1))
            ticks(l, AT_SUMS)
            shifted_to_regular(gs, g, side)
            ticks(l, AT_PLACED)
        else:
            ticks(l, AT_SUMS)
            for one in range(2):
                table_back(one)
                ticks(l, AT_TABLE, one)
            advance(small_flow(0))
            windows_to_grid(gs, grad_tokens, side, False)
            ticks(l, AT_PLACED)

    def last(at):
        total = mid[1, at, :] + b_red[1:2, :] + dot(hidden[1, 0, at, :], w_red[0, 1])

        def add(i, total):
            return total + dot(hidden[1, i, at, :], w_red[i, 1])

        g[at, :] = lax.fori_loop(1, shards, add, total)

    over_blocks(last)
    windows_to_grid(g, out, side, True)
    ticks(0, AT_OUT)

    advance(*LAST)
    while not all(flow.done for flow in flows):
        advance(*(n for n, flow in enumerate(flows) if not flow.done))


def lanes_table(lanes):
    layers, heads = lanes.shape[0], lanes.shape[1] // 2
    both = lanes.reshape(layers, 2, heads, 128)
    span = SPAN_SIDE * PITCH

    def square(part, back):
        return jnp.roll(part, back, axis=-1)[..., :span].reshape(layers, heads, SPAN_SIDE, PITCH)

    right = square(both[:, 0], (WIN - 1) * PITCH)[..., :WIN]
    left = square(both[:, 1], WIN * PITCH)[..., PITCH - WIN + 1 :]
    whole = jnp.concatenate([left, right], axis=-1)
    return whole.reshape(layers, heads, SPAN_SIDE * SPAN_SIDE).transpose(0, 2, 1)


def on_device(
    mesh_shape,
    tokens,
    crop_ids,
    norm_gain,
    norm_bias,
    input_proj,
    input_bias,
    position_table,
    output_proj,
    output_bias,
    expand_weight,
    expand_bias,
    reduce_weight,
    reduce_bias,
    cotangent,
):
    _, side, _, width = tokens.shape
    layers, _, ff = expand_weight.shape
    win, shards = mesh_shape
    ids = crop_ids.transpose(1, 0, 2)
    windows = (side // WIN) ** 2
    rows = windows * SLOTS
    attn_rows, feed_rows = 4 * width, 2 * ff
    fused = win % 4 == 0 and attn_rows % (16 * PART * win * shards) == 0 and ff % (16 * win) == 0
    vmem = pl.BlockSpec(memory_space=pltpu.VMEM)
    hbm = pl.BlockSpec(memory_space=pl.ANY)
    if fused:
        w_exp, w_red = expand_weight, reduce_weight
        b_exp = expand_bias
    else:
        w_exp = lax.all_gather(expand_weight, "mlp", axis=0)
        w_red = lax.all_gather(reduce_weight, "mlp", axis=0)
        b_exp = lax.all_gather(expand_bias, "mlp", axis=0).astype(F32)
    scratch = [
        pltpu.VMEM((layers, rows, width), F32),
        pltpu.VMEM((layers, rows, width), BF16),
        pltpu.VMEM((layers, rows, 3 * width), BF16),
        pltpu.VMEM((layers, windows, GROUPS, SLOTS, GQ), BF16),
        pltpu.VMEM((layers, rows, width), BF16),
        pltpu.VMEM((layers, rows, width), F32),
        pltpu.VMEM((layers, rows, width), BF16),
        pltpu.VMEM((layers, shards, rows, ff), BF16),
        pltpu.VMEM((layers, shards, rows, ff), BF16),
        pltpu.VMEM((layers, rows, 128), F32),
        pltpu.VMEM((layers, GROUPS, SLOTS, GQ), F32),
        pltpu.VMEM((layers, GROUPS, SLOTS, GQ), F32),
        pltpu.VMEM((rows, width), F32),
        pltpu.VMEM((rows, width), F32),
        pltpu.VMEM((rows, width), BF16),
        pltpu.VMEM((shards, rows, ff), BF16),
        pltpu.VMEM((rows, 3 * width), BF16),
        pltpu.VMEM((rows, width), BF16),
        pltpu.VMEM((shards, 8, ff), F32),
    ]
    small_shape = (layers, SMALL_ROWS, width)
    scratch += [
        pltpu.VMEM((2, 128, 128), F32),
        pltpu.VMEM((2, 16, 128), F32),
        pltpu.VMEM(input_proj.shape, BF16),
        pltpu.VMEM((width, rows), BF16),
        pltpu.VMEM((width, rows), BF16),
        pltpu.VMEM((128, 256), F32),
        pltpu.VMEM((256, 128), F32),
        pltpu.VMEM((side, 32, 128), F32),
        pltpu.SemaphoreType.DMA((layers * GROUPS * 3,)),
    ]
    if fused:
        plane, depth = 2 * shards, win // 4
        _, shapes = flow_table(mesh_shape, width, ff)
        scratch += [
            pltpu.VMEM((layers, attn_rows, width), BF16),
            pltpu.VMEM((layers, shards, feed_rows, width), BF16),
            pltpu.VMEM(small_shape, F32),
            pltpu.VMEM((shards, layers, width, ff), BF16),
            pltpu.VMEM((shards, 8, ff), F32),
            pltpu.VMEM((shards, layers, ff, width), BF16),
        ]
        scratch += [
            pltpu.VMEM((members, count, width), F32)
            for count in (SMALL_ROWS, SMALL_EARLY)
            for members in (2, plane, depth)
        ]
        scratch += [pltpu.VMEM(shape, BF16) for group in shapes for shape in group]
        scratch += [
            pltpu.SemaphoreType.DMA((3 + len(shapes),)),
            pltpu.SemaphoreType.DMA((256,)),
            pltpu.SemaphoreType.DMA((256,)),
        ]
    outs = pl.pallas_call(
        functools.partial(kernel, side, mesh_shape if fused else None),
        out_shape=(
            jax.ShapeDtypeStruct(tokens.shape[1:], BF16),
            jax.ShapeDtypeStruct(tokens.shape[1:], BF16),
            jax.ShapeDtypeStruct((layers, attn_rows, width), BF16),
            jax.ShapeDtypeStruct((layers, feed_rows, width) if fused else (layers, shards, feed_rows, width), BF16),
            jax.ShapeDtypeStruct(small_shape, F32),
        ),
        in_specs=[vmem] * 4 + [hbm] + [vmem] * 4 + ([hbm, vmem, hbm] if fused else [vmem] * 3) + [vmem] * 2,
        out_specs=[vmem] * 2 + ([hbm] * 2 if fused else [vmem] * 2) + [vmem],
        scratch_shapes=scratch,
        compiler_params=pltpu.CompilerParams(
            vmem_limit_bytes=64 * 1024 * 1024,
            **(dict(collective_id=0, has_side_effects=True) if fused else {}),
        ),
    )(
        tokens[0],
        ids,
        norm_gain,
        norm_bias,
        input_proj,
        input_bias,
        position_table.transpose(2, 0, 1),
        output_proj,
        output_bias,
        w_exp,
        b_exp,
        w_red,
        reduce_bias,
        cotangent[0],
    )
    out, grad_tokens, d_attn, d_feed, small = outs
    if not fused:
        d_attn, small = lax.psum((d_attn, small), ("win", "mlp"))
        d_feed = lax.psum(lax.psum_scatter(d_feed, "mlp", scatter_dimension=1, tiled=False), "win")
    if fused and ff % width == 0 and width % 128 == 0 and side % 2 == 0:
        return finish(out, grad_tokens, d_attn, d_feed, small, side, ff)
    parts = d_attn.reshape(layers, PART, attn_rows // PART, width)
    d_in = jnp.concatenate(
        [parts[:, grp, :width, p * GLANES : (p + 1) * GLANES] for p in range(3) for grp in range(GROUPS)], axis=2
    )
    d_out = parts[:, :, width:].reshape(layers, width, width)
    if ff % width == 0:
        d_exp, d_red = (
            jnp.concatenate([d_feed[:, c : c + width] for c in range(first, first + ff, width)], axis=2)
            for first in (0, ff)
        )
        d_red = d_red.swapaxes(1, 2)
    else:
        d_exp, d_red = d_feed[:, :ff].swapaxes(1, 2), d_feed[:, ff:]
    span = min(width, ff)
    d_bexp = small[:, SMALL_EXPAND : SMALL_EXPAND + shards * (ff // span), :span].reshape(layers, shards, ff)
    d_bexp = lax.dynamic_index_in_dim(d_bexp, lax.axis_index("mlp"), 1, keepdims=False)
    d_table = jnp.stack([small[0, SMALL_TABLE[l] : SMALL_TABLE[l] + 8] for l in range(layers)])
    return (
        out[None],
        grad_tokens[None],
        small[:, 0:2],
        small[:, 2:4],
        d_in.astype(F32),
        small[:, 4:6],
        lanes_table(d_table.reshape(layers, 2 * HEADS, 128)),
        d_out.astype(F32),
        small[:, 6],
        d_exp.astype(F32),
        d_bexp,
        d_red.astype(F32),
        small[:, 7],
    )


def finish_kernel(blocks, *refs):
    attn, feed, out, grad_tokens, small = refs[:5]
    (out_to, grad_to, gain, offset, d_in, b_in, table, d_out, b_out, d_exp, b_exp, d_red, b_red) = refs[5:18]
    tall, a_held, f_held, in_held, out_held, exp_held, red_held, grid_held, in_sems, out_sems = refs[18:]
    layers, _, width = attn.shape
    part = width + width // PART
    ff = blocks * width
    passing = [
        pltpu.make_async_copy(out, grid_held.at[0], in_sems.at[2 * layers]),
        pltpu.make_async_copy(grad_tokens, grid_held.at[1], in_sems.at[2 * layers + 1]),
    ]
    arriving = [
        [
            pltpu.make_async_copy(attn.at[l], a_held.at[l], in_sems.at[2 * l]),
            pltpu.make_async_copy(feed.at[l], f_held.at[l], in_sems.at[2 * l + 1]),
        ]
        for l in range(layers)
    ]
    for pair in arriving:
        for copy in pair:
            copy.start()
    for copy in passing:
        copy.start()
    leaving = []

    def leave(src, dst):
        copy = pltpu.make_async_copy(src, dst, out_sems.at[len(leaving)])
        copy.start()
        leaving.append(copy)

    for l in range(layers):
        arriving[l][0].wait()
        for grp in range(GROUPS):
            first = grp * part
            for p in range(3):
                at = p * width + grp * GLANES
                in_held[l, :, at : at + GLANES] = a_held[l, first : first + width, p * GLANES : (p + 1) * GLANES].astype(F32)
            rows = width // PART
            out_held[l, grp * rows : (grp + 1) * rows, :] = a_held[l, first + width : first + part, :].astype(F32)
        leave(in_held.at[l], d_in.at[l])
        passing[l].wait()
        leave(grid_held.at[l], (out_to, grad_to)[l].at[0])
        leave(out_held.at[l], d_out.at[l])
        arriving[l][1].wait()
        for b in range(blocks):
            cols = slice(b * width, (b + 1) * width)
            exp_held[l, :, cols] = f_held[l, cols, :].astype(F32)
        leave(exp_held.at[l], d_exp.at[l])
        for b in range(blocks):
            cols = slice(b * width, (b + 1) * width)
            red_held[l, cols, :] = f_held[l, ff + b * width : ff + (b + 1) * width, :].astype(F32).T
        leave(red_held.at[l], d_red.at[l])

    for l in range(2):
        gain[l] = small[l, 0:2, :]
        offset[l] = small[l, 2:4, :]
        b_in[l] = small[l, 4:6, :]
        b_out[l : l + 1, :] = small[l, 6:7, :]
        b_red[l : l + 1, :] = small[l, 7:8, :]
        for b in range(blocks):
            row = SMALL_EXPAND + lax.axis_index("mlp") * blocks + b
            b_exp[l : l + 1, b * width : (b + 1) * width] = small[l, pl.ds(row, 1), :]
        turned = []
        for s in range(2):
            heads = []
            for h in range(HEADS):
                n = s * HEADS + h
                row = SMALL_TABLE[l] + n // 3
                heads.append(small[0, row : row + 1, n % 3 * 128 : (n % 3 + 1) * 128])
            heads.append(jnp.zeros((128 - HEADS, 128), F32))
            turned.append(jnp.concatenate(heads, axis=0).T)
        tall[...] = jnp.zeros(tall.shape, F32)
        for lane, entry, count, s in table_spans():
            tall[entry : entry + count, :] = turned[s][lane : lane + count]
        wide = tall[...].T
        for h in range(HEADS):
            table[h, l : l + 1, :] = wide[h : h + 1, : table.shape[2]]
    for copy in leaving:
        copy.wait()


def finish(out, grad_tokens, d_attn, d_feed, small, side, ff):
    layers, _, width = d_attn.shape
    blocks = ff // width
    vmem = pl.BlockSpec(memory_space=pltpu.VMEM)
    hbm = pl.BlockSpec(memory_space=pl.ANY)
    span = SPAN_SIDE * SPAN_SIDE
    shape = lambda *dims: jax.ShapeDtypeStruct(dims, F32)
    grid_shape = jax.ShapeDtypeStruct((1, side, side, width), BF16)
    large = ((layers, width, 3 * width), (layers, width, width), (layers, width, ff), (layers, ff, width))
    made = pl.pallas_call(
        functools.partial(finish_kernel, blocks),
        in_specs=[hbm] * 4 + [vmem],
        out_specs=[hbm, hbm, vmem, vmem, hbm, vmem, vmem, hbm, vmem, hbm, vmem, hbm, vmem],
        out_shape=[
            grid_shape,
            grid_shape,
            shape(layers, 2, width),
            shape(layers, 2, width),
            shape(*large[0]),
            shape(layers, 2, width),
            shape(HEADS, layers, span),
            shape(*large[1]),
            shape(layers, width),
            shape(*large[2]),
            shape(layers, ff),
            shape(*large[3]),
            shape(layers, width),
        ],
        scratch_shapes=[
            pltpu.VMEM((256, 128), F32),
            pltpu.VMEM(d_attn.shape, BF16),
            pltpu.VMEM(d_feed.shape, BF16),
            *(pltpu.VMEM(dims, F32) for dims in large),
            pltpu.VMEM((2,) + out.shape, BF16),
            pltpu.SemaphoreType.DMA((2 + 2 * layers,)),
            pltpu.SemaphoreType.DMA((2 + 4 * layers,)),
        ],
        compiler_params=pltpu.CompilerParams(vmem_limit_bytes=64 * 1024 * 1024),
    )(d_attn, d_feed, out, grad_tokens, small)
    return (*made[:6], made[6].transpose(1, 2, 0), *made[7:])


def solution(mesh):
    tokens = P(("win", "mlp"), None, None, None)
    placed = (
        tokens,
        P(("win", "mlp"), None, None),
        P(),
        P(),
        P(),
        P(),
        P(),
        P(),
        P(),
        P(None, None, "mlp"),
        P(None, "mlp"),
        P(None, "mlp", None),
        P(),
        tokens,
    )
    return jax.shard_map(
        functools.partial(on_device, (mesh.shape["win"], mesh.shape["mlp"])),
        mesh=mesh,
        in_specs=placed,
        out_specs=(
            tokens,
            tokens,
            P(),
            P(),
            P(),
            P(),
            P(),
            P(),
            P(),
            P(None, None, "mlp"),
            P(None, "mlp"),
            P(None, "mlp", None),
            P(),
        ),
        check_vma=False,
    )
```

```python
import functools

import jax
import jax.numpy as jnp
from jax import lax
from jax.experimental import pallas as pl
from jax.experimental.pallas import tpu as pltpu
from jax.sharding import PartitionSpec as P

HEADS = 12
HEAD_DIM = 32
WIN = 7
SHIFT = 3
SPAN_SIDE = 2 * WIN - 1

EPS = 1e-05
MASKED = -1e30

PITCH = 8
SLOTS = WIN * PITCH
GROUP = 4
GROUPS = HEADS // GROUP
GLANES = GROUP * HEAD_DIM
GQ = GROUP * SLOTS

F32 = jnp.float32
BF16 = jnp.bfloat16

ERF_P = 0.4
ERF_C = (
    0.22567691835428957,
    0.22565742813591003,
    0.2069437219941218,
    0.18213740047970625,
    0.06806251607656177,
    0.1868261013466735,
    -0.09530889147438172,
)


LOG2E = 1.4426950408889634
BELL = 0.3989422804014327


def dot(a, b):
    return lax.dot_general(a, b, (((1,), (0,)), ((), ())), preferred_element_type=F32)


def dot_nt(a, b):
    return lax.dot_general(a, b, (((1,), (1,)), ((), ())), preferred_element_type=F32)


def dot_tn(a, b):
    return lax.dot_general(a, b, (((0,), (0,)), ((), ())), preferred_element_type=F32)


def gelu_pair(u):
    bell = jnp.exp2(u * u * (-0.5 * LOG2E))
    size = jnp.abs(u)
    t = 1.0 / (1.0 + (ERF_P * 0.5**0.5) * size)
    poly = 0.5 * ERF_C[-1] * t + 0.5 * ERF_C[-2]
    for coef in ERF_C[-3::-1]:
        poly = poly * t + 0.5 * coef
    tail = bell * (t * poly)
    phi = jnp.where(u < 0, tail, 1.0 - tail)
    return jnp.maximum(u, 0.0) - size * tail, phi + u * (bell * BELL)


def norm_stats(v):
    centred = v - jnp.mean(v, axis=-1, keepdims=True)
    rstd = lax.rsqrt(jnp.mean(centred * centred, axis=-1, keepdims=True) + EPS)
    return centred * rstd, rstd


def norm_back(v, gain, upstream):
    xhat, rstd = norm_stats(v)
    scaled = upstream * gain
    inner = (
        scaled
        - jnp.mean(scaled, axis=-1, keepdims=True)
        - xhat * jnp.mean(scaled * xhat, axis=-1, keepdims=True)
    )
    return rstd * inner, jnp.sum(upstream * xhat, axis=0, keepdims=True), jnp.sum(upstream, axis=0, keepdims=True)


def iota(shape, dim):
    return lax.broadcasted_iota(jnp.int32, shape, dim)


def expand_heads(rows):
    head = iota(rows.shape, 1) // HEAD_DIM
    return jnp.concatenate([jnp.where(head == j, rows, 0.0) for j in range(GROUP)], axis=0).astype(BF16)


def fold_heads(rows):
    head = iota((SLOTS, GLANES), 1) // HEAD_DIM
    out = rows[:SLOTS]
    for j in range(1, GROUP):
        out = jnp.where(head == j, rows[j * SLOTS : (j + 1) * SLOTS], out)
    return out


def by_window(parts):
    return jnp.concatenate(
        [jnp.concatenate(parts[w * GROUPS : (w + 1) * GROUPS], axis=1) for w in range(BLOCK_WINDOWS)], axis=0
    )


def window_row(per_side, wr, wc, r):
    return pl.multiple_of((wr * per_side + wc) * SLOTS + r * PITCH, PITCH)


def grid_to_windows(src, side, shifted, emit):
    per_side = side // WIN

    def step(wr, carry):
        for r in range(WIN):
            row = lax.rem(wr * WIN + r + (SHIFT if shifted else 0), side)
            line = src[row].astype(F32)
            width = line.shape[1]
            if line.shape[0] < 32:
                line = jnp.concatenate([line, jnp.zeros((32 - line.shape[0], width), F32)], axis=0)
            if shifted:
                i = iota(line.shape, 0)
                line = jnp.where(i < side - SHIFT, pltpu.roll(line, 32 - SHIFT, 0), pltpu.roll(line, side - SHIFT, 0))
            for wc in range(per_side):
                part = line if wc == 0 else pltpu.roll(line, 32 - WIN * wc, 0)
                part = part[:PITCH]
                part = jnp.where(iota(part.shape, 0) < WIN, part, 0.0)
                emit(wr, wc, r, part)
        return carry

    lax.fori_loop(0, per_side, step, 0)


def windows_to_grid(src, dst, side, shifted):
    per_side = side // WIN

    def step(wr, carry):
        for r in range(WIN):
            row = lax.rem(wr * WIN + r + (SHIFT if shifted else 0), side)
            width = src.shape[1]
            line = jnp.zeros((32, width), F32)
            i = iota(line.shape, 0)
            for wc in range(per_side):
                tile = src[pl.ds(window_row(per_side, wr, wc, r), PITCH), :]
                tile = jnp.concatenate([tile, jnp.zeros((32 - PITCH, width), F32)], axis=0)
                if wc:
                    tile = pltpu.roll(tile, WIN * wc, 0)
                line = jnp.where((i >= WIN * wc) & (i < WIN * (wc + 1)), tile, line)
            if shifted:
                line = jnp.where(i < SHIFT, pltpu.roll(line, 32 - side + SHIFT, 0), pltpu.roll(line, SHIFT, 0))
            dst[row] = line[:side].astype(dst.dtype)
        return carry

    lax.fori_loop(0, per_side, step, 0)


def regular_to_shifted(src, dst, side):
    per_side = side // WIN

    def step(wr, carry):
        below = lax.rem(wr + 1, per_side)
        for r in range(WIN):
            sr, srr = (wr, r + SHIFT) if r + SHIFT < WIN else (below, r + SHIFT - WIN)
            for wc in range(per_side):
                here = src[pl.ds(window_row(per_side, sr, wc, srr), PITCH), :]
                right = src[pl.ds(window_row(per_side, sr, (wc + 1) % per_side, srr), PITCH), :]
                i = iota(here.shape, 0)
                tile = jnp.where(
                    i < WIN - SHIFT,
                    pltpu.roll(here, PITCH - SHIFT, 0),
                    jnp.where(i < WIN, pltpu.roll(right, WIN - SHIFT, 0), 0.0),
                )
                dst[pl.ds(window_row(per_side, wr, wc, r), PITCH), :] = tile
        return carry

    lax.fori_loop(0, per_side, step, 0)


def shifted_to_regular(src, dst, side):
    per_side = side // WIN

    def step(wr, carry):
        above = lax.rem(wr + per_side - 1, per_side)
        for r in range(WIN):
            sr, srr = (wr, r - SHIFT) if r >= SHIFT else (above, r - SHIFT + WIN)
            for wc in range(per_side):
                here = src[pl.ds(window_row(per_side, sr, wc, srr), PITCH), :]
                left = src[pl.ds(window_row(per_side, sr, (wc + per_side - 1) % per_side, srr), PITCH), :]
                i = iota(here.shape, 0)
                tile = jnp.where(
                    i < SHIFT,
                    pltpu.roll(left, PITCH - (WIN - SHIFT), 0),
                    jnp.where(i < WIN, pltpu.roll(here, SHIFT, 0), 0.0),
                )
                dst[pl.ds(window_row(per_side, wr, wc, r), PITCH), :] = tile
        return carry

    lax.fori_loop(0, per_side, step, 0)


BLOCK_WINDOWS = 4
LINE_UNROLL, ATTEND_UNROLL, UP_UNROLL, BACK_UNROLL = 4, 2, 1, 2
ROWS_BLOCK = BLOCK_WINDOWS * SLOTS
JOBS = [
    (w, grp, slice(w * SLOTS, (w + 1) * SLOTS)) for w in range(BLOCK_WINDOWS) for grp in range(GROUPS)
]
GAIN_1, GAIN_2, OFFSET_1, OFFSET_2, BIAS_Q, BIAS_V, BIAS_OUT, BIAS_REDUCE = range(8)
SMALL_EXPAND = 8
SMALL_EARLY = 16
SMALL_TABLE = {0: 16, 1: 24}
SMALL_ROWS = 32
ADD_ROWS = 96
SEMAPHORES = 320
PART = 3


def table_spans():
    spans = []
    for dr in range(SPAN_SIDE):
        at = PITCH * (dr - WIN + 1)
        spans.append((at % 128, dr * SPAN_SIDE + WIN - 1, WIN, 0))
        spans.append(((at - PITCH) % 128 + PITCH - WIN + 1, dr * SPAN_SIDE, WIN - 1, 1))
    return spans


CORE, X, Y, Z, MLP, PLANE = range(6)


class Links:
    def __init__(self, mesh_shape, send_sem, recv_sem):
        self.win, self.mlp = mesh_shape
        self.send_sem, self.recv_sem = send_sem, recv_sem
        w, m = lax.axis_index("win"), lax.axis_index("mlp")
        self.core, self.x, self.z, self.m = lax.rem(w, 2), lax.rem(lax.div(w, 2), 2), lax.div(w, 4), m
        self.depth = self.win // 4
        self.groups = {
            CORE: (2, self.core, lambda q: self.at(core=q)),
            X: (2, self.x, lambda q: self.at(x=q)),
            Z: (self.depth, self.z, lambda q: self.at(z=q)),
            MLP: (self.mlp, m, lambda q: self.at(m=q)),
            Y: (self.mlp, m, lambda q: self.at(m=q)),
            PLANE: (
                2 * self.mlp,
                self.x * self.mlp + m,
                lambda q: self.at(x=lax.div(q, self.mlp), m=lax.rem(q, self.mlp)),
            ),
        }
        self.used = 0

    def at(self, core=None, x=None, z=None, m=None):
        core = self.core if core is None else core
        x = self.x if x is None else x
        z = self.z if z is None else z
        m = self.m if m is None else m
        return ((z * 2 + x) * 2 + core, m)

    def peers(self, group):
        size, me, _ = self.groups[group]
        return [(d, lax.rem(me + d, size)) for d in range(1, size)]

    def me(self, group):
        return self.groups[group][1]

    def size(self, group):
        return self.groups[group][0]

    def greet(self):
        sem = pltpu.get_barrier_semaphore()
        for group in (CORE, PLANE, Z):
            for _, q in self.peers(group):
                pl.semaphore_signal(
                    sem, inc=1, device_id=self.groups[group][2](q), device_id_type=pl.DeviceIdType.MESH
                )

    def meet(self):
        pl.semaphore_wait(pltpu.get_barrier_semaphore(), sum(self.size(g) - 1 for g in (CORE, PLANE, Z)))

    def reserve(self, count):
        first = self.used
        self.used += count
        assert self.used <= SEMAPHORES
        return first

    def copy(self, group, q, src, dst, n):
        return pltpu.make_async_remote_copy(
            src_ref=src,
            dst_ref=dst,
            send_sem=self.send_sem.at[n],
            recv_sem=self.recv_sem.at[n],
            device_id=self.groups[group][2](q),
            device_id_type=pl.DeviceIdType.MESH,
        )


def add_rows(dst, sources, count):
    step = next(n for n in (ADD_ROWS, 64, 48, 32, 16) if count % n == 0)

    def one(i, carry):
        at = pl.ds(pl.multiple_of(i * step, 16), step)
        total = dst[at, :].astype(F32)
        for source in sources:
            total = total + source[at, :].astype(F32)
        dst[at, :] = total.astype(dst.dtype)
        return carry

    lax.fori_loop(0, count // step, one, 0)


REDUCE, EXPAND, ATTEND = range(3)
FLOWS = (
    (REDUCE, 1, 0, 0, 3, 0, (CORE, PLANE, Z)),
    (REDUCE, 1, 0, 0, 3, 1, (CORE, PLANE, Z)),
    (REDUCE, 1, 0, 0, 3, 2, (CORE, PLANE, Z)),
    (EXPAND, 1, 0, 0, 3, 0, (CORE, PLANE, Z)),
    (EXPAND, 1, 0, 0, 3, 1, (CORE, PLANE, Z)),
    (EXPAND, 1, 0, 0, 3, 2, (CORE, PLANE, Z)),
    (ATTEND, 1, 0, 1, 1, 0, (CORE, X, Y, Z)),
    (ATTEND, 1, 1, 1, 1, 0, (CORE, Y, X, Z)),
    (ATTEND, 1, 2, 1, 3, 0, (CORE, Y, Z, X)),
    (ATTEND, 1, 2, 1, 3, 1, (CORE, Y, Z, X)),
    (ATTEND, 1, 2, 1, 3, 2, (CORE, Y, Z, X)),
    (REDUCE, 0, 0, 0, 3, 0, (CORE, PLANE, Z)),
    (REDUCE, 0, 0, 0, 3, 1, (CORE, PLANE, Z)),
    (REDUCE, 0, 0, 0, 3, 2, (CORE, PLANE, Z)),
    (EXPAND, 0, 0, 0, 3, 0, (CORE, MLP, X, Z)),
    (EXPAND, 0, 0, 0, 3, 1, (CORE, MLP, X, Z)),
    (EXPAND, 0, 0, 0, 3, 2, (CORE, MLP, X, Z)),
    (ATTEND, 0, 0, 1, 1, 0, (CORE, PLANE, Z)),
    (ATTEND, 0, 1, 1, 1, 0, (CORE, PLANE, Z)),
    (ATTEND, 0, 2, 1, 1, 0, (CORE, PLANE, Z)),
)


def flow_table(mesh_shape, width, ff):
    part = 4 * width // PART
    win, mlp = mesh_shape
    sizes = {CORE: 2, X: 2, Y: mlp, Z: win // 4, MLP: mlp, PLANE: 2 * mlp}
    flows, shapes = [], []
    for kind, l, first, count, splits, split, stages in FLOWS:
        if kind == ATTEND:
            first, rows = first * part, count * part
        else:
            first, rows = (ff if kind == REDUCE else 0), ff
        lanes = (split * (width // splits), width // splits)
        slots = 1 if kind == ATTEND else mlp
        flows.append((l, kind != ATTEND, (first, rows), lanes, stages))
        landing = []
        for stage in stages:
            if stage == MLP:
                slots = 1
            elif stage == PLANE and slots > 1:
                slots, rows = 1, rows // 2
            else:
                rows //= sizes[stage]
            landing.append((sizes[stage] - 1, slots, rows, lanes[1]))
        shapes.append(landing)
    return flows, shapes


def small_flow(l):
    return len(FLOWS) + 1 - l


class Flow:
    def __init__(self, links, staged, out, slots, span, lanes, stages, buffers, local_sem):
        self.links, self.staged, self.out, self.local_sem = links, staged, out, local_sem
        self.stages, self.buffers, self.lanes = stages, buffers, pl.ds(*lanes)
        self.spans, self.slots, self.down = [span], [slots], []
        for n, stage in enumerate(stages):
            first, rows = self.spans[-1]
            if stage == MLP:
                slots = 1
            elif stage == PLANE and slots > 1:
                slots, rows = 1, rows // 2
                first = first + links.x * rows
                self.down.insert(0, (n, X))
            else:
                rows = rows // links.size(stage)
                first = first + links.me(stage) * rows
                self.down.insert(0, (n, stage))
            self.spans.append((first, rows))
            self.slots.append(slots)
        self.steps = len(stages) + len(self.down)
        self.sems = [links.reserve(links.size(group) - 1) for group in stages + tuple(group for _, group in self.down)]

    def copies(self, k):
        links = self.links
        made = []
        if k < len(self.stages):
            stage, slots = self.stages[k], self.slots[k]
            (first, _), (_, rows) = self.spans[k], self.spans[k + 1]
            for d, q in links.peers(stage):
                if stage == MLP:
                    slot, at = pl.ds(d, 1), first
                elif stage == PLANE and slots > 1:
                    slot, at = pl.ds(d % links.mlp, 1), first + lax.div(q, links.mlp) * rows
                else:
                    slot, at = pl.ds(0, slots), first + q * rows
                src = self.staged.at[slot, pl.ds(pl.multiple_of(at, 16), rows), self.lanes]
                made.append(links.copy(stage, q, src, self.buffers[k].at[d - 1], self.sems[k] + d - 1))
            return made
        n, group = self.down[k - len(self.stages)]
        src = self.mine(n + 1, self.staged.at[0] if k == len(self.stages) else self.out)
        for d, q in links.peers(group):
            made.append(links.copy(group, q, src, self.mine(n + 1, self.out), self.sems[k] + d - 1))
        return made

    def mine(self, n, ref):
        first, rows = self.spans[n]
        return ref.at[pl.ds(pl.multiple_of(first, 16), rows), self.lanes]

    def local(self):
        return pltpu.make_async_copy(
            self.mine(len(self.stages), self.staged.at[0]), self.mine(len(self.stages), self.out), self.local_sem
        )

    def advance(self, k):
        if k:
            for copy in self.copies(k - 1):
                copy.wait()
            if k - 1 < len(self.stages):
                for slot in range(self.slots[k]):
                    add_rows(
                        self.mine(k, self.staged.at[slot]),
                        [self.buffers[k - 1].at[d - 1, slot] for d, _ in self.links.peers(self.stages[k - 1])],
                        self.spans[k][1],
                    )
            elif k - 1 == len(self.stages):
                self.local().wait()
        if k < self.steps:
            if k == len(self.stages):
                self.local().start()
            for copy in self.copies(k):
                copy.start()


class SmallFlow:
    def __init__(self, links, value, buffers, out):
        self.links, self.value, self.buffers, self.out = links, value, buffers, out
        self.stages = (CORE, PLANE, Z)
        self.sems = [links.reserve(links.size(stage) - 1) for stage in self.stages]
        self.steps = len(self.stages)

    def copies(self, k):
        stage, buffer = self.stages[k], self.buffers[k]
        me = self.links.me(stage)
        return [
            self.links.copy(stage, q, buffer.at[me], buffer.at[me], self.sems[k] + d - 1)
            for d, q in self.links.peers(stage)
        ]

    def advance(self, k):
        total = self.value[...] if k == 0 else None
        if k:
            for copy in self.copies(k - 1):
                copy.wait()
            buffer = self.buffers[k - 1]
            total = buffer[0]
            for j in range(1, buffer.shape[0]):
                total = total + buffer[j]
        if k < len(self.stages):
            self.buffers[k][self.links.me(self.stages[k])] = total
            for copy in self.copies(k):
                copy.start()
        else:
            self.out[...] = total


(AT_REDUCE, AT_FEED, AT_EXPAND, AT_MIDDLE, AT_ATTEND, AT_GROUP, AT_INPUT, AT_SUMS, AT_TABLE, AT_PLACED, AT_OUT) = range(11)
PLAN = {
    (1, AT_MIDDLE, 2): (0,),
    (1, AT_MIDDLE, 3): (1, 2),
    (1, AT_ATTEND, 0): (4, 5, 3),
    (1, AT_ATTEND, 2): (0,),
    (1, AT_ATTEND, 3): (6,),
    (1, AT_GROUP, 1): (1,),
    (1, AT_ATTEND, 5): (2, 7),
    (1, AT_INPUT, 0): (0,),
    (1, AT_INPUT, 1): (4, 9, 10, 8),
    (1, AT_INPUT, 2): (1,),
    (1, AT_PLACED, 0): (5,),
    (0, AT_REDUCE, 0): (20, 2, 0, 3),
    (0, AT_FEED, 0): (4, 13, 9, 1, 6, 10, 11, 5, 8, 12, 7),
    (0, AT_FEED, 1): (20, 2, 0),
    (0, AT_EXPAND, 0): (4, 0, 3, 13, 9),
    (0, AT_MIDDLE, 0): (1, 6, 10, 14),
    (0, AT_MIDDLE, 1): (15, 16, 1, 5),
    (0, AT_MIDDLE, 2): (8,),
    (0, AT_MIDDLE, 3): (11,),
    (0, AT_ATTEND, 0): (20,),
    (0, AT_ATTEND, 1): (12, 3, 7),
    (0, AT_GROUP, 0): (13, 2, 14),
    (0, AT_ATTEND, 2): (4, 9, 2, 17, 6, 10, 5, 11, 15, 8),
    (0, AT_ATTEND, 3): (4, 5, 3),
    (0, AT_GROUP, 1): (14, 9, 12, 16),
    (0, AT_ATTEND, 4): (18, 3, 7, 13),
    (0, AT_ATTEND, 5): (17, 6, 10),
    (0, AT_GROUP, 2): (15, 8, 11),
    (0, AT_INPUT, 1): (16, 14, 19),
    (0, AT_INPUT, 2): (9,),
    (0, AT_TABLE, 0): (12,),
    (0, AT_TABLE, 1): (18, 13, 6, 7),
    (0, AT_PLACED, 0): (17, 11),
    (0, AT_OUT, 0): (19, 13, 9, 10, 21, 11, 15, 8, 12, 16),
}
LAST = (9, 14, 6, 18, 12, 7, 17, 6, 10, 19, 10, 15, 21, 14, 8, 16, 18, 8, 14, 7, 19, 15, 7, 17, 16, 15, 17, 16, 18, 21, 18, 19, 19)


def number_steps():
    count = [1] * (len(FLOWS) + 2)

    def number(names):
        pairs = []
        for n in names:
            pairs.append((n, count[n]))
            count[n] += 1
        return tuple(pairs)

    return {key: number(names) for key, names in PLAN.items()}, number(LAST), count


STEPS, TAIL, COUNT = number_steps()


def kernel(side, mesh_shape, *refs):
    refs = list(refs)

    def take(n):
        got = refs[:n]
        del refs[:n]
        return got

    tokens, ids, gain, offset, global_in, b_in, table, w_out, b_out, w_exp, b_exp, w_red, b_red, cot = take(14)
    fused = mesh_shape is not None
    out, grad_tokens, d_attn, d_feed, small = take(5)
    (x, normed, qkv, probs, mixed, mid, second, hidden, slope) = take(9)
    (keys, bias, bias_sum, g, gs, gz, gb_low, dqkv, go, d_bexp, turn, spread, w_in, turned, gz_turned, wide, tall, hot_grid, in_sems) = take(19)
    flows = []
    if fused:
        out_attn, out_feed, out_small = d_attn, d_feed, small
        d_attn, d_feed, small = take(3)
        local_exp, local_bexp, local_red = w_exp, b_exp, w_red
        w_exp, b_exp, w_red = take(3)
        small_buffers = [take(3) for _ in range(2)]
        flow_rows, shapes = flow_table(mesh_shape, x.shape[2], local_exp.shape[2])
        landing = [take(len(shape)) for shape in shapes]
        local_sems, send_sem, recv_sem = take(3)
        links = Links(mesh_shape, send_sem, recv_sem)
        for n, (l, feed_flow, span, lanes, stages) in enumerate(flow_rows):
            flows.append(
                Flow(
                    links,
                    d_feed.at[l] if feed_flow else d_attn.at[pl.ds(l, 1)],
                    out_feed.at[l] if feed_flow else out_attn.at[l],
                    mesh_shape[1] if feed_flow else 1,
                    span,
                    lanes,
                    stages,
                    landing[n],
                    local_sems.at[3 + n],
                )
            )
        for l in (1, 0):
            part = pl.ds(0, SMALL_EARLY if l else SMALL_ROWS)
            flows.append(SmallFlow(links, small.at[l, part], small_buffers[l], out_small.at[l, part]))

    def advance(*pairs):
        if fused:
            for n, k in pairs:
                flows[n].advance(k)

    def begin(kind, l, part=0):
        advance(
            *((n, 0) for n, flow in enumerate(FLOWS) if flow[:2] == (kind, l) and (kind != ATTEND or flow[2] + flow[3] - 1 == part))
        )

    def ticks(l, point, i=0):
        advance(*STEPS.get((l, point, i), ()))

    def ticks_in_loop(l, point, i, n, unroll, j):
        for (at_l, at_point, at_i), names in STEPS.items():
            if fused and (at_l, at_point) == (l, point) and at_i % unroll == j:
                if isinstance(i, int):
                    if i == at_i:
                        advance(*names)
                else:
                    pl.when(n == at_i // unroll)(functools.partial(advance, *names))

    per_side = side // WIN
    windows = per_side * per_side
    rows = windows * SLOTS
    blocks = rows // ROWS_BLOCK
    shards, _, width, ff = w_exp.shape
    chunk = 256 if ff % 256 == 0 else ff
    blocked = ff % width == 0
    part_rows = 4 * width // PART

    gathers = [
        pltpu.make_async_copy(
            global_in.at[l, :, pl.ds(p * width + grp * GLANES, GLANES)],
            w_in.at[l, :, pl.ds(grp * width + p * GLANES, GLANES)],
            in_sems.at[(l * GROUPS + grp) * 3 + p],
        )
        for l in range(2)
        for grp in range(GROUPS)
        for p in range(3)
    ]
    for copy in gathers:
        copy.start()
    if fused:
        links.greet()
        own = [
            pltpu.make_async_copy(local_exp, w_exp.at[0], local_sems.at[0]),
            pltpu.make_async_copy(local_red, w_red.at[0], local_sems.at[1]),
        ]
        for copy in own:
            copy.start()
        b_exp[0, 0:2, :] = local_bexp[...].astype(F32)
        halves = (
            pl.ds(pl.multiple_of(links.core * (width // 2), 16), width // 2),
            pl.ds(pl.multiple_of(links.core * (ff // 2), 16), ff // 2),
        )
        weights = ((local_exp, w_exp, halves[0], width // 4), (local_red, w_red, halves[1], ff // 4))
        fetch_sems = links.reserve(4 * (shards - 1))
        relay_sems = links.reserve(2 * (shards - 1))
        pass_sems = links.reserve(4 * (shards - 1))
        bias_sems = links.reserve(shards - 1)

        def quarter(n):
            rows = weights[n][3]
            return pl.ds(pl.multiple_of((links.core * 2 + links.x) * rows, 16), rows)

        def fetches(l, n):
            source, dest, half, _ = weights[n]
            part = quarter(n) if l else half
            return [
                links.copy(MLP, q, source.at[l, part], dest.at[shards - d, l, part], fetch_sems + (2 * l + n) * (shards - 1) + d - 1)
                for d, q in links.peers(MLP)
            ]

        def relays(n):
            dest, part = weights[n][1], quarter(n)
            ((_, beside),) = links.peers(X)
            return [
                links.copy(X, beside, dest.at[d, 1, part], dest.at[d, 1, part], relay_sems + n * (shards - 1) + d - 1)
                for d, _ in links.peers(MLP)
            ]

        def passes(l, n):
            _, dest, half, _ = weights[n]
            ((_, sibling),) = links.peers(CORE)
            return [
                links.copy(CORE, sibling, dest.at[d, l, half], dest.at[d, l, half], pass_sems + (2 * l + n) * (shards - 1) + d - 1)
                for d, _ in links.peers(MLP)
            ]

        def bias_fetches():
            return [links.copy(MLP, q, b_exp.at[0], b_exp.at[shards - d], bias_sems + d - 1) for d, q in links.peers(MLP)]

        def fetch_all():
            for copy in bias_fetches():
                copy.start()
            for l in range(2):
                for n in range(2):
                    for copy in fetches(l, n):
                        copy.start()

        def relay(n):
            for copy in fetches(1, n):
                copy.wait()
            for copy in relays(n):
                copy.start()

        def pass_on(l, n):
            for copy in relays(n) if l else fetches(l, n):
                copy.wait()
            for copy in passes(l, n):
                copy.start()

        def passed(l, n):
            for copy in passes(l, n):
                copy.wait()

    def over_blocks(body, tick=None, after=None, unroll=1):
        def step(n, carry):
            for j in range(unroll):
                i = n * unroll + j
                body(pl.ds(i * ROWS_BLOCK if isinstance(i, int) else pl.multiple_of(i * ROWS_BLOCK, ROWS_BLOCK), ROWS_BLOCK))
                if tick:
                    ticks_in_loop(*tick, i, n, unroll, j)
                if after:
                    after(i)
            return carry

        if unroll == blocks:
            step(0, 0)
        else:
            lax.fori_loop(0, blocks // unroll, step, 0)

    wide[...] = jnp.zeros(wide.shape, F32)
    for row in range(side):
        wide[row : row + 1, :side] = ids[row].astype(F32)
    by_column = wide[:, :128].T[:32]
    for row in range(side):
        hot_grid[row] = jnp.broadcast_to(by_column[:, row : row + 1], (32, 128))
    wide[...] = jnp.zeros(wide.shape, F32)

    def put_tokens(wr, wc, r, tile):
        x[0, pl.ds(window_row(per_side, wr, wc, r), PITCH), :] = tile

    grid_to_windows(tokens, side, False, put_tokens)
    if fused:
        links.meet()
        fetch_all()

    def prepare(l):
        shifted = l == 1

        def put_keys(wr, wc, r, tile, shifted=shifted):
            lane = iota(tile.shape, 1).astype(F32)
            slot = iota(tile.shape, 0)
            label = tile
            if shifted:
                row_at = wr * WIN + r
                row_label = jnp.where(row_at >= side - WIN, 1, 0) + jnp.where(row_at >= side - SHIFT, 1, 0)
                col_at = wc * WIN + slot
                col_label = jnp.where(col_at >= side - WIN, 1, 0) + jnp.where(col_at >= side - SHIFT, 1, 0)
                label = label + (12 * row_label + 4 * col_label).astype(F32)
            hot = jnp.where((lane == label) & (slot < WIN), 1.0, 0.0)
            keys[l, pl.ds(window_row(per_side, wr, wc, r), PITCH), :] = hot

        grid_to_windows(hot_grid, side, shifted, put_keys)

        krow = iota((SLOTS, 128), 0)
        qlane = iota((SLOTS, 128), 1)
        ahead = (qlane & (PITCH - 1)) >= (krow & (PITCH - 1))
        turn[...] = jnp.zeros(turn.shape, F32)
        for h in range(HEADS):
            wide[h : h + 1, : table.shape[2]] = table[h, l : l + 1, :]
        tall[...] = wide[...].T
        for lane, entry, count, s in table_spans():
            turn[s, lane : lane + count, :] = tall[entry : entry + count, :]
        for s in range(2):
            spread[s] = turn[s].T[: spread.shape[1]]
        for grp in range(GROUPS):
            low = jnp.zeros((SLOTS, 128), F32)
            high = jnp.zeros((SLOTS, 128), F32)
            for j in range(GROUP):
                h = grp * GROUP + j
                both = [
                    pltpu.roll(
                        jnp.broadcast_to(spread[s, h : h + 1, :], (SLOTS, 128)),
                        0,
                        1,
                        stride=1,
                        stride_axis=0,
                    )
                    for s in range(2)
                ]
                one = jnp.where(ahead, both[0], both[1])
                at = j * SLOTS
                if at < 128:
                    moved = pltpu.roll(one, at, 1) if at else one
                    low = jnp.where((qlane >= at) & (qlane < at + SLOTS), moved, low)
                if at + SLOTS > 128:
                    moved = pltpu.roll(one, (at - 128) % 128, 1)
                    high = jnp.where((qlane >= at - 128) & (qlane < at - 128 + SLOTS), moved, high)
            bias[l, grp, :, :128] = low
            bias[l, grp, :, 128:] = high[:, : GQ - 128]

    def put_cot(wr, wc, r, tile):
        g[pl.ds(window_row(per_side, wr, wc, r), PITCH), :] = tile

    def add_small(l, at, value):
        small[l, at : at + 1, :] += value

    def lower(at, l):
        g_now = g[at, :]
        add_small(l, BIAS_REDUCE, jnp.sum(g_now, axis=0, keepdims=True))
        gz[at, :] = g_now.astype(BF16)

    def feed_up(at, i, l):
        s = second[l, at, :]
        jobs = [slice(c, c + chunk) for c in range(0, ff, chunk)]
        befores = [dot(s, w_exp[i, l, :, cols]) for cols in jobs]
        for before, cols in zip(befores, jobs):
            value, slope_now = gelu_pair(before + b_exp[i, l : l + 1, cols])
            hidden[l, i, at, cols] = value.astype(BF16)
            slope[l, i, at, cols] = slope_now.astype(BF16)

    def feed_down(at, i, l):
        gs[at, :] += dot(hidden[l, i, at, :], w_red[i, l])

    def feed_back(at, i, l):
        g_low = gz[at, :]
        jobs = [slice(c, c + chunk) for c in range(0, ff, chunk)]
        ghs = [dot_nt(g_low, w_red[i, l, cols, :]) for cols in jobs]
        for gh, cols in zip(ghs, jobs):
            gb = gh * slope[l, i, at, cols].astype(F32)
            d_bexp[i, 0:1, cols] += jnp.sum(gb, axis=0, keepdims=True)
            gb_low[i, at, cols] = gb.astype(BF16)
        gs[at, :] += dot_nt(gb_low[i, at, :], w_exp[i, l])

    def reduce_weights(i, l):
        if blocked:
            for c in range(0, ff, width):
                d_feed[l, i, ff + c : ff + c + width, :] = dot(gz_turned[...], hidden[l, i, :, c : c + width]).astype(BF16)
        else:
            d_feed[l, i, ff:, :] = dot_tn(hidden[l, i], gz[...]).astype(BF16)

    def expand_weights(i, l):
        if blocked:
            for c in range(0, ff, width):
                d_feed[l, i, c : c + width, :] = dot(turned[...], gb_low[i, :, c : c + width]).astype(BF16)
        else:
            d_feed[l, i, :ff, :] = dot_tn(gb_low[i], second[l]).astype(BF16)

    def over_shards(first, body):
        def step(i, carry):
            body(i)
            return carry

        lax.fori_loop(first, shards, step, 0)

    small[...] = jnp.zeros(small.shape, F32)
    prepare(0)

    for l in range(2):
        bias_row = jnp.concatenate(
            [
                one[:, grp * GLANES : (grp + 1) * GLANES]
                for grp in range(GROUPS)
                for one in (b_in[l, 0:1, :], jnp.zeros((1, width), F32), b_in[l, 1:2, :])
            ],
            axis=1,
        )
        if l == 0:
            for copy in gathers:
                copy.wait()

        def project(at, l=l, bias_row=bias_row):
            xhat, _ = norm_stats(x[l, at, :])
            a = (xhat * gain[l, 0:1, :] + offset[l, 0:1, :]).astype(BF16)
            normed[l, at, :] = a
            for c in range(3):
                cols = slice(c * width, (c + 1) * width)
                qkv[l, at, cols] = (dot(a, w_in[l, :, cols]) + bias_row[:, cols]).astype(BF16)

        over_blocks(project, unroll=LINE_UNROLL)

        def attend(i, l=l):
            at = pl.ds(pl.multiple_of(i * ROWS_BLOCK, ROWS_BLOCK), ROWS_BLOCK)
            q, k, v = (
                [
                    qkv[l, at, grp * width + p * GLANES : grp * width + (p + 1) * GLANES].astype(F32)
                    for grp in range(GROUPS)
                ]
                for p in range(3)
            )
            hot = keys[l, at, :]
            allowed = []
            for w in range(BLOCK_WINDOWS):
                hot_w = hot[w * SLOTS : (w + 1) * SLOTS]
                same = dot_nt(hot_w.astype(BF16), jnp.concatenate([hot_w] * GROUP, axis=0).astype(BF16))
                allowed.append(same > 0.5)
            scores = [
                dot_nt(k[grp][here].astype(BF16), expand_heads(q[grp][here])) for _, grp, here in JOBS
            ]
            scores = [
                jnp.where(allowed[w], s * HEAD_DIM**-0.5 + bias[l, grp], MASKED)
                for s, (w, grp, _) in zip(scores, JOBS)
            ]
            tops = [jnp.max(s, axis=0, keepdims=True) for s in scores]
            raised = [jnp.exp(s - top) for s, top in zip(scores, tops)]
            shares = [1.0 / jnp.sum(e, axis=0, keepdims=True) for e in raised]
            ps = [(e * share).astype(BF16) for e, share in zip(raised, shares)]
            for p, (w, grp, _) in zip(ps, JOBS):
                probs[l, BLOCK_WINDOWS * i + w, grp] = p
            outs = [
                fold_heads(dot_tn(p, v[grp][here].astype(BF16))) for p, (_, grp, here) in zip(ps, JOBS)
            ]
            mixed[l, at, :] = by_window(outs).astype(BF16)

        def attend_step(n, carry):
            for j in range(ATTEND_UNROLL):
                attend(n * ATTEND_UNROLL + j)
            return carry

        lax.fori_loop(0, blocks // ATTEND_UNROLL, attend_step, 0)

        def middle(at, l=l):
            m = x[l, at, :] + dot(mixed[l, at, :], w_out[l]) + b_out[l : l + 1, :]
            mid[l, at, :] = m
            xhat, _ = norm_stats(m)
            second[l, at, :] = (xhat * gain[l, 1:2, :] + offset[l, 1:2, :]).astype(BF16)
            if l == 0:
                gs[at, :] = m + b_red[l : l + 1, :]

        if fused and l == 1:
            relay(0)
        over_blocks(middle, unroll=LINE_UNROLL)
        if l == 1:
            break
        if fused:
            pass_on(0, 0)
            for copy in own:
                copy.wait()

        def up(i):
            if fused:

                @pl.when(i == 1)
                def _():
                    for copy in bias_fetches():
                        copy.wait()
                    passed(0, 0)

            def second_fetch(block):
                if fused:
                    pl.when((i == 1) & (block == blocks // 2))(functools.partial(pass_on, 0, 1))

            over_blocks(functools.partial(feed_up, i=i, l=0), after=second_fetch, unroll=UP_UNROLL)

        over_shards(0, up)
        prepare(1)
        grid_to_windows(cot, side, True, put_cot)
        over_blocks(functools.partial(lower, l=1))
        if blocked:
            gz_turned[...] = gz[...].T
        if fused:
            passed(0, 1)
        over_shards(0, lambda i: over_blocks(functools.partial(feed_down, i=i, l=0), unroll=2))
        regular_to_shifted(gs, x.at[1], side)

    d_bexp[...] = jnp.zeros(d_bexp.shape, F32)
    if blocked:
        turned[...] = second[1].T
    gs[...] = jnp.zeros(gs.shape, F32)
    if fused:
        relay(1)

    def both_ways(i):
        if fused:

            @pl.when(i == 1)
            def _():
                pass_on(1, 1)
                passed(1, 0)

        over_blocks(functools.partial(feed_up, i=i, l=1), unroll=UP_UNROLL)
        if fused:
            pl.when(i == 0)(functools.partial(pass_on, 1, 0))
            pl.when(i == 1)(functools.partial(passed, 1, 1))
        over_blocks(functools.partial(feed_back, i=i, l=1), unroll=BACK_UNROLL)
        reduce_weights(i, 1)
        expand_weights(i, 1)

    over_shards(0, both_ways)

    def table_back(l):
        krow = iota((SLOTS, 128), 0)
        qlane = iota((SLOTS, 128), 1)
        ahead = (qlane & (PITCH - 1)) >= (krow & (PITCH - 1))
        kept = (ahead & (qlane < SLOTS), jnp.logical_not(ahead) & (qlane < SLOTS))
        lined = []
        for grp in range(GROUPS):
            low = bias_sum[l, grp, :, :128]
            high = jnp.concatenate([bias_sum[l, grp, :, 128:], jnp.zeros((SLOTS, 256 - GQ), F32)], axis=1)
            for j in range(GROUP):
                at = j * SLOTS
                if at + SLOTS <= 128:
                    one = pltpu.roll(low, 128 - at, 1) if at else low
                elif at < 128:
                    one = jnp.where(qlane < 128 - at, pltpu.roll(low, 128 - at, 1), pltpu.roll(high, 128 - at, 1))
                else:
                    one = pltpu.roll(high, (256 - at) % 128, 1)
                lined.append(one)
        picked = [jnp.where(keep, one, 0.0) for keep in kept for one in lined]
        tiles = [one[:PITCH] for one in picked]
        for r in range(1, WIN):
            turned_rows = [pltpu.roll(one[r * PITCH : (r + 1) * PITCH], 128 - r * PITCH, 1) for one in picked]
            tiles = [tile + one for tile, one in zip(tiles, turned_rows)]
        odd = iota((PITCH, 128), 0)
        for step in (1, 2, 4):
            tiles = [jnp.where((odd & step) > 0, pltpu.roll(tile, 128 - step, 1), tile) for tile in tiles]
        for n, tile in enumerate(tiles):
            row = SMALL_TABLE[l] + n // 3
            small[0, row : row + 1, n % 3 * 128 : (n % 3 + 1) * 128] = jnp.sum(tile, axis=0, keepdims=True)


    for l in (1, 0):

        if l == 0:
            over_blocks(functools.partial(lower, l=0))
            if blocked:
                gz_turned[...] = gz[...].T
            over_shards(0, functools.partial(reduce_weights, l=0))
        begin(REDUCE, l)
        ticks(l, AT_REDUCE)
        if l == 0:
            d_bexp[...] = jnp.zeros(d_bexp.shape, F32)

            gs[...] = jnp.zeros(gs.shape, F32)

            def back(i):
                over_blocks(functools.partial(feed_back, i=i, l=0), unroll=BACK_UNROLL)
                for key, names in STEPS.items():
                    if fused and key[:2] == (0, AT_FEED):
                        pl.when(i == key[2])(functools.partial(advance, *names))

            over_shards(0, back)
        span = min(width, ff)
        for n in range(shards * (ff // span)):
            i, c = n // (ff // span), n % (ff // span) * span
            row = n
            if fused:
                row = lax.rem(links.m + i, shards) * (ff // span) + n % (ff // span)
            small[l, pl.ds(SMALL_EXPAND + row, 1), :span] = d_bexp[i, 0:1, c : c + span]

        if l == 0:
            if blocked:
                turned[...] = second[0].T
            over_shards(0, functools.partial(expand_weights, l=0))
        begin(EXPAND, l)
        ticks(l, AT_EXPAND)

        def middle_back(at, l=l):
            dmid, dgain, doffset = norm_back(mid[l, at, :], gain[l, 1:2, :], gs[at, :])
            add_small(l, GAIN_2, dgain)
            add_small(l, OFFSET_2, doffset)
            gm = g[at, :] + dmid
            g[at, :] = gm
            add_small(l, BIAS_OUT, jnp.sum(gm, axis=0, keepdims=True))
            low = gm.astype(BF16)
            gz[at, :] = low
            go[at, :] = dot_nt(low, w_out[l]).astype(BF16)

        over_blocks(middle_back, (l, AT_MIDDLE), unroll=LINE_UNROLL)
        d_mixed = dot_tn(mixed[l], gz[...]).astype(BF16)
        for part in range(PART):
            at = part * part_rows + width
            d_attn[l, at : at + width // PART, :] = d_mixed[part * (width // PART) : (part + 1) * (width // PART)]
        bias_sum[l] = jnp.zeros(bias_sum.shape[1:], F32)
        turned[...] = normed[l].T

        def attend_back(i, carry, grp, l=l):
            count = windows // 2
            at = pl.ds(pl.multiple_of(i * count * SLOTS, count * SLOTS), count * SLOTS)
            parts = [pl.ds(pl.multiple_of(grp * width + p * GLANES, GLANES), GLANES) for p in range(3)]
            lanes = pl.ds(pl.multiple_of(grp * GLANES, GLANES), GLANES)
            heres = [slice(w * SLOTS, (w + 1) * SLOTS) for w in range(count)]
            q, k, v = (qkv[l, at, part].astype(F32) for part in parts)
            go_now = go[at, lanes].astype(F32)
            go_all = [expand_heads(go_now[here]) for here in heres]
            dps = [dot_nt(v[here].astype(BF16), one) for one, here in zip(go_all, heres)]
            lows = [probs[l, count * i + w, grp] for w in range(count)]
            dvs = [dot(p, one) for p, one in zip(lows, go_all)]
            ps = [p.astype(F32) for p in lows]
            pds = [p * dp for p, dp in zip(ps, dps)]
            totals = [jnp.sum(pd, axis=0, keepdims=True) for pd in pds]
            dss = [(pd - p * total).astype(BF16) for pd, p, total in zip(pds, ps, totals)]
            dqs = [
                fold_heads(dot_tn(ds, k[here].astype(BF16))) * HEAD_DIM**-0.5 for ds, here in zip(dss, heres)
            ]
            dks = [dot(ds, expand_heads(q[here])) * HEAD_DIM**-0.5 for ds, here in zip(dss, heres)]
            total = bias_sum[l, grp]
            for ds in dss:
                total = total + ds.astype(F32)
            bias_sum[l, grp] = total
            for row, part, made in zip((BIAS_Q, None, BIAS_V), parts, (dqs, dks, dvs)):
                whole = jnp.concatenate(made, axis=0)
                if row is not None:
                    small[l, row : row + 1, lanes] += jnp.sum(whole, axis=0, keepdims=True)
                dqkv[at, part] = whole.astype(BF16)
            for key, names in STEPS.items():
                if fused and key[:2] == (l, AT_ATTEND):
                    pl.when((grp == key[2] // 2) & (i == key[2] % 2))(functools.partial(advance, *names))
            return carry

        def attend_group(grp, carry, l=l):
            lax.fori_loop(0, 2, functools.partial(attend_back, grp=grp), 0)
            at = pl.multiple_of(grp * part_rows, 16)
            cols = pl.ds(pl.multiple_of(grp * width, GLANES), width)
            d_attn[l, pl.ds(at, width), :] = dot(turned[...], dqkv[:, cols]).astype(BF16)
            for g_now in range(GROUPS):

                def after(g_now=g_now):
                    begin(ATTEND, l, g_now)
                    ticks(l, AT_GROUP, g_now)

                if fused:
                    pl.when(grp == g_now)(after)
            return carry

        lax.fori_loop(0, GROUPS, attend_group, 0)

        def input_back(at, l=l):
            ga = dot_nt(dqkv[at, :], w_in[l])
            dx, dgain, doffset = norm_back(x[l, at, :], gain[l, 0:1, :], ga)
            add_small(l, GAIN_1, dgain)
            add_small(l, OFFSET_1, doffset)
            gs[at, :] = g[at, :] + dx

        over_blocks(input_back, (l, AT_INPUT), unroll=LINE_UNROLL)
        if l == 1:
            advance((small_flow(1), 0))
            ticks(l, AT_SUMS)
            shifted_to_regular(gs, g, side)
            ticks(l, AT_PLACED)
        else:
            ticks(l, AT_SUMS)
            for one in range(2):
                table_back(one)
                ticks(l, AT_TABLE, one)
            advance((small_flow(0), 0))
            windows_to_grid(gs, grad_tokens, side, False)
            ticks(l, AT_PLACED)

    def last(at):
        total = mid[1, at, :] + b_red[1:2, :] + dot(hidden[1, 0, at, :], w_red[0, 1])

        def add(i, total):
            return total + dot(hidden[1, i, at, :], w_red[i, 1])

        g[at, :] = lax.fori_loop(1, shards, add, total)

    over_blocks(last)
    windows_to_grid(g, out, side, True)
    ticks(0, AT_OUT)

    advance(*TAIL)
    for k in range(1, 1 + max((flow.steps for flow in flows), default=0)):
        advance(*((n, k) for n, flow in enumerate(flows) if COUNT[n] <= k <= flow.steps))


def lanes_table(lanes):
    layers, heads = lanes.shape[0], lanes.shape[1] // 2
    both = lanes.reshape(layers, 2, heads, 128)
    span = SPAN_SIDE * PITCH

    def square(part, back):
        return jnp.roll(part, back, axis=-1)[..., :span].reshape(layers, heads, SPAN_SIDE, PITCH)

    right = square(both[:, 0], (WIN - 1) * PITCH)[..., :WIN]
    left = square(both[:, 1], WIN * PITCH)[..., PITCH - WIN + 1 :]
    whole = jnp.concatenate([left, right], axis=-1)
    return whole.reshape(layers, heads, SPAN_SIDE * SPAN_SIDE).transpose(0, 2, 1)


def on_device(
    mesh_shape,
    tokens,
    crop_ids,
    norm_gain,
    norm_bias,
    input_proj,
    input_bias,
    position_table,
    output_proj,
    output_bias,
    expand_weight,
    expand_bias,
    reduce_weight,
    reduce_bias,
    cotangent,
):
    _, side, _, width = tokens.shape
    layers, _, ff = expand_weight.shape
    win, shards = mesh_shape
    ids = crop_ids.transpose(1, 0, 2)
    windows = (side // WIN) ** 2
    rows = windows * SLOTS
    attn_rows, feed_rows = 4 * width, 2 * ff
    fused = win % 4 == 0 and attn_rows % (16 * PART * win * shards) == 0 and ff % (16 * win) == 0
    vmem = pl.BlockSpec(memory_space=pltpu.VMEM)
    hbm = pl.BlockSpec(memory_space=pl.ANY)
    if fused:
        w_exp, w_red = expand_weight, reduce_weight
        b_exp = expand_bias
    else:
        w_exp = lax.all_gather(expand_weight, "mlp", axis=0)
        w_red = lax.all_gather(reduce_weight, "mlp", axis=0)
        b_exp = lax.all_gather(expand_bias, "mlp", axis=0).astype(F32)
    scratch = [
        pltpu.VMEM((layers, rows, width), F32),
        pltpu.VMEM((layers, rows, width), BF16),
        pltpu.VMEM((layers, rows, 3 * width), BF16),
        pltpu.VMEM((layers, windows, GROUPS, SLOTS, GQ), BF16),
        pltpu.VMEM((layers, rows, width), BF16),
        pltpu.VMEM((layers, rows, width), F32),
        pltpu.VMEM((layers, rows, width), BF16),
        pltpu.VMEM((layers, shards, rows, ff), BF16),
        pltpu.VMEM((layers, shards, rows, ff), BF16),
        pltpu.VMEM((layers, rows, 128), F32),
        pltpu.VMEM((layers, GROUPS, SLOTS, GQ), F32),
        pltpu.VMEM((layers, GROUPS, SLOTS, GQ), F32),
        pltpu.VMEM((rows, width), F32),
        pltpu.VMEM((rows, width), F32),
        pltpu.VMEM((rows, width), BF16),
        pltpu.VMEM((shards, rows, ff), BF16),
        pltpu.VMEM((rows, 3 * width), BF16),
        pltpu.VMEM((rows, width), BF16),
        pltpu.VMEM((shards, 8, ff), F32),
    ]
    small_shape = (layers, SMALL_ROWS, width)
    scratch += [
        pltpu.VMEM((2, 128, 128), F32),
        pltpu.VMEM((2, 16, 128), F32),
        pltpu.VMEM(input_proj.shape, BF16),
        pltpu.VMEM((width, rows), BF16),
        pltpu.VMEM((width, rows), BF16),
        pltpu.VMEM((128, 256), F32),
        pltpu.VMEM((256, 128), F32),
        pltpu.VMEM((side, 32, 128), F32),
        pltpu.SemaphoreType.DMA((layers * GROUPS * 3,)),
    ]
    if fused:
        plane, depth = 2 * shards, win // 4
        _, shapes = flow_table(mesh_shape, width, ff)
        scratch += [
            pltpu.VMEM((layers, attn_rows, width), BF16),
            pltpu.VMEM((layers, shards, feed_rows, width), BF16),
            pltpu.VMEM(small_shape, F32),
            pltpu.VMEM((shards, layers, width, ff), BF16),
            pltpu.VMEM((shards, 8, ff), F32),
            pltpu.VMEM((shards, layers, ff, width), BF16),
        ]
        scratch += [
            pltpu.VMEM((members, count, width), F32)
            for count in (SMALL_ROWS, SMALL_EARLY)
            for members in (2, plane, depth)
        ]
        scratch += [pltpu.VMEM(shape, BF16) for group in shapes for shape in group]
        scratch += [
            pltpu.SemaphoreType.DMA((3 + len(shapes),)),
            pltpu.SemaphoreType.DMA((SEMAPHORES,)),
            pltpu.SemaphoreType.DMA((SEMAPHORES,)),
        ]
    outs = pl.pallas_call(
        functools.partial(kernel, side, mesh_shape if fused else None),
        out_shape=(
            jax.ShapeDtypeStruct(tokens.shape[1:], BF16),
            jax.ShapeDtypeStruct(tokens.shape[1:], BF16),
            jax.ShapeDtypeStruct((layers, attn_rows, width), BF16),
            jax.ShapeDtypeStruct((layers, feed_rows, width) if fused else (layers, shards, feed_rows, width), BF16),
            jax.ShapeDtypeStruct(small_shape, F32),
        ),
        in_specs=[vmem] * 4 + [hbm] + [vmem] * 4 + ([hbm, vmem, hbm] if fused else [vmem] * 3) + [vmem] * 2,
        out_specs=[vmem] * 2 + ([hbm] * 2 if fused else [vmem] * 2) + [vmem],
        scratch_shapes=scratch,
        compiler_params=pltpu.CompilerParams(
            vmem_limit_bytes=64 * 1024 * 1024,
            **(dict(collective_id=0, has_side_effects=True) if fused else {}),
        ),
    )(
        tokens[0],
        ids,
        norm_gain,
        norm_bias,
        input_proj,
        input_bias,
        position_table.transpose(2, 0, 1),
        output_proj,
        output_bias,
        w_exp,
        b_exp,
        w_red,
        reduce_bias,
        cotangent[0],
    )
    out, grad_tokens, d_attn, d_feed, small = outs
    if not fused:
        d_attn, small = lax.psum((d_attn, small), ("win", "mlp"))
        d_feed = lax.psum(lax.psum_scatter(d_feed, "mlp", scatter_dimension=1, tiled=False), "win")
    if fused and ff % width == 0 and width % 128 == 0 and side % 2 == 0:
        return finish(out, grad_tokens, d_attn, d_feed, small, side, ff)
    parts = d_attn.reshape(layers, PART, attn_rows // PART, width)
    d_in = jnp.concatenate(
        [parts[:, grp, :width, p * GLANES : (p + 1) * GLANES] for p in range(3) for grp in range(GROUPS)], axis=2
    )
    d_out = parts[:, :, width:].reshape(layers, width, width)
    if ff % width == 0:
        d_exp, d_red = (
            jnp.concatenate([d_feed[:, c : c + width] for c in range(first, first + ff, width)], axis=2)
            for first in (0, ff)
        )
        d_red = d_red.swapaxes(1, 2)
    else:
        d_exp, d_red = d_feed[:, :ff].swapaxes(1, 2), d_feed[:, ff:]
    span = min(width, ff)
    d_bexp = small[:, SMALL_EXPAND : SMALL_EXPAND + shards * (ff // span), :span].reshape(layers, shards, ff)
    d_bexp = lax.dynamic_index_in_dim(d_bexp, lax.axis_index("mlp"), 1, keepdims=False)
    d_table = jnp.stack([small[0, SMALL_TABLE[l] : SMALL_TABLE[l] + 8] for l in range(layers)])
    return (
        out[None],
        grad_tokens[None],
        small[:, 0:2],
        small[:, 2:4],
        d_in.astype(F32),
        small[:, 4:6],
        lanes_table(d_table.reshape(layers, 2 * HEADS, 128)),
        d_out.astype(F32),
        small[:, 6],
        d_exp.astype(F32),
        d_bexp,
        d_red.astype(F32),
        small[:, 7],
    )


def finish_kernel(blocks, *refs):
    attn, feed, out, grad_tokens, small = refs[:5]
    (out_to, grad_to, gain, offset, d_in, b_in, table, d_out, b_out, d_exp, b_exp, d_red, b_red) = refs[5:18]
    tall, a_held, f_held, in_held, out_held, exp_held, red_held, grid_held, in_sems, out_sems = refs[18:]
    layers, _, width = attn.shape
    part = width + width // PART
    ff = blocks * width
    passing = [
        pltpu.make_async_copy(out, grid_held.at[0], in_sems.at[2 * layers]),
        pltpu.make_async_copy(grad_tokens, grid_held.at[1], in_sems.at[2 * layers + 1]),
    ]
    arriving = [
        [
            pltpu.make_async_copy(attn.at[l], a_held.at[l], in_sems.at[2 * l]),
            pltpu.make_async_copy(feed.at[l], f_held.at[l], in_sems.at[2 * l + 1]),
        ]
        for l in range(layers)
    ]
    for pair in arriving:
        for copy in pair:
            copy.start()
    for copy in passing:
        copy.start()
    leaving = []

    def leave(src, dst):
        copy = pltpu.make_async_copy(src, dst, out_sems.at[len(leaving)])
        copy.start()
        leaving.append(copy)

    for l in range(layers):
        arriving[l][0].wait()
        for grp in range(GROUPS):
            first = grp * part
            for p in range(3):
                at = p * width + grp * GLANES
                in_held[l, :, at : at + GLANES] = a_held[l, first : first + width, p * GLANES : (p + 1) * GLANES].astype(F32)
            rows = width // PART
            out_held[l, grp * rows : (grp + 1) * rows, :] = a_held[l, first + width : first + part, :].astype(F32)
        leave(in_held.at[l], d_in.at[l])
        passing[l].wait()
        leave(grid_held.at[l], (out_to, grad_to)[l].at[0])
        leave(out_held.at[l], d_out.at[l])
        arriving[l][1].wait()
        for b in range(blocks):
            cols = slice(b * width, (b + 1) * width)
            exp_held[l, :, cols] = f_held[l, cols, :].astype(F32)
        leave(exp_held.at[l], d_exp.at[l])
        for b in range(blocks):
            cols = slice(b * width, (b + 1) * width)
            red_held[l, cols, :] = f_held[l, ff + b * width : ff + (b + 1) * width, :].astype(F32).T
        leave(red_held.at[l], d_red.at[l])

    for l in range(2):
        gain[l] = small[l, 0:2, :]
        offset[l] = small[l, 2:4, :]
        b_in[l] = small[l, 4:6, :]
        b_out[l : l + 1, :] = small[l, 6:7, :]
        b_red[l : l + 1, :] = small[l, 7:8, :]
        for b in range(blocks):
            row = SMALL_EXPAND + lax.axis_index("mlp") * blocks + b
            b_exp[l : l + 1, b * width : (b + 1) * width] = small[l, pl.ds(row, 1), :]
        turned = []
        for s in range(2):
            heads = []
            for h in range(HEADS):
                n = s * HEADS + h
                row = SMALL_TABLE[l] + n // 3
                heads.append(small[0, row : row + 1, n % 3 * 128 : (n % 3 + 1) * 128])
            heads.append(jnp.zeros((128 - HEADS, 128), F32))
            turned.append(jnp.concatenate(heads, axis=0).T)
        tall[...] = jnp.zeros(tall.shape, F32)
        for lane, entry, count, s in table_spans():
            tall[entry : entry + count, :] = turned[s][lane : lane + count]
        wide = tall[...].T
        for h in range(HEADS):
            table[h, l : l + 1, :] = wide[h : h + 1, : table.shape[2]]
    for copy in leaving:
        copy.wait()


def finish(out, grad_tokens, d_attn, d_feed, small, side, ff):
    layers, _, width = d_attn.shape
    blocks = ff // width
    vmem = pl.BlockSpec(memory_space=pltpu.VMEM)
    hbm = pl.BlockSpec(memory_space=pl.ANY)
    span = SPAN_SIDE * SPAN_SIDE
    shape = lambda *dims: jax.ShapeDtypeStruct(dims, F32)
    grid_shape = jax.ShapeDtypeStruct((1, side, side, width), BF16)
    large = ((layers, width, 3 * width), (layers, width, width), (layers, width, ff), (layers, ff, width))
    made = pl.pallas_call(
        functools.partial(finish_kernel, blocks),
        in_specs=[hbm] * 4 + [vmem],
        out_specs=[hbm, hbm, vmem, vmem, hbm, vmem, vmem, hbm, vmem, hbm, vmem, hbm, vmem],
        out_shape=[
            grid_shape,
            grid_shape,
            shape(layers, 2, width),
            shape(layers, 2, width),
            shape(*large[0]),
            shape(layers, 2, width),
            shape(HEADS, layers, span),
            shape(*large[1]),
            shape(layers, width),
            shape(*large[2]),
            shape(layers, ff),
            shape(*large[3]),
            shape(layers, width),
        ],
        scratch_shapes=[
            pltpu.VMEM((256, 128), F32),
            pltpu.VMEM(d_attn.shape, BF16),
            pltpu.VMEM(d_feed.shape, BF16),
            *(pltpu.VMEM(dims, F32) for dims in large),
            pltpu.VMEM((2,) + out.shape, BF16),
            pltpu.SemaphoreType.DMA((2 + 2 * layers,)),
            pltpu.SemaphoreType.DMA((2 + 4 * layers,)),
        ],
        compiler_params=pltpu.CompilerParams(vmem_limit_bytes=64 * 1024 * 1024),
    )(d_attn, d_feed, out, grad_tokens, small)
    return (*made[:6], made[6].transpose(1, 2, 0), *made[7:])


def solution(mesh):
    tokens = P(("win", "mlp"), None, None, None)
    placed = (
        tokens,
        P(("win", "mlp"), None, None),
        P(),
        P(),
        P(),
        P(),
        P(),
        P(),
        P(),
        P(None, None, "mlp"),
        P(None, "mlp"),
        P(None, "mlp", None),
        P(),
        tokens,
    )
    return jax.shard_map(
        functools.partial(on_device, (mesh.shape["win"], mesh.shape["mlp"])),
        mesh=mesh,
        in_specs=placed,
        out_specs=(
            tokens,
            tokens,
            P(),
            P(),
            P(),
            P(),
            P(),
            P(),
            P(),
            P(None, None, "mlp"),
            P(None, "mlp"),
            P(None, "mlp", None),
            P(),
        ),
        check_vma=False,
    )
```

```python
import functools

import jax
import jax.numpy as jnp
from jax import lax
from jax.experimental import pallas as pl
from jax.experimental.pallas import tpu as pltpu
from jax.sharding import PartitionSpec as P

HEADS = 12
HEAD_DIM = 32
WIN = 7
SHIFT = 3
SPAN_SIDE = 2 * WIN - 1

EPS = 1e-05
MASKED = -1e30

PITCH = 8
SLOTS = WIN * PITCH
GROUP = 4
GROUPS = HEADS // GROUP
GLANES = GROUP * HEAD_DIM
GQ = GROUP * SLOTS

F32 = jnp.float32
BF16 = jnp.bfloat16

ERF_P = 0.4
ERF_C = (
    0.22567691835428957,
    0.22565742813591003,
    0.2069437219941218,
    0.18213740047970625,
    0.06806251607656177,
    0.1868261013466735,
    -0.09530889147438172,
)


LOG2E = 1.4426950408889634
BELL = 0.3989422804014327


def dot(a, b):
    return lax.dot_general(a, b, (((1,), (0,)), ((), ())), preferred_element_type=F32)


def dot_nt(a, b):
    return lax.dot_general(a, b, (((1,), (1,)), ((), ())), preferred_element_type=F32)


def dot_tn(a, b):
    return lax.dot_general(a, b, (((0,), (0,)), ((), ())), preferred_element_type=F32)


def gelu_pair(u):
    bell = jnp.exp2(u * u * (-0.5 * LOG2E))
    size = jnp.abs(u)
    t = 1.0 / (1.0 + (ERF_P * 0.5**0.5) * size)
    poly = 0.5 * ERF_C[-1] * t + 0.5 * ERF_C[-2]
    for coef in ERF_C[-3::-1]:
        poly = poly * t + 0.5 * coef
    tail = bell * (t * poly)
    phi = jnp.where(u < 0, tail, 1.0 - tail)
    return jnp.maximum(u, 0.0) - size * tail, phi + u * (bell * BELL)


def norm_stats(v):
    centred = v - jnp.mean(v, axis=-1, keepdims=True)
    rstd = lax.rsqrt(jnp.mean(centred * centred, axis=-1, keepdims=True) + EPS)
    return centred * rstd, rstd


def norm_back(v, gain, upstream):
    xhat, rstd = norm_stats(v)
    scaled = upstream * gain
    inner = (
        scaled
        - jnp.mean(scaled, axis=-1, keepdims=True)
        - xhat * jnp.mean(scaled * xhat, axis=-1, keepdims=True)
    )
    return rstd * inner, jnp.sum(upstream * xhat, axis=0, keepdims=True), jnp.sum(upstream, axis=0, keepdims=True)


def iota(shape, dim):
    return lax.broadcasted_iota(jnp.int32, shape, dim)


def expand_heads(rows):
    head = iota(rows.shape, 1) // HEAD_DIM
    return jnp.concatenate([jnp.where(head == j, rows, 0.0) for j in range(GROUP)], axis=0).astype(BF16)


def fold_heads(rows):
    head = iota((SLOTS, GLANES), 1) // HEAD_DIM
    out = rows[:SLOTS]
    for j in range(1, GROUP):
        out = jnp.where(head == j, rows[j * SLOTS : (j + 1) * SLOTS], out)
    return out


def by_window(parts):
    return jnp.concatenate(
        [jnp.concatenate(parts[w * GROUPS : (w + 1) * GROUPS], axis=1) for w in range(BLOCK_WINDOWS)], axis=0
    )


def window_row(per_side, wr, wc, r):
    return pl.multiple_of((wr * per_side + wc) * SLOTS + r * PITCH, PITCH)


def grid_to_windows(src, side, shifted, emit):
    per_side = side // WIN

    def step(wr, carry):
        for r in range(WIN):
            row = lax.rem(wr * WIN + r + (SHIFT if shifted else 0), side)
            line = src[row].astype(F32)
            width = line.shape[1]
            if line.shape[0] < 32:
                line = jnp.concatenate([line, jnp.zeros((32 - line.shape[0], width), F32)], axis=0)
            if shifted:
                i = iota(line.shape, 0)
                line = jnp.where(i < side - SHIFT, pltpu.roll(line, 32 - SHIFT, 0), pltpu.roll(line, side - SHIFT, 0))
            for wc in range(per_side):
                part = line if wc == 0 else pltpu.roll(line, 32 - WIN * wc, 0)
                part = part[:PITCH]
                part = jnp.where(iota(part.shape, 0) < WIN, part, 0.0)
                emit(wr, wc, r, part)
        return carry

    lax.fori_loop(0, per_side, step, 0)


def windows_to_grid(src, dst, side, shifted):
    per_side = side // WIN

    def step(wr, carry):
        for r in range(WIN):
            row = lax.rem(wr * WIN + r + (SHIFT if shifted else 0), side)
            width = src.shape[1]
            line = jnp.zeros((32, width), F32)
            i = iota(line.shape, 0)
            for wc in range(per_side):
                tile = src[pl.ds(window_row(per_side, wr, wc, r), PITCH), :]
                tile = jnp.concatenate([tile, jnp.zeros((32 - PITCH, width), F32)], axis=0)
                if wc:
                    tile = pltpu.roll(tile, WIN * wc, 0)
                line = jnp.where((i >= WIN * wc) & (i < WIN * (wc + 1)), tile, line)
            if shifted:
                line = jnp.where(i < SHIFT, pltpu.roll(line, 32 - side + SHIFT, 0), pltpu.roll(line, SHIFT, 0))
            dst[row] = line[:side].astype(dst.dtype)
        return carry

    lax.fori_loop(0, per_side, step, 0)


def regular_to_shifted(src, dst, side):
    per_side = side // WIN

    def step(wr, carry):
        below = lax.rem(wr + 1, per_side)
        for r in range(WIN):
            sr, srr = (wr, r + SHIFT) if r + SHIFT < WIN else (below, r + SHIFT - WIN)
            for wc in range(per_side):
                here = src[pl.ds(window_row(per_side, sr, wc, srr), PITCH), :]
                right = src[pl.ds(window_row(per_side, sr, (wc + 1) % per_side, srr), PITCH), :]
                i = iota(here.shape, 0)
                tile = jnp.where(
                    i < WIN - SHIFT,
                    pltpu.roll(here, PITCH - SHIFT, 0),
                    jnp.where(i < WIN, pltpu.roll(right, WIN - SHIFT, 0), 0.0),
                )
                dst[pl.ds(window_row(per_side, wr, wc, r), PITCH), :] = tile
        return carry

    lax.fori_loop(0, per_side, step, 0)


def shifted_to_regular(src, dst, side):
    per_side = side // WIN

    def step(wr, carry):
        above = lax.rem(wr + per_side - 1, per_side)
        for r in range(WIN):
            sr, srr = (wr, r - SHIFT) if r >= SHIFT else (above, r - SHIFT + WIN)
            for wc in range(per_side):
                here = src[pl.ds(window_row(per_side, sr, wc, srr), PITCH), :]
                left = src[pl.ds(window_row(per_side, sr, (wc + per_side - 1) % per_side, srr), PITCH), :]
                i = iota(here.shape, 0)
                tile = jnp.where(
                    i < SHIFT,
                    pltpu.roll(left, PITCH - (WIN - SHIFT), 0),
                    jnp.where(i < WIN, pltpu.roll(here, SHIFT, 0), 0.0),
                )
                dst[pl.ds(window_row(per_side, wr, wc, r), PITCH), :] = tile
        return carry

    lax.fori_loop(0, per_side, step, 0)


BLOCK_WINDOWS = 4
LINE_UNROLL, ATTEND_UNROLL, UP_UNROLL, BACK_UNROLL = 4, 4, 1, 4
ROWS_BLOCK = BLOCK_WINDOWS * SLOTS
JOBS = [
    (w, grp, slice(w * SLOTS, (w + 1) * SLOTS)) for w in range(BLOCK_WINDOWS) for grp in range(GROUPS)
]
GAIN_1, GAIN_2, OFFSET_1, OFFSET_2, BIAS_Q, BIAS_V, BIAS_OUT, BIAS_REDUCE = range(8)
SMALL_EXPAND = 8
SMALL_EARLY = 16
SMALL_TABLE = {0: 16, 1: 24}
SMALL_ROWS = 32
ADD_ROWS = 96
SEMAPHORES = 320
PART = 3


def table_spans():
    spans = []
    for dr in range(SPAN_SIDE):
        at = PITCH * (dr - WIN + 1)
        spans.append((at % 128, dr * SPAN_SIDE + WIN - 1, WIN, 0))
        spans.append(((at - PITCH) % 128 + PITCH - WIN + 1, dr * SPAN_SIDE, WIN - 1, 1))
    return spans


CORE, X, Y, Z, MLP, PLANE = range(6)


class Links:
    def __init__(self, mesh_shape, send_sem, recv_sem):
        self.win, self.mlp = mesh_shape
        self.send_sem, self.recv_sem = send_sem, recv_sem
        w, m = lax.axis_index("win"), lax.axis_index("mlp")
        self.core, self.x, self.z, self.m = lax.rem(w, 2), lax.rem(lax.div(w, 2), 2), lax.div(w, 4), m
        self.depth = self.win // 4
        self.groups = {
            CORE: (2, self.core, lambda q: self.at(core=q)),
            X: (2, self.x, lambda q: self.at(x=q)),
            Z: (self.depth, self.z, lambda q: self.at(z=q)),
            MLP: (self.mlp, m, lambda q: self.at(m=q)),
            Y: (self.mlp, m, lambda q: self.at(m=q)),
            PLANE: (
                2 * self.mlp,
                self.x * self.mlp + m,
                lambda q: self.at(x=lax.div(q, self.mlp), m=lax.rem(q, self.mlp)),
            ),
        }
        self.used = 0

    def at(self, core=None, x=None, z=None, m=None):
        core = self.core if core is None else core
        x = self.x if x is None else x
        z = self.z if z is None else z
        m = self.m if m is None else m
        return ((z * 2 + x) * 2 + core, m)

    def peers(self, group):
        size, me, _ = self.groups[group]
        return [(d, lax.rem(me + d, size)) for d in range(1, size)]

    def me(self, group):
        return self.groups[group][1]

    def size(self, group):
        return self.groups[group][0]

    def greet(self):
        sem = pltpu.get_barrier_semaphore()
        for group in (CORE, PLANE, Z):
            for _, q in self.peers(group):
                pl.semaphore_signal(
                    sem, inc=1, device_id=self.groups[group][2](q), device_id_type=pl.DeviceIdType.MESH
                )

    def meet(self):
        pl.semaphore_wait(pltpu.get_barrier_semaphore(), sum(self.size(g) - 1 for g in (CORE, PLANE, Z)))

    def reserve(self, count):
        first = self.used
        self.used += count
        assert self.used <= SEMAPHORES
        return first

    def copy(self, group, q, src, dst, n):
        return pltpu.make_async_remote_copy(
            src_ref=src,
            dst_ref=dst,
            send_sem=self.send_sem.at[n],
            recv_sem=self.recv_sem.at[n],
            device_id=self.groups[group][2](q),
            device_id_type=pl.DeviceIdType.MESH,
        )


def add_rows(dst, sources, count):
    step = next(n for n in (ADD_ROWS, 64, 48, 32, 16) if count % n == 0)

    def one(i, carry):
        at = pl.ds(pl.multiple_of(i * step, 16), step)
        total = dst[at, :].astype(F32)
        for source in sources:
            total = total + source[at, :].astype(F32)
        dst[at, :] = total.astype(dst.dtype)
        return carry

    lax.fori_loop(0, count // step, one, 0)


REDUCE, EXPAND, ATTEND = range(3)
FLOWS = (
    (REDUCE, 1, 0, 0, 3, 0, (CORE, PLANE, Z)),
    (REDUCE, 1, 0, 0, 3, 1, (CORE, PLANE, Z)),
    (REDUCE, 1, 0, 0, 3, 2, (CORE, PLANE, Z)),
    (EXPAND, 1, 0, 0, 3, 0, (CORE, PLANE, Z)),
    (EXPAND, 1, 0, 0, 3, 1, (CORE, PLANE, Z)),
    (EXPAND, 1, 0, 0, 3, 2, (CORE, PLANE, Z)),
    (ATTEND, 1, 0, 1, 1, 0, (CORE, X, Y, Z)),
    (ATTEND, 1, 1, 1, 1, 0, (CORE, Y, Z, X)),
    (ATTEND, 1, 2, 1, 1, 0, (CORE, Y, X, Z)),
    (REDUCE, 0, 0, 0, 3, 0, (CORE, PLANE, Z)),
    (REDUCE, 0, 0, 0, 3, 1, (CORE, PLANE, Z)),
    (REDUCE, 0, 0, 0, 3, 2, (CORE, PLANE, Z)),
    (EXPAND, 0, 0, 0, 3, 0, (CORE, MLP, X, Z)),
    (EXPAND, 0, 0, 0, 3, 1, (CORE, MLP, X, Z)),
    (EXPAND, 0, 0, 0, 3, 2, (CORE, MLP, X, Z)),
    (ATTEND, 0, 0, 1, 1, 0, (CORE, PLANE, Z)),
    (ATTEND, 0, 1, 1, 1, 0, (CORE, PLANE, Z)),
    (ATTEND, 0, 2, 1, 3, 0, (CORE, PLANE, Z)),
    (ATTEND, 0, 2, 1, 3, 1, (CORE, PLANE, Z)),
    (ATTEND, 0, 2, 1, 3, 2, (CORE, PLANE, Z)),
)


def flow_table(mesh_shape, width, ff):
    part = 4 * width // PART
    win, mlp = mesh_shape
    sizes = {CORE: 2, X: 2, Y: mlp, Z: win // 4, MLP: mlp, PLANE: 2 * mlp}
    flows, shapes = [], []
    for kind, l, first, count, splits, split, stages in FLOWS:
        if kind == ATTEND:
            first, rows = first * part, count * part
        else:
            first, rows = (ff if kind == REDUCE else 0), ff
        lanes = (split * (width // splits), width // splits)
        slots = 1 if kind == ATTEND else mlp
        flows.append((l, kind != ATTEND, (first, rows), lanes, stages))
        landing = []
        for stage in stages:
            if stage == MLP:
                slots = 1
            elif stage == PLANE and slots > 1:
                slots, rows = 1, rows // 2
            else:
                rows //= sizes[stage]
            landing.append((sizes[stage] - 1, slots, rows, lanes[1]))
        shapes.append(landing)
    return flows, shapes


def small_flow(l):
    return len(FLOWS) + 1 - l


class Flow:
    def __init__(self, links, staged, out, slots, span, lanes, stages, buffers, local_sem):
        self.links, self.staged, self.out, self.local_sem = links, staged, out, local_sem
        self.stages, self.buffers, self.lanes = stages, buffers, pl.ds(*lanes)
        self.spans, self.slots, self.down = [span], [slots], []
        for n, stage in enumerate(stages):
            first, rows = self.spans[-1]
            if stage == MLP:
                slots = 1
            elif stage == PLANE and slots > 1:
                slots, rows = 1, rows // 2
                first = first + links.x * rows
                self.down.insert(0, (n, X))
            else:
                rows = rows // links.size(stage)
                first = first + links.me(stage) * rows
                self.down.insert(0, (n, stage))
            self.spans.append((first, rows))
            self.slots.append(slots)
        self.steps = len(stages) + len(self.down)
        self.sems = [links.reserve(links.size(group) - 1) for group in stages + tuple(group for _, group in self.down)]

    def copies(self, k):
        links = self.links
        made = []
        if k < len(self.stages):
            stage, slots = self.stages[k], self.slots[k]
            (first, _), (_, rows) = self.spans[k], self.spans[k + 1]
            for d, q in links.peers(stage):
                if stage == MLP:
                    slot, at = pl.ds(d, 1), first
                elif stage == PLANE and slots > 1:
                    slot, at = pl.ds(d % links.mlp, 1), first + lax.div(q, links.mlp) * rows
                else:
                    slot, at = pl.ds(0, slots), first + q * rows
                src = self.staged.at[slot, pl.ds(pl.multiple_of(at, 16), rows), self.lanes]
                made.append(links.copy(stage, q, src, self.buffers[k].at[d - 1], self.sems[k] + d - 1))
            return made
        n, group = self.down[k - len(self.stages)]
        src = self.mine(n + 1, self.staged.at[0] if k == len(self.stages) else self.out)
        for d, q in links.peers(group):
            made.append(links.copy(group, q, src, self.mine(n + 1, self.out), self.sems[k] + d - 1))
        return made

    def mine(self, n, ref):
        first, rows = self.spans[n]
        return ref.at[pl.ds(pl.multiple_of(first, 16), rows), self.lanes]

    def local(self):
        return pltpu.make_async_copy(
            self.mine(len(self.stages), self.staged.at[0]), self.mine(len(self.stages), self.out), self.local_sem
        )

    def advance(self, k):
        if k:
            for copy in self.copies(k - 1):
                copy.wait()
            if k - 1 < len(self.stages):
                for slot in range(self.slots[k]):
                    add_rows(
                        self.mine(k, self.staged.at[slot]),
                        [self.buffers[k - 1].at[d - 1, slot] for d, _ in self.links.peers(self.stages[k - 1])],
                        self.spans[k][1],
                    )
            elif k - 1 == len(self.stages):
                self.local().wait()
        if k < self.steps:
            if k == len(self.stages):
                self.local().start()
            for copy in self.copies(k):
                copy.start()


class SmallFlow:
    def __init__(self, links, value, buffers, out):
        self.links, self.value, self.buffers, self.out = links, value, buffers, out
        self.stages = (CORE, PLANE, Z)
        self.sems = [links.reserve(links.size(stage) - 1) for stage in self.stages]
        self.steps = len(self.stages)

    def copies(self, k):
        stage, buffer = self.stages[k], self.buffers[k]
        me = self.links.me(stage)
        return [
            self.links.copy(stage, q, buffer.at[me], buffer.at[me], self.sems[k] + d - 1)
            for d, q in self.links.peers(stage)
        ]

    def advance(self, k):
        total = self.value[...] if k == 0 else None
        if k:
            for copy in self.copies(k - 1):
                copy.wait()
            buffer = self.buffers[k - 1]
            total = buffer[0].astype(F32)
            for j in range(1, buffer.shape[0]):
                total = total + buffer[j].astype(F32)
        if k < len(self.stages):
            self.buffers[k][self.links.me(self.stages[k])] = total.astype(BF16)
            for copy in self.copies(k):
                copy.start()
        else:
            self.out[...] = total


(AT_REDUCE, AT_FEED, AT_EXPAND, AT_MIDDLE, AT_ATTEND, AT_GROUP, AT_INPUT, AT_SUMS, AT_TABLE, AT_PLACED, AT_OUT) = range(11)
PLAN = {
    (1, AT_MIDDLE, 2): (0,),
    (1, AT_MIDDLE, 3): (1, 2),
    (1, AT_ATTEND, 0): (5, 3, 4),
    (1, AT_ATTEND, 2): (0,),
    (1, AT_ATTEND, 3): (6,),
    (1, AT_GROUP, 1): (1,),
    (1, AT_ATTEND, 5): (7, 2),
    (1, AT_INPUT, 0): (0,),
    (1, AT_INPUT, 2): (5, 8),
    (1, AT_INPUT, 3): (1,),
    (0, AT_REDUCE, 0): (2, 20, 3, 4, 0),
    (0, AT_FEED, 0): (9, 5, 7, 11, 6, 1, 10),
    (0, AT_FEED, 1): (8, 0, 2, 20),
    (0, AT_EXPAND, 0): (0, 3, 4),
    (0, AT_MIDDLE, 0): (9, 5),
    (0, AT_MIDDLE, 1): (12,),
    (0, AT_MIDDLE, 2): (13, 14),
    (0, AT_MIDDLE, 3): (11, 7, 6, 1),
    (0, AT_ATTEND, 0): (20, 1),
    (0, AT_ATTEND, 1): (3, 8, 10, 4),
    (0, AT_ATTEND, 2): (12, 9, 5, 15, 7, 2, 11),
    (0, AT_ATTEND, 3): (5, 13, 2, 6, 3),
    (0, AT_ATTEND, 4): (8, 12, 3, 16, 14, 10, 4),
    (0, AT_ATTEND, 5): (9,),
    (0, AT_GROUP, 2): (15, 7, 11, 4),
    (0, AT_INPUT, 0): (17, 18, 19, 13, 6),
    (0, AT_INPUT, 2): (8,),
    (0, AT_TABLE, 0): (16, 12),
    (0, AT_TABLE, 1): (14, 10),
    (0, AT_PLACED, 0): (9, 15),
    (0, AT_OUT, 0): (17, 9, 18, 7, 11, 6, 19, 13, 21),
}
LAST = (8, 16, 11, 12, 10, 14, 15, 17, 7, 18, 6, 19, 10, 13, 7, 21, 12, 16, 6, 8, 12, 17, 18, 8, 19, 13, 15, 14, 13, 15, 16, 21, 17, 16, 17, 18, 19, 14, 18, 19, 14)


def number_steps():
    count = [1] * (len(FLOWS) + 2)

    def number(names):
        pairs = []
        for n in names:
            pairs.append((n, count[n]))
            count[n] += 1
        return tuple(pairs)

    return {key: number(names) for key, names in PLAN.items()}, number(LAST), count


STEPS, TAIL, COUNT = number_steps()


def kernel(side, mesh_shape, *refs):
    refs = list(refs)

    def take(n):
        got = refs[:n]
        del refs[:n]
        return got

    tokens, ids, gain, offset, global_in, b_in, table, w_out, b_out, w_exp, b_exp, w_red, b_red, cot = take(14)
    fused = mesh_shape is not None
    out, grad_tokens, d_attn, d_feed, small = take(5)
    (x, normed, qkv, probs, mixed, mid, second, hidden, slope) = take(9)
    (keys, bias, bias_sum, g, gs, gz, gb_low, dqkv, go, d_bexp, turn, spread, w_in, turned, gz_turned, wide, tall, hot_grid, in_sems) = take(19)
    flows = []
    if fused:
        out_attn, out_feed, out_small = d_attn, d_feed, small
        d_attn, d_feed, small = take(3)
        local_exp, local_bexp, local_red = w_exp, b_exp, w_red
        w_exp, b_exp, w_red = take(3)
        small_buffers = [take(3) for _ in range(2)]
        flow_rows, shapes = flow_table(mesh_shape, x.shape[2], local_exp.shape[2])
        landing = [take(len(shape)) for shape in shapes]
        local_sems, send_sem, recv_sem = take(3)
        links = Links(mesh_shape, send_sem, recv_sem)
        for n, (l, feed_flow, span, lanes, stages) in enumerate(flow_rows):
            flows.append(
                Flow(
                    links,
                    d_feed.at[l] if feed_flow else d_attn.at[pl.ds(l, 1)],
                    out_feed.at[l] if feed_flow else out_attn.at[l],
                    mesh_shape[1] if feed_flow else 1,
                    span,
                    lanes,
                    stages,
                    landing[n],
                    local_sems.at[3 + n],
                )
            )
        for l in (1, 0):
            part = pl.ds(0, SMALL_EARLY if l else SMALL_ROWS)
            flows.append(SmallFlow(links, small.at[l, part], small_buffers[l], out_small.at[l, part]))

    def advance(*pairs):
        if fused:
            for n, k in pairs:
                flows[n].advance(k)

    def begin(kind, l, part=0):
        advance(
            *((n, 0) for n, flow in enumerate(FLOWS) if flow[:2] == (kind, l) and (kind != ATTEND or flow[2] + flow[3] - 1 == part))
        )

    def ticks(l, point, i=0):
        advance(*STEPS.get((l, point, i), ()))

    def ticks_in_loop(l, point, i, n, unroll, j):
        for (at_l, at_point, at_i), names in STEPS.items():
            if fused and (at_l, at_point) == (l, point) and at_i % unroll == j:
                if isinstance(i, int):
                    if i == at_i:
                        advance(*names)
                else:
                    pl.when(n == at_i // unroll)(functools.partial(advance, *names))

    per_side = side // WIN
    windows = per_side * per_side
    rows = windows * SLOTS
    blocks = rows // ROWS_BLOCK
    shards, _, width, ff = w_exp.shape
    chunk = 256 if ff % 256 == 0 else ff
    blocked = ff % width == 0
    part_rows = 4 * width // PART

    gathers = [
        pltpu.make_async_copy(
            global_in.at[l, :, pl.ds(p * width + grp * GLANES, GLANES)],
            w_in.at[l, :, pl.ds(grp * width + p * GLANES, GLANES)],
            in_sems.at[(l * GROUPS + grp) * 3 + p],
        )
        for l in range(2)
        for grp in range(GROUPS)
        for p in range(3)
    ]
    for copy in gathers:
        copy.start()
    if fused:
        links.greet()
        own = [
            pltpu.make_async_copy(local_exp, w_exp.at[0], local_sems.at[0]),
            pltpu.make_async_copy(local_red, w_red.at[0], local_sems.at[1]),
        ]
        for copy in own:
            copy.start()
        b_exp[0, 0:2, :] = local_bexp[...].astype(F32)
        halves = (
            pl.ds(pl.multiple_of(links.core * (width // 2), 16), width // 2),
            pl.ds(pl.multiple_of(links.core * (ff // 2), 16), ff // 2),
        )
        weights = ((local_exp, w_exp, halves[0], width // 4), (local_red, w_red, halves[1], ff // 4))
        fetch_sems = links.reserve(4 * (shards - 1))
        relay_sems = links.reserve(2 * (shards - 1))
        pass_sems = links.reserve(4 * (shards - 1))
        bias_sems = links.reserve(shards - 1)

        def quarter(n):
            rows = weights[n][3]
            return pl.ds(pl.multiple_of((links.core * 2 + links.x) * rows, 16), rows)

        def fetches(l, n):
            source, dest, half, _ = weights[n]
            part = quarter(n) if l else half
            return [
                links.copy(MLP, q, source.at[l, part], dest.at[shards - d, l, part], fetch_sems + (2 * l + n) * (shards - 1) + d - 1)
                for d, q in links.peers(MLP)
            ]

        def relays(n):
            dest, part = weights[n][1], quarter(n)
            ((_, beside),) = links.peers(X)
            return [
                links.copy(X, beside, dest.at[d, 1, part], dest.at[d, 1, part], relay_sems + n * (shards - 1) + d - 1)
                for d, _ in links.peers(MLP)
            ]

        def passes(l, n):
            _, dest, half, _ = weights[n]
            ((_, sibling),) = links.peers(CORE)
            return [
                links.copy(CORE, sibling, dest.at[d, l, half], dest.at[d, l, half], pass_sems + (2 * l + n) * (shards - 1) + d - 1)
                for d, _ in links.peers(MLP)
            ]

        def bias_fetches():
            return [links.copy(MLP, q, b_exp.at[0], b_exp.at[shards - d], bias_sems + d - 1) for d, q in links.peers(MLP)]

        def fetch_all():
            for copy in bias_fetches():
                copy.start()
            for l in range(2):
                for n in range(2):
                    for copy in fetches(l, n):
                        copy.start()

        def relay(n):
            for copy in fetches(1, n):
                copy.wait()
            for copy in relays(n):
                copy.start()

        def pass_on(l, n):
            for copy in relays(n) if l else fetches(l, n):
                copy.wait()
            for copy in passes(l, n):
                copy.start()

        def passed(l, n):
            for copy in passes(l, n):
                copy.wait()

    def over_blocks(body, tick=None, after=None, unroll=1):
        def step(n, carry):
            for j in range(unroll):
                i = n * unroll + j
                body(pl.ds(i * ROWS_BLOCK if isinstance(i, int) else pl.multiple_of(i * ROWS_BLOCK, ROWS_BLOCK), ROWS_BLOCK))
                if tick:
                    ticks_in_loop(*tick, i, n, unroll, j)
                if after:
                    after(i)
            return carry

        if unroll == blocks:
            step(0, 0)
        else:
            lax.fori_loop(0, blocks // unroll, step, 0)

    wide[...] = jnp.zeros(wide.shape, F32)
    for row in range(side):
        wide[row : row + 1, :side] = ids[row].astype(F32)
    by_column = wide[:, :128].T[:32]
    for row in range(side):
        hot_grid[row] = jnp.broadcast_to(by_column[:, row : row + 1], (32, 128))
    wide[...] = jnp.zeros(wide.shape, F32)

    def put_tokens(wr, wc, r, tile):
        x[0, pl.ds(window_row(per_side, wr, wc, r), PITCH), :] = tile

    grid_to_windows(tokens, side, False, put_tokens)
    if fused:
        links.meet()
        fetch_all()

    def prepare(l):
        shifted = l == 1

        def put_keys(wr, wc, r, tile, shifted=shifted):
            lane = iota(tile.shape, 1).astype(F32)
            slot = iota(tile.shape, 0)
            label = tile
            if shifted:
                row_at = wr * WIN + r
                row_label = jnp.where(row_at >= side - WIN, 1, 0) + jnp.where(row_at >= side - SHIFT, 1, 0)
                col_at = wc * WIN + slot
                col_label = jnp.where(col_at >= side - WIN, 1, 0) + jnp.where(col_at >= side - SHIFT, 1, 0)
                label = label + (12 * row_label + 4 * col_label).astype(F32)
            hot = jnp.where((lane == label) & (slot < WIN), 1.0, 0.0)
            keys[l, pl.ds(window_row(per_side, wr, wc, r), PITCH), :] = hot

        grid_to_windows(hot_grid, side, shifted, put_keys)

        krow = iota((SLOTS, 128), 0)
        qlane = iota((SLOTS, 128), 1)
        ahead = (qlane & (PITCH - 1)) >= (krow & (PITCH - 1))
        turn[...] = jnp.zeros(turn.shape, F32)
        for h in range(HEADS):
            wide[h : h + 1, : table.shape[2]] = table[h, l : l + 1, :]
        tall[...] = wide[...].T
        for lane, entry, count, s in table_spans():
            turn[s, lane : lane + count, :] = tall[entry : entry + count, :]
        for s in range(2):
            spread[s] = turn[s].T[: spread.shape[1]]
        for grp in range(GROUPS):
            low = jnp.zeros((SLOTS, 128), F32)
            high = jnp.zeros((SLOTS, 128), F32)
            for j in range(GROUP):
                h = grp * GROUP + j
                both = [
                    pltpu.roll(
                        jnp.broadcast_to(spread[s, h : h + 1, :], (SLOTS, 128)),
                        0,
                        1,
                        stride=1,
                        stride_axis=0,
                    )
                    for s in range(2)
                ]
                one = jnp.where(ahead, both[0], both[1])
                at = j * SLOTS
                if at < 128:
                    moved = pltpu.roll(one, at, 1) if at else one
                    low = jnp.where((qlane >= at) & (qlane < at + SLOTS), moved, low)
                if at + SLOTS > 128:
                    moved = pltpu.roll(one, (at - 128) % 128, 1)
                    high = jnp.where((qlane >= at - 128) & (qlane < at - 128 + SLOTS), moved, high)
            bias[l, grp, :, :128] = low
            bias[l, grp, :, 128:] = high[:, : GQ - 128]

    def put_cot(wr, wc, r, tile):
        g[pl.ds(window_row(per_side, wr, wc, r), PITCH), :] = tile

    def add_small(l, at, value):
        small[l, at : at + 1, :] += value

    def lower(at, l):
        g_now = g[at, :]
        add_small(l, BIAS_REDUCE, jnp.sum(g_now, axis=0, keepdims=True))
        gz[at, :] = g_now.astype(BF16)

    def feed_up(at, i, l):
        s = second[l, at, :]
        jobs = [slice(c, c + chunk) for c in range(0, ff, chunk)]
        befores = [dot(s, w_exp[i, l, :, cols]) for cols in jobs]
        for before, cols in zip(befores, jobs):
            value, slope_now = gelu_pair(before + b_exp[i, l : l + 1, cols])
            hidden[l, i, at, cols] = value.astype(BF16)
            slope[l, i, at, cols] = slope_now.astype(BF16)

    def feed_down(at, i, l):
        gs[at, :] += dot(hidden[l, i, at, :], w_red[i, l])

    def feed_back(at, i, l):
        g_low = gz[at, :]
        jobs = [slice(c, c + chunk) for c in range(0, ff, chunk)]
        ghs = [dot_nt(g_low, w_red[i, l, cols, :]) for cols in jobs]
        for gh, cols in zip(ghs, jobs):
            gb = gh * slope[l, i, at, cols].astype(F32)
            d_bexp[i, 0:1, cols] += jnp.sum(gb, axis=0, keepdims=True)
            gb_low[i, at, cols] = gb.astype(BF16)
        gs[at, :] += dot_nt(gb_low[i, at, :], w_exp[i, l])

    def reduce_weights(i, l):
        if blocked:
            for c in range(0, ff, width):
                d_feed[l, i, ff + c : ff + c + width, :] = dot(gz_turned[...], hidden[l, i, :, c : c + width]).astype(BF16)
        else:
            d_feed[l, i, ff:, :] = dot_tn(hidden[l, i], gz[...]).astype(BF16)

    def expand_weights(i, l):
        if blocked:
            for c in range(0, ff, width):
                d_feed[l, i, c : c + width, :] = dot(turned[...], gb_low[i, :, c : c + width]).astype(BF16)
        else:
            d_feed[l, i, :ff, :] = dot_tn(gb_low[i], second[l]).astype(BF16)

    def over_shards(first, body):
        def step(i, carry):
            body(i)
            return carry

        lax.fori_loop(first, shards, step, 0)

    small[...] = jnp.zeros(small.shape, F32)
    prepare(0)

    for l in range(2):
        bias_row = jnp.concatenate(
            [
                one[:, grp * GLANES : (grp + 1) * GLANES]
                for grp in range(GROUPS)
                for one in (b_in[l, 0:1, :], jnp.zeros((1, width), F32), b_in[l, 1:2, :])
            ],
            axis=1,
        )
        if l == 0:
            for copy in gathers:
                copy.wait()

        def project(at, l=l, bias_row=bias_row):
            xhat, _ = norm_stats(x[l, at, :])
            a = (xhat * gain[l, 0:1, :] + offset[l, 0:1, :]).astype(BF16)
            normed[l, at, :] = a
            for c in range(3):
                cols = slice(c * width, (c + 1) * width)
                qkv[l, at, cols] = (dot(a, w_in[l, :, cols]) + bias_row[:, cols]).astype(BF16)

        over_blocks(project, unroll=LINE_UNROLL)

        def attend(i, l=l):
            at = pl.ds(pl.multiple_of(i * ROWS_BLOCK, ROWS_BLOCK), ROWS_BLOCK)
            q, k, v = (
                [
                    qkv[l, at, grp * width + p * GLANES : grp * width + (p + 1) * GLANES].astype(F32)
                    for grp in range(GROUPS)
                ]
                for p in range(3)
            )
            hot = keys[l, at, :]
            allowed = []
            for w in range(BLOCK_WINDOWS):
                hot_w = hot[w * SLOTS : (w + 1) * SLOTS]
                same = dot_nt(hot_w.astype(BF16), jnp.concatenate([hot_w] * GROUP, axis=0).astype(BF16))
                allowed.append(same > 0.5)
            scores = [
                dot_nt(k[grp][here].astype(BF16), expand_heads(q[grp][here])) for _, grp, here in JOBS
            ]
            scores = [
                jnp.where(allowed[w], s * HEAD_DIM**-0.5 + bias[l, grp], MASKED)
                for s, (w, grp, _) in zip(scores, JOBS)
            ]
            tops = [jnp.max(s, axis=0, keepdims=True) for s in scores]
            raised = [jnp.exp(s - top) for s, top in zip(scores, tops)]
            shares = [1.0 / jnp.sum(e, axis=0, keepdims=True) for e in raised]
            ps = [(e * share).astype(BF16) for e, share in zip(raised, shares)]
            for p, (w, grp, _) in zip(ps, JOBS):
                probs[l, BLOCK_WINDOWS * i + w, grp] = p
            outs = [
                fold_heads(dot_tn(p, v[grp][here].astype(BF16))) for p, (_, grp, here) in zip(ps, JOBS)
            ]
            mixed[l, at, :] = by_window(outs).astype(BF16)

        def attend_step(n, carry):
            for j in range(ATTEND_UNROLL):
                attend(n * ATTEND_UNROLL + j)
            return carry

        lax.fori_loop(0, blocks // ATTEND_UNROLL, attend_step, 0)

        def middle(at, l=l):
            m = x[l, at, :] + dot(mixed[l, at, :], w_out[l]) + b_out[l : l + 1, :]
            mid[l, at, :] = m
            xhat, _ = norm_stats(m)
            second[l, at, :] = (xhat * gain[l, 1:2, :] + offset[l, 1:2, :]).astype(BF16)
            if l == 0:
                gs[at, :] = m + b_red[l : l + 1, :]

        if fused and l == 1:
            relay(0)
        over_blocks(middle, unroll=LINE_UNROLL)
        if l == 1:
            break
        if fused:
            pass_on(0, 0)
            for copy in own:
                copy.wait()

        def up(i):
            if fused:

                @pl.when(i == 1)
                def _():
                    for copy in bias_fetches():
                        copy.wait()
                    passed(0, 0)

            def second_fetch(block):
                if fused:
                    pl.when((i == 1) & (block == blocks // 2))(functools.partial(pass_on, 0, 1))

            over_blocks(functools.partial(feed_up, i=i, l=0), after=second_fetch, unroll=UP_UNROLL)

        over_shards(0, up)
        prepare(1)
        grid_to_windows(cot, side, True, put_cot)
        over_blocks(functools.partial(lower, l=1))
        if blocked:
            gz_turned[...] = gz[...].T
        if fused:
            passed(0, 1)
        over_shards(0, lambda i: over_blocks(functools.partial(feed_down, i=i, l=0), unroll=2))
        regular_to_shifted(gs, x.at[1], side)

    d_bexp[...] = jnp.zeros(d_bexp.shape, F32)
    if blocked:
        turned[...] = second[1].T
    gs[...] = jnp.zeros(gs.shape, F32)
    if fused:
        relay(1)

    def both_ways(i):
        if fused:

            @pl.when(i == 1)
            def _():
                pass_on(1, 1)
                passed(1, 0)

        over_blocks(functools.partial(feed_up, i=i, l=1), unroll=UP_UNROLL)
        if fused:
            pl.when(i == 0)(functools.partial(pass_on, 1, 0))
            pl.when(i == 1)(functools.partial(passed, 1, 1))
        over_blocks(functools.partial(feed_back, i=i, l=1), unroll=BACK_UNROLL)
        reduce_weights(i, 1)
        expand_weights(i, 1)

    over_shards(0, both_ways)

    def table_back(l):
        krow = iota((SLOTS, 128), 0)
        qlane = iota((SLOTS, 128), 1)
        ahead = (qlane & (PITCH - 1)) >= (krow & (PITCH - 1))
        kept = (ahead & (qlane < SLOTS), jnp.logical_not(ahead) & (qlane < SLOTS))
        lined = []
        for grp in range(GROUPS):
            low = bias_sum[l, grp, :, :128]
            high = jnp.concatenate([bias_sum[l, grp, :, 128:], jnp.zeros((SLOTS, 256 - GQ), F32)], axis=1)
            for j in range(GROUP):
                at = j * SLOTS
                if at + SLOTS <= 128:
                    one = pltpu.roll(low, 128 - at, 1) if at else low
                elif at < 128:
                    one = jnp.where(qlane < 128 - at, pltpu.roll(low, 128 - at, 1), pltpu.roll(high, 128 - at, 1))
                else:
                    one = pltpu.roll(high, (256 - at) % 128, 1)
                lined.append(one)
        picked = [jnp.where(keep, one, 0.0) for keep in kept for one in lined]
        tiles = [one[:PITCH] for one in picked]
        for r in range(1, WIN):
            turned_rows = [pltpu.roll(one[r * PITCH : (r + 1) * PITCH], 128 - r * PITCH, 1) for one in picked]
            tiles = [tile + one for tile, one in zip(tiles, turned_rows)]
        odd = iota((PITCH, 128), 0)
        for step in (1, 2, 4):
            tiles = [jnp.where((odd & step) > 0, pltpu.roll(tile, 128 - step, 1), tile) for tile in tiles]
        for n, tile in enumerate(tiles):
            row = SMALL_TABLE[l] + n // 3
            small[0, row : row + 1, n % 3 * 128 : (n % 3 + 1) * 128] = jnp.sum(tile, axis=0, keepdims=True)


    for l in (1, 0):

        if l == 0:
            over_blocks(functools.partial(lower, l=0))
            if blocked:
                gz_turned[...] = gz[...].T
            over_shards(0, functools.partial(reduce_weights, l=0))
        begin(REDUCE, l)
        ticks(l, AT_REDUCE)
        if l == 0:
            d_bexp[...] = jnp.zeros(d_bexp.shape, F32)

            gs[...] = jnp.zeros(gs.shape, F32)

            def back(i):
                over_blocks(functools.partial(feed_back, i=i, l=0), unroll=BACK_UNROLL)
                for key, names in STEPS.items():
                    if fused and key[:2] == (0, AT_FEED):
                        pl.when(i == key[2])(functools.partial(advance, *names))

            over_shards(0, back)
        span = min(width, ff)
        for n in range(shards * (ff // span)):
            i, c = n // (ff // span), n % (ff // span) * span
            row = n
            if fused:
                row = lax.rem(links.m + i, shards) * (ff // span) + n % (ff // span)
            small[l, pl.ds(SMALL_EXPAND + row, 1), :span] = d_bexp[i, 0:1, c : c + span]

        if l == 0:
            if blocked:
                turned[...] = second[0].T
            over_shards(0, functools.partial(expand_weights, l=0))
        begin(EXPAND, l)
        ticks(l, AT_EXPAND)

        def middle_back(at, l=l):
            dmid, dgain, doffset = norm_back(mid[l, at, :], gain[l, 1:2, :], gs[at, :])
            add_small(l, GAIN_2, dgain)
            add_small(l, OFFSET_2, doffset)
            gm = g[at, :] + dmid
            g[at, :] = gm
            add_small(l, BIAS_OUT, jnp.sum(gm, axis=0, keepdims=True))
            low = gm.astype(BF16)
            gz[at, :] = low
            go[at, :] = dot_nt(low, w_out[l]).astype(BF16)

        over_blocks(middle_back, (l, AT_MIDDLE), unroll=LINE_UNROLL)
        d_mixed = dot_tn(mixed[l], gz[...]).astype(BF16)
        for part in range(PART):
            at = part * part_rows + width
            d_attn[l, at : at + width // PART, :] = d_mixed[part * (width // PART) : (part + 1) * (width // PART)]
        bias_sum[l] = jnp.zeros(bias_sum.shape[1:], F32)
        turned[...] = normed[l].T

        def attend_back(i, carry, grp, l=l):
            count = windows // 2
            at = pl.ds(pl.multiple_of(i * count * SLOTS, count * SLOTS), count * SLOTS)
            parts = [pl.ds(pl.multiple_of(grp * width + p * GLANES, GLANES), GLANES) for p in range(3)]
            lanes = pl.ds(pl.multiple_of(grp * GLANES, GLANES), GLANES)
            heres = [slice(w * SLOTS, (w + 1) * SLOTS) for w in range(count)]
            q, k, v = (qkv[l, at, part].astype(F32) for part in parts)
            go_now = go[at, lanes].astype(F32)
            go_all = [expand_heads(go_now[here]) for here in heres]
            dps = [dot_nt(v[here].astype(BF16), one) for one, here in zip(go_all, heres)]
            lows = [probs[l, count * i + w, grp] for w in range(count)]
            dvs = [dot(p, one) for p, one in zip(lows, go_all)]
            ps = [p.astype(F32) for p in lows]
            pds = [p * dp for p, dp in zip(ps, dps)]
            totals = [jnp.sum(pd, axis=0, keepdims=True) for pd in pds]
            dss = [(pd - p * total).astype(BF16) for pd, p, total in zip(pds, ps, totals)]
            dqs = [
                fold_heads(dot_tn(ds, k[here].astype(BF16))) * HEAD_DIM**-0.5 for ds, here in zip(dss, heres)
            ]
            dks = [dot(ds, expand_heads(q[here])) * HEAD_DIM**-0.5 for ds, here in zip(dss, heres)]
            total = bias_sum[l, grp]
            for ds in dss:
                total = total + ds.astype(F32)
            bias_sum[l, grp] = total
            for row, part, made in zip((BIAS_Q, None, BIAS_V), parts, (dqs, dks, dvs)):
                whole = jnp.concatenate(made, axis=0)
                if row is not None:
                    small[l, row : row + 1, lanes] += jnp.sum(whole, axis=0, keepdims=True)
                dqkv[at, part] = whole.astype(BF16)
            for key, names in STEPS.items():
                if fused and key[:2] == (l, AT_ATTEND):
                    pl.when((grp == key[2] // 2) & (i == key[2] % 2))(functools.partial(advance, *names))
            return carry

        def attend_group(grp, carry, l=l):
            lax.fori_loop(0, 2, functools.partial(attend_back, grp=grp), 0)
            at = pl.multiple_of(grp * part_rows, 16)
            cols = pl.ds(pl.multiple_of(grp * width, GLANES), width)
            d_attn[l, pl.ds(at, width), :] = dot(turned[...], dqkv[:, cols]).astype(BF16)
            for g_now in range(GROUPS):

                def after(g_now=g_now):
                    begin(ATTEND, l, g_now)
                    ticks(l, AT_GROUP, g_now)

                if fused:
                    pl.when(grp == g_now)(after)
            return carry

        lax.fori_loop(0, GROUPS, attend_group, 0)

        def input_back(at, l=l):
            ga = dot_nt(dqkv[at, :], w_in[l])
            dx, dgain, doffset = norm_back(x[l, at, :], gain[l, 0:1, :], ga)
            add_small(l, GAIN_1, dgain)
            add_small(l, OFFSET_1, doffset)
            gs[at, :] = g[at, :] + dx

        over_blocks(input_back, (l, AT_INPUT), unroll=LINE_UNROLL)
        if l == 1:
            advance((small_flow(1), 0))
            ticks(l, AT_SUMS)
            shifted_to_regular(gs, g, side)
            ticks(l, AT_PLACED)
        else:
            ticks(l, AT_SUMS)
            for one in range(2):
                table_back(one)
                ticks(l, AT_TABLE, one)
            advance((small_flow(0), 0))
            windows_to_grid(gs, grad_tokens, side, False)
            ticks(l, AT_PLACED)

    def last(at):
        total = mid[1, at, :] + b_red[1:2, :] + dot(hidden[1, 0, at, :], w_red[0, 1])

        def add(i, total):
            return total + dot(hidden[1, i, at, :], w_red[i, 1])

        g[at, :] = lax.fori_loop(1, shards, add, total)

    over_blocks(last)
    windows_to_grid(g, out, side, True)
    ticks(0, AT_OUT)

    advance(*TAIL)
    for k in range(1, 1 + max((flow.steps for flow in flows), default=0)):
        advance(*((n, k) for n, flow in enumerate(flows) if COUNT[n] <= k <= flow.steps))


def lanes_table(lanes):
    layers, heads = lanes.shape[0], lanes.shape[1] // 2
    both = lanes.reshape(layers, 2, heads, 128)
    span = SPAN_SIDE * PITCH

    def square(part, back):
        return jnp.roll(part, back, axis=-1)[..., :span].reshape(layers, heads, SPAN_SIDE, PITCH)

    right = square(both[:, 0], (WIN - 1) * PITCH)[..., :WIN]
    left = square(both[:, 1], WIN * PITCH)[..., PITCH - WIN + 1 :]
    whole = jnp.concatenate([left, right], axis=-1)
    return whole.reshape(layers, heads, SPAN_SIDE * SPAN_SIDE).transpose(0, 2, 1)


def on_device(
    mesh_shape,
    tokens,
    crop_ids,
    norm_gain,
    norm_bias,
    input_proj,
    input_bias,
    position_table,
    output_proj,
    output_bias,
    expand_weight,
    expand_bias,
    reduce_weight,
    reduce_bias,
    cotangent,
):
    _, side, _, width = tokens.shape
    layers, _, ff = expand_weight.shape
    win, shards = mesh_shape
    ids = crop_ids.transpose(1, 0, 2)
    windows = (side // WIN) ** 2
    rows = windows * SLOTS
    attn_rows, feed_rows = 4 * width, 2 * ff
    fused = win % 4 == 0 and attn_rows % (16 * PART * win * shards) == 0 and ff % (16 * win) == 0
    vmem = pl.BlockSpec(memory_space=pltpu.VMEM)
    hbm = pl.BlockSpec(memory_space=pl.ANY)
    if fused:
        w_exp, w_red = expand_weight, reduce_weight
        b_exp = expand_bias
    else:
        w_exp = lax.all_gather(expand_weight, "mlp", axis=0)
        w_red = lax.all_gather(reduce_weight, "mlp", axis=0)
        b_exp = lax.all_gather(expand_bias, "mlp", axis=0).astype(F32)
    scratch = [
        pltpu.VMEM((layers, rows, width), F32),
        pltpu.VMEM((layers, rows, width), BF16),
        pltpu.VMEM((layers, rows, 3 * width), BF16),
        pltpu.VMEM((layers, windows, GROUPS, SLOTS, GQ), BF16),
        pltpu.VMEM((layers, rows, width), BF16),
        pltpu.VMEM((layers, rows, width), F32),
        pltpu.VMEM((layers, rows, width), BF16),
        pltpu.VMEM((layers, shards, rows, ff), BF16),
        pltpu.VMEM((layers, shards, rows, ff), BF16),
        pltpu.VMEM((layers, rows, 128), F32),
        pltpu.VMEM((layers, GROUPS, SLOTS, GQ), F32),
        pltpu.VMEM((layers, GROUPS, SLOTS, GQ), F32),
        pltpu.VMEM((rows, width), F32),
        pltpu.VMEM((rows, width), F32),
        pltpu.VMEM((rows, width), BF16),
        pltpu.VMEM((shards, rows, ff), BF16),
        pltpu.VMEM((rows, 3 * width), BF16),
        pltpu.VMEM((rows, width), BF16),
        pltpu.VMEM((shards, 8, ff), F32),
    ]
    small_shape = (layers, SMALL_ROWS, width)
    scratch += [
        pltpu.VMEM((2, 128, 128), F32),
        pltpu.VMEM((2, 16, 128), F32),
        pltpu.VMEM(input_proj.shape, BF16),
        pltpu.VMEM((width, rows), BF16),
        pltpu.VMEM((width, rows), BF16),
        pltpu.VMEM((128, 256), F32),
        pltpu.VMEM((256, 128), F32),
        pltpu.VMEM((side, 32, 128), F32),
        pltpu.SemaphoreType.DMA((layers * GROUPS * 3,)),
    ]
    if fused:
        plane, depth = 2 * shards, win // 4
        _, shapes = flow_table(mesh_shape, width, ff)
        scratch += [
            pltpu.VMEM((layers, attn_rows, width), BF16),
            pltpu.VMEM((layers, shards, feed_rows, width), BF16),
            pltpu.VMEM(small_shape, F32),
            pltpu.VMEM((shards, layers, width, ff), BF16),
            pltpu.VMEM((shards, 8, ff), F32),
            pltpu.VMEM((shards, layers, ff, width), BF16),
        ]
        scratch += [
            pltpu.VMEM((members, count, width), BF16)
            for count in (SMALL_ROWS, SMALL_EARLY)
            for members in (2, plane, depth)
        ]
        scratch += [pltpu.VMEM(shape, BF16) for group in shapes for shape in group]
        scratch += [
            pltpu.SemaphoreType.DMA((3 + len(shapes),)),
            pltpu.SemaphoreType.DMA((SEMAPHORES,)),
            pltpu.SemaphoreType.DMA((SEMAPHORES,)),
        ]
    outs = pl.pallas_call(
        functools.partial(kernel, side, mesh_shape if fused else None),
        out_shape=(
            jax.ShapeDtypeStruct(tokens.shape[1:], BF16),
            jax.ShapeDtypeStruct(tokens.shape[1:], BF16),
            jax.ShapeDtypeStruct((layers, attn_rows, width), BF16),
            jax.ShapeDtypeStruct((layers, feed_rows, width) if fused else (layers, shards, feed_rows, width), BF16),
            jax.ShapeDtypeStruct(small_shape, F32),
        ),
        in_specs=[vmem] * 4 + [hbm] + [vmem] * 4 + ([hbm, vmem, hbm] if fused else [vmem] * 3) + [vmem] * 2,
        out_specs=[vmem] * 2 + ([hbm] * 2 if fused else [vmem] * 2) + [vmem],
        scratch_shapes=scratch,
        compiler_params=pltpu.CompilerParams(
            vmem_limit_bytes=64 * 1024 * 1024,
            **(dict(collective_id=0, has_side_effects=True) if fused else {}),
        ),
    )(
        tokens[0],
        ids,
        norm_gain,
        norm_bias,
        input_proj,
        input_bias,
        position_table.transpose(2, 0, 1),
        output_proj,
        output_bias,
        w_exp,
        b_exp,
        w_red,
        reduce_bias,
        cotangent[0],
    )
    out, grad_tokens, d_attn, d_feed, small = outs
    if not fused:
        d_attn, small = lax.psum((d_attn, small), ("win", "mlp"))
        d_feed = lax.psum(lax.psum_scatter(d_feed, "mlp", scatter_dimension=1, tiled=False), "win")
    if fused and ff % width == 0 and width % 128 == 0 and side % 2 == 0:
        return finish(out, grad_tokens, d_attn, d_feed, small, side, ff)
    parts = d_attn.reshape(layers, PART, attn_rows // PART, width)
    d_in = jnp.concatenate(
        [parts[:, grp, :width, p * GLANES : (p + 1) * GLANES] for p in range(3) for grp in range(GROUPS)], axis=2
    )
    d_out = parts[:, :, width:].reshape(layers, width, width)
    if ff % width == 0:
        d_exp, d_red = (
            jnp.concatenate([d_feed[:, c : c + width] for c in range(first, first + ff, width)], axis=2)
            for first in (0, ff)
        )
        d_red = d_red.swapaxes(1, 2)
    else:
        d_exp, d_red = d_feed[:, :ff].swapaxes(1, 2), d_feed[:, ff:]
    span = min(width, ff)
    d_bexp = small[:, SMALL_EXPAND : SMALL_EXPAND + shards * (ff // span), :span].reshape(layers, shards, ff)
    d_bexp = lax.dynamic_index_in_dim(d_bexp, lax.axis_index("mlp"), 1, keepdims=False)
    d_table = jnp.stack([small[0, SMALL_TABLE[l] : SMALL_TABLE[l] + 8] for l in range(layers)])
    return (
        out[None],
        grad_tokens[None],
        small[:, 0:2],
        small[:, 2:4],
        d_in.astype(F32),
        small[:, 4:6],
        lanes_table(d_table.reshape(layers, 2 * HEADS, 128)),
        d_out.astype(F32),
        small[:, 6],
        d_exp.astype(F32),
        d_bexp,
        d_red.astype(F32),
        small[:, 7],
    )


def finish_kernel(blocks, *refs):
    attn, feed, out, grad_tokens, small = refs[:5]
    (out_to, grad_to, gain, offset, d_in, b_in, table, d_out, b_out, d_exp, b_exp, d_red, b_red) = refs[5:18]
    tall, a_held, f_held, in_held, out_held, exp_held, red_held, grid_held, in_sems, out_sems = refs[18:]
    layers, _, width = attn.shape
    part = width + width // PART
    ff = blocks * width
    passing = [
        pltpu.make_async_copy(out, grid_held.at[0], in_sems.at[2 * layers]),
        pltpu.make_async_copy(grad_tokens, grid_held.at[1], in_sems.at[2 * layers + 1]),
    ]
    arriving = [
        [
            pltpu.make_async_copy(attn.at[l], a_held.at[l], in_sems.at[2 * l]),
            pltpu.make_async_copy(feed.at[l], f_held.at[l], in_sems.at[2 * l + 1]),
        ]
        for l in range(layers)
    ]
    for pair in arriving:
        for copy in pair:
            copy.start()
    for copy in passing:
        copy.start()
    leaving = []

    def leave(src, dst):
        copy = pltpu.make_async_copy(src, dst, out_sems.at[len(leaving)])
        copy.start()
        leaving.append(copy)

    for l in range(layers):
        arriving[l][0].wait()
        for grp in range(GROUPS):
            first = grp * part
            for p in range(3):
                at = p * width + grp * GLANES
                in_held[l, :, at : at + GLANES] = a_held[l, first : first + width, p * GLANES : (p + 1) * GLANES].astype(F32)
            rows = width // PART
            out_held[l, grp * rows : (grp + 1) * rows, :] = a_held[l, first + width : first + part, :].astype(F32)
        leave(in_held.at[l], d_in.at[l])
        passing[l].wait()
        leave(grid_held.at[l], (out_to, grad_to)[l].at[0])
        leave(out_held.at[l], d_out.at[l])
        arriving[l][1].wait()
        for b in range(blocks):
            cols = slice(b * width, (b + 1) * width)
            exp_held[l, :, cols] = f_held[l, cols, :].astype(F32)
        leave(exp_held.at[l], d_exp.at[l])
        for b in range(blocks):
            cols = slice(b * width, (b + 1) * width)
            red_held[l, cols, :] = f_held[l, ff + b * width : ff + (b + 1) * width, :].astype(F32).T
        leave(red_held.at[l], d_red.at[l])

    for l in range(2):
        gain[l] = small[l, 0:2, :]
        offset[l] = small[l, 2:4, :]
        b_in[l] = small[l, 4:6, :]
        b_out[l : l + 1, :] = small[l, 6:7, :]
        b_red[l : l + 1, :] = small[l, 7:8, :]
        for b in range(blocks):
            row = SMALL_EXPAND + lax.axis_index("mlp") * blocks + b
            b_exp[l : l + 1, b * width : (b + 1) * width] = small[l, pl.ds(row, 1), :]
        turned = []
        for s in range(2):
            heads = []
            for h in range(HEADS):
                n = s * HEADS + h
                row = SMALL_TABLE[l] + n // 3
                heads.append(small[0, row : row + 1, n % 3 * 128 : (n % 3 + 1) * 128])
            heads.append(jnp.zeros((128 - HEADS, 128), F32))
            turned.append(jnp.concatenate(heads, axis=0).T)
        tall[...] = jnp.zeros(tall.shape, F32)
        for lane, entry, count, s in table_spans():
            tall[entry : entry + count, :] = turned[s][lane : lane + count]
        wide = tall[...].T
        for h in range(HEADS):
            table[h, l : l + 1, :] = wide[h : h + 1, : table.shape[2]]
    for copy in leaving:
        copy.wait()


def finish(out, grad_tokens, d_attn, d_feed, small, side, ff):
    layers, _, width = d_attn.shape
    blocks = ff // width
    vmem = pl.BlockSpec(memory_space=pltpu.VMEM)
    hbm = pl.BlockSpec(memory_space=pl.ANY)
    span = SPAN_SIDE * SPAN_SIDE
    shape = lambda *dims: jax.ShapeDtypeStruct(dims, F32)
    grid_shape = jax.ShapeDtypeStruct((1, side, side, width), BF16)
    large = ((layers, width, 3 * width), (layers, width, width), (layers, width, ff), (layers, ff, width))
    made = pl.pallas_call(
        functools.partial(finish_kernel, blocks),
        in_specs=[hbm] * 4 + [vmem],
        out_specs=[hbm, hbm, vmem, vmem, hbm, vmem, vmem, hbm, vmem, hbm, vmem, hbm, vmem],
        out_shape=[
            grid_shape,
            grid_shape,
            shape(layers, 2, width),
            shape(layers, 2, width),
            shape(*large[0]),
            shape(layers, 2, width),
            shape(HEADS, layers, span),
            shape(*large[1]),
            shape(layers, width),
            shape(*large[2]),
            shape(layers, ff),
            shape(*large[3]),
            shape(layers, width),
        ],
        scratch_shapes=[
            pltpu.VMEM((256, 128), F32),
            pltpu.VMEM(d_attn.shape, BF16),
            pltpu.VMEM(d_feed.shape, BF16),
            *(pltpu.VMEM(dims, F32) for dims in large),
            pltpu.VMEM((2,) + out.shape, BF16),
            pltpu.SemaphoreType.DMA((2 + 2 * layers,)),
            pltpu.SemaphoreType.DMA((2 + 4 * layers,)),
        ],
        compiler_params=pltpu.CompilerParams(vmem_limit_bytes=64 * 1024 * 1024),
    )(d_attn, d_feed, out, grad_tokens, small)
    return (*made[:6], made[6].transpose(1, 2, 0), *made[7:])


def solution(mesh):
    tokens = P(("win", "mlp"), None, None, None)
    placed = (
        tokens,
        P(("win", "mlp"), None, None),
        P(),
        P(),
        P(),
        P(),
        P(),
        P(),
        P(),
        P(None, None, "mlp"),
        P(None, "mlp"),
        P(None, "mlp", None),
        P(),
        tokens,
    )
    return jax.shard_map(
        functools.partial(on_device, (mesh.shape["win"], mesh.shape["mlp"])),
        mesh=mesh,
        in_specs=placed,
        out_specs=(
            tokens,
            tokens,
            P(),
            P(),
            P(),
            P(),
            P(),
            P(),
            P(),
            P(None, None, "mlp"),
            P(None, "mlp"),
            P(None, "mlp", None),
            P(),
        ),
        check_vma=False,
    )
```

```python
import functools

import jax
import jax.numpy as jnp
from jax import lax
from jax.experimental import pallas as pl
from jax.experimental.pallas import tpu as pltpu
from jax.sharding import PartitionSpec as P

HEADS = 12
HEAD_DIM = 32
WIN = 7
SHIFT = 3
SPAN_SIDE = 2 * WIN - 1

EPS = 1e-05
MASKED = -1e30

PITCH = 8
SLOTS = WIN * PITCH
GROUP = 4
GROUPS = HEADS // GROUP
GLANES = GROUP * HEAD_DIM
GQ = GROUP * SLOTS

F32 = jnp.float32
BF16 = jnp.bfloat16

ERF_P = 0.4
ERF_C = (
    0.22567691835428957,
    0.22565742813591003,
    0.2069437219941218,
    0.18213740047970625,
    0.06806251607656177,
    0.1868261013466735,
    -0.09530889147438172,
)


LOG2E = 1.4426950408889634
BELL = 0.3989422804014327


def dot(a, b):
    return lax.dot_general(a, b, (((1,), (0,)), ((), ())), preferred_element_type=F32)


def dot_nt(a, b):
    return lax.dot_general(a, b, (((1,), (1,)), ((), ())), preferred_element_type=F32)


def dot_tn(a, b):
    return lax.dot_general(a, b, (((0,), (0,)), ((), ())), preferred_element_type=F32)


def gelu_pair(u):
    bell = jnp.exp2(u * u * (-0.5 * LOG2E))
    size = jnp.abs(u)
    t = 1.0 / (1.0 + (ERF_P * 0.5**0.5) * size)
    poly = 0.5 * ERF_C[-1] * t + 0.5 * ERF_C[-2]
    for coef in ERF_C[-3::-1]:
        poly = poly * t + 0.5 * coef
    tail = bell * (t * poly)
    phi = jnp.where(u < 0, tail, 1.0 - tail)
    return jnp.maximum(u, 0.0) - size * tail, phi + u * (bell * BELL)


def norm_stats(v):
    centred = v - jnp.mean(v, axis=-1, keepdims=True)
    rstd = lax.rsqrt(jnp.mean(centred * centred, axis=-1, keepdims=True) + EPS)
    return centred * rstd, rstd


def norm_back(v, gain, upstream):
    xhat, rstd = norm_stats(v)
    scaled = upstream * gain
    inner = (
        scaled
        - jnp.mean(scaled, axis=-1, keepdims=True)
        - xhat * jnp.mean(scaled * xhat, axis=-1, keepdims=True)
    )
    return rstd * inner, jnp.sum(upstream * xhat, axis=0, keepdims=True), jnp.sum(upstream, axis=0, keepdims=True)


def iota(shape, dim):
    return lax.broadcasted_iota(jnp.int32, shape, dim)


def expand_heads(rows):
    head = iota(rows.shape, 1) // HEAD_DIM
    return jnp.concatenate([jnp.where(head == j, rows, 0.0) for j in range(GROUP)], axis=0).astype(BF16)


def fold_heads(rows):
    head = iota((SLOTS, GLANES), 1) // HEAD_DIM
    out = rows[:SLOTS]
    for j in range(1, GROUP):
        out = jnp.where(head == j, rows[j * SLOTS : (j + 1) * SLOTS], out)
    return out


def by_window(parts):
    return jnp.concatenate(
        [jnp.concatenate(parts[w * GROUPS : (w + 1) * GROUPS], axis=1) for w in range(BLOCK_WINDOWS)], axis=0
    )


def window_row(per_side, wr, wc, r):
    return pl.multiple_of((wr * per_side + wc) * SLOTS + r * PITCH, PITCH)


def grid_to_windows(src, side, shifted, emit):
    per_side = side // WIN

    def step(wr, carry):
        for r in range(WIN):
            row = lax.rem(wr * WIN + r + (SHIFT if shifted else 0), side)
            line = src[row].astype(F32)
            width = line.shape[1]
            if line.shape[0] < 32:
                line = jnp.concatenate([line, jnp.zeros((32 - line.shape[0], width), F32)], axis=0)
            if shifted:
                i = iota(line.shape, 0)
                line = jnp.where(i < side - SHIFT, pltpu.roll(line, 32 - SHIFT, 0), pltpu.roll(line, side - SHIFT, 0))
            for wc in range(per_side):
                part = line if wc == 0 else pltpu.roll(line, 32 - WIN * wc, 0)
                part = part[:PITCH]
                part = jnp.where(iota(part.shape, 0) < WIN, part, 0.0)
                emit(wr, wc, r, part)
        return carry

    lax.fori_loop(0, per_side, step, 0)


def windows_to_grid(src, dst, side, shifted):
    per_side = side // WIN

    def step(wr, carry):
        for r in range(WIN):
            row = lax.rem(wr * WIN + r + (SHIFT if shifted else 0), side)
            width = src.shape[1]
            line = jnp.zeros((32, width), F32)
            i = iota(line.shape, 0)
            for wc in range(per_side):
                tile = src[pl.ds(window_row(per_side, wr, wc, r), PITCH), :]
                tile = jnp.concatenate([tile, jnp.zeros((32 - PITCH, width), F32)], axis=0)
                if wc:
                    tile = pltpu.roll(tile, WIN * wc, 0)
                line = jnp.where((i >= WIN * wc) & (i < WIN * (wc + 1)), tile, line)
            if shifted:
                line = jnp.where(i < SHIFT, pltpu.roll(line, 32 - side + SHIFT, 0), pltpu.roll(line, SHIFT, 0))
            dst[row] = line[:side].astype(dst.dtype)
        return carry

    lax.fori_loop(0, per_side, step, 0)


def regular_to_shifted(src, dst, side):
    per_side = side // WIN

    def step(wr, carry):
        below = lax.rem(wr + 1, per_side)
        for r in range(WIN):
            sr, srr = (wr, r + SHIFT) if r + SHIFT < WIN else (below, r + SHIFT - WIN)
            for wc in range(per_side):
                here = src[pl.ds(window_row(per_side, sr, wc, srr), PITCH), :]
                right = src[pl.ds(window_row(per_side, sr, (wc + 1) % per_side, srr), PITCH), :]
                i = iota(here.shape, 0)
                tile = jnp.where(
                    i < WIN - SHIFT,
                    pltpu.roll(here, PITCH - SHIFT, 0),
                    jnp.where(i < WIN, pltpu.roll(right, WIN - SHIFT, 0), 0.0),
                )
                dst[pl.ds(window_row(per_side, wr, wc, r), PITCH), :] = tile
        return carry

    lax.fori_loop(0, per_side, step, 0)


def shifted_to_regular(src, dst, side):
    per_side = side // WIN

    def step(wr, carry):
        above = lax.rem(wr + per_side - 1, per_side)
        for r in range(WIN):
            sr, srr = (wr, r - SHIFT) if r >= SHIFT else (above, r - SHIFT + WIN)
            for wc in range(per_side):
                here = src[pl.ds(window_row(per_side, sr, wc, srr), PITCH), :]
                left = src[pl.ds(window_row(per_side, sr, (wc + per_side - 1) % per_side, srr), PITCH), :]
                i = iota(here.shape, 0)
                tile = jnp.where(
                    i < SHIFT,
                    pltpu.roll(left, PITCH - (WIN - SHIFT), 0),
                    jnp.where(i < WIN, pltpu.roll(here, SHIFT, 0), 0.0),
                )
                dst[pl.ds(window_row(per_side, wr, wc, r), PITCH), :] = tile
        return carry

    lax.fori_loop(0, per_side, step, 0)


BLOCK_WINDOWS = 4
LINE_UNROLL, ATTEND_UNROLL, UP_UNROLL, BACK_UNROLL = 4, 2, 1, 4
ROWS_BLOCK = BLOCK_WINDOWS * SLOTS
JOBS = [
    (w, grp, slice(w * SLOTS, (w + 1) * SLOTS)) for w in range(BLOCK_WINDOWS) for grp in range(GROUPS)
]
GAIN_1, GAIN_2, OFFSET_1, OFFSET_2, BIAS_Q, BIAS_V, BIAS_OUT, BIAS_REDUCE = range(8)
SMALL_EXPAND = 8
SMALL_EARLY = 16
SMALL_TABLE = {0: 16, 1: 24}
SMALL_ROWS = 32
ADD_ROWS = 96
SEMAPHORES = 320
PART = 3


def table_spans():
    spans = []
    for dr in range(SPAN_SIDE):
        at = PITCH * (dr - WIN + 1)
        spans.append((at % 128, dr * SPAN_SIDE + WIN - 1, WIN, 0))
        spans.append(((at - PITCH) % 128 + PITCH - WIN + 1, dr * SPAN_SIDE, WIN - 1, 1))
    return spans


CORE, X, Y, Z, MLP, PLANE = range(6)


class Links:
    def __init__(self, mesh_shape, send_sem, recv_sem):
        self.win, self.mlp = mesh_shape
        self.send_sem, self.recv_sem = send_sem, recv_sem
        w, m = lax.axis_index("win"), lax.axis_index("mlp")
        self.core, self.x, self.z, self.m = lax.rem(w, 2), lax.rem(lax.div(w, 2), 2), lax.div(w, 4), m
        self.depth = self.win // 4
        self.groups = {
            CORE: (2, self.core, lambda q: self.at(core=q)),
            X: (2, self.x, lambda q: self.at(x=q)),
            Z: (self.depth, self.z, lambda q: self.at(z=q)),
            MLP: (self.mlp, m, lambda q: self.at(m=q)),
            Y: (self.mlp, m, lambda q: self.at(m=q)),
            PLANE: (
                2 * self.mlp,
                self.x * self.mlp + m,
                lambda q: self.at(x=lax.div(q, self.mlp), m=lax.rem(q, self.mlp)),
            ),
        }
        self.used = 0

    def at(self, core=None, x=None, z=None, m=None):
        core = self.core if core is None else core
        x = self.x if x is None else x
        z = self.z if z is None else z
        m = self.m if m is None else m
        return ((z * 2 + x) * 2 + core, m)

    def peers(self, group):
        size, me, _ = self.groups[group]
        return [(d, lax.rem(me + d, size)) for d in range(1, size)]

    def me(self, group):
        return self.groups[group][1]

    def size(self, group):
        return self.groups[group][0]

    def greet(self):
        sem = pltpu.get_barrier_semaphore()
        for group in (CORE, PLANE, Z):
            for _, q in self.peers(group):
                pl.semaphore_signal(
                    sem, inc=1, device_id=self.groups[group][2](q), device_id_type=pl.DeviceIdType.MESH
                )

    def meet(self):
        pl.semaphore_wait(pltpu.get_barrier_semaphore(), sum(self.size(g) - 1 for g in (CORE, PLANE, Z)))

    def reserve(self, count):
        first = self.used
        self.used += count
        assert self.used <= SEMAPHORES
        return first

    def copy(self, group, q, src, dst, n):
        return pltpu.make_async_remote_copy(
            src_ref=src,
            dst_ref=dst,
            send_sem=self.send_sem.at[n],
            recv_sem=self.recv_sem.at[n],
            device_id=self.groups[group][2](q),
            device_id_type=pl.DeviceIdType.MESH,
        )


def add_rows(dst, sources, count):
    step = next(n for n in (ADD_ROWS, 64, 48, 32, 16) if count % n == 0)

    def one(i, carry):
        at = pl.ds(pl.multiple_of(i * step, 16), step)
        total = dst[at, :].astype(F32)
        for source in sources:
            total = total + source[at, :].astype(F32)
        dst[at, :] = total.astype(dst.dtype)
        return carry

    lax.fori_loop(0, count // step, one, 0)


REDUCE, EXPAND, ATTEND = range(3)
FLOWS = (
    (REDUCE, 1, 0, 0, 3, 0, (CORE, PLANE, Z)),
    (REDUCE, 1, 0, 0, 3, 1, (CORE, PLANE, Z)),
    (REDUCE, 1, 0, 0, 3, 2, (CORE, PLANE, Z)),
    (EXPAND, 1, 0, 0, 3, 0, (CORE, PLANE, Z)),
    (EXPAND, 1, 0, 0, 3, 1, (CORE, PLANE, Z)),
    (EXPAND, 1, 0, 0, 3, 2, (CORE, PLANE, Z)),
    (ATTEND, 1, 0, 1, 1, 0, (CORE, X, Y, Z)),
    (ATTEND, 1, 1, 1, 1, 0, (CORE, Y, Z, X)),
    (ATTEND, 1, 2, 1, 1, 0, (CORE, Y, X, Z)),
    (REDUCE, 0, 0, 0, 3, 0, (CORE, PLANE, Z)),
    (REDUCE, 0, 0, 0, 3, 1, (CORE, PLANE, Z)),
    (REDUCE, 0, 0, 0, 3, 2, (CORE, PLANE, Z)),
    (EXPAND, 0, 0, 0, 3, 0, (CORE, MLP, X, Z)),
    (EXPAND, 0, 0, 0, 3, 1, (CORE, MLP, X, Z)),
    (EXPAND, 0, 0, 0, 3, 2, (CORE, MLP, X, Z)),
    (ATTEND, 0, 0, 1, 1, 0, (CORE, PLANE, Z)),
    (ATTEND, 0, 1, 1, 1, 0, (CORE, PLANE, Z)),
    (ATTEND, 0, 2, 1, 3, 0, (CORE, PLANE, Z)),
    (ATTEND, 0, 2, 1, 3, 1, (CORE, PLANE, Z)),
    (ATTEND, 0, 2, 1, 3, 2, (CORE, PLANE, Z)),
)


def flow_table(mesh_shape, width, ff):
    part = 4 * width // PART
    win, mlp = mesh_shape
    sizes = {CORE: 2, X: 2, Y: mlp, Z: win // 4, MLP: mlp, PLANE: 2 * mlp}
    flows, shapes = [], []
    for kind, l, first, count, splits, split, stages in FLOWS:
        if kind == ATTEND:
            first, rows = first * part, count * part
        else:
            first, rows = (ff if kind == REDUCE else 0), ff
        lanes = (split * (width // splits), width // splits)
        slots = 1 if kind == ATTEND else mlp
        flows.append((l, kind != ATTEND, (first, rows), lanes, stages))
        landing = []
        for stage in stages:
            if stage == MLP:
                slots = 1
            elif stage == PLANE and slots > 1:
                slots, rows = 1, rows // 2
            else:
                rows //= sizes[stage]
            landing.append((sizes[stage] - 1, slots, rows, lanes[1]))
        shapes.append(landing)
    return flows, shapes


def small_flow(l):
    return len(FLOWS) + 1 - l


class Flow:
    def __init__(self, links, staged, out, slots, span, lanes, stages, buffers, local_sem):
        self.links, self.staged, self.out, self.local_sem = links, staged, out, local_sem
        self.stages, self.buffers, self.lanes = stages, buffers, pl.ds(*lanes)
        self.spans, self.slots, self.down = [span], [slots], []
        for n, stage in enumerate(stages):
            first, rows = self.spans[-1]
            if stage == MLP:
                slots = 1
            elif stage == PLANE and slots > 1:
                slots, rows = 1, rows // 2
                first = first + links.x * rows
                self.down.insert(0, (n, X))
            else:
                rows = rows // links.size(stage)
                first = first + links.me(stage) * rows
                self.down.insert(0, (n, stage))
            self.spans.append((first, rows))
            self.slots.append(slots)
        self.steps = len(stages) + len(self.down)
        self.sems = [links.reserve(links.size(group) - 1) for group in stages + tuple(group for _, group in self.down)]

    def copies(self, k):
        links = self.links
        made = []
        if k < len(self.stages):
            stage, slots = self.stages[k], self.slots[k]
            (first, _), (_, rows) = self.spans[k], self.spans[k + 1]
            for d, q in links.peers(stage):
                if stage == MLP:
                    slot, at = pl.ds(d, 1), first
                elif stage == PLANE and slots > 1:
                    slot, at = pl.ds(d % links.mlp, 1), first + lax.div(q, links.mlp) * rows
                else:
                    slot, at = pl.ds(0, slots), first + q * rows
                src = self.staged.at[slot, pl.ds(pl.multiple_of(at, 16), rows), self.lanes]
                made.append(links.copy(stage, q, src, self.buffers[k].at[d - 1], self.sems[k] + d - 1))
            return made
        n, group = self.down[k - len(self.stages)]
        src = self.mine(n + 1, self.staged.at[0] if k == len(self.stages) else self.out)
        for d, q in links.peers(group):
            made.append(links.copy(group, q, src, self.mine(n + 1, self.out), self.sems[k] + d - 1))
        return made

    def mine(self, n, ref):
        first, rows = self.spans[n]
        return ref.at[pl.ds(pl.multiple_of(first, 16), rows), self.lanes]

    def local(self):
        return pltpu.make_async_copy(
            self.mine(len(self.stages), self.staged.at[0]), self.mine(len(self.stages), self.out), self.local_sem
        )

    def advance(self, k):
        if k:
            for copy in self.copies(k - 1):
                copy.wait()
            if k - 1 < len(self.stages):
                for slot in range(self.slots[k]):
                    add_rows(
                        self.mine(k, self.staged.at[slot]),
                        [self.buffers[k - 1].at[d - 1, slot] for d, _ in self.links.peers(self.stages[k - 1])],
                        self.spans[k][1],
                    )
            elif k - 1 == len(self.stages):
                self.local().wait()
        if k < self.steps:
            if k == len(self.stages):
                self.local().start()
            for copy in self.copies(k):
                copy.start()


class SmallFlow:
    def __init__(self, links, value, buffers, out):
        self.links, self.value, self.buffers, self.out = links, value, buffers, out
        self.stages = (CORE, PLANE, Z)
        self.sems = [links.reserve(links.size(stage) - 1) for stage in self.stages]
        self.steps = len(self.stages)

    def copies(self, k):
        stage, buffer = self.stages[k], self.buffers[k]
        me = self.links.me(stage)
        return [
            self.links.copy(stage, q, buffer.at[me], buffer.at[me], self.sems[k] + d - 1)
            for d, q in self.links.peers(stage)
        ]

    def advance(self, k):
        total = self.value[...] if k == 0 else None
        if k:
            for copy in self.copies(k - 1):
                copy.wait()
            buffer = self.buffers[k - 1]
            total = buffer[0].astype(F32)
            for j in range(1, buffer.shape[0]):
                total = total + buffer[j].astype(F32)
        if k < len(self.stages):
            self.buffers[k][self.links.me(self.stages[k])] = total.astype(BF16)
            for copy in self.copies(k):
                copy.start()
        else:
            self.out[...] = total


(AT_REDUCE, AT_FEED, AT_EXPAND, AT_MIDDLE, AT_ATTEND, AT_GROUP, AT_INPUT, AT_SUMS, AT_TABLE, AT_PLACED, AT_OUT) = range(11)
PLAN = {
    (1, AT_MIDDLE, 2): (0,),
    (1, AT_MIDDLE, 3): (1, 2),
    (1, AT_ATTEND, 0): (5, 3, 4),
    (1, AT_ATTEND, 2): (0,),
    (1, AT_ATTEND, 3): (6,),
    (1, AT_GROUP, 1): (1,),
    (1, AT_ATTEND, 5): (7, 2),
    (1, AT_INPUT, 0): (0,),
    (1, AT_INPUT, 2): (5, 8),
    (1, AT_INPUT, 3): (1,),
    (0, AT_REDUCE, 0): (2, 20, 3, 4, 0),
    (0, AT_FEED, 0): (9, 5, 7, 11, 6, 1, 10),
    (0, AT_FEED, 1): (8, 0, 2, 20),
    (0, AT_EXPAND, 0): (0, 3, 4),
    (0, AT_MIDDLE, 0): (9, 5),
    (0, AT_MIDDLE, 1): (12,),
    (0, AT_MIDDLE, 2): (13, 14),
    (0, AT_MIDDLE, 3): (11, 7, 6, 1),
    (0, AT_ATTEND, 0): (20, 1),
    (0, AT_ATTEND, 1): (3, 8, 10, 4),
    (0, AT_ATTEND, 2): (12, 9, 5, 15, 7, 2, 11),
    (0, AT_ATTEND, 3): (5, 13, 2, 6, 3),
    (0, AT_ATTEND, 4): (8, 12, 3, 16, 14, 10, 4),
    (0, AT_ATTEND, 5): (9,),
    (0, AT_GROUP, 2): (15, 7, 11, 4),
    (0, AT_INPUT, 0): (17, 18, 19, 13, 6),
    (0, AT_INPUT, 2): (8,),
    (0, AT_TABLE, 0): (16, 12),
    (0, AT_TABLE, 1): (14, 10),
    (0, AT_PLACED, 0): (9, 15),
    (0, AT_OUT, 0): (17, 9, 18, 7, 11, 6, 19, 13, 21),
}
LAST = (8, 16, 11, 12, 10, 14, 15, 17, 7, 18, 6, 19, 10, 13, 7, 21, 12, 16, 6, 8, 12, 17, 18, 8, 19, 13, 15, 14, 13, 15, 16, 21, 17, 16, 17, 18, 19, 14, 18, 19, 14)


def number_steps():
    count = [1] * (len(FLOWS) + 2)

    def number(names):
        pairs = []
        for n in names:
            pairs.append((n, count[n]))
            count[n] += 1
        return tuple(pairs)

    return {key: number(names) for key, names in PLAN.items()}, number(LAST), count


STEPS, TAIL, COUNT = number_steps()


def kernel(side, mesh_shape, *refs):
    refs = list(refs)

    def take(n):
        got = refs[:n]
        del refs[:n]
        return got

    tokens, ids, gain, offset, global_in, b_in, table, w_out, b_out, w_exp, b_exp, w_red, b_red, cot = take(14)
    fused = mesh_shape is not None
    out, grad_tokens, d_attn, d_feed, small = take(5)
    (x, normed, qkv, probs, mixed, mid, second, hidden, slope) = take(9)
    (keys, bias, bias_sum, g, gs, gz, gb_low, dqkv, go, d_bexp, turn, spread, w_in, turned, gz_turned, wide, tall, hot_grid, in_sems) = take(19)
    flows = []
    if fused:
        out_attn, out_feed, out_small = d_attn, d_feed, small
        d_attn, d_feed, small = take(3)
        local_exp, local_bexp, local_red = w_exp, b_exp, w_red
        w_exp, b_exp, w_red = take(3)
        small_buffers = [take(3) for _ in range(2)]
        flow_rows, shapes = flow_table(mesh_shape, x.shape[2], local_exp.shape[2])
        landing = [take(len(shape)) for shape in shapes]
        local_sems, send_sem, recv_sem = take(3)
        links = Links(mesh_shape, send_sem, recv_sem)
        for n, (l, feed_flow, span, lanes, stages) in enumerate(flow_rows):
            flows.append(
                Flow(
                    links,
                    d_feed.at[l] if feed_flow else d_attn.at[pl.ds(l, 1)],
                    out_feed.at[l] if feed_flow else out_attn.at[l],
                    mesh_shape[1] if feed_flow else 1,
                    span,
                    lanes,
                    stages,
                    landing[n],
                    local_sems.at[3 + n],
                )
            )
        for l in (1, 0):
            part = pl.ds(0, SMALL_EARLY if l else SMALL_ROWS)
            flows.append(SmallFlow(links, small.at[l, part], small_buffers[l], out_small.at[l, part]))

    def advance(*pairs):
        if fused:
            for n, k in pairs:
                flows[n].advance(k)

    def begin(kind, l, part=0):
        advance(
            *((n, 0) for n, flow in enumerate(FLOWS) if flow[:2] == (kind, l) and (kind != ATTEND or flow[2] + flow[3] - 1 == part))
        )

    def ticks(l, point, i=0):
        advance(*STEPS.get((l, point, i), ()))

    def ticks_in_loop(l, point, i, n, unroll, j):
        for (at_l, at_point, at_i), names in STEPS.items():
            if fused and (at_l, at_point) == (l, point) and at_i % unroll == j:
                if isinstance(i, int):
                    if i == at_i:
                        advance(*names)
                else:
                    pl.when(n == at_i // unroll)(functools.partial(advance, *names))

    per_side = side // WIN
    windows = per_side * per_side
    rows = windows * SLOTS
    blocks = rows // ROWS_BLOCK
    shards, _, width, ff = w_exp.shape
    chunk = 256 if ff % 256 == 0 else ff
    blocked = ff % width == 0
    part_rows = 4 * width // PART

    gathers = [
        pltpu.make_async_copy(
            global_in.at[l, :, pl.ds(p * width + grp * GLANES, GLANES)],
            w_in.at[l, :, pl.ds(grp * width + p * GLANES, GLANES)],
            in_sems.at[(l * GROUPS + grp) * 3 + p],
        )
        for l in range(2)
        for grp in range(GROUPS)
        for p in range(3)
    ]
    for copy in gathers:
        copy.start()
    if fused:
        links.greet()
        own = [
            pltpu.make_async_copy(local_exp, w_exp.at[0], local_sems.at[0]),
            pltpu.make_async_copy(local_red, w_red.at[0], local_sems.at[1]),
        ]
        for copy in own:
            copy.start()
        b_exp[0, 0:2, :] = local_bexp[...].astype(F32)
        halves = (
            pl.ds(pl.multiple_of(links.core * (width // 2), 16), width // 2),
            pl.ds(pl.multiple_of(links.core * (ff // 2), 16), ff // 2),
        )
        weights = ((local_exp, w_exp, halves[0], width // 4), (local_red, w_red, halves[1], ff // 4))
        fetch_sems = links.reserve(4 * (shards - 1))
        relay_sems = links.reserve(2 * (shards - 1))
        pass_sems = links.reserve(4 * (shards - 1))
        bias_sems = links.reserve(shards - 1)

        def quarter(n):
            rows = weights[n][3]
            return pl.ds(pl.multiple_of((links.core * 2 + links.x) * rows, 16), rows)

        def fetches(l, n):
            source, dest, half, _ = weights[n]
            part = quarter(n) if l else half
            return [
                links.copy(MLP, q, source.at[l, part], dest.at[shards - d, l, part], fetch_sems + (2 * l + n) * (shards - 1) + d - 1)
                for d, q in links.peers(MLP)
            ]

        def relays(n):
            dest, part = weights[n][1], quarter(n)
            ((_, beside),) = links.peers(X)
            return [
                links.copy(X, beside, dest.at[d, 1, part], dest.at[d, 1, part], relay_sems + n * (shards - 1) + d - 1)
                for d, _ in links.peers(MLP)
            ]

        def passes(l, n):
            _, dest, half, _ = weights[n]
            ((_, sibling),) = links.peers(CORE)
            return [
                links.copy(CORE, sibling, dest.at[d, l, half], dest.at[d, l, half], pass_sems + (2 * l + n) * (shards - 1) + d - 1)
                for d, _ in links.peers(MLP)
            ]

        def bias_fetches():
            return [links.copy(MLP, q, b_exp.at[0], b_exp.at[shards - d], bias_sems + d - 1) for d, q in links.peers(MLP)]

        def fetch_all():
            for copy in bias_fetches():
                copy.start()
            for l in range(2):
                for n in range(2):
                    for copy in fetches(l, n):
                        copy.start()

        def relay(n):
            for copy in fetches(1, n):
                copy.wait()
            for copy in relays(n):
                copy.start()

        def pass_on(l, n):
            for copy in relays(n) if l else fetches(l, n):
                copy.wait()
            for copy in passes(l, n):
                copy.start()

        def passed(l, n):
            for copy in passes(l, n):
                copy.wait()

    def over_blocks(body, tick=None, after=None, unroll=1):
        def step(n, carry):
            for j in range(unroll):
                i = n * unroll + j
                body(pl.ds(i * ROWS_BLOCK if isinstance(i, int) else pl.multiple_of(i * ROWS_BLOCK, ROWS_BLOCK), ROWS_BLOCK))
                if tick:
                    ticks_in_loop(*tick, i, n, unroll, j)
                if after:
                    after(i)
            return carry

        if unroll == blocks:
            step(0, 0)
        else:
            lax.fori_loop(0, blocks // unroll, step, 0)

    wide[...] = jnp.zeros(wide.shape, F32)
    for row in range(side):
        wide[row : row + 1, :side] = ids[row].astype(F32)
    by_column = wide[:, :128].T[:32]
    for row in range(side):
        hot_grid[row] = jnp.broadcast_to(by_column[:, row : row + 1], (32, 128))
    wide[...] = jnp.zeros(wide.shape, F32)

    def put_tokens(wr, wc, r, tile):
        x[0, pl.ds(window_row(per_side, wr, wc, r), PITCH), :] = tile

    grid_to_windows(tokens, side, False, put_tokens)
    if fused:
        links.meet()
        fetch_all()

    def prepare(l):
        shifted = l == 1

        def put_keys(wr, wc, r, tile, shifted=shifted):
            lane = iota(tile.shape, 1).astype(F32)
            slot = iota(tile.shape, 0)
            label = tile
            if shifted:
                row_at = wr * WIN + r
                row_label = jnp.where(row_at >= side - WIN, 1, 0) + jnp.where(row_at >= side - SHIFT, 1, 0)
                col_at = wc * WIN + slot
                col_label = jnp.where(col_at >= side - WIN, 1, 0) + jnp.where(col_at >= side - SHIFT, 1, 0)
                label = label + (12 * row_label + 4 * col_label).astype(F32)
            hot = jnp.where((lane == label) & (slot < WIN), 1.0, 0.0)
            keys[l, pl.ds(window_row(per_side, wr, wc, r), PITCH), :] = hot

        grid_to_windows(hot_grid, side, shifted, put_keys)

        krow = iota((SLOTS, 128), 0)
        qlane = iota((SLOTS, 128), 1)
        ahead = (qlane & (PITCH - 1)) >= (krow & (PITCH - 1))
        turn[...] = jnp.zeros(turn.shape, F32)
        for h in range(HEADS):
            wide[h : h + 1, : table.shape[2]] = table[h, l : l + 1, :]
        tall[...] = wide[...].T
        for lane, entry, count, s in table_spans():
            turn[s, lane : lane + count, :] = tall[entry : entry + count, :]
        for s in range(2):
            spread[s] = turn[s].T[: spread.shape[1]]
        for grp in range(GROUPS):
            low = jnp.zeros((SLOTS, 128), F32)
            high = jnp.zeros((SLOTS, 128), F32)
            for j in range(GROUP):
                h = grp * GROUP + j
                both = [
                    pltpu.roll(
                        jnp.broadcast_to(spread[s, h : h + 1, :], (SLOTS, 128)),
                        0,
                        1,
                        stride=1,
                        stride_axis=0,
                    )
                    for s in range(2)
                ]
                one = jnp.where(ahead, both[0], both[1])
                at = j * SLOTS
                if at < 128:
                    moved = pltpu.roll(one, at, 1) if at else one
                    low = jnp.where((qlane >= at) & (qlane < at + SLOTS), moved, low)
                if at + SLOTS > 128:
                    moved = pltpu.roll(one, (at - 128) % 128, 1)
                    high = jnp.where((qlane >= at - 128) & (qlane < at - 128 + SLOTS), moved, high)
            bias[l, grp, :, :128] = low
            bias[l, grp, :, 128:] = high[:, : GQ - 128]

    def put_cot(wr, wc, r, tile):
        g[pl.ds(window_row(per_side, wr, wc, r), PITCH), :] = tile

    def add_small(l, at, value):
        small[l, at : at + 1, :] += value

    def lower(at, l):
        g_now = g[at, :]
        add_small(l, BIAS_REDUCE, jnp.sum(g_now, axis=0, keepdims=True))
        gz[at, :] = g_now.astype(BF16)

    def feed_up(at, i, l):
        s = second[l, at, :]
        jobs = [slice(c, c + chunk) for c in range(0, ff, chunk)]
        befores = [dot(s, w_exp[i, l, :, cols]) for cols in jobs]
        for before, cols in zip(befores, jobs):
            value, slope_now = gelu_pair(before + b_exp[i, l : l + 1, cols])
            hidden[l, i, at, cols] = value.astype(BF16)
            slope[l, i, at, cols] = slope_now.astype(BF16)

    def feed_down(at, i, l):
        gs[at, :] += dot(hidden[l, i, at, :], w_red[i, l])

    def feed_back(at, i, l):
        g_low = gz[at, :]
        jobs = [slice(c, c + chunk) for c in range(0, ff, chunk)]
        ghs = [dot_nt(g_low, w_red[i, l, cols, :]) for cols in jobs]
        for gh, cols in zip(ghs, jobs):
            gb = gh * slope[l, i, at, cols].astype(F32)
            d_bexp[i, 0:1, cols] += jnp.sum(gb, axis=0, keepdims=True)
            gb_low[i, at, cols] = gb.astype(BF16)
        gs[at, :] += dot_nt(gb_low[i, at, :], w_exp[i, l])

    def reduce_weights(i, l):
        if blocked:
            for c in range(0, ff, width):
                d_feed[l, i, ff + c : ff + c + width, :] = dot(gz_turned[...], hidden[l, i, :, c : c + width]).astype(BF16)
        else:
            d_feed[l, i, ff:, :] = dot_tn(hidden[l, i], gz[...]).astype(BF16)

    def expand_weights(i, l):
        if blocked:
            for c in range(0, ff, width):
                d_feed[l, i, c : c + width, :] = dot(turned[...], gb_low[i, :, c : c + width]).astype(BF16)
        else:
            d_feed[l, i, :ff, :] = dot_tn(gb_low[i], second[l]).astype(BF16)

    def over_shards(first, body):
        def step(i, carry):
            body(i)
            return carry

        lax.fori_loop(first, shards, step, 0)

    small[...] = jnp.zeros(small.shape, F32)
    prepare(0)

    for l in range(2):
        bias_row = jnp.concatenate(
            [
                one[:, grp * GLANES : (grp + 1) * GLANES]
                for grp in range(GROUPS)
                for one in (b_in[l, 0:1, :], jnp.zeros((1, width), F32), b_in[l, 1:2, :])
            ],
            axis=1,
        )
        if l == 0:
            for copy in gathers:
                copy.wait()

        def project(at, l=l, bias_row=bias_row):
            xhat, _ = norm_stats(x[l, at, :])
            a = (xhat * gain[l, 0:1, :] + offset[l, 0:1, :]).astype(BF16)
            normed[l, at, :] = a
            for c in range(3):
                cols = slice(c * width, (c + 1) * width)
                qkv[l, at, cols] = (dot(a, w_in[l, :, cols]) + bias_row[:, cols]).astype(BF16)

        over_blocks(project, unroll=LINE_UNROLL)

        def attend(i, l=l):
            at = pl.ds(pl.multiple_of(i * ROWS_BLOCK, ROWS_BLOCK), ROWS_BLOCK)
            q, k, v = (
                [
                    qkv[l, at, grp * width + p * GLANES : grp * width + (p + 1) * GLANES].astype(F32)
                    for grp in range(GROUPS)
                ]
                for p in range(3)
            )
            hot = keys[l, at, :]
            allowed = []
            for w in range(BLOCK_WINDOWS):
                hot_w = hot[w * SLOTS : (w + 1) * SLOTS]
                same = dot_nt(hot_w.astype(BF16), jnp.concatenate([hot_w] * GROUP, axis=0).astype(BF16))
                allowed.append(same > 0.5)
            scores = [
                dot_nt(k[grp][here].astype(BF16), expand_heads(q[grp][here])) for _, grp, here in JOBS
            ]
            scores = [
                jnp.where(allowed[w], s * HEAD_DIM**-0.5 + bias[l, grp], MASKED)
                for s, (w, grp, _) in zip(scores, JOBS)
            ]
            tops = [jnp.max(s, axis=0, keepdims=True) for s in scores]
            raised = [jnp.exp(s - top) for s, top in zip(scores, tops)]
            shares = [1.0 / jnp.sum(e, axis=0, keepdims=True) for e in raised]
            ps = [(e * share).astype(BF16) for e, share in zip(raised, shares)]
            for p, (w, grp, _) in zip(ps, JOBS):
                probs[l, BLOCK_WINDOWS * i + w, grp] = p
            outs = [
                fold_heads(dot_tn(p, v[grp][here].astype(BF16))) for p, (_, grp, here) in zip(ps, JOBS)
            ]
            mixed[l, at, :] = by_window(outs).astype(BF16)

        def attend_step(n, carry):
            for j in range(ATTEND_UNROLL):
                attend(n * ATTEND_UNROLL + j)
            return carry

        lax.fori_loop(0, blocks // ATTEND_UNROLL, attend_step, 0)

        def middle(at, l=l):
            m = x[l, at, :] + dot(mixed[l, at, :], w_out[l]) + b_out[l : l + 1, :]
            mid[l, at, :] = m
            xhat, _ = norm_stats(m)
            second[l, at, :] = (xhat * gain[l, 1:2, :] + offset[l, 1:2, :]).astype(BF16)
            if l == 0:
                gs[at, :] = m + b_red[l : l + 1, :]

        if fused and l == 1:
            relay(0)
        over_blocks(middle, unroll=LINE_UNROLL)
        if l == 1:
            break
        if fused:
            pass_on(0, 0)
            for copy in own:
                copy.wait()

        def up(i):
            if fused:

                @pl.when(i == 1)
                def _():
                    for copy in bias_fetches():
                        copy.wait()
                    passed(0, 0)

            def second_fetch(block):
                if fused:
                    pl.when((i == 1) & (block == blocks // 2))(functools.partial(pass_on, 0, 1))

            over_blocks(functools.partial(feed_up, i=i, l=0), after=second_fetch, unroll=UP_UNROLL)

        over_shards(0, up)
        prepare(1)
        grid_to_windows(cot, side, True, put_cot)
        over_blocks(functools.partial(lower, l=1))
        if blocked:
            gz_turned[...] = gz[...].T
        if fused:
            passed(0, 1)
        over_shards(0, lambda i: over_blocks(functools.partial(feed_down, i=i, l=0), unroll=2))
        regular_to_shifted(gs, x.at[1], side)

    d_bexp[...] = jnp.zeros(d_bexp.shape, F32)
    if blocked:
        turned[...] = second[1].T
    gs[...] = jnp.zeros(gs.shape, F32)
    if fused:
        relay(1)

    def both_ways(i):
        if fused:

            @pl.when(i == 1)
            def _():
                pass_on(1, 1)
                passed(1, 0)

        over_blocks(functools.partial(feed_up, i=i, l=1), unroll=UP_UNROLL)
        if fused:
            pl.when(i == 0)(functools.partial(pass_on, 1, 0))
            pl.when(i == 1)(functools.partial(passed, 1, 1))
        over_blocks(functools.partial(feed_back, i=i, l=1), unroll=BACK_UNROLL)
        reduce_weights(i, 1)
        expand_weights(i, 1)

    over_shards(0, both_ways)

    def table_back(l):
        krow = iota((SLOTS, 128), 0)
        qlane = iota((SLOTS, 128), 1)
        ahead = (qlane & (PITCH - 1)) >= (krow & (PITCH - 1))
        kept = (ahead & (qlane < SLOTS), jnp.logical_not(ahead) & (qlane < SLOTS))
        lined = []
        for grp in range(GROUPS):
            low = bias_sum[l, grp, :, :128]
            high = jnp.concatenate([bias_sum[l, grp, :, 128:], jnp.zeros((SLOTS, 256 - GQ), F32)], axis=1)
            for j in range(GROUP):
                at = j * SLOTS
                if at + SLOTS <= 128:
                    one = pltpu.roll(low, 128 - at, 1) if at else low
                elif at < 128:
                    one = jnp.where(qlane < 128 - at, pltpu.roll(low, 128 - at, 1), pltpu.roll(high, 128 - at, 1))
                else:
                    one = pltpu.roll(high, (256 - at) % 128, 1)
                lined.append(one)
        picked = [jnp.where(keep, one, 0.0) for keep in kept for one in lined]
        tiles = [one[:PITCH] for one in picked]
        for r in range(1, WIN):
            turned_rows = [pltpu.roll(one[r * PITCH : (r + 1) * PITCH], 128 - r * PITCH, 1) for one in picked]
            tiles = [tile + one for tile, one in zip(tiles, turned_rows)]
        odd = iota((PITCH, 128), 0)
        for step in (1, 2, 4):
            tiles = [jnp.where((odd & step) > 0, pltpu.roll(tile, 128 - step, 1), tile) for tile in tiles]
        for n, tile in enumerate(tiles):
            row = SMALL_TABLE[l] + n // 3
            small[0, row : row + 1, n % 3 * 128 : (n % 3 + 1) * 128] = jnp.sum(tile, axis=0, keepdims=True)


    for l in (1, 0):

        if l == 0:
            over_blocks(functools.partial(lower, l=0))
            if blocked:
                gz_turned[...] = gz[...].T
            over_shards(0, functools.partial(reduce_weights, l=0))
        begin(REDUCE, l)
        ticks(l, AT_REDUCE)
        if l == 0:
            d_bexp[...] = jnp.zeros(d_bexp.shape, F32)

            gs[...] = jnp.zeros(gs.shape, F32)

            def back(i):
                over_blocks(functools.partial(feed_back, i=i, l=0), unroll=BACK_UNROLL)
                for key, names in STEPS.items():
                    if fused and key[:2] == (0, AT_FEED):
                        pl.when(i == key[2])(functools.partial(advance, *names))

            over_shards(0, back)
        span = min(width, ff)
        for n in range(shards * (ff // span)):
            i, c = n // (ff // span), n % (ff // span) * span
            row = n
            if fused:
                row = lax.rem(links.m + i, shards) * (ff // span) + n % (ff // span)
            small[l, pl.ds(SMALL_EXPAND + row, 1), :span] = d_bexp[i, 0:1, c : c + span]

        if l == 0:
            if blocked:
                turned[...] = second[0].T
            over_shards(0, functools.partial(expand_weights, l=0))
        begin(EXPAND, l)
        ticks(l, AT_EXPAND)

        def middle_back(at, l=l):
            dmid, dgain, doffset = norm_back(mid[l, at, :], gain[l, 1:2, :], gs[at, :])
            add_small(l, GAIN_2, dgain)
            add_small(l, OFFSET_2, doffset)
            gm = g[at, :] + dmid
            g[at, :] = gm
            add_small(l, BIAS_OUT, jnp.sum(gm, axis=0, keepdims=True))
            low = gm.astype(BF16)
            gz[at, :] = low
            go[at, :] = dot_nt(low, w_out[l]).astype(BF16)

        over_blocks(middle_back, (l, AT_MIDDLE), unroll=LINE_UNROLL)
        d_mixed = dot_tn(mixed[l], gz[...]).astype(BF16)
        for part in range(PART):
            at = part * part_rows + width
            d_attn[l, at : at + width // PART, :] = d_mixed[part * (width // PART) : (part + 1) * (width // PART)]
        bias_sum[l] = jnp.zeros(bias_sum.shape[1:], F32)
        turned[...] = normed[l].T

        def attend_back(i, carry, grp, l=l):
            count = windows // 2
            at = pl.ds(pl.multiple_of(i * count * SLOTS, count * SLOTS), count * SLOTS)
            parts = [pl.ds(pl.multiple_of(grp * width + p * GLANES, GLANES), GLANES) for p in range(3)]
            lanes = pl.ds(pl.multiple_of(grp * GLANES, GLANES), GLANES)
            heres = [slice(w * SLOTS, (w + 1) * SLOTS) for w in range(count)]
            q, k, v = (qkv[l, at, part].astype(F32) for part in parts)
            go_now = go[at, lanes].astype(F32)
            go_all = [expand_heads(go_now[here]) for here in heres]
            dps = [dot_nt(v[here].astype(BF16), one) for one, here in zip(go_all, heres)]
            lows = [probs[l, count * i + w, grp] for w in range(count)]
            dvs = [dot(p, one) for p, one in zip(lows, go_all)]
            ps = [p.astype(F32) for p in lows]
            pds = [p * dp for p, dp in zip(ps, dps)]
            totals = [jnp.sum(pd, axis=0, keepdims=True) for pd in pds]
            dss = [(pd - p * total).astype(BF16) for pd, p, total in zip(pds, ps, totals)]
            dqs = [
                fold_heads(dot_tn(ds, k[here].astype(BF16))) * HEAD_DIM**-0.5 for ds, here in zip(dss, heres)
            ]
            dks = [dot(ds, expand_heads(q[here])) * HEAD_DIM**-0.5 for ds, here in zip(dss, heres)]
            total = bias_sum[l, grp]
            for ds in dss:
                total = total + ds.astype(F32)
            bias_sum[l, grp] = total
            for row, part, made in zip((BIAS_Q, None, BIAS_V), parts, (dqs, dks, dvs)):
                whole = jnp.concatenate(made, axis=0)
                if row is not None:
                    small[l, row : row + 1, lanes] += jnp.sum(whole, axis=0, keepdims=True)
                dqkv[at, part] = whole.astype(BF16)
            for key, names in STEPS.items():
                if fused and key[:2] == (l, AT_ATTEND):
                    pl.when((grp == key[2] // 2) & (i == key[2] % 2))(functools.partial(advance, *names))
            return carry

        def attend_group(grp, carry, l=l):
            lax.fori_loop(0, 2, functools.partial(attend_back, grp=grp), 0)
            at = pl.multiple_of(grp * part_rows, 16)
            cols = pl.ds(pl.multiple_of(grp * width, GLANES), width)
            d_attn[l, pl.ds(at, width), :] = dot(turned[...], dqkv[:, cols]).astype(BF16)
            for g_now in range(GROUPS):

                def after(g_now=g_now):
                    begin(ATTEND, l, g_now)
                    ticks(l, AT_GROUP, g_now)

                if fused:
                    pl.when(grp == g_now)(after)
            return carry

        lax.fori_loop(0, GROUPS, attend_group, 0)

        def input_back(at, l=l):
            ga = dot_nt(dqkv[at, :], w_in[l])
            dx, dgain, doffset = norm_back(x[l, at, :], gain[l, 0:1, :], ga)
            add_small(l, GAIN_1, dgain)
            add_small(l, OFFSET_1, doffset)
            gs[at, :] = g[at, :] + dx

        over_blocks(input_back, (l, AT_INPUT), unroll=LINE_UNROLL)
        if l == 1:
            advance((small_flow(1), 0))
            ticks(l, AT_SUMS)
            shifted_to_regular(gs, g, side)
            ticks(l, AT_PLACED)
        else:
            ticks(l, AT_SUMS)
            for one in range(2):
                table_back(one)
                ticks(l, AT_TABLE, one)
            advance((small_flow(0), 0))
            windows_to_grid(gs, grad_tokens, side, False)
            ticks(l, AT_PLACED)

    def last(at):
        total = mid[1, at, :] + b_red[1:2, :] + dot(hidden[1, 0, at, :], w_red[0, 1])

        def add(i, total):
            return total + dot(hidden[1, i, at, :], w_red[i, 1])

        g[at, :] = lax.fori_loop(1, shards, add, total)

    over_blocks(last)
    windows_to_grid(g, out, side, True)
    ticks(0, AT_OUT)

    advance(*TAIL)
    for k in range(1, 1 + max((flow.steps for flow in flows), default=0)):
        advance(*((n, k) for n, flow in enumerate(flows) if COUNT[n] <= k <= flow.steps))


def lanes_table(lanes):
    layers, heads = lanes.shape[0], lanes.shape[1] // 2
    both = lanes.reshape(layers, 2, heads, 128)
    span = SPAN_SIDE * PITCH

    def square(part, back):
        return jnp.roll(part, back, axis=-1)[..., :span].reshape(layers, heads, SPAN_SIDE, PITCH)

    right = square(both[:, 0], (WIN - 1) * PITCH)[..., :WIN]
    left = square(both[:, 1], WIN * PITCH)[..., PITCH - WIN + 1 :]
    whole = jnp.concatenate([left, right], axis=-1)
    return whole.reshape(layers, heads, SPAN_SIDE * SPAN_SIDE).transpose(0, 2, 1)


def on_device(
    mesh_shape,
    tokens,
    crop_ids,
    norm_gain,
    norm_bias,
    input_proj,
    input_bias,
    position_table,
    output_proj,
    output_bias,
    expand_weight,
    expand_bias,
    reduce_weight,
    reduce_bias,
    cotangent,
):
    _, side, _, width = tokens.shape
    layers, _, ff = expand_weight.shape
    win, shards = mesh_shape
    ids = crop_ids.transpose(1, 0, 2)
    windows = (side // WIN) ** 2
    rows = windows * SLOTS
    attn_rows, feed_rows = 4 * width, 2 * ff
    fused = win % 4 == 0 and attn_rows % (16 * PART * win * shards) == 0 and ff % (16 * win) == 0
    vmem = pl.BlockSpec(memory_space=pltpu.VMEM)
    hbm = pl.BlockSpec(memory_space=pl.ANY)
    if fused:
        w_exp, w_red = expand_weight, reduce_weight
        b_exp = expand_bias
    else:
        w_exp = lax.all_gather(expand_weight, "mlp", axis=0)
        w_red = lax.all_gather(reduce_weight, "mlp", axis=0)
        b_exp = lax.all_gather(expand_bias, "mlp", axis=0).astype(F32)
    scratch = [
        pltpu.VMEM((layers, rows, width), F32),
        pltpu.VMEM((layers, rows, width), BF16),
        pltpu.VMEM((layers, rows, 3 * width), BF16),
        pltpu.VMEM((layers, windows, GROUPS, SLOTS, GQ), BF16),
        pltpu.VMEM((layers, rows, width), BF16),
        pltpu.VMEM((layers, rows, width), F32),
        pltpu.VMEM((layers, rows, width), BF16),
        pltpu.VMEM((layers, shards, rows, ff), BF16),
        pltpu.VMEM((layers, shards, rows, ff), BF16),
        pltpu.VMEM((layers, rows, 128), F32),
        pltpu.VMEM((layers, GROUPS, SLOTS, GQ), F32),
        pltpu.VMEM((layers, GROUPS, SLOTS, GQ), F32),
        pltpu.VMEM((rows, width), F32),
        pltpu.VMEM((rows, width), F32),
        pltpu.VMEM((rows, width), BF16),
        pltpu.VMEM((shards, rows, ff), BF16),
        pltpu.VMEM((rows, 3 * width), BF16),
        pltpu.VMEM((rows, width), BF16),
        pltpu.VMEM((shards, 8, ff), F32),
    ]
    small_shape = (layers, SMALL_ROWS, width)
    scratch += [
        pltpu.VMEM((2, 128, 128), F32),
        pltpu.VMEM((2, 16, 128), F32),
        pltpu.VMEM(input_proj.shape, BF16),
        pltpu.VMEM((width, rows), BF16),
        pltpu.VMEM((width, rows), BF16),
        pltpu.VMEM((128, 256), F32),
        pltpu.VMEM((256, 128), F32),
        pltpu.VMEM((side, 32, 128), F32),
        pltpu.SemaphoreType.DMA((layers * GROUPS * 3,)),
    ]
    if fused:
        plane, depth = 2 * shards, win // 4
        _, shapes = flow_table(mesh_shape, width, ff)
        scratch += [
            pltpu.VMEM((layers, attn_rows, width), BF16),
            pltpu.VMEM((layers, shards, feed_rows, width), BF16),
            pltpu.VMEM(small_shape, F32),
            pltpu.VMEM((shards, layers, width, ff), BF16),
            pltpu.VMEM((shards, 8, ff), F32),
            pltpu.VMEM((shards, layers, ff, width), BF16),
        ]
        scratch += [
            pltpu.VMEM((members, count, width), BF16)
            for count in (SMALL_ROWS, SMALL_EARLY)
            for members in (2, plane, depth)
        ]
        scratch += [pltpu.VMEM(shape, BF16) for group in shapes for shape in group]
        scratch += [
            pltpu.SemaphoreType.DMA((3 + len(shapes),)),
            pltpu.SemaphoreType.DMA((SEMAPHORES,)),
            pltpu.SemaphoreType.DMA((SEMAPHORES,)),
        ]
    outs = pl.pallas_call(
        functools.partial(kernel, side, mesh_shape if fused else None),
        out_shape=(
            jax.ShapeDtypeStruct(tokens.shape[1:], BF16),
            jax.ShapeDtypeStruct(tokens.shape[1:], BF16),
            jax.ShapeDtypeStruct((layers, attn_rows, width), BF16),
            jax.ShapeDtypeStruct((layers, feed_rows, width) if fused else (layers, shards, feed_rows, width), BF16),
            jax.ShapeDtypeStruct(small_shape, F32),
        ),
        in_specs=[vmem] * 4 + [hbm] + [vmem] * 4 + ([hbm, vmem, hbm] if fused else [vmem] * 3) + [vmem] * 2,
        out_specs=[vmem] * 2 + ([hbm] * 2 if fused else [vmem] * 2) + [vmem],
        scratch_shapes=scratch,
        compiler_params=pltpu.CompilerParams(
            vmem_limit_bytes=64 * 1024 * 1024,
            **(dict(collective_id=0, has_side_effects=True) if fused else {}),
        ),
    )(
        tokens[0],
        ids,
        norm_gain,
        norm_bias,
        input_proj,
        input_bias,
        position_table.transpose(2, 0, 1),
        output_proj,
        output_bias,
        w_exp,
        b_exp,
        w_red,
        reduce_bias,
        cotangent[0],
    )
    out, grad_tokens, d_attn, d_feed, small = outs
    if not fused:
        d_attn, small = lax.psum((d_attn, small), ("win", "mlp"))
        d_feed = lax.psum(lax.psum_scatter(d_feed, "mlp", scatter_dimension=1, tiled=False), "win")
    if fused and ff % width == 0 and width % 128 == 0 and side % 2 == 0:
        return finish(out, grad_tokens, d_attn, d_feed, small, side, ff)
    parts = d_attn.reshape(layers, PART, attn_rows // PART, width)
    d_in = jnp.concatenate(
        [parts[:, grp, :width, p * GLANES : (p + 1) * GLANES] for p in range(3) for grp in range(GROUPS)], axis=2
    )
    d_out = parts[:, :, width:].reshape(layers, width, width)
    if ff % width == 0:
        d_exp, d_red = (
            jnp.concatenate([d_feed[:, c : c + width] for c in range(first, first + ff, width)], axis=2)
            for first in (0, ff)
        )
        d_red = d_red.swapaxes(1, 2)
    else:
        d_exp, d_red = d_feed[:, :ff].swapaxes(1, 2), d_feed[:, ff:]
    span = min(width, ff)
    d_bexp = small[:, SMALL_EXPAND : SMALL_EXPAND + shards * (ff // span), :span].reshape(layers, shards, ff)
    d_bexp = lax.dynamic_index_in_dim(d_bexp, lax.axis_index("mlp"), 1, keepdims=False)
    d_table = jnp.stack([small[0, SMALL_TABLE[l] : SMALL_TABLE[l] + 8] for l in range(layers)])
    return (
        out[None],
        grad_tokens[None],
        small[:, 0:2],
        small[:, 2:4],
        d_in.astype(F32),
        small[:, 4:6],
        lanes_table(d_table.reshape(layers, 2 * HEADS, 128)),
        d_out.astype(F32),
        small[:, 6],
        d_exp.astype(F32),
        d_bexp,
        d_red.astype(F32),
        small[:, 7],
    )


def finish_kernel(blocks, *refs):
    attn, feed, out, grad_tokens, small = refs[:5]
    (out_to, grad_to, gain, offset, d_in, b_in, table, d_out, b_out, d_exp, b_exp, d_red, b_red) = refs[5:18]
    tall, a_held, f_held, in_held, out_held, exp_held, red_held, grid_held, in_sems, out_sems = refs[18:]
    layers, _, width = attn.shape
    part = width + width // PART
    ff = blocks * width
    passing = [
        pltpu.make_async_copy(out, grid_held.at[0], in_sems.at[2 * layers]),
        pltpu.make_async_copy(grad_tokens, grid_held.at[1], in_sems.at[2 * layers + 1]),
    ]
    arriving = [
        [
            pltpu.make_async_copy(attn.at[l], a_held.at[l], in_sems.at[2 * l]),
            pltpu.make_async_copy(feed.at[l], f_held.at[l], in_sems.at[2 * l + 1]),
        ]
        for l in range(layers)
    ]
    for pair in arriving:
        for copy in pair:
            copy.start()
    for copy in passing:
        copy.start()
    leaving = []

    def leave(src, dst):
        copy = pltpu.make_async_copy(src, dst, out_sems.at[len(leaving)])
        copy.start()
        leaving.append(copy)

    for l in range(layers):
        arriving[l][0].wait()
        for grp in range(GROUPS):
            first = grp * part
            for p in range(3):
                at = p * width + grp * GLANES
                in_held[l, :, at : at + GLANES] = a_held[l, first : first + width, p * GLANES : (p + 1) * GLANES].astype(F32)
            rows = width // PART
            out_held[l, grp * rows : (grp + 1) * rows, :] = a_held[l, first + width : first + part, :].astype(F32)
        leave(in_held.at[l], d_in.at[l])
        passing[l].wait()
        leave(grid_held.at[l], (out_to, grad_to)[l].at[0])
        leave(out_held.at[l], d_out.at[l])
        arriving[l][1].wait()
        for b in range(blocks):
            cols = slice(b * width, (b + 1) * width)
            exp_held[l, :, cols] = f_held[l, cols, :].astype(F32)
        leave(exp_held.at[l], d_exp.at[l])
        for b in range(blocks):
            cols = slice(b * width, (b + 1) * width)
            red_held[l, cols, :] = f_held[l, ff + b * width : ff + (b + 1) * width, :].astype(F32).T
        leave(red_held.at[l], d_red.at[l])

    for l in range(2):
        gain[l] = small[l, 0:2, :]
        offset[l] = small[l, 2:4, :]
        b_in[l] = small[l, 4:6, :]
        b_out[l : l + 1, :] = small[l, 6:7, :]
        b_red[l : l + 1, :] = small[l, 7:8, :]
        for b in range(blocks):
            row = SMALL_EXPAND + lax.axis_index("mlp") * blocks + b
            b_exp[l : l + 1, b * width : (b + 1) * width] = small[l, pl.ds(row, 1), :]
        turned = []
        for s in range(2):
            heads = []
            for h in range(HEADS):
                n = s * HEADS + h
                row = SMALL_TABLE[l] + n // 3
                heads.append(small[0, row : row + 1, n % 3 * 128 : (n % 3 + 1) * 128])
            heads.append(jnp.zeros((128 - HEADS, 128), F32))
            turned.append(jnp.concatenate(heads, axis=0).T)
        tall[...] = jnp.zeros(tall.shape, F32)
        for lane, entry, count, s in table_spans():
            tall[entry : entry + count, :] = turned[s][lane : lane + count]
        wide = tall[...].T
        for h in range(HEADS):
            table[h, l : l + 1, :] = wide[h : h + 1, : table.shape[2]]
    for copy in leaving:
        copy.wait()


def finish(out, grad_tokens, d_attn, d_feed, small, side, ff):
    layers, _, width = d_attn.shape
    blocks = ff // width
    vmem = pl.BlockSpec(memory_space=pltpu.VMEM)
    hbm = pl.BlockSpec(memory_space=pl.ANY)
    span = SPAN_SIDE * SPAN_SIDE
    shape = lambda *dims: jax.ShapeDtypeStruct(dims, F32)
    grid_shape = jax.ShapeDtypeStruct((1, side, side, width), BF16)
    large = ((layers, width, 3 * width), (layers, width, width), (layers, width, ff), (layers, ff, width))
    made = pl.pallas_call(
        functools.partial(finish_kernel, blocks),
        in_specs=[hbm] * 4 + [vmem],
        out_specs=[hbm, hbm, vmem, vmem, hbm, vmem, vmem, hbm, vmem, hbm, vmem, hbm, vmem],
        out_shape=[
            grid_shape,
            grid_shape,
            shape(layers, 2, width),
            shape(layers, 2, width),
            shape(*large[0]),
            shape(layers, 2, width),
            shape(HEADS, layers, span),
            shape(*large[1]),
            shape(layers, width),
            shape(*large[2]),
            shape(layers, ff),
            shape(*large[3]),
            shape(layers, width),
        ],
        scratch_shapes=[
            pltpu.VMEM((256, 128), F32),
            pltpu.VMEM(d_attn.shape, BF16),
            pltpu.VMEM(d_feed.shape, BF16),
            *(pltpu.VMEM(dims, F32) for dims in large),
            pltpu.VMEM((2,) + out.shape, BF16),
            pltpu.SemaphoreType.DMA((2 + 2 * layers,)),
            pltpu.SemaphoreType.DMA((2 + 4 * layers,)),
        ],
        compiler_params=pltpu.CompilerParams(vmem_limit_bytes=64 * 1024 * 1024),
    )(d_attn, d_feed, out, grad_tokens, small)
    return (*made[:6], made[6].transpose(1, 2, 0), *made[7:])


def solution(mesh):
    tokens = P(("win", "mlp"), None, None, None)
    placed = (
        tokens,
        P(("win", "mlp"), None, None),
        P(),
        P(),
        P(),
        P(),
        P(),
        P(),
        P(),
        P(None, None, "mlp"),
        P(None, "mlp"),
        P(None, "mlp", None),
        P(),
        tokens,
    )
    return jax.shard_map(
        functools.partial(on_device, (mesh.shape["win"], mesh.shape["mlp"])),
        mesh=mesh,
        in_specs=placed,
        out_specs=(
            tokens,
            tokens,
            P(),
            P(),
            P(),
            P(),
            P(),
            P(),
            P(),
            P(None, None, "mlp"),
            P(None, "mlp"),
            P(None, "mlp", None),
            P(),
        ),
        check_vma=False,
    )
```
